32 devices in a mesh: tok: 8 (over z, y), grp: 4 (over x, core).
Axes of the slice: x: 2, y: 2, z: 4, core: 2. Of those that a mesh axis runs over, the one named last changes fastest.
Arguments:
- tokens: bfloat16 [12288, 1024], P(('tok', 'grp')), may hold values from -6 to 6
- norm_gain: float32 [1024], replicated, may hold values from 0.25 to 1.75
- input_weight: bfloat16 [1024, 3072], P('tok', 'grp')
- output_weight: bfloat16 [1024, 1024], P('tok', 'grp'), may hold values from -2 to 2
- segment_ids: int32 [12288], replicated, may hold values from 0 to 23, never falling along the last dimension, each value on 1 to 1024 neighbouring positions
- page_owner: int32 [3072, 1], P(('tok', 'grp')), may hold values from 0 to 7; in each aligned block of 96 rows (0 to 95, 96 to 191, ...) at most 24 rows name the same one
Outputs:
- attended: bfloat16 [12288, 1024], P(('tok', 'grp'))
- cache_pages: bfloat16 [6144, 8192], P(('tok', 'grp'))
The draws below stay inside these ranges and needn't reach their ends.
Inputs may be any that keep to these rules, and one draw needn't show every extreme that they name: `segment_ids`: segment ids never fall along the pack; every id occurs on 1 to 1024 consecutive tokens, and some document has exactly 1024 tokens. `page_owner`: within the 96 pages of one device no owner is named more than 24 times, and in some device one owner is named exactly 24 times.
All inputs are finite; a program needn't handle non-finite values.
Results may differ from the reference program's by a relative error of at most 0.0089.
Values may be sent and summed in bfloat16 or wider, within the bound.
No kernel may reach another device: no remote copies, remote signals or barrier semaphores. Data moves between devices by JAX's collectives and lax.ppermute only.
A program may use at most 128 MiB of HBM per device.

```python
import math
import jax
import jax.numpy as jnp
import numpy as np
from jax import lax

D = 1024
H = 16
TOK_DEV = 384
SPAN = 1024
PAGE = 4
TOKENS = 12288
DOCS = 24
PAGES_DEV = 96
PAGES = 3072
CAP = 24
REACH = 3
N_TOK = 8
N_GRP = 4


def draw_input_weight(key, part):
    first_key = jax.random.fold_in(jax.random.fold_in(key, 11), 0)
    entries = jax.random.normal(first_key, (D, 3 * D), jnp.float32) * D ** (-0.5)
    return entries.astype(jnp.bfloat16)


def levels(stream_key, dims, cuts, low, largest):
    def one(axis_at, shards_of):
        draws = jax.random.uniform(jax.random.fold_in(jax.random.fold_in(stream_key, 6), axis_at), (shards_of,), jnp.float32, low / len(cuts), largest / len(cuts))
        return jnp.repeat(jnp.exp(draws), dims[axis_at] // shards_of).reshape((-1,) + (1,) * (len(dims) - axis_at - 1))

    level = one(*cuts[0])
    for cut in cuts[1:]:
        level = level * one(*cut)
    return level


def length_profile(amount, total, bound, slope):
    weights = [(1 << 20) // math.isqrt(standing ** slope) + 1 for standing in range(2, amount + 1)]
    rest, counts = total - bound - (amount - 1), [1] * (amount - 1)
    while rest > 0:
        free = [i for i in range(amount - 1) if counts[i] < bound]
        whole, budget = sum([weights[i] for i in free]), rest
        for i in free:
            more = min(bound - counts[i], max(1, budget * weights[i] // whole), rest)
            counts[i] = counts[i] + more
            rest = rest - more
    return np.array([bound] + counts)


def ragged(rng, count, total, most, skew):
    if count == 2:
        one = jax.random.randint(rng, (), max(1, total - most), min(most, total - 1) + 1)
        return jnp.stack([one, total - one])
    tallies = jnp.asarray(length_profile(count, total, most, skew), jnp.int32)
    couples = (count - 1) // 2
    giver, receiver = tallies[1:1 + 2 * couples:2], tallies[2:2 + 2 * couples:2]
    room = jnp.minimum(giver - 1, most - receiver)
    shifted = jax.random.randint(jax.random.fold_in(rng, 1), (couples,), 0, 1 << 20) % (room + 1)
    tallies = tallies.at[1:1 + 2 * couples:2].set(giver - shifted).at[2:2 + 2 * couples:2].set(receiver + shifted)
    return tallies[jax.random.permutation(jax.random.fold_in(rng, 2), count)]


def shared_out(rng, own, number, rows, number_of, top, limit, skew):
    order = jax.random.permutation(rng, number_of)
    heavy_load, ordinary = load_shares(number_of, rows * top, limit, skew, True), load_shares(number_of, rows * top, limit, skew, False)
    places = jnp.arange(number_of)

    def named(lengths, turn):
        used = int((lengths > 0).sum())
        fixed = max(1, used // 4)
        moved = fixed + (places - fixed + turn * (used - fixed)) % max(1, number_of - fixed)
        return jnp.zeros((number_of,), jnp.int32).at[order[jnp.where(places < fixed, places, moved)]].set(jnp.asarray(lengths, jnp.int32))

    lengths = jnp.where(number % 4 == 0, named(heavy_load, number // 4), named(ordinary, number - number // 4 - 1))
    mixed = jax.random.permutation(jax.random.fold_in(own, 3), number_of)
    donor, taker = mixed[0:number_of // 2 * 2:2], mixed[1:number_of // 2 * 2:2]
    slack = jnp.minimum(lengths[donor] - 1, limit - lengths[taker]) // 2
    slack = jnp.where((donor == order[0]) | (taker == order[0]) | (lengths[taker] == 0), 0, jnp.maximum(slack, 0))
    moved = jax.random.randint(jax.random.fold_in(own, 4), (number_of // 2,), 0, 1 << 20) % (slack + 1)
    lengths = lengths.at[donor].add(-moved).at[taker].add(moved)
    members = jnp.searchsorted(jnp.cumsum(lengths), jnp.arange(rows * top), side="right").astype(jnp.int32)
    table = members.reshape(top, rows).T
    table = table[jax.random.permutation(jax.random.fold_in(own, 1), rows)]
    turn = jax.random.randint(jax.random.fold_in(own, 2), (rows, 1), 0, top)
    return jnp.take_along_axis(table, (jnp.arange(top)[None, :] + turn) % top, axis=1)


def load_shares(amount, total, most, lean, full):
    portions = [(1 << 20) // math.isqrt(standing ** lean) + 1 for standing in range(1, amount + 1)]
    largest = most if full else min(most, max(-(-total // amount), total * portions[0] // sum(portions)))
    least = 1 if total - largest >= amount - 1 else 0
    counts, rest = [largest] + [least] * (amount - 1), total - largest - least * (amount - 1)
    while rest > 0:
        movable = [i for i in range(1, amount) if counts[i] < largest] or [i for i in range(1, amount) if counts[i] < most]
        mass, budget = sum([portions[i] for i in movable]), rest
        for i in movable:
            more = min(most - counts[i], max(1, budget * portions[i] // mass), rest)
            counts[i] = counts[i] + more
            rest = rest - more
    return np.array(counts)


def centred(key, extent, width, bound, pieces=(), kind=jnp.bfloat16):
    level = levels(key, extent, pieces, -0.22, 0.18) if pieces else 1.0
    array = jax.random.normal(key, extent, jnp.float32) * width * level
    return jnp.minimum(jnp.maximum(array, -bound), bound).astype(kind)


def setup_inputs(seed: int = 0) -> dict:
    key_list = jax.random.split(jax.random.key(seed), 7)
    tokens = centred(key_list[0], (TOKENS, D), 1.0, 6.0, ((0, 32),))
    norm_gain = jnp.clip(1.0 + 0.15 * jax.random.normal(key_list[1], (D,), jnp.float32), 0.25, 1.75)
    input_weight = draw_input_weight(jax.random.fold_in(key_list[6], 71), 0)
    output_weight = centred(key_list[3], (D, D), (max(1, D // 128)) ** -0.5, 2.0, ((0, 8), (1, 4)))
    segment_ids = jnp.searchsorted(jnp.cumsum(ragged(key_list[4], DOCS, TOKENS, SPAN, 2)), jnp.arange(TOKENS), side="right").astype(jnp.int32)
    page_owner_keys = jax.random.split(jax.random.fold_in(key_list[5], 1), PAGES // PAGES_DEV)
    page_owner_turns = jax.random.permutation(jax.random.fold_in(key_list[5], 3), PAGES // PAGES_DEV)
    page_owner = jax.vmap(lambda own, number: shared_out(jax.random.fold_in(key_list[5], 2), own, number, PAGES_DEV, N_TOK, 1, CAP, 2))(page_owner_keys, page_owner_turns).reshape((PAGES, 1))
    return {"tokens": tokens, "norm_gain": norm_gain, "input_weight": input_weight, "output_weight": output_weight, "segment_ids": segment_ids, "page_owner": page_owner}


NEG_FILL = -1e+30
ROPE_BASE = 160000.0
EPSILON = 1e-05

def layer_norm(tokens, norm_gain):
    values = tokens.astype(jnp.float32)
    center = lax.optimization_barrier(jnp.mean(values, axis=-1, keepdims=True))
    spread = lax.optimization_barrier(jnp.mean(jnp.square(values - center), axis=-1, keepdims=True))
    return ((values - center) * lax.rsqrt(spread + EPSILON) * norm_gain.astype(jnp.float32)).astype(jnp.bfloat16)

def rotate(block_part, positions, head_count):
    row_count = block_part.shape[0]
    head_dim = block_part.shape[1] // head_count
    half_dim = head_dim // 2
    shaped = block_part.reshape(row_count, head_count, head_dim)
    inverse = 1.0 / ROPE_BASE ** (jnp.arange(half_dim, dtype=jnp.float32) * 2.0 / head_dim)
    angles = positions.astype(jnp.float32)[:, None] * inverse[None, :]
    cosine = jnp.concatenate([jnp.cos(angles), jnp.cos(angles)], axis=1)[:, None, :]
    sine_table = jnp.concatenate([jnp.sin(angles), jnp.sin(angles)], axis=1)[:, None, :]
    turned = jnp.concatenate([-shaped[..., half_dim:], shaped[..., :half_dim]], axis=-1)
    return (shaped * cosine + turned * sine_table).reshape(row_count, head_count * head_dim).astype(jnp.bfloat16)

def positions_of(segment_ids, own_ids, first_row):
    starts = jnp.searchsorted(segment_ids, own_ids, side='left').astype(jnp.int32)
    return first_row + jnp.arange(own_ids.shape[0], dtype=jnp.int32) - starts

def attend_block(queries, key_window, value_window, query_ids, window_ids, head_count):
    row_count = queries.shape[0]
    window_len = key_window.shape[0]
    head_dim = queries.shape[1] // head_count
    score_scale = head_dim ** (-0.5)
    query_heads = queries.reshape(row_count, head_count, head_dim).astype(jnp.float32)
    key_heads = key_window.reshape(window_len, head_count, head_dim).astype(jnp.float32)
    value_heads = value_window.reshape(window_len, head_count, head_dim).astype(jnp.float32)
    scores = jnp.einsum('tnd,snd->nts', query_heads, key_heads) * score_scale
    allowed = query_ids[:, None] == window_ids[None, :]
    scores = jnp.where(allowed[None], scores, NEG_FILL)
    row_peak = lax.optimization_barrier(jnp.max(scores, axis=-1, keepdims=True))
    exponent = jnp.exp(scores - row_peak)
    row_total = lax.optimization_barrier(jnp.sum(exponent, axis=-1))
    weights = exponent.astype(jnp.bfloat16)
    mixed_rows = jnp.einsum('nts,snd->tnd', weights.astype(jnp.float32), value_heads)
    mixed_rows = mixed_rows / jnp.transpose(row_total)[:, :, None]
    return mixed_rows.reshape(row_count, head_count * head_dim).astype(jnp.bfloat16)

def reference(tokens, norm_gain, input_weight, output_weight, segment_ids, page_owner):
    device_count = N_TOK * N_GRP
    normed = layer_norm(tokens, norm_gain)

    def project(block_index):
        first_row = block_index * TOK_DEV
        row_block = lax.dynamic_slice_in_dim(normed, first_row, TOK_DEV, 0)
        joined = jnp.dot(row_block, input_weight, preferred_element_type=jnp.float32)
        own_ids = lax.dynamic_slice_in_dim(segment_ids, first_row, TOK_DEV, 0)
        positions = positions_of(segment_ids, own_ids, first_row)
        queries = rotate(joined[:, :D], positions, H)
        key_rows = rotate(joined[:, D:2 * D], positions, H)
        value_rows = joined[:, 2 * D:].astype(jnp.bfloat16)
        return (queries, key_rows, value_rows)
    indices = jnp.arange(device_count, dtype=jnp.int32)
    queries, key_rows, value_rows = lax.map(project, indices)
    keys_flat = key_rows.reshape(TOKENS, D)
    values_flat = value_rows.reshape(TOKENS, D)
    margin = REACH * TOK_DEV
    keys_pad = jnp.pad(keys_flat, ((margin, margin), (0, 0)))
    values_pad = jnp.pad(values_flat, ((margin, margin), (0, 0)))
    ids_pad = jnp.pad(segment_ids, (margin, margin), constant_values=-1)
    window_len = (2 * REACH + 1) * TOK_DEV

    def attend_one(operands):
        block_index, query_block = operands
        first_row = block_index * TOK_DEV
        key_window = lax.dynamic_slice_in_dim(keys_pad, first_row, window_len, 0)
        value_window = lax.dynamic_slice_in_dim(values_pad, first_row, window_len, 0)
        window_ids = lax.dynamic_slice_in_dim(ids_pad, first_row, window_len, 0)
        query_ids = lax.dynamic_slice_in_dim(segment_ids, first_row, TOK_DEV, 0)
        return attend_block(query_block, key_window, value_window, query_ids, window_ids, H)
    mixed_all = lax.map(attend_one, (indices, queries)).reshape(TOKENS, D)
    attended = jnp.dot(mixed_all, output_weight, preferred_element_type=jnp.float32).astype(jnp.bfloat16)
    page_rows = jnp.concatenate([keys_flat, values_flat], axis=1).reshape(PAGES, 2 * PAGE * D)
    owners = page_owner[:, 0].reshape(device_count, PAGES_DEV)
    same_owner = owners[:, :, None] == owners[:, None, :]
    earlier_mask = jnp.arange(PAGES_DEV)[:, None] > jnp.arange(PAGES_DEV)[None, :]
    page_ranks = lax.optimization_barrier(jnp.sum((same_owner & earlier_mask[None]).astype(jnp.int32), axis=2))
    source = jnp.arange(device_count, dtype=jnp.int32)[:, None]
    target = (owners * N_GRP + source % N_GRP) * (N_TOK * CAP) + source // N_GRP * CAP + page_ranks
    cache_pages = jnp.zeros((device_count * N_TOK * CAP, 2 * PAGE * D), jnp.bfloat16)
    cache_pages = cache_pages.at[target.reshape(-1)].set(page_rows)
    return (attended, cache_pages)
```

```python
import functools
import math

import jax
import jax.numpy as jnp
from jax import lax
from jax.experimental import pallas as pl
from jax.experimental.pallas import tpu as pltpu
from jax.sharding import PartitionSpec as P

H = 16
SPAN = 1024
PAGE = 4

NEG_FILL = -1e30
ROPE_BASE = 160000.0
EPSILON = 1e-05
TILE = 256
CHUNK = 512
PARTS = 3
VMEM_LIMIT = 48 * 1024 * 1024


def flipped(value, axis, bit):
    count = lax.axis_size(axis)
    return lax.ppermute(value, axis, [(source, source ^ bit) for source in range(count)])


def shifted(value, axis, steps):
    count = lax.axis_size(axis)
    initial, last = (max(0, -steps), min(count, count - steps))
    return lax.ppermute(value, axis, [(source, source + steps) for source in range(initial, last)])


def flip_gather(value, axis):
    blocks = {0: value}
    bit = lax.axis_size(axis) // 2
    while bit:
        for distance in list(blocks):
            blocks[distance ^ bit] = flipped(blocks[distance], axis, bit)
        bit //= 2
    return [blocks[distance] for distance in range(lax.axis_size(axis))]


def project_kernel(group_size, peers, capacity, meta, *refs):
    tokens = refs[:group_size]
    gain, weight, cosine, sine, slots = refs[group_size : group_size + 5]
    query_out, chunk_a, chunk_b, chunk_c, send_out = refs[group_size + 5 : group_size + 10]
    normed, pairs, page_source = refs[group_size + 10 :]
    step = pl.program_id(0)
    rows = normed.shape[0]
    width = query_out.shape[1]

    for distance in range(group_size):

        @pl.when(step == distance)
        def _():
            values = tokens[distance][...].astype(jnp.float32)
            centred = values - jnp.mean(values, axis=-1, keepdims=True)
            spread = jnp.mean(jnp.square(centred), axis=-1, keepdims=True)
            normed[...] = (centred * lax.rsqrt(spread + EPSILON) * gain[...]).astype(jnp.bfloat16)

    def part(number):
        columns = pl.ds(pl.multiple_of(meta[1 + number] * width, width), width)
        return jnp.dot(normed[...], weight[:, columns], preferred_element_type=jnp.float32)

    first_half = lax.rem(lax.broadcasted_iota(jnp.int32, (rows, 128), 1), 64) < 32

    def rotate(values):
        turned = []
        for start in range(0, width, 128):
            piece = values[:, start : start + 128]
            partner = jnp.where(first_half, pltpu.roll(piece, 96, 1), pltpu.roll(piece, 32, 1))
            turned.append(piece * cosine[...] + partner * sine[...])
        return jnp.concatenate(turned, axis=1).astype(jnp.bfloat16)

    query_out[...] = rotate(part(0))
    keys = rotate(part(1))
    values = part(2).astype(jnp.bfloat16)
    block = meta[0] ^ step
    own_rows = pl.ds(pl.multiple_of(block * rows, 128), rows)
    pairs[own_rows, :width] = keys
    pairs[own_rows, width:] = values
    lane_groups = 2 * width // 128
    for lane_group in range(lane_groups):
        source = keys if lane_group < lane_groups // 2 else values
        start = lane_group % (lane_groups // 2) * 128
        page_source[lane_group] = source[:, start : start + 128].astype(jnp.float32)

    pages = rows // PAGE
    slot_count = peers * capacity
    chosen = (
        lax.broadcasted_iota(jnp.int32, (slot_count, pages), 0) == slots[0]
    ).astype(jnp.bfloat16)
    for turn in range(PAGE):
        page_part = jnp.concatenate(
            [
                page_source[lane_group, pl.ds(turn, pages, stride=PAGE), :].astype(jnp.bfloat16)
                for lane_group in range(lane_groups)
            ],
            axis=1,
        )
        placed = jnp.dot(chosen, page_part, preferred_element_type=jnp.float32)
        columns = slice(turn * 2 * width, (turn + 1) * 2 * width)
        for peer in range(peers):
            send_out[peer, 0, :, columns] = placed[
                peer * capacity : (peer + 1) * capacity
            ].astype(jnp.bfloat16)

    @pl.when(step == group_size - 1)
    def _():
        for number, chunk in enumerate((chunk_a, chunk_b, chunk_c)):
            chunk[...] = pairs[number * CHUNK : (number + 1) * CHUNK, :]


def project(meta, tokens, gain, weight, cosine, sine, slots, peers, capacity):
    group_size = len(tokens)
    rows, model_width = tokens[0].shape
    group_rows = rows * group_size
    width = weight.shape[1] // PARTS
    whole = lambda shape: pl.BlockSpec(shape, lambda i, m: (0,) * len(shape))
    block = lambda shape: pl.BlockSpec(shape, lambda i, m: (m[0] ^ i, 0))
    pages = rows // PAGE
    flops = 2 * group_rows * model_width * PARTS * width
    return pl.pallas_call(
        functools.partial(project_kernel, group_size, peers, capacity),
        grid_spec=pltpu.PrefetchScalarGridSpec(
            num_scalar_prefetch=1,
            grid=(group_size,),
            in_specs=[whole((rows, model_width))] * group_size
            + [
                whole((1, model_width)),
                whole(weight.shape),
                block((rows, 128)),
                block((rows, 128)),
                pl.BlockSpec((1, 1, pages), lambda i, m: (m[0] ^ i, 0, 0)),
            ],
            out_specs=[block((rows, width))]
            + [whole((CHUNK, 2 * width))] * 3
            + [
                pl.BlockSpec(
                    (peers, 1, capacity, 2 * PAGE * width), lambda i, m: (0, m[0] ^ i, 0, 0)
                )
            ],
            scratch_shapes=[
                pltpu.VMEM((rows, model_width), jnp.bfloat16),
                pltpu.VMEM((group_rows, 2 * width), jnp.bfloat16),
                pltpu.VMEM((2 * width // 128, rows, 128), jnp.float32),
            ],
        ),
        out_shape=[jax.ShapeDtypeStruct((group_rows, width), jnp.bfloat16)]
        + [jax.ShapeDtypeStruct((CHUNK, 2 * width), jnp.bfloat16)] * 3
        + [
            jax.ShapeDtypeStruct((peers, group_size, capacity, 2 * PAGE * width), jnp.bfloat16)
        ],
        compiler_params=pltpu.CompilerParams(vmem_limit_bytes=VMEM_LIMIT),
        cost_estimate=pl.CostEstimate(flops=flops, bytes_accessed=10 << 20, transcendentals=0),
        name="project",
    )(meta, *tokens, gain, weight, cosine, sine, slots)


def attend_kernel(head_count, meta, *refs):
    queries, starts, ends = refs[:3]
    chunks = refs[3:10]
    same_out, other_out = refs[10:12]
    pairs, masked, total, mixed, sems = refs[12:]
    step = pl.program_id(0)
    width = queries.shape[1]
    head_dim = width // head_count
    rows = same_out.shape[0]
    scale = head_dim ** (-0.5) * math.log2(math.e)

    @pl.when(step == 0)
    def _():
        copies = [
            pltpu.make_async_copy(
                chunk, pairs.at[pl.ds(number * CHUNK, CHUNK), :], sems.at[number]
            )
            for number, chunk in enumerate(chunks)
        ]
        for copy in copies:
            copy.start()
        for copy in copies:
            copy.wait()

    lane_head = lax.broadcasted_iota(jnp.int32, (TILE, width), 1) // head_dim
    for head in range(head_count):
        masked[head] = jnp.where(lane_head == head, queries[...], jnp.zeros((), jnp.bfloat16))
    total[...] = jnp.zeros_like(total)
    first, last = starts[...], ends[...]

    def visit(number, carry):
        peaks, sums = carry
        base = pl.multiple_of(number * TILE, TILE)
        keys = pairs[pl.ds(base, TILE), :width]
        values = pairs[pl.ds(base, TILE), width:].T
        index = base + lax.broadcasted_iota(jnp.int32, (TILE, TILE), 0)
        allowed = (index >= first) & (index < last)
        new_peaks, new_sums = [], []
        for head in range(head_count):
            scores = lax.dot_general(
                keys, masked[head], (((1,), (1,)), ((), ())), preferred_element_type=jnp.float32
            )
            scores = jnp.where(allowed, scores * scale, NEG_FILL)
            peak = jnp.maximum(peaks[head], jnp.max(scores, axis=0, keepdims=True))
            fade = jnp.exp2(peaks[head] - peak)
            exponent = jnp.exp2(scores - peak)
            new_peaks.append(peak)
            new_sums.append(sums[head] * fade + jnp.sum(exponent, axis=0, keepdims=True))
            dims = slice(head * head_dim, (head + 1) * head_dim)
            total[dims, :] = total[dims, :] * fade + jnp.dot(
                values[dims, :],
                exponent.astype(jnp.bfloat16),
                preferred_element_type=jnp.float32,
            )
        return tuple(new_peaks), tuple(new_sums)

    tile = meta[1] + step
    nothing = tuple(jnp.zeros((1, TILE), jnp.float32) for _ in range(head_count))
    lowest = tuple(jnp.full((1, TILE), NEG_FILL, jnp.float32) for _ in range(head_count))
    _, sums = lax.fori_loop(meta[2 + 2 * tile], meta[3 + 2 * tile], visit, (lowest, nothing))
    for head in range(head_count):
        dims = slice(head * head_dim, (head + 1) * head_dim)
        total[dims, :] = total[dims, :] / sums[head]
    mixed[pl.ds(pl.multiple_of(step * TILE, TILE), TILE), :] = total[...].T.astype(jnp.bfloat16)

    @pl.when(step == pl.num_programs(0) - 1)
    def _():
        same = meta[0]
        same_out[...] = mixed[pl.ds(pl.multiple_of(same * rows, 128), rows), :]
        other_out[...] = mixed[pl.ds(pl.multiple_of((1 - same) * rows, 128), rows), :]


def attend(meta, queries, starts, ends, chunks, rows, head_count):
    width = queries.shape[1]
    tiles = 2 * rows // TILE
    whole = pl.BlockSpec((rows, width), lambda i, m: (0, 0))
    window_rows = len(chunks) * CHUNK
    return pl.pallas_call(
        functools.partial(attend_kernel, head_count),
        grid_spec=pltpu.PrefetchScalarGridSpec(
            num_scalar_prefetch=1,
            grid=(tiles,),
            in_specs=[
                pl.BlockSpec((TILE, width), lambda i, m: (m[1] + i, 0)),
                pl.BlockSpec((1, TILE), lambda i, m: (0, m[1] + i)),
                pl.BlockSpec((1, TILE), lambda i, m: (0, m[1] + i)),
            ]
            + [pl.BlockSpec(memory_space=pl.ANY)] * len(chunks),
            out_specs=[whole, whole],
            scratch_shapes=[
                pltpu.VMEM((window_rows, 2 * width), jnp.bfloat16),
                pltpu.VMEM((head_count, TILE, width), jnp.bfloat16),
                pltpu.VMEM((width, TILE), jnp.float32),
                pltpu.VMEM((2 * rows, width), jnp.bfloat16),
                pltpu.SemaphoreType.DMA((len(chunks),)),
            ],
        ),
        out_shape=[jax.ShapeDtypeStruct((rows, width), jnp.bfloat16)] * 2,
        compiler_params=pltpu.CompilerParams(vmem_limit_bytes=VMEM_LIMIT),
        cost_estimate=pl.CostEstimate(
            flops=8 * rows * 1024 * width,
            bytes_accessed=5 << 20,
            transcendentals=2 * rows * 1024 * head_count,
        ),
        name="attend",
    )(meta, queries, starts, ends, *chunks)


def output_kernel(group_size, meta, *refs):
    mixed, weight, result = refs[:group_size], refs[group_size], refs[group_size + 1]
    width = mixed[0].shape[1]
    total = None
    for distance in range(group_size):
        depth = pl.ds(pl.multiple_of((meta[0] ^ distance) * width, width), width)
        term = jnp.dot(mixed[distance][...], weight[depth, :], preferred_element_type=jnp.float32)
        total = term if total is None else total + term
    result[...] = total.astype(jnp.bfloat16)


def output_projection(meta, mixed, weight):
    rows, width = mixed[0].shape
    depth, columns = weight.shape
    tile = min(columns, 512)
    return pl.pallas_call(
        functools.partial(output_kernel, len(mixed)),
        grid_spec=pltpu.PrefetchScalarGridSpec(
            num_scalar_prefetch=1,
            grid=(columns // tile,),
            in_specs=[pl.BlockSpec((rows, width), lambda i, m: (0, 0))] * len(mixed)
            + [pl.BlockSpec((depth, tile), lambda i, m: (0, i))],
            out_specs=pl.BlockSpec((rows, tile), lambda i, m: (0, i)),
        ),
        out_shape=jax.ShapeDtypeStruct((rows, columns), jnp.bfloat16),
        compiler_params=pltpu.CompilerParams(vmem_limit_bytes=VMEM_LIMIT),
        cost_estimate=pl.CostEstimate(
            flops=2 * rows * depth * columns, bytes_accessed=4 << 20, transcendentals=0
        ),
        name="output_projection",
    )(meta, *mixed, weight)


def unpack_kernel(group_size, received, pages):
    width = received.shape[-1] // (2 * PAGE)
    for source in range(group_size):
        for turn in range(2 * PAGE):
            start = turn * group_size * width + source * width
            pages[0, :, start : start + width] = received[
                0, source, :, turn * width : (turn + 1) * width
            ]


def unpack(received):
    peers, group_size, capacity, part = received.shape
    return pl.pallas_call(
        functools.partial(unpack_kernel, group_size),
        grid=(peers,),
        in_specs=[pl.BlockSpec((1, group_size, capacity, part), lambda i: (i, 0, 0, 0))],
        out_specs=pl.BlockSpec((1, capacity, group_size * part), lambda i: (i, 0, 0)),
        out_shape=jax.ShapeDtypeStruct((peers, capacity, group_size * part), jnp.bfloat16),
        compiler_params=pltpu.CompilerParams(vmem_limit_bytes=VMEM_LIMIT),
        cost_estimate=pl.CostEstimate(flops=0, bytes_accessed=6 << 20, transcendentals=0),
        name="unpack",
    )(received)


def rope_tables(positions):
    half_dim = 32
    inverse = 1.0 / ROPE_BASE ** (jnp.arange(half_dim, dtype=jnp.float32) * 2.0 / (2 * half_dim))
    angles = positions.astype(jnp.float32)[:, None] * jnp.tile(inverse, 4)[None, :]
    sign = jnp.where(jnp.arange(4 * half_dim) % (2 * half_dim) < half_dim, -1.0, 1.0)
    return jnp.cos(angles), jnp.sin(angles) * sign[None, :].astype(jnp.float32)


def per_device(tokens, norm_gain, input_weight, output_weight, segment_ids, page_owner):
    rows, model_width = tokens.shape
    peers, group_size = lax.axis_size("tok"), lax.axis_size("grp")
    place, member = lax.axis_index("tok"), lax.axis_index("grp")
    group_rows = rows * group_size
    width = model_width // group_size
    head_count = H // group_size
    pages = rows // PAGE

    pieces = [
        lax.ppermute(
            input_weight[:, number * width : (number + 1) * width],
            "grp",
            [(source, (PARTS * source + number) % group_size) for source in range(group_size)],
        )
        for number in range(PARTS)
    ]
    weight = lax.all_gather(jnp.concatenate(pieces, axis=1), "tok", axis=0, tiled=True)
    token_blocks = flip_gather(tokens, "grp")
    owners = lax.all_gather(page_owner[:, 0], "grp", axis=0)
    last_weight = lax.all_gather(output_weight, ("tok", "grp"), axis=0)
    last_weight = (
        last_weight.reshape((peers, group_size) + output_weight.shape)
        .transpose(0, 2, 1, 3)
        .reshape(model_width, model_width)
    )

    first_row = place * group_rows
    padded_ids = jnp.concatenate(
        [
            jnp.full((SPAN,), -1, jnp.int32),
            segment_ids,
            jnp.full((SPAN,), 1 << 30, jnp.int32),
        ]
    )
    window_ids = lax.dynamic_slice_in_dim(padded_ids, first_row, group_rows + 2 * SPAN, 0)
    own_ids = window_ids[SPAN : SPAN + group_rows]
    starts = jnp.sum((window_ids[None, :] < own_ids[:, None]).astype(jnp.int32), axis=1)
    ends = jnp.sum((window_ids[None, :] <= own_ids[:, None]).astype(jnp.int32), axis=1)
    positions = SPAN + jnp.arange(group_rows, dtype=jnp.int32) - starts
    cosine, sine = rope_tables(positions)

    capacity = max(2, (2 * pages + peers - 1) // peers)
    earlier = jnp.arange(pages)[:, None] > jnp.arange(pages)[None, :]
    same = owners[:, :, None] == owners[:, None, :]
    ranks = jnp.sum((same & earlier[None]).astype(jnp.int32), axis=2)
    slots = (owners * capacity + ranks)[:, None, :]

    order = [(number * group_size + member) % PARTS for number in range(PARTS)]
    meta = jnp.stack([member] + order).astype(jnp.int32)
    queries, chunk_a, chunk_b, chunk_c, send = project(
        meta, token_blocks, norm_gain[None, :], weight, cosine, sine, slots, peers, capacity
    )

    before_c = shifted(chunk_c, "tok", 1)
    after_a = shifted(chunk_a, "tok", -1)
    before_b = shifted(chunk_b, "tok", 1)
    after_b = shifted(chunk_b, "tok", -1)
    chunks = [before_b, before_c, chunk_a, chunk_b, chunk_c, after_a, after_b]

    received = lax.all_to_all(
        send.reshape((peers * group_size,) + send.shape[2:]),
        ("tok", "grp"),
        split_axis=0,
        concat_axis=0,
        tiled=True,
    )
    cache_pages = unpack(received.reshape(send.shape)).reshape(
        peers * capacity, 2 * PAGE * model_width
    )

    tile_first = starts[::TILE] // TILE
    tile_last = (ends[TILE - 1 :: TILE] + TILE - 1) // TILE
    ranges = jnp.stack([tile_first, tile_last], axis=1).reshape(-1)
    mixed = [None] * group_size
    for far in reversed(range(group_size // 2)):
        half = (member // 2) ^ far
        head_meta = jnp.stack([member % 2, half * (2 * rows // TILE)]).astype(jnp.int32)
        outs = attend(
            jnp.concatenate([head_meta, ranges]),
            queries,
            starts[None, :],
            ends[None, :],
            chunks,
            rows,
            head_count,
        )
        for near in range(2):
            distance = 2 * far + near
            mixed[distance] = (
                flipped(outs[near], "grp", distance) if distance else outs[near]
            )
    attended = output_projection(member[None].astype(jnp.int32), mixed, last_weight)
    return attended, cache_pages


def solution(mesh):
    placed = (
        P(("tok", "grp"), None),
        P(),
        P("tok", "grp"),
        P("tok", "grp"),
        P(),
        P(("tok", "grp"), None),
    )
    return jax.shard_map(
        per_device,
        mesh=mesh,
        in_specs=placed,
        out_specs=(P(("tok", "grp"), None), P(("tok", "grp"), None)),
        check_vma=False,
    )
```

```python
import functools
import math

import jax
import jax.numpy as jnp
from jax import lax
from jax.experimental import pallas as pl
from jax.experimental.pallas import tpu as pltpu
from jax.sharding import PartitionSpec as P

H = 16
SPAN = 1024
PAGE = 4
HEAD_DIM = 64

NEG_FILL = -1e30
ROPE_BASE = 160000.0
EPSILON = 1e-05
TILE = 256
PARTS = 3
PAIR = 2
ONES_ROWS = 16
HEAD_ROWS = HEAD_DIM + ONES_ROWS
VMEM_LIMIT = 60 * 1024 * 1024
PARAMS = pltpu.CompilerParams(vmem_limit_bytes=VMEM_LIMIT)


def flipped(value, axis, bit):
    count = lax.axis_size(axis)
    return lax.ppermute(value, axis, [(source, source ^ bit) for source in range(count)])


def shifted(value, axis, steps):
    count = lax.axis_size(axis)
    initial, last = (max(0, -steps), min(count, count - steps))
    return lax.ppermute(value, axis, [(source, source + steps) for source in range(initial, last)])


def norm_kernel(tokens, gain, normed):
    values = tokens[...].astype(jnp.float32)
    centred = values - jnp.mean(values, axis=-1, keepdims=True)
    spread = jnp.mean(jnp.square(centred), axis=-1, keepdims=True)
    normed[...] = (centred * lax.rsqrt(spread + EPSILON) * gain[...]).astype(jnp.bfloat16)


def layer_norm(tokens, gain):
    rows, width = tokens.shape
    tile = rows // 3
    return pl.pallas_call(
        norm_kernel,
        grid=(3,),
        in_specs=[
            pl.BlockSpec((tile, width), lambda i: (i, 0)),
            pl.BlockSpec((1, width), lambda i: (0, 0)),
        ],
        out_specs=pl.BlockSpec((tile, width), lambda i: (i, 0)),
        out_shape=jax.ShapeDtypeStruct(tokens.shape, jnp.bfloat16),
        compiler_params=PARAMS,
        name="layer_norm",
    )(tokens, gain)


def project_kernel(layout, weight_count, peers, capacity, meta, *refs):
    operands = 1 + max(entry[0] for pieces in layout for entry in pieces)
    tokens = refs[:operands]
    weights = refs[operands : operands + weight_count]
    cosine, sine, slots, query_out, chunk_a, chunk_b, chunk_c, send_out = refs[
        operands + weight_count : operands + weight_count + 8
    ]
    blocks, weight, pairs, page_source, sems = refs[operands + weight_count + 8 :]
    step = pl.program_id(0)
    steps = len(layout)
    rows = blocks.shape[1]
    width = query_out.shape[1]
    shard = weights[0].shape[0] // 2

    def arrivals(distance):
        return [
            pltpu.make_async_copy(
                tokens[operand],
                blocks.at[distance, pl.ds(offset, count), :],
                sems.at[distance, number],
            )
            for number, (operand, offset, count) in enumerate(layout[distance])
        ]

    @pl.when(step == 0)
    def _():
        for distance in range(steps):
            for copy in arrivals(distance):
                copy.start()
        for plane in range(weight_count):
            for low in range(2):
                row = pl.multiple_of((meta[1] ^ (2 * plane + low)) * shard, shard)
                for number in range(PARTS):
                    column = pl.multiple_of(meta[2 + number] * width, width)
                    weight[pl.ds(row, shard), number * width : (number + 1) * width] = weights[
                        plane
                    ][low * shard : (low + 1) * shard, pl.ds(column, width)]

    for distance in range(steps):

        @pl.when(step == distance)
        def _():
            for copy in arrivals(distance):
                copy.wait()

    joined = jnp.dot(blocks[step], weight[...], preferred_element_type=jnp.float32)
    cosines = jnp.concatenate([cosine[...]] * 4, axis=0).T
    sines = jnp.concatenate([-sine[...], sine[...]] * 2, axis=0).T
    first_half = lax.rem(lax.broadcasted_iota(jnp.int32, (rows, width), 1), HEAD_DIM) < (
        HEAD_DIM // 2
    )

    def rotate(values):
        partner = jnp.where(
            first_half,
            pltpu.roll(values, width - HEAD_DIM // 2, 1),
            pltpu.roll(values, HEAD_DIM // 2, 1),
        )
        return values * cosines + partner * sines

    scale = HEAD_DIM ** (-0.5) * math.log2(math.e)
    query_out[...] = (rotate(joined[:, :width]) * scale).astype(jnp.bfloat16)
    keys = rotate(joined[:, width : 2 * width]).astype(jnp.bfloat16)
    values = joined[:, 2 * width :].astype(jnp.bfloat16)
    block = meta[0] ^ step
    own_rows = pl.ds(pl.multiple_of(block * rows, 128), rows)
    pairs[own_rows, :width] = keys
    pairs[own_rows, width:] = values
    page_source[0] = keys.astype(jnp.float32)
    page_source[1] = values.astype(jnp.float32)

    pages = rows // PAGE
    slot_count = peers * capacity
    chosen = (
        lax.broadcasted_iota(jnp.int32, (slot_count, pages), 0) == slots[0]
    ).astype(jnp.bfloat16)
    for turn in range(PAGE):
        page_part = jnp.concatenate(
            [
                page_source[half, pl.ds(turn, pages, stride=PAGE), :].astype(jnp.bfloat16)
                for half in range(2)
            ],
            axis=1,
        )
        placed = jnp.dot(chosen, page_part, preferred_element_type=jnp.float32)
        columns = slice(turn * 2 * width, (turn + 1) * 2 * width)
        for peer in range(peers):
            send_out[peer, 0, 0, :, columns] = placed[
                peer * capacity : (peer + 1) * capacity
            ].astype(jnp.bfloat16)

    @pl.when(step == steps - 1)
    def _():
        for number, chunk in enumerate((chunk_a, chunk_b, chunk_c)):
            chunk[...] = pairs[number * SPAN : (number + 1) * SPAN, :]


def project(meta, layout, operands, weights, cosine, sine, slots, rows, peers, capacity):
    steps = len(layout)
    model_width = operands[0].shape[1]
    group_rows = rows * steps
    width = weights[0].shape[1] // PARTS
    pages = rows // PAGE
    members = steps // PAIR
    whole = lambda shape: pl.BlockSpec(shape, lambda i, m: (0,) * len(shape))
    table = pl.BlockSpec((HEAD_DIM // 2, rows), lambda i, m: (0, m[0] ^ i))
    send_shape = (peers, members, PAIR, capacity, 2 * PAGE * width)
    return pl.pallas_call(
        functools.partial(project_kernel, layout, len(weights), peers, capacity),
        grid_spec=pltpu.PrefetchScalarGridSpec(
            num_scalar_prefetch=1,
            grid=(steps,),
            in_specs=[pl.BlockSpec(memory_space=pl.ANY)] * len(operands)
            + [whole(weights[0].shape)] * len(weights)
            + [table, table, pl.BlockSpec((1, 1, pages), lambda i, m: (m[0] ^ i, 0, 0))],
            out_specs=[pl.BlockSpec((rows, width), lambda i, m: (m[0] ^ i, 0))]
            + [whole((SPAN, 2 * width))] * 3
            + [
                pl.BlockSpec(
                    (peers, 1, 1) + send_shape[3:],
                    lambda i, m: (0, (m[0] ^ i) % members, (m[0] ^ i) // members, 0, 0),
                )
            ],
            scratch_shapes=[
                pltpu.VMEM((steps, rows, model_width), jnp.bfloat16),
                pltpu.VMEM((model_width, PARTS * width), jnp.bfloat16),
                pltpu.VMEM((group_rows, 2 * width), jnp.bfloat16),
                pltpu.VMEM((2, rows, width), jnp.float32),
                pltpu.SemaphoreType.DMA((steps, 2)),
            ],
        ),
        out_shape=[jax.ShapeDtypeStruct((group_rows, width), jnp.bfloat16)]
        + [jax.ShapeDtypeStruct((SPAN, 2 * width), jnp.bfloat16)] * 3
        + [jax.ShapeDtypeStruct(send_shape, jnp.bfloat16)],
        compiler_params=PARAMS,
        cost_estimate=pl.CostEstimate(
            flops=2 * group_rows * model_width * PARTS * width,
            bytes_accessed=12 << 20,
            transcendentals=0,
        ),
        name="project",
    )(meta, *operands, *weights, cosine, sine, slots)


def mask_heads(queries, masked):
    head_of_lane = lax.broadcasted_iota(jnp.int32, queries.shape, 1) // HEAD_DIM
    for head in range(masked.shape[0]):
        masked[head] = jnp.where(head_of_lane == head, queries[...], jnp.zeros((), jnp.bfloat16))


def with_ones(values):
    turned = values.T
    ones = jnp.ones((ONES_ROWS, values.shape[0]), values.dtype)
    rows = []
    for head in range(values.shape[1] // HEAD_DIM):
        rows += [turned[head * HEAD_DIM : (head + 1) * HEAD_DIM], ones]
    return jnp.concatenate(rows, axis=0)


def visit(keys, values, first_key, masked, starts, ends, total, peaks):
    index = first_key + lax.broadcasted_iota(jnp.int32, (TILE, TILE), 0)
    allowed = (index >= starts) & (index < ends)
    new_peaks = []
    for head, old_peak in enumerate(peaks):
        scores = lax.dot_general(
            keys, masked[head], (((1,), (1,)), ((), ())), preferred_element_type=jnp.float32
        )
        scores = jnp.where(allowed, scores, NEG_FILL)
        peak = jnp.maximum(old_peak, jnp.max(scores, axis=0, keepdims=True))
        fade = jnp.exp2(old_peak - peak)
        weights = jnp.exp2(scores - peak).astype(jnp.bfloat16)
        own = slice(head * HEAD_ROWS, (head + 1) * HEAD_ROWS)
        total[own, :] = total[own, :] * fade + jnp.dot(
            values[own, :], weights, preferred_element_type=jnp.float32
        )
        new_peaks.append(peak)
    return tuple(new_peaks)


def attend_kernel(ranges, queries, starts, ends, chunk_a, chunk_b, chunk_c, total, peak_out, *scratch):
    masked, values = scratch
    step = pl.program_id(0)
    width = queries.shape[1]
    heads = width // HEAD_DIM
    per_chunk = SPAN // TILE
    chunks = (chunk_a, chunk_b, chunk_c)

    @pl.when(step == 0)
    def _():
        for number in range(len(chunks) * per_chunk):
            rows = slice(number % per_chunk * TILE, (number % per_chunk + 1) * TILE)
            values[number] = with_ones(chunks[number // per_chunk][rows, width:])

    mask_heads(queries, masked)
    total[...] = jnp.zeros_like(total)
    first, last = starts[...], ends[...]
    peaks = tuple(jnp.full((1, TILE), NEG_FILL, jnp.float32) for _ in range(heads))
    for number, chunk in enumerate(chunks):
        base = (number + 1) * per_chunk

        def one(block, peaks):
            rows = pl.ds(pl.multiple_of((block - base) * TILE, TILE), TILE)
            return visit(
                chunk[rows, :width],
                values[block - per_chunk],
                block * TILE,
                masked,
                first,
                last,
                total.at[0],
                peaks,
            )

        begin = jnp.maximum(ranges[2 * step], base)
        peaks = lax.fori_loop(
            begin, jnp.minimum(ranges[2 * step + 1], base + per_chunk), one, peaks
        )
    for head in range(heads):
        peak_out[0, head : head + 1, :] = peaks[head]


def finish_kernel(meta, queries, starts, ends, before, after, total, peak_in, *refs):
    outs = refs[:-3]
    masked, sums, mixed = refs[-3:]
    step = pl.program_id(0)
    width = queries.shape[1]
    heads = width // HEAD_DIM
    per_chunk = SPAN // TILE
    own_blocks = pl.num_programs(0)
    sums[...] = total[0]
    begin, end = meta[1 + 2 * step], meta[2 + 2 * step]

    @pl.when((begin < per_chunk) | (end > per_chunk + own_blocks))
    def _():
        mask_heads(queries, masked)
        first, last = starts[...], ends[...]
        peaks = tuple(peak_in[0, head : head + 1, :] for head in range(heads))
        for chunk, base in ((before, 0), (after, per_chunk + own_blocks)):

            def one(block, peaks):
                rows = pl.ds(pl.multiple_of((block - base) * TILE, TILE), TILE)
                return visit(
                    chunk[rows, :width],
                    with_ones(chunk[rows, width:]),
                    block * TILE,
                    masked,
                    first,
                    last,
                    sums,
                    peaks,
                )

            peaks = lax.fori_loop(
                jnp.maximum(begin, base), jnp.minimum(end, base + per_chunk), one, peaks
            )

    parts = []
    for head in range(heads):
        row = head * HEAD_ROWS
        parts.append(sums[row : row + HEAD_DIM, :] / sums[row + HEAD_DIM : row + HEAD_DIM + 1, :])
    tile_rows = pl.ds(pl.multiple_of(step * TILE, TILE), TILE)
    mixed[tile_rows, :] = jnp.concatenate(parts, axis=0).T.astype(jnp.bfloat16)

    @pl.when(step == pl.num_programs(0) - 1)
    def _():
        rows = outs[0].shape[0]
        for distance, out in enumerate(outs):
            out[...] = mixed[pl.ds(pl.multiple_of((meta[0] ^ distance) * rows, 128), rows), :]


def attend_specs(width, prefetched):
    spec = lambda shape, index: pl.BlockSpec(shape, lambda i, m: index(i))
    return [
        spec((TILE, width), lambda i: (i, 0)),
        spec((1, TILE), lambda i: (0, i)),
        spec((1, TILE), lambda i: (0, i)),
    ] + [spec((SPAN, 2 * width), lambda i: (0, 0))] * prefetched


def attend_local(ranges, queries, starts, ends, chunks):
    group_rows, width = queries.shape
    heads = width // HEAD_DIM
    tiles = group_rows // TILE
    blocks = len(chunks) * SPAN // TILE
    return pl.pallas_call(
        attend_kernel,
        grid_spec=pltpu.PrefetchScalarGridSpec(
            num_scalar_prefetch=1,
            grid=(tiles,),
            in_specs=attend_specs(width, len(chunks)),
            out_specs=[
                pl.BlockSpec((1, heads * HEAD_ROWS, TILE), lambda i, m: (i, 0, 0)),
                pl.BlockSpec((1, 8, TILE), lambda i, m: (i, 0, 0)),
            ],
            scratch_shapes=[
                pltpu.VMEM((heads, TILE, width), jnp.bfloat16),
                pltpu.VMEM((blocks, heads * HEAD_ROWS, TILE), jnp.bfloat16),
            ],
        ),
        out_shape=[
            jax.ShapeDtypeStruct((tiles, heads * HEAD_ROWS, TILE), jnp.float32),
            jax.ShapeDtypeStruct((tiles, 8, TILE), jnp.float32),
        ],
        compiler_params=PARAMS,
        cost_estimate=pl.CostEstimate(
            flops=16 * group_rows * 1024 * width,
            bytes_accessed=5 << 20,
            transcendentals=group_rows * 1024 * heads,
        ),
        name="attend_local",
    )(ranges, queries, starts, ends, *chunks)


def attend_finish(meta, queries, starts, ends, before, after, total, peaks, rows):
    group_rows, width = queries.shape
    heads = width // HEAD_DIM
    tiles = group_rows // TILE
    members = group_rows // rows
    return pl.pallas_call(
        finish_kernel,
        grid_spec=pltpu.PrefetchScalarGridSpec(
            num_scalar_prefetch=1,
            grid=(tiles,),
            in_specs=attend_specs(width, 2)
            + [
                pl.BlockSpec((1,) + total.shape[1:], lambda i, m: (i, 0, 0)),
                pl.BlockSpec((1,) + peaks.shape[1:], lambda i, m: (i, 0, 0)),
            ],
            out_specs=[pl.BlockSpec((rows, width), lambda i, m: (0, 0))] * members,
            scratch_shapes=[
                pltpu.VMEM((heads, TILE, width), jnp.bfloat16),
                pltpu.VMEM(total.shape[1:], jnp.float32),
                pltpu.VMEM((group_rows, width), jnp.bfloat16),
            ],
        ),
        out_shape=[jax.ShapeDtypeStruct((rows, width), jnp.bfloat16)] * members,
        compiler_params=PARAMS,
        cost_estimate=pl.CostEstimate(
            flops=4 * group_rows * 1024 * width,
            bytes_accessed=5 << 20,
            transcendentals=group_rows * 256 * heads,
        ),
        name="attend_finish",
    )(meta, queries, starts, ends, before, after, total, peaks)


def output_kernel(members, meta, *refs):
    parts, weight, result, mixed = refs[:members], refs[members], refs[-2], refs[-1]
    width = parts[0].shape[1]

    @pl.when(pl.program_id(0) == 0)
    def _():
        for distance in range(members):
            source = meta[0] ^ distance
            head_pair = PAIR * (source % (members // PAIR)) + source // (members // PAIR)
            columns = pl.ds(pl.multiple_of(head_pair * width, width), width)
            mixed[:, columns] = parts[distance][...]

    result[...] = jnp.dot(
        mixed[...], weight[...], preferred_element_type=jnp.float32
    ).astype(jnp.bfloat16)


def output_projection(meta, parts, weight):
    rows, width = parts[0].shape
    depth = width * len(parts)
    tile = weight.shape[1]
    steps = weight.shape[0] // depth
    return pl.pallas_call(
        functools.partial(output_kernel, len(parts)),
        grid_spec=pltpu.PrefetchScalarGridSpec(
            num_scalar_prefetch=1,
            grid=(steps,),
            in_specs=[pl.BlockSpec((rows, width), lambda i, m: (0, 0))] * len(parts)
            + [pl.BlockSpec((depth, tile), lambda i, m: (i, 0))],
            out_specs=pl.BlockSpec((rows, tile), lambda i, m: (0, i)),
            scratch_shapes=[pltpu.VMEM((rows, depth), jnp.bfloat16)],
        ),
        out_shape=jax.ShapeDtypeStruct((rows, steps * tile), jnp.bfloat16),
        compiler_params=PARAMS,
        cost_estimate=pl.CostEstimate(
            flops=2 * rows * depth * steps * tile, bytes_accessed=4 << 20, transcendentals=0
        ),
        name="output_projection",
    )(meta, *parts, weight)


def unpack_kernel(received, pages):
    _, pair, members, _, capacity, part = received.shape
    width = part // (2 * PAGE)
    for low in range(pair):
        for high in range(members):
            head_pair = PAIR * high + low
            for turn in range(2 * PAGE):
                start = (turn * pair * members + head_pair) * width
                pages[0, :, start : start + width] = received[
                    0, low, high, 0, :, turn * width : (turn + 1) * width
                ]


def unpack(received):
    planes, pair, members, sources, capacity, part = received.shape
    return pl.pallas_call(
        unpack_kernel,
        grid=(planes, sources),
        in_specs=[
            pl.BlockSpec(
                (1, pair, members, 1, capacity, part), lambda i, j: (i, 0, 0, j, 0, 0)
            )
        ],
        out_specs=pl.BlockSpec(
            (1, capacity, pair * members * part), lambda i, j: (i * sources + j, 0, 0)
        ),
        out_shape=jax.ShapeDtypeStruct(
            (planes * sources, capacity, pair * members * part), jnp.bfloat16
        ),
        compiler_params=PARAMS,
        cost_estimate=pl.CostEstimate(flops=0, bytes_accessed=6 << 20, transcendentals=0),
        name="unpack",
    )(received)


def rope_tables(positions):
    half_dim = HEAD_DIM // 2
    inverse = 1.0 / ROPE_BASE ** (jnp.arange(half_dim, dtype=jnp.float32) * 2.0 / HEAD_DIM)
    angles = inverse[:, None] * positions.astype(jnp.float32)[None, :]
    return jnp.cos(angles), jnp.sin(angles)


def document_bounds(window_ids, rows, blocks):
    reach = SPAN + rows
    firsts = jnp.arange(blocks, dtype=jnp.int32)[:, None] * rows
    own = window_ids[SPAN : SPAN + rows * blocks].reshape(blocks, rows)
    behind = jnp.stack([window_ids[k * rows : k * rows + reach] for k in range(blocks)])
    ahead = jnp.stack(
        [window_ids[SPAN + k * rows : SPAN + k * rows + reach] for k in range(blocks)]
    )
    starts = jnp.sum((behind[:, None, :] < own[:, :, None]).astype(jnp.int32), axis=2) + firsts
    ends = (
        jnp.sum((ahead[:, None, :] <= own[:, :, None]).astype(jnp.int32), axis=2)
        + firsts
        + SPAN
    )
    return starts.reshape(-1), ends.reshape(-1)


def per_device(tokens, norm_gain, input_weight, output_weight, segment_ids, page_owner):
    rows, model_width = tokens.shape
    peers, members = lax.axis_size("tok"), lax.axis_size("grp")
    place, column = lax.axis_index("tok"), lax.axis_index("grp")
    low = place % PAIR
    blocks = PAIR * members
    member = low * members + column
    group_rows = rows * blocks
    width = model_width // blocks
    pages = rows // PAGE

    shard = input_weight.reshape(input_weight.shape[0], PARTS, PAIR, width)
    mine = lax.dynamic_index_in_dim(shard, low, 2, keepdims=False)
    theirs = lax.dynamic_index_in_dim(shard, 1 - low, 2, keepdims=False)
    both = jnp.concatenate([mine, flipped(theirs, "tok", 1)], axis=0)
    pieces = [
        lax.ppermute(
            both[:, number],
            "grp",
            [(source, (PARTS * source + number) % members) for source in range(members)],
        )
        for number in range(PARTS)
    ]
    planes = {0: jnp.concatenate(pieces, axis=1)}
    bit = peers // 2
    while bit > 1:
        for distance in list(planes):
            planes[distance ^ bit] = flipped(planes[distance], "tok", bit)
        bit //= 2
    weights = [planes[distance] for distance in range(0, peers, 2)]

    own = layer_norm(tokens, norm_gain[None, :])
    across, along = flipped(own, "grp", 2), flipped(own, "tok", 1)
    half = rows // 2
    corner_top = flipped(across[:half], "tok", 1)
    corner_bottom = flipped(along[half:], "grp", 2)
    operands = [own, across, along, corner_top, corner_bottom]
    operands += [flipped(operand, "grp", 1) for operand in operands]
    layout = [None] * blocks
    for near in range(2):
        shift = 5 * near
        layout[near] = [(shift, 0, rows)]
        layout[2 + near] = [(shift + 1, 0, rows)]
        layout[4 + near] = [(shift + 2, 0, rows)]
        layout[6 + near] = [(shift + 3, 0, half), (shift + 4, half, half)]

    owners = page_owner[:, 0]
    capacity = max(2, (2 * pages + peers - 1) // peers)
    earlier = jnp.arange(pages)[:, None] > jnp.arange(pages)[None, :]
    ranks = jnp.sum(((owners[:, None] == owners[None, :]) & earlier).astype(jnp.int32), axis=1)
    slots = {0: (owners * capacity + ranks)[None]}
    for axis, bit, flag in (("grp", 1, 1), ("grp", 2, 2), ("tok", 1, 4)):
        slots[flag] = flipped(slots[0], axis, bit)
        slots[0] = jnp.concatenate([slots[0], slots[flag]], axis=0)
    slots = slots[0][jnp.arange(blocks) ^ member][:, None, :]

    first_row = place // PAIR * group_rows
    padded_ids = jnp.concatenate(
        [
            jnp.full((SPAN,), -1, jnp.int32),
            segment_ids,
            jnp.full((SPAN,), 1 << 30, jnp.int32),
        ]
    )
    window_ids = lax.dynamic_slice_in_dim(padded_ids, first_row, group_rows + 2 * SPAN, 0)
    starts, ends = document_bounds(window_ids, rows, blocks)
    positions = SPAN + jnp.arange(group_rows, dtype=jnp.int32) - starts
    cosine, sine = rope_tables(positions)
    ranges = jnp.stack(
        [starts[::TILE] // TILE, (ends[TILE - 1 :: TILE] + TILE - 1) // TILE], axis=1
    ).reshape(-1)

    order = [
        (number * members + column) % PARTS for number in range(PARTS)
    ]
    meta = jnp.stack([member, place] + order).astype(jnp.int32)
    queries, chunk_a, chunk_b, chunk_c, send = project(
        meta, layout, operands, weights, cosine, sine, slots, rows, peers, capacity
    )

    before = shifted(chunk_c, "tok", PAIR)
    after = shifted(chunk_a, "tok", -PAIR)
    received = lax.all_to_all(
        send.reshape((peers * members,) + send.shape[2:]),
        ("tok", "grp"),
        split_axis=0,
        concat_axis=0,
        tiled=True,
    )

    last_columns = lax.all_gather(output_weight, "tok", axis=0, tiled=True)
    queries, last_columns = lax.optimization_barrier((queries, last_columns))
    last_weight = lax.all_gather(last_columns, "grp", axis=0, tiled=True)

    bounds = (starts[None, :], ends[None, :])
    total, peaks = attend_local(ranges, queries, *bounds, (chunk_a, chunk_b, chunk_c))
    own_member = member[None].astype(jnp.int32)
    mixed = attend_finish(
        jnp.concatenate([own_member, ranges]),
        queries,
        *bounds,
        before,
        after,
        total,
        peaks,
        rows,
    )
    flat = peers * members
    parts = [mixed[0]] + [
        lax.ppermute(
            mixed[distance],
            ("tok", "grp"),
            [(source, source ^ distance) for source in range(flat)],
        )
        for distance in range(1, blocks)
    ]
    attended = output_projection(own_member, parts, last_weight)

    cache_pages = unpack(
        received.reshape((peers // PAIR, PAIR, members) + send.shape[2:])
    ).reshape(peers * capacity, 2 * PAGE * model_width)
    return attended, cache_pages


def solution(mesh):
    placed = (
        P(("tok", "grp"), None),
        P(),
        P("tok", "grp"),
        P("tok", "grp"),
        P(),
        P(("tok", "grp"), None),
    )
    return jax.shard_map(
        per_device,
        mesh=mesh,
        in_specs=placed,
        out_specs=(P(("tok", "grp"), None), P(("tok", "grp"), None)),
        check_vma=False,
    )
```

```python
import functools
import math

import jax
import jax.numpy as jnp
from jax import lax
from jax.experimental import pallas as pl
from jax.experimental.pallas import tpu as pltpu
from jax.sharding import PartitionSpec as P

H = 16
SPAN = 1024
PAGE = 4
HEAD_DIM = 64

NEG_FILL = -1e30
ROPE_BASE = 160000.0
EPSILON = 1e-05
TILE = 256
PARTS = 3
PAIR = 2
ONES_ROWS = 16
HEAD_ROWS = HEAD_DIM + ONES_ROWS
EXTRA_ROWS = 16
KEYS = 512
SCALE = HEAD_DIM ** (-0.5) * math.log2(math.e)
VMEM_LIMIT = 60 * 1024 * 1024
PARAMS = pltpu.CompilerParams(vmem_limit_bytes=VMEM_LIMIT)


def flipped(value, axis, bit):
    count = lax.axis_size(axis)
    return lax.ppermute(value, axis, [(source, source ^ bit) for source in range(count)])


def shifted(value, axis, steps):
    count = lax.axis_size(axis)
    initial, last = (max(0, -steps), min(count, count - steps))
    return lax.ppermute(value, axis, [(source, source + steps) for source in range(initial, last)])


def natural_gather(value, axis):
    place = lax.axis_index(axis)
    bit = 1
    while bit < lax.axis_size(axis):
        other = flipped(value, axis, bit)
        first = (place & bit) == 0
        value = jnp.concatenate(
            [jnp.where(first, value, other), jnp.where(first, other, value)], axis=0
        )
        bit *= 2
    return value


def norm_kernel(capacity, tokens, gain, owner_row, owner_column, normed):
    rows = tokens.shape[0]
    values = tokens[...].astype(jnp.float32)
    centred = values - jnp.mean(values, axis=-1, keepdims=True)
    spread = jnp.mean(jnp.square(centred), axis=-1, keepdims=True)
    normed[:rows, :] = (centred * lax.rsqrt(spread + EPSILON) * gain[...]).astype(jnp.bfloat16)
    lanes = normed.shape[1]
    pages = owner_column.shape[0]
    earlier = lax.broadcasted_iota(jnp.int32, (pages, lanes), 0) < lax.broadcasted_iota(
        jnp.int32, (pages, lanes), 1
    )
    same = (owner_column[...] == owner_row[...]) & earlier
    ranks = jnp.sum(jnp.where(same, 1.0, 0.0), axis=0, keepdims=True)
    slots = owner_row[...].astype(jnp.float32) * capacity + ranks
    normed[rows:, :] = jnp.broadcast_to(slots, (EXTRA_ROWS, lanes)).astype(jnp.bfloat16)


def layer_norm(tokens, gain, owners, capacity):
    rows, width = tokens.shape
    owner_row = jnp.pad(owners, (0, width - owners.shape[0]), constant_values=-1)[None, :]
    return pl.pallas_call(
        functools.partial(norm_kernel, capacity),
        out_shape=jax.ShapeDtypeStruct((rows + EXTRA_ROWS, width), jnp.bfloat16),
        compiler_params=PARAMS,
        name="layer_norm",
    )(tokens, gain, owner_row, owners[:, None])


def project_kernel(first, layout, weight_count, peers, capacity, meta, *refs):
    operands = 1 + max(entry[0] for pieces in layout for entry in pieces)
    tokens = refs[:operands]
    weights = refs[operands : operands + weight_count]
    cosine, sine = refs[operands + weight_count : operands + weight_count + 2]
    query_out, pair_out, send_out, blocks, weight, page_source, sems = refs[-7:]
    step = pl.program_id(0)
    steps = len(layout)
    rows = query_out.shape[0]
    width = query_out.shape[1]
    shard = weights[0].shape[0] // 2

    def arrivals(number):
        return [
            pltpu.make_async_copy(
                tokens[operand],
                blocks.at[number, pl.ds(offset, count), :],
                sems.at[number, place],
            )
            for place, (operand, offset, count) in enumerate(layout[number])
        ]

    @pl.when(step == 0)
    def _():
        for number in range(steps):
            for copy in arrivals(number):
                copy.start()
        for plane in range(weight_count):
            for low in range(2):
                row = pl.multiple_of((meta[1] ^ (2 * plane + low)) * shard, shard)
                for number in range(PARTS):
                    column = pl.multiple_of(meta[2 + number] * width, width)
                    weight[pl.ds(row, shard), number * width : (number + 1) * width] = weights[
                        plane
                    ][low * shard : (low + 1) * shard, pl.ds(column, width)]

    for number in range(steps):

        @pl.when(step == number)
        def _():
            for copy in arrivals(number):
                copy.wait()

    joined = jnp.dot(blocks[step, :rows, :], weight[...], preferred_element_type=jnp.float32)
    cosines = jnp.concatenate([cosine[...]] * 4, axis=0).T
    sines = jnp.concatenate([-sine[...], sine[...]] * 2, axis=0).T
    first_half = lax.rem(lax.broadcasted_iota(jnp.int32, (rows, width), 1), HEAD_DIM) < (
        HEAD_DIM // 2
    )

    def rotate(values):
        partner = jnp.where(
            first_half,
            pltpu.roll(values, width - HEAD_DIM // 2, 1),
            pltpu.roll(values, HEAD_DIM // 2, 1),
        )
        return (values * cosines + partner * sines).astype(jnp.bfloat16)

    query_out[...] = rotate(joined[:, :width])
    keys = rotate(joined[:, width : 2 * width])
    values = joined[:, 2 * width :].astype(jnp.bfloat16)
    pair_out[:, :width] = keys
    pair_out[:, width:] = values
    page_source[0] = keys.astype(jnp.float32)
    page_source[1] = values.astype(jnp.float32)

    pages = rows // PAGE
    slot_count = peers * capacity
    slots = blocks[step, rows : rows + EXTRA_ROWS, :128].astype(jnp.float32)[:1, :pages]
    chosen = (
        lax.broadcasted_iota(jnp.int32, (slot_count, pages), 0).astype(jnp.float32) == slots
    ).astype(jnp.bfloat16)
    for turn in range(PAGE):
        page_part = jnp.concatenate(
            [
                page_source[half, pl.ds(turn, pages, stride=PAGE), :].astype(jnp.bfloat16)
                for half in range(2)
            ],
            axis=1,
        )
        placed = jnp.dot(chosen, page_part, preferred_element_type=jnp.float32)
        columns = slice(turn * 2 * width, (turn + 1) * 2 * width)
        for peer in range(peers):
            send_out[peer, 0, 0, :, columns] = placed[
                peer * capacity : (peer + 1) * capacity
            ].astype(jnp.bfloat16)


def project(meta, first, layout, operands, weights, cosine, sine, rows, blocks, peers, capacity, into):
    steps = len(layout)
    model_width = operands[0].shape[1]
    group_rows = rows * blocks
    width = weights[0].shape[1] // PARTS
    members = blocks // PAIR
    whole = lambda shape: pl.BlockSpec(shape, lambda i, m: (0,) * len(shape))
    place = lambda i, m: m[0] ^ (first + i)
    table = pl.BlockSpec((HEAD_DIM // 2, rows), lambda i, m: (0, place(i, m)))
    send_shape = (peers, members, PAIR, capacity, 2 * PAGE * width)
    return pl.pallas_call(
        functools.partial(project_kernel, first, layout, len(weights), peers, capacity),
        grid_spec=pltpu.PrefetchScalarGridSpec(
            num_scalar_prefetch=1,
            grid=(steps,),
            in_specs=[pl.BlockSpec(memory_space=pl.ANY)] * len(operands)
            + [whole(weights[0].shape)] * len(weights)
            + [table, table]
            + [pl.BlockSpec(memory_space=pl.ANY)] * len(into),
            out_specs=[
                pl.BlockSpec((rows, width), lambda i, m: (place(i, m), 0)),
                pl.BlockSpec((rows, 2 * width), lambda i, m: (place(i, m), 0)),
                pl.BlockSpec(
                    (peers, 1, 1) + send_shape[3:],
                    lambda i, m: (0, place(i, m) % members, place(i, m) // members, 0, 0),
                ),
            ],
            scratch_shapes=[
                pltpu.VMEM((steps, rows + EXTRA_ROWS, model_width), jnp.bfloat16),
                pltpu.VMEM((model_width, PARTS * width), jnp.bfloat16),
                pltpu.VMEM((2, rows, width), jnp.float32),
                pltpu.SemaphoreType.DMA((steps, 2)),
            ],
        ),
        out_shape=[
            jax.ShapeDtypeStruct((group_rows, width), jnp.bfloat16),
            jax.ShapeDtypeStruct((group_rows, 2 * width), jnp.bfloat16),
            jax.ShapeDtypeStruct(send_shape, jnp.bfloat16),
        ],
        input_output_aliases={
            1 + len(operands) + len(weights) + 2 + number: number for number in range(len(into))
        },
        compiler_params=PARAMS,
        cost_estimate=pl.CostEstimate(
            flops=2 * steps * rows * model_width * PARTS * width,
            bytes_accessed=(3 * steps) << 19,
            transcendentals=0,
        ),
        name="project",
    )(meta, *operands, *weights, cosine, sine, *into)


def mask_heads(queries, masked):
    head_of_lane = lax.broadcasted_iota(jnp.int32, queries.shape, 1) // HEAD_DIM
    for head in range(masked.shape[0]):
        masked[head] = jnp.where(head_of_lane == head, queries[...], jnp.zeros((), jnp.bfloat16))


def with_ones(values):
    turned = values.T
    ones = jnp.ones((ONES_ROWS, values.shape[0]), values.dtype)
    rows = []
    for head in range(values.shape[1] // HEAD_DIM):
        rows += [turned[head * HEAD_DIM : (head + 1) * HEAD_DIM], ones]
    return jnp.concatenate(rows, axis=0)


def sweep(begin, end, base, pairs, values_of, masked, starts, ends, total, peaks):
    width = pairs.shape[1] // 2
    held = pairs.shape[0] // TILE
    begin = jnp.maximum(begin, base)
    end = jnp.minimum(end, base + held)
    last = jnp.minimum(ends, end * TILE)

    def one(number, peaks):
        wanted = begin + number * (KEYS // TILE)
        block = jnp.minimum(wanted, base + held - KEYS // TILE)
        row = pl.multiple_of((block - base) * TILE, TILE)
        keys = pairs[pl.ds(row, KEYS), :width]
        values = values_of(row)
        index = block * TILE + lax.broadcasted_iota(jnp.int32, (KEYS, TILE), 0)
        allowed = (index >= jnp.maximum(starts, wanted * TILE)) & (index < last)
        new_peaks = []
        for head, old_peak in enumerate(peaks):
            scores = lax.dot_general(
                keys, masked[head], (((1,), (1,)), ((), ())), preferred_element_type=jnp.float32
            )
            scores = jnp.where(allowed, scores * SCALE, NEG_FILL)
            peak = jnp.maximum(old_peak, jnp.max(scores, axis=0, keepdims=True))
            fade = jnp.exp2(old_peak - peak)
            weights = jnp.exp2(scores - peak).astype(jnp.bfloat16)
            own = slice(head * HEAD_ROWS, (head + 1) * HEAD_ROWS)
            total[own, :] = total[own, :] * fade + jnp.dot(
                values[own, :], weights, preferred_element_type=jnp.float32
            )
            new_peaks.append(peak)
        return tuple(new_peaks)

    steps = jnp.maximum(end - begin + KEYS // TILE - 1, 0) // (KEYS // TILE)
    return lax.fori_loop(0, steps, one, peaks)


def attend_kernel(ranges, queries, starts, ends, pairs, total, peak_out, masked, values):
    step = pl.program_id(0)
    width = queries.shape[1]
    heads = width // HEAD_DIM
    per_span = SPAN // TILE

    @pl.when(step == 0)
    def _():
        for number in range(pairs.shape[0] // TILE):
            rows = slice(number * TILE, (number + 1) * TILE)
            values[:, rows] = with_ones(pairs[rows, width:])

    mask_heads(queries, masked)
    total[...] = jnp.zeros_like(total)
    peaks = sweep(
        ranges[2 * step],
        ranges[2 * step + 1],
        per_span,
        pairs,
        lambda row: values[:, pl.ds(row, KEYS)],
        masked,
        starts[...],
        ends[...],
        total.at[0],
        tuple(jnp.full((1, TILE), NEG_FILL, jnp.float32) for _ in range(heads)),
    )
    for head in range(heads):
        peak_out[0, head : head + 1, :] = peaks[head]


def finish_kernel(meta, queries, starts, ends, before, after, total, peak_in, *refs):
    outs = refs[:-3]
    masked, sums, mixed = refs[-3:]
    step = pl.program_id(0)
    width = queries.shape[1]
    heads = width // HEAD_DIM
    per_span = SPAN // TILE
    own_tiles = pl.num_programs(0)
    sums[...] = total[0]
    begin, end = meta[1 + 2 * step], meta[2 + 2 * step]

    @pl.when((begin < per_span) | (end > per_span + own_tiles))
    def _():
        mask_heads(queries, masked)
        peaks = tuple(peak_in[0, head : head + 1, :] for head in range(heads))
        for chunk, base in ((before, 0), (after, per_span + own_tiles)):
            peaks = sweep(
                begin,
                end,
                base,
                chunk,
                lambda row: with_ones(chunk[pl.ds(row, KEYS), width:]),
                masked,
                starts[...],
                ends[...],
                sums,
                peaks,
            )

    parts = []
    for head in range(heads):
        row = head * HEAD_ROWS
        parts.append(sums[row : row + HEAD_DIM, :] / sums[row + HEAD_DIM : row + HEAD_DIM + 1, :])
    tile_rows = pl.ds(pl.multiple_of(step * TILE, TILE), TILE)
    mixed[tile_rows, :] = jnp.concatenate(parts, axis=0).T.astype(jnp.bfloat16)

    @pl.when(step == own_tiles - 1)
    def _():
        rows = outs[0].shape[0]
        for distance, out in enumerate(outs):
            out[...] = mixed[pl.ds(pl.multiple_of((meta[0] ^ distance) * rows, 128), rows), :]


def attend_specs(width, held):
    spec = lambda shape, index: pl.BlockSpec(shape, lambda i, m: index(i))
    return [
        spec((TILE, width), lambda i: (i, 0)),
        spec((1, TILE), lambda i: (0, i)),
        spec((1, TILE), lambda i: (0, i)),
    ] + [spec((rows, 2 * width), lambda i: (0, 0)) for rows in held]


def attend_local(ranges, queries, starts, ends, pairs):
    group_rows, width = queries.shape
    heads = width // HEAD_DIM
    tiles = group_rows // TILE
    return pl.pallas_call(
        attend_kernel,
        grid_spec=pltpu.PrefetchScalarGridSpec(
            num_scalar_prefetch=1,
            grid=(tiles,),
            in_specs=attend_specs(width, (group_rows,)),
            out_specs=[
                pl.BlockSpec((1, heads * HEAD_ROWS, TILE), lambda i, m: (i, 0, 0)),
                pl.BlockSpec((1, 8, TILE), lambda i, m: (i, 0, 0)),
            ],
            scratch_shapes=[
                pltpu.VMEM((heads, TILE, width), jnp.bfloat16),
                pltpu.VMEM((heads * HEAD_ROWS, group_rows), jnp.bfloat16),
            ],
        ),
        out_shape=[
            jax.ShapeDtypeStruct((tiles, heads * HEAD_ROWS, TILE), jnp.float32),
            jax.ShapeDtypeStruct((tiles, 8, TILE), jnp.float32),
        ],
        compiler_params=PARAMS,
        cost_estimate=pl.CostEstimate(
            flops=16 * group_rows * 1024 * width,
            bytes_accessed=5 << 20,
            transcendentals=group_rows * 1024 * heads,
        ),
        name="attend_local",
    )(ranges, queries, starts, ends, pairs)


def attend_finish(meta, queries, starts, ends, before, after, total, peaks, rows):
    group_rows, width = queries.shape
    heads = width // HEAD_DIM
    tiles = group_rows // TILE
    members = group_rows // rows
    return pl.pallas_call(
        finish_kernel,
        grid_spec=pltpu.PrefetchScalarGridSpec(
            num_scalar_prefetch=1,
            grid=(tiles,),
            in_specs=attend_specs(width, (SPAN, SPAN))
            + [
                pl.BlockSpec((1,) + total.shape[1:], lambda i, m: (i, 0, 0)),
                pl.BlockSpec((1,) + peaks.shape[1:], lambda i, m: (i, 0, 0)),
            ],
            out_specs=[pl.BlockSpec((rows, width), lambda i, m: (0, 0))] * members,
            scratch_shapes=[
                pltpu.VMEM((heads, TILE, width), jnp.bfloat16),
                pltpu.VMEM(total.shape[1:], jnp.float32),
                pltpu.VMEM((group_rows, width), jnp.bfloat16),
            ],
        ),
        out_shape=[jax.ShapeDtypeStruct((rows, width), jnp.bfloat16)] * members,
        compiler_params=PARAMS,
        cost_estimate=pl.CostEstimate(
            flops=4 * group_rows * 1024 * width,
            bytes_accessed=5 << 20,
            transcendentals=group_rows * 256 * heads,
        ),
        name="attend_finish",
    )(meta, queries, starts, ends, before, after, total, peaks)


def output_kernel(members, meta, *refs):
    parts, weight, result, mixed = refs[:members], refs[members], refs[-2], refs[-1]
    width = parts[0].shape[1]

    @pl.when(pl.program_id(0) == 0)
    def _():
        for distance in range(members):
            source = meta[0] ^ distance
            head_pair = PAIR * (source % (members // PAIR)) + source // (members // PAIR)
            columns = pl.ds(pl.multiple_of(head_pair * width, width), width)
            mixed[:, columns] = parts[distance][...]

    result[...] = jnp.dot(
        mixed[...], weight[...], preferred_element_type=jnp.float32
    ).astype(jnp.bfloat16)


def output_projection(meta, parts, weight):
    rows, width = parts[0].shape
    depth = width * len(parts)
    tile = weight.shape[1]
    steps = weight.shape[0] // depth
    return pl.pallas_call(
        functools.partial(output_kernel, len(parts)),
        grid_spec=pltpu.PrefetchScalarGridSpec(
            num_scalar_prefetch=1,
            grid=(steps,),
            in_specs=[pl.BlockSpec((rows, width), lambda i, m: (0, 0))] * len(parts)
            + [pl.BlockSpec((depth, tile), lambda i, m: (i, 0))],
            out_specs=pl.BlockSpec((rows, tile), lambda i, m: (0, i)),
            scratch_shapes=[pltpu.VMEM((rows, depth), jnp.bfloat16)],
        ),
        out_shape=jax.ShapeDtypeStruct((rows, steps * tile), jnp.bfloat16),
        compiler_params=PARAMS,
        cost_estimate=pl.CostEstimate(
            flops=2 * rows * depth * steps * tile, bytes_accessed=4 << 20, transcendentals=0
        ),
        name="output_projection",
    )(meta, *parts, weight)


def unpack_kernel(received, pages):
    _, pair, members, sources, capacity, part = received.shape
    width = part // (2 * PAGE)
    for source in range(sources):
        for low in range(pair):
            for high in range(members):
                head_pair = PAIR * high + low
                for turn in range(2 * PAGE):
                    start = (turn * pair * members + head_pair) * width
                    pages[source, :, start : start + width] = received[
                        0, low, high, source, :, turn * width : (turn + 1) * width
                    ]


def unpack(received):
    planes, pair, members, sources, capacity, part = received.shape
    return pl.pallas_call(
        unpack_kernel,
        grid=(planes,),
        in_specs=[
            pl.BlockSpec(
                (1, pair, members, sources, capacity, part), lambda i: (i, 0, 0, 0, 0, 0)
            )
        ],
        out_specs=pl.BlockSpec((sources, capacity, pair * members * part), lambda i: (i, 0, 0)),
        out_shape=jax.ShapeDtypeStruct(
            (planes * sources, capacity, pair * members * part), jnp.bfloat16
        ),
        compiler_params=pltpu.CompilerParams(vmem_limit_bytes=24 * 1024 * 1024),
        cost_estimate=pl.CostEstimate(flops=0, bytes_accessed=6 << 20, transcendentals=0),
        name="unpack",
    )(received)


def rope_tables(positions):
    half_dim = HEAD_DIM // 2
    inverse = 1.0 / ROPE_BASE ** (jnp.arange(half_dim, dtype=jnp.float32) * 2.0 / HEAD_DIM)
    angles = inverse[:, None] * positions.astype(jnp.float32)[None, :]
    return jnp.cos(angles), jnp.sin(angles)


def document_bounds(window_ids, rows, blocks):
    reach = SPAN + rows
    firsts = jnp.arange(blocks, dtype=jnp.int32)[:, None] * rows
    own = window_ids[SPAN : SPAN + rows * blocks].reshape(blocks, rows)
    behind = jnp.stack([window_ids[k * rows : k * rows + reach] for k in range(blocks)])
    ahead = jnp.stack(
        [window_ids[SPAN + k * rows : SPAN + k * rows + reach] for k in range(blocks)]
    )
    starts = jnp.sum((behind[:, None, :] < own[:, :, None]).astype(jnp.int32), axis=2) + firsts
    ends = (
        jnp.sum((ahead[:, None, :] <= own[:, :, None]).astype(jnp.int32), axis=2)
        + firsts
        + SPAN
    )
    return starts.reshape(-1), ends.reshape(-1)


def per_device(tokens, norm_gain, input_weight, output_weight, segment_ids, page_owner):
    rows, model_width = tokens.shape
    peers, members = lax.axis_size("tok"), lax.axis_size("grp")
    place, column = lax.axis_index("tok"), lax.axis_index("grp")
    low = place % PAIR
    blocks = PAIR * members
    member = low * members + column
    group_rows = rows * blocks
    width = model_width // blocks
    pages = rows // PAGE

    flat = peers * members
    owners = page_owner[:, 0]
    capacity = max(2, (2 * pages + peers - 1) // peers)
    halves = []
    for parity in range(PAIR):
        pieces = []
        for number in range(PARTS):
            start = number * PAIR * width
            choices = [input_weight[:, start : start + width], input_weight[:, start + width : start + 2 * width]]
            piece = jnp.where((low ^ parity) == 0, choices[0], choices[1])
            route = []
            for source in range(flat):
                row, column_from = divmod(source, members)
                target = (row ^ parity) * members + (PARTS * column_from + number) % members
                route.append((source, target))
            pieces.append(lax.ppermute(piece, ("tok", "grp"), route))
        halves.append(jnp.concatenate(pieces, axis=1))
    plane = jnp.concatenate(halves, axis=0)
    own = layer_norm(tokens, norm_gain[None, :], owners, capacity)
    own, plane = lax.optimization_barrier((own, plane))
    planes = {0: plane}
    bit = peers // 2
    while bit > 1:
        for distance in list(planes):
            planes[distance ^ bit] = flipped(planes[distance], "tok", bit)
        bit //= 2
    weights = [planes[distance] for distance in range(0, peers, 2)]

    across, along = flipped(own, "grp", 2), flipped(own, "tok", 1)
    held = rows + EXTRA_ROWS
    half = rows // 2
    corner_top = flipped(across[:half], "tok", 1)
    corner_bottom = flipped(along[half:], "grp", 2)
    near_blocks = [own, across, along]
    near_blocks += [flipped(block, "grp", 1) for block in near_blocks]
    near_layout = [[(number, 0, held)] for number in (0, 3, 1, 4, 2, 5)]
    corners = [corner_top, corner_bottom]
    corners += [flipped(corner, "grp", 1) for corner in corners]
    corner_layout = [
        [(number, 0, half), (number + 1, half, held - half)] for number in (0, 2)
    ]

    first_row = place // PAIR * group_rows
    padded_ids = jnp.concatenate(
        [
            jnp.full((SPAN,), -1, jnp.int32),
            segment_ids,
            jnp.full((SPAN,), 1 << 30, jnp.int32),
        ]
    )
    window_ids = lax.dynamic_slice_in_dim(padded_ids, first_row, group_rows + 2 * SPAN, 0)
    starts, ends = document_bounds(window_ids, rows, blocks)
    positions = SPAN + jnp.arange(group_rows, dtype=jnp.int32) - starts
    cosine, sine = rope_tables(positions)
    ranges = jnp.stack(
        [starts[::TILE] // TILE, (ends[TILE - 1 :: TILE] + TILE - 1) // TILE], axis=1
    ).reshape(-1)

    order = [
        (number * members + column) % PARTS for number in range(PARTS)
    ]
    meta = jnp.stack([member, place] + order).astype(jnp.int32)
    sizes = (weights, cosine, sine, rows, blocks, peers, capacity)
    begun = project(meta, 0, near_layout, near_blocks, *sizes, ())
    queries, pairs, send = project(meta, len(near_layout), corner_layout, corners, *sizes, begun)

    before = shifted(pairs[group_rows - SPAN :], "tok", PAIR)
    after = shifted(pairs[:SPAN], "tok", -PAIR)
    received = lax.all_to_all(
        send.reshape((peers * members,) + send.shape[2:]),
        ("tok", "grp"),
        split_axis=0,
        concat_axis=0,
        tiled=True,
    )

    last_shard, queries = lax.optimization_barrier((output_weight, queries))
    last_weight = natural_gather(natural_gather(last_shard, "tok"), "grp")

    bounds = (starts[None, :], ends[None, :])
    total, peaks = attend_local(ranges, queries, *bounds, pairs)
    own_member = member[None].astype(jnp.int32)
    mixed = attend_finish(
        jnp.concatenate([own_member, ranges]),
        queries,
        *bounds,
        before,
        after,
        total,
        peaks,
        rows,
    )
    parts = [mixed[0]] + [
        lax.ppermute(
            mixed[distance],
            ("tok", "grp"),
            [(source, source ^ distance) for source in range(flat)],
        )
        for distance in range(1, blocks)
    ]
    attended = output_projection(own_member, parts, last_weight)

    cache_pages = unpack(
        received.reshape((peers // PAIR, PAIR, members) + send.shape[2:])
    ).reshape(peers * capacity, 2 * PAGE * model_width)
    return attended, cache_pages


def solution(mesh):
    placed = (
        P(("tok", "grp"), None),
        P(),
        P("tok", "grp"),
        P("tok", "grp"),
        P(),
        P(("tok", "grp"), None),
    )
    return jax.shard_map(
        per_device,
        mesh=mesh,
        in_specs=placed,
        out_specs=(P(("tok", "grp"), None), P(("tok", "grp"), None)),
        check_vma=False,
    )
```

```python
import functools
import math

import jax
import jax.numpy as jnp
from jax import lax
from jax.experimental import pallas as pl
from jax.experimental.pallas import tpu as pltpu
from jax.sharding import PartitionSpec as P

H = 16
SPAN = 1024
PAGE = 4
HEAD_DIM = 64

NEG_FILL = -1e30
ROPE_BASE = 160000.0
EPSILON = 1e-05
TILE = 256
PARTS = 3
PAIR = 2
ONES_ROWS = 16
HEAD_ROWS = HEAD_DIM + ONES_ROWS
EXTRA_ROWS = 16
KEYS = 512
SCALE = HEAD_DIM ** (-0.5) * math.log2(math.e)
VMEM_LIMIT = 60 * 1024 * 1024
PARAMS = pltpu.CompilerParams(vmem_limit_bytes=VMEM_LIMIT)


def flipped(value, axis, bit):
    count = lax.axis_size(axis)
    return lax.ppermute(value, axis, [(source, source ^ bit) for source in range(count)])


def shifted(value, axis, steps):
    count = lax.axis_size(axis)
    initial, last = (max(0, -steps), min(count, count - steps))
    return lax.ppermute(value, axis, [(source, source + steps) for source in range(initial, last)])


def doubled(value, axis, bit, low):
    other = flipped(value, axis, bit)
    first = (lax.axis_index(axis) & bit) == 0
    pair = jnp.stack([jnp.where(first, value, other), jnp.where(first, other, value)], axis=low)
    return pair.reshape((-1,) + value.shape[1:])


def norm_kernel(capacity, tokens, gain, owner_row, normed, owners):
    rows = tokens.shape[0]
    values = tokens[...].astype(jnp.float32)
    centred = values - jnp.mean(values, axis=-1, keepdims=True)
    spread = jnp.mean(jnp.square(centred), axis=-1, keepdims=True)
    normed[:rows, :] = (centred * lax.rsqrt(spread + EPSILON) * gain[...]).astype(jnp.bfloat16)
    pages = owner_row.shape[1]
    owners[...] = jnp.full(owners.shape, -1.0, jnp.float32)
    owners[:1, :pages] = owner_row[...].astype(jnp.float32)
    lanes = owners.shape[1]
    across = jnp.broadcast_to(owners[:1, :], (lanes, lanes))
    earlier = lax.broadcasted_iota(jnp.int32, (lanes, lanes), 0) < lax.broadcasted_iota(
        jnp.int32, (lanes, lanes), 1
    )
    same = (across.T == across) & earlier
    ranks = jnp.sum(jnp.where(same, 1.0, 0.0), axis=0, keepdims=True)
    slots = owners[:1, :] * capacity + ranks
    normed[rows:, :] = jnp.zeros((EXTRA_ROWS, normed.shape[1]), jnp.bfloat16)
    normed[rows:, :lanes] = jnp.broadcast_to(slots, (EXTRA_ROWS, lanes)).astype(jnp.bfloat16)


def layer_norm(tokens, gain, owners, capacity):
    rows, width = tokens.shape
    lanes = -(-owners.shape[0] // 128) * 128
    return pl.pallas_call(
        functools.partial(norm_kernel, capacity),
        out_shape=jax.ShapeDtypeStruct((rows + EXTRA_ROWS, width), jnp.bfloat16),
        scratch_shapes=[pltpu.VMEM((8, lanes), jnp.float32)],
        compiler_params=PARAMS,
        name="layer_norm",
    )(tokens, gain, owners[None, :])


def project_kernel(first, layout, weight_count, peers, capacity, meta, *refs):
    operands = 1 + max(entry[0] for pieces in layout for entry in pieces)
    tokens = refs[:operands]
    weights = refs[operands : operands + weight_count]
    cosine, sine = refs[operands + weight_count : operands + weight_count + 2]
    query_out, pair_out, send_out, blocks, weight, page_source, sems = refs[-7:]
    step = pl.program_id(0)
    steps = len(layout)
    rows = query_out.shape[0]
    width = query_out.shape[1]
    shard = weights[0].shape[0] // 2

    def arrivals(number):
        return [
            pltpu.make_async_copy(
                tokens[operand],
                blocks.at[number, pl.ds(offset, count), :],
                sems.at[number, place],
            )
            for place, (operand, offset, count) in enumerate(layout[number])
        ]

    @pl.when(step == 0)
    def _():
        for number in range(steps):
            for copy in arrivals(number):
                copy.start()
        for plane in range(weight_count):
            for low in range(2):
                row = pl.multiple_of((meta[1] ^ (2 * plane + low)) * shard, shard)
                for number in range(PARTS):
                    column = pl.multiple_of(meta[2 + number] * width, width)
                    weight[pl.ds(row, shard), number * width : (number + 1) * width] = weights[
                        plane
                    ][low * shard : (low + 1) * shard, pl.ds(column, width)]

    for number in range(steps):

        @pl.when(step == number)
        def _():
            for copy in arrivals(number):
                copy.wait()

    joined = jnp.dot(blocks[step, :rows, :], weight[...], preferred_element_type=jnp.float32)
    cosines = jnp.concatenate([cosine[...]] * 4, axis=0).T
    sines = jnp.concatenate([-sine[...], sine[...]] * 2, axis=0).T
    first_half = lax.rem(lax.broadcasted_iota(jnp.int32, (rows, width), 1), HEAD_DIM) < (
        HEAD_DIM // 2
    )

    def rotate(values):
        partner = jnp.where(
            first_half,
            pltpu.roll(values, width - HEAD_DIM // 2, 1),
            pltpu.roll(values, HEAD_DIM // 2, 1),
        )
        return (values * cosines + partner * sines).astype(jnp.bfloat16)

    query_out[...] = rotate(joined[:, :width])
    keys = rotate(joined[:, width : 2 * width])
    values = joined[:, 2 * width :].astype(jnp.bfloat16)
    pair_out[:, :width] = keys
    pair_out[:, width:] = values
    page_source[0] = keys.astype(jnp.float32)
    page_source[1] = values.astype(jnp.float32)

    pages = rows // PAGE
    slot_count = peers * capacity
    slots = blocks[step, rows : rows + EXTRA_ROWS, :128].astype(jnp.float32)[:1, :pages]
    chosen = (
        lax.broadcasted_iota(jnp.int32, (slot_count, pages), 0).astype(jnp.float32) == slots
    ).astype(jnp.bfloat16)
    for turn in range(PAGE):
        page_part = jnp.concatenate(
            [
                page_source[half, pl.ds(turn, pages, stride=PAGE), :].astype(jnp.bfloat16)
                for half in range(2)
            ],
            axis=1,
        )
        placed = jnp.dot(chosen, page_part, preferred_element_type=jnp.float32)
        columns = slice(turn * 2 * width, (turn + 1) * 2 * width)
        for peer in range(peers):
            send_out[peer, 0, :, columns] = placed[
                peer * capacity : (peer + 1) * capacity
            ].astype(jnp.bfloat16)


def project(meta, first, layout, operands, weights, cosine, sine, rows, blocks, peers, capacity, into):
    steps = len(layout)
    model_width = operands[0].shape[1]
    group_rows = rows * blocks
    width = weights[0].shape[1] // PARTS
    members = blocks // PAIR
    whole = lambda shape: pl.BlockSpec(shape, lambda i, m: (0,) * len(shape))
    place = lambda i, m: m[0] ^ (first + i)
    table = pl.BlockSpec((HEAD_DIM // 2, rows), lambda i, m: (0, place(i, m)))
    send_shape = (peers, members, capacity, 2 * PAGE * width)
    return pl.pallas_call(
        functools.partial(project_kernel, first, layout, len(weights), peers, capacity),
        grid_spec=pltpu.PrefetchScalarGridSpec(
            num_scalar_prefetch=1,
            grid=(steps,),
            in_specs=[pl.BlockSpec(memory_space=pl.ANY)] * len(operands)
            + [whole(weights[0].shape)] * len(weights)
            + [table, table]
            + [pl.BlockSpec(memory_space=pl.ANY)] * len(into),
            out_specs=[
                pl.BlockSpec((rows, width), lambda i, m: (place(i, m), 0)),
                pl.BlockSpec((rows, 2 * width), lambda i, m: (place(i, m), 0)),
                pl.BlockSpec(
                    (peers, 1) + send_shape[2:], lambda i, m: (0, place(i, m) % members, 0, 0)
                ),
            ],
            scratch_shapes=[
                pltpu.VMEM((steps, rows + EXTRA_ROWS, model_width), jnp.bfloat16),
                pltpu.VMEM((model_width, PARTS * width), jnp.bfloat16),
                pltpu.VMEM((2, rows, width), jnp.float32),
                pltpu.SemaphoreType.DMA((steps, 2)),
            ],
        ),
        out_shape=[
            jax.ShapeDtypeStruct((group_rows, width), jnp.bfloat16),
            jax.ShapeDtypeStruct((group_rows, 2 * width), jnp.bfloat16),
            jax.ShapeDtypeStruct(send_shape, jnp.bfloat16),
        ],
        input_output_aliases={
            1 + len(operands) + len(weights) + 2 + number: number for number in range(len(into))
        },
        compiler_params=PARAMS,
        cost_estimate=pl.CostEstimate(
            flops=2 * steps * rows * model_width * PARTS * width,
            bytes_accessed=(3 * steps) << 19,
            transcendentals=0,
        ),
        name="project",
    )(meta, *operands, *weights, cosine, sine, *into)


def mask_heads(queries, masked):
    head_of_lane = lax.broadcasted_iota(jnp.int32, queries.shape, 1) // HEAD_DIM
    for head in range(masked.shape[0]):
        masked[head] = jnp.where(head_of_lane == head, queries[...], jnp.zeros((), jnp.bfloat16))


def with_ones(values):
    turned = values.T
    ones = jnp.ones((ONES_ROWS, values.shape[0]), values.dtype)
    rows = []
    for head in range(values.shape[1] // HEAD_DIM):
        rows += [turned[head * HEAD_DIM : (head + 1) * HEAD_DIM], ones]
    return jnp.concatenate(rows, axis=0)


def sweep(begin, end, base, pairs, values_of, masked, starts, ends, total, peaks):
    width = pairs.shape[1] // 2
    held = pairs.shape[0] // TILE
    begin = jnp.maximum(begin, base)
    end = jnp.minimum(end, base + held)
    last = jnp.minimum(ends, end * TILE)

    def one(number, peaks):
        wanted = begin + number * (KEYS // TILE)
        block = jnp.minimum(wanted, base + held - KEYS // TILE)
        row = pl.multiple_of((block - base) * TILE, TILE)
        keys = pairs[pl.ds(row, KEYS), :width]
        values = values_of(row)
        index = block * TILE + lax.broadcasted_iota(jnp.int32, (KEYS, TILE), 0)
        allowed = (index >= jnp.maximum(starts, wanted * TILE)) & (index < last)
        new_peaks = []
        for head, old_peak in enumerate(peaks):
            scores = lax.dot_general(
                keys, masked[head], (((1,), (1,)), ((), ())), preferred_element_type=jnp.float32
            )
            scores = jnp.where(allowed, scores * SCALE, NEG_FILL)
            peak = jnp.maximum(old_peak, jnp.max(scores, axis=0, keepdims=True))
            fade = jnp.exp2(old_peak - peak)
            weights = jnp.exp2(scores - peak).astype(jnp.bfloat16)
            own = slice(head * HEAD_ROWS, (head + 1) * HEAD_ROWS)
            total[own, :] = total[own, :] * fade + jnp.dot(
                values[own, :], weights, preferred_element_type=jnp.float32
            )
            new_peaks.append(peak)
        return tuple(new_peaks)

    steps = jnp.maximum(end - begin + KEYS // TILE - 1, 0) // (KEYS // TILE)
    return lax.fori_loop(0, steps, one, peaks)


def attend_kernel(ranges, queries, starts, ends, pairs, total, peak_out, masked, values):
    step = pl.program_id(0)
    width = queries.shape[1]
    heads = width // HEAD_DIM
    per_span = SPAN // TILE

    @pl.when(step == 0)
    def _():
        for number in range(pairs.shape[0] // TILE):
            rows = slice(number * TILE, (number + 1) * TILE)
            values[:, rows] = with_ones(pairs[rows, width:])

    mask_heads(queries, masked)
    total[...] = jnp.zeros_like(total)
    peaks = sweep(
        ranges[2 * step],
        ranges[2 * step + 1],
        per_span,
        pairs,
        lambda row: values[:, pl.ds(row, KEYS)],
        masked,
        starts[...],
        ends[...],
        total.at[0],
        tuple(jnp.full((1, TILE), NEG_FILL, jnp.float32) for _ in range(heads)),
    )
    for head in range(heads):
        peak_out[0, head : head + 1, :] = peaks[head]


def finish_kernel(meta, queries, starts, ends, before, after, total, peak_in, *refs):
    outs = refs[:-3]
    masked, sums, mixed = refs[-3:]
    step = pl.program_id(0)
    width = queries.shape[1]
    heads = width // HEAD_DIM
    per_span = SPAN // TILE
    own_tiles = pl.num_programs(0)
    sums[...] = total[0]
    begin, end = meta[1 + 2 * step], meta[2 + 2 * step]

    @pl.when((begin < per_span) | (end > per_span + own_tiles))
    def _():
        mask_heads(queries, masked)
        peaks = tuple(peak_in[0, head : head + 1, :] for head in range(heads))
        for chunk, base in ((before, 0), (after, per_span + own_tiles)):
            peaks = sweep(
                begin,
                end,
                base,
                chunk,
                lambda row: with_ones(chunk[pl.ds(row, KEYS), width:]),
                masked,
                starts[...],
                ends[...],
                sums,
                peaks,
            )

    parts = []
    for head in range(heads):
        row = head * HEAD_ROWS
        parts.append(sums[row : row + HEAD_DIM, :] / sums[row + HEAD_DIM : row + HEAD_DIM + 1, :])
    tile_rows = pl.ds(pl.multiple_of(step * TILE, TILE), TILE)
    mixed[tile_rows, :] = jnp.concatenate(parts, axis=0).T.astype(jnp.bfloat16)

    @pl.when(step == own_tiles - 1)
    def _():
        rows = outs[0].shape[0]
        for distance, out in enumerate(outs):
            out[...] = mixed[pl.ds(pl.multiple_of((meta[0] ^ distance) * rows, 128), rows), :]


def attend_specs(width, held):
    spec = lambda shape, index: pl.BlockSpec(shape, lambda i, m: index(i))
    return [
        spec((TILE, width), lambda i: (i, 0)),
        spec((1, TILE), lambda i: (0, i)),
        spec((1, TILE), lambda i: (0, i)),
    ] + [spec((rows, 2 * width), lambda i: (0, 0)) for rows in held]


def attend_local(ranges, queries, starts, ends, pairs):
    group_rows, width = queries.shape
    heads = width // HEAD_DIM
    tiles = group_rows // TILE
    return pl.pallas_call(
        attend_kernel,
        grid_spec=pltpu.PrefetchScalarGridSpec(
            num_scalar_prefetch=1,
            grid=(tiles,),
            in_specs=attend_specs(width, (group_rows,)),
            out_specs=[
                pl.BlockSpec((1, heads * HEAD_ROWS, TILE), lambda i, m: (i, 0, 0)),
                pl.BlockSpec((1, 8, TILE), lambda i, m: (i, 0, 0)),
            ],
            scratch_shapes=[
                pltpu.VMEM((heads, TILE, width), jnp.bfloat16),
                pltpu.VMEM((heads * HEAD_ROWS, group_rows), jnp.bfloat16),
            ],
        ),
        out_shape=[
            jax.ShapeDtypeStruct((tiles, heads * HEAD_ROWS, TILE), jnp.float32),
            jax.ShapeDtypeStruct((tiles, 8, TILE), jnp.float32),
        ],
        compiler_params=PARAMS,
        cost_estimate=pl.CostEstimate(
            flops=16 * group_rows * 1024 * width,
            bytes_accessed=5 << 20,
            transcendentals=group_rows * 1024 * heads,
        ),
        name="attend_local",
    )(ranges, queries, starts, ends, pairs)


def attend_finish(meta, queries, starts, ends, before, after, total, peaks, rows):
    group_rows, width = queries.shape
    heads = width // HEAD_DIM
    tiles = group_rows // TILE
    members = group_rows // rows
    return pl.pallas_call(
        finish_kernel,
        grid_spec=pltpu.PrefetchScalarGridSpec(
            num_scalar_prefetch=1,
            grid=(tiles,),
            in_specs=attend_specs(width, (SPAN, SPAN))
            + [
                pl.BlockSpec((1,) + total.shape[1:], lambda i, m: (i, 0, 0)),
                pl.BlockSpec((1,) + peaks.shape[1:], lambda i, m: (i, 0, 0)),
            ],
            out_specs=[pl.BlockSpec((rows, width), lambda i, m: (0, 0))] * members,
            scratch_shapes=[
                pltpu.VMEM((heads, TILE, width), jnp.bfloat16),
                pltpu.VMEM(total.shape[1:], jnp.float32),
                pltpu.VMEM((group_rows, width), jnp.bfloat16),
            ],
        ),
        out_shape=[jax.ShapeDtypeStruct((rows, width), jnp.bfloat16)] * members,
        compiler_params=PARAMS,
        cost_estimate=pl.CostEstimate(
            flops=4 * group_rows * 1024 * width,
            bytes_accessed=5 << 20,
            transcendentals=group_rows * 256 * heads,
        ),
        name="attend_finish",
    )(meta, queries, starts, ends, before, after, total, peaks)


def output_kernel(members, meta, *refs):
    parts, weight, result, mixed = refs[:members], refs[members], refs[-2], refs[-1]
    width = parts[0].shape[1]

    @pl.when(pl.program_id(0) == 0)
    def _():
        for distance in range(members):
            source = meta[0] ^ distance
            head_pair = PAIR * (source % (members // PAIR)) + source // (members // PAIR)
            columns = pl.ds(pl.multiple_of(head_pair * width, width), width)
            mixed[:, columns] = parts[distance][...]

    result[...] = jnp.dot(
        mixed[...], weight[...], preferred_element_type=jnp.float32
    ).astype(jnp.bfloat16)


def output_projection(meta, parts, weight):
    rows, width = parts[0].shape
    depth = width * len(parts)
    tile = weight.shape[1]
    steps = weight.shape[0] // depth
    return pl.pallas_call(
        functools.partial(output_kernel, len(parts)),
        grid_spec=pltpu.PrefetchScalarGridSpec(
            num_scalar_prefetch=1,
            grid=(steps,),
            in_specs=[pl.BlockSpec((rows, width), lambda i, m: (0, 0))] * len(parts)
            + [pl.BlockSpec((depth, tile), lambda i, m: (i, 0))],
            out_specs=pl.BlockSpec((rows, tile), lambda i, m: (0, i)),
            scratch_shapes=[pltpu.VMEM((rows, depth), jnp.bfloat16)],
        ),
        out_shape=jax.ShapeDtypeStruct((rows, steps * tile), jnp.bfloat16),
        compiler_params=PARAMS,
        cost_estimate=pl.CostEstimate(
            flops=2 * rows * depth * steps * tile, bytes_accessed=4 << 20, transcendentals=0
        ),
        name="output_projection",
    )(meta, *parts, weight)


def unpack_kernel(own_row, other_row, pages):
    _, pair, members, capacity, part = own_row.shape
    width = part // (2 * PAGE)
    for source in range(pair):
        for low in range(pair):
            received = own_row if source == low else other_row
            for high in range(members):
                for turn in range(2 * PAGE):
                    start = (turn * pair * members + PAIR * high + low) * width
                    pages[source, :, start : start + width] = received[
                        0, low, high, :, turn * width : (turn + 1) * width
                    ]


def unpack(own_row, other_row):
    planes, pair, members, capacity, part = own_row.shape
    block = pl.BlockSpec((1,) + own_row.shape[1:], lambda i: (i, 0, 0, 0, 0))
    return pl.pallas_call(
        unpack_kernel,
        grid=(planes,),
        in_specs=[block, block],
        out_specs=pl.BlockSpec((pair, capacity, pair * members * part), lambda i: (i, 0, 0)),
        out_shape=jax.ShapeDtypeStruct(
            (planes * pair, capacity, pair * members * part), jnp.bfloat16
        ),
        compiler_params=pltpu.CompilerParams(vmem_limit_bytes=24 * 1024 * 1024),
        cost_estimate=pl.CostEstimate(flops=0, bytes_accessed=6 << 20, transcendentals=0),
        name="unpack",
    )(own_row, other_row)


def rope_tables(positions):
    half_dim = HEAD_DIM // 2
    inverse = 1.0 / ROPE_BASE ** (jnp.arange(half_dim, dtype=jnp.float32) * 2.0 / HEAD_DIM)
    angles = inverse[:, None] * positions.astype(jnp.float32)[None, :]
    return jnp.cos(angles), jnp.sin(angles)


def document_bounds(window_ids, rows, blocks):
    reach = SPAN + rows
    firsts = jnp.arange(blocks, dtype=jnp.int32)[:, None] * rows
    own = window_ids[SPAN : SPAN + rows * blocks].reshape(blocks, rows)
    behind = jnp.stack([window_ids[k * rows : k * rows + reach] for k in range(blocks)])
    ahead = jnp.stack(
        [window_ids[SPAN + k * rows : SPAN + k * rows + reach] for k in range(blocks)]
    )
    starts = jnp.sum((behind[:, None, :] < own[:, :, None]).astype(jnp.int32), axis=2) + firsts
    ends = (
        jnp.sum((ahead[:, None, :] <= own[:, :, None]).astype(jnp.int32), axis=2)
        + firsts
        + SPAN
    )
    return starts.reshape(-1), ends.reshape(-1)


def per_device(tokens, norm_gain, input_weight, output_weight, segment_ids, page_owner):
    rows, model_width = tokens.shape
    peers, members = lax.axis_size("tok"), lax.axis_size("grp")
    place, column = lax.axis_index("tok"), lax.axis_index("grp")
    low = place % PAIR
    blocks = PAIR * members
    member = low * members + column
    group_rows = rows * blocks
    width = model_width // blocks
    pages = rows // PAGE

    flat = peers * members
    owners = page_owner[:, 0]
    capacity = max(2, (2 * pages + peers - 1) // peers)
    halves = []
    for parity in range(PAIR):
        pieces = []
        for number in range(PARTS):
            start = number * PAIR * width
            choices = [input_weight[:, start : start + width], input_weight[:, start + width : start + 2 * width]]
            piece = jnp.where((low ^ parity) == 0, choices[0], choices[1])
            route = []
            for source in range(flat):
                row, column_from = divmod(source, members)
                target = (row ^ parity) * members + (PARTS * column_from + number) % members
                route.append((source, target))
            pieces.append(lax.ppermute(piece, ("tok", "grp"), route))
        halves.append(jnp.concatenate(pieces, axis=1))
    plane = jnp.concatenate(halves, axis=0)
    own = layer_norm(tokens, norm_gain[None, :], owners, capacity)
    own, plane = lax.optimization_barrier((own, plane))
    planes = {0: plane}
    bit = peers // 2
    while bit > 1:
        for distance in list(planes):
            planes[distance ^ bit] = flipped(planes[distance], "tok", bit)
        bit //= 2
    weights = [planes[distance] for distance in range(0, peers, 2)]

    across, along = flipped(own, "grp", 2), flipped(own, "tok", 1)
    held = rows + EXTRA_ROWS
    half = rows // 2
    corner_top = flipped(across[:half], "tok", 1)
    corner_bottom = flipped(along[half:], "grp", 2)
    near_blocks = [own, flipped(own, "grp", 1), across, flipped(across, "grp", 1)]
    near_layout = [[(number, 0, held)] for number in range(4)]

    last_weight = output_weight
    bit = PAIR
    while bit < peers:
        last_weight = doubled(last_weight, "tok", bit, 0)
        bit *= 2
    last_weight = last_weight.reshape((peers // PAIR,) + output_weight.shape)
    last_weight = doubled(last_weight, "tok", 1, 1).reshape(model_width, output_weight.shape[1])

    first_row = place // PAIR * group_rows
    padded_ids = jnp.concatenate(
        [
            jnp.full((SPAN,), -1, jnp.int32),
            segment_ids,
            jnp.full((SPAN,), 1 << 30, jnp.int32),
        ]
    )
    window_ids = lax.dynamic_slice_in_dim(padded_ids, first_row, group_rows + 2 * SPAN, 0)
    starts, ends = document_bounds(window_ids, rows, blocks)
    positions = SPAN + jnp.arange(group_rows, dtype=jnp.int32) - starts
    cosine, sine = rope_tables(positions)
    ranges = jnp.stack(
        [starts[::TILE] // TILE, (ends[TILE - 1 :: TILE] + TILE - 1) // TILE], axis=1
    ).reshape(-1)

    order = [
        (number * members + column) % PARTS for number in range(PARTS)
    ]
    meta = jnp.stack([member, place] + order).astype(jnp.int32)
    sizes = (weights, cosine, sine, rows, blocks, peers, capacity)

    def to_owners(send):
        received = lax.all_to_all(
            send.reshape((flat,) + send.shape[2:]),
            ("tok", "grp"),
            split_axis=0,
            concat_axis=0,
            tiled=True,
        )
        return received.reshape((peers // PAIR, PAIR, members) + send.shape[2:])

    queries, pairs, send = project(meta, 0, near_layout, near_blocks, *sizes, ())
    own_row = to_owners(send)
    corner_top, corner_bottom, queries = lax.optimization_barrier(
        (corner_top, corner_bottom, queries)
    )
    far_blocks = [along, flipped(along, "grp", 1), corner_top, corner_bottom]
    far_blocks += [flipped(corner_top, "grp", 1), flipped(corner_bottom, "grp", 1)]
    far_layout = [[(0, 0, held)], [(1, 0, held)]]
    far_layout += [[(number, 0, half), (number + 1, half, held - half)] for number in (2, 4)]
    queries, pairs, send = project(meta, 4, far_layout, far_blocks, *sizes, (queries, pairs))
    before = shifted(pairs[group_rows - SPAN :], "tok", PAIR)
    after = shifted(pairs[:SPAN], "tok", -PAIR)
    other_row = to_owners(send)

    last_weight, pairs = lax.optimization_barrier((last_weight, pairs))
    last_weight = doubled(last_weight[None], "grp", 2, 0)

    bounds = (starts[None, :], ends[None, :])
    total, peaks = attend_local(ranges, queries, *bounds, pairs)
    last_weight, total = lax.optimization_barrier((last_weight, total))
    last_weight = doubled(last_weight, "grp", 1, 1).reshape(members * model_width, -1)
    own_member = member[None].astype(jnp.int32)
    mixed = attend_finish(
        jnp.concatenate([own_member, ranges]),
        queries,
        *bounds,
        before,
        after,
        total,
        peaks,
        rows,
    )
    parts = [mixed[0]] + [
        lax.ppermute(
            mixed[distance],
            ("tok", "grp"),
            [(source, source ^ distance) for source in range(flat)],
        )
        for distance in range(1, blocks)
    ]
    attended = output_projection(own_member, parts, last_weight)

    cache_pages = unpack(own_row, other_row).reshape(
        peers * capacity, 2 * PAGE * model_width
    )
    return attended, cache_pages


def solution(mesh):
    placed = (
        P(("tok", "grp"), None),
        P(),
        P("tok", "grp"),
        P("tok", "grp"),
        P(),
        P(("tok", "grp"), None),
    )
    return jax.shard_map(
        per_device,
        mesh=mesh,
        in_specs=placed,
        out_specs=(P(("tok", "grp"), None), P(("tok", "grp"), None)),
        check_vma=False,
    )
```

```python
import functools
import math

import jax
import jax.numpy as jnp
from jax import lax
from jax.experimental import pallas as pl
from jax.experimental.pallas import tpu as pltpu
from jax.sharding import PartitionSpec as P

H = 16
SPAN = 1024
PAGE = 4
HEAD_DIM = 64

NEG_FILL = -1e30
ROPE_BASE = 160000.0
EPSILON = 1e-05
TILE = 256
PARTS = 3
PAIR = 2
ONES_ROWS = 16
HEAD_ROWS = HEAD_DIM + ONES_ROWS
EXTRA_ROWS = 16
KEYS = 512
SCALE = HEAD_DIM ** (-0.5) * math.log2(math.e)
VMEM_LIMIT = 60 * 1024 * 1024
PARAMS = pltpu.CompilerParams(vmem_limit_bytes=VMEM_LIMIT)


def flipped(value, axis, bit):
    count = lax.axis_size(axis)
    return lax.ppermute(value, axis, [(source, source ^ bit) for source in range(count)])


def shifted(value, axis, steps):
    count = lax.axis_size(axis)
    initial, last = (max(0, -steps), min(count, count - steps))
    return lax.ppermute(value, axis, [(source, source + steps) for source in range(initial, last)])


def doubled(value, axis, bit, low):
    other = flipped(value, axis, bit)
    first = (lax.axis_index(axis) & bit) == 0
    pair = jnp.stack([jnp.where(first, value, other), jnp.where(first, other, value)], axis=low)
    return pair.reshape((-1,) + value.shape[1:])


def norm_kernel(capacity, tokens, gain, owner_row, top, bottom, owners):
    half = top.shape[0]
    rest = tokens.shape[0] - half
    values = tokens[...].astype(jnp.float32)
    centred = values - jnp.mean(values, axis=-1, keepdims=True)
    spread = jnp.mean(jnp.square(centred), axis=-1, keepdims=True)
    normed = (centred * lax.rsqrt(spread + EPSILON) * gain[...]).astype(jnp.bfloat16)
    top[...] = normed[:half]
    bottom[:rest, :] = normed[half:]
    pages = owner_row.shape[1]
    owners[...] = jnp.full(owners.shape, -1.0, jnp.float32)
    owners[:1, :pages] = owner_row[...].astype(jnp.float32)
    lanes = owners.shape[1]
    across = jnp.broadcast_to(owners[:1, :], (lanes, lanes))
    earlier = lax.broadcasted_iota(jnp.int32, (lanes, lanes), 0) < lax.broadcasted_iota(
        jnp.int32, (lanes, lanes), 1
    )
    same = (across.T == across) & earlier
    ranks = jnp.sum(jnp.where(same, 1.0, 0.0), axis=0, keepdims=True)
    slots = owners[:1, :] * capacity + ranks
    bottom[rest:, :] = jnp.zeros((EXTRA_ROWS, bottom.shape[1]), jnp.bfloat16)
    bottom[rest:, :lanes] = jnp.broadcast_to(slots, (EXTRA_ROWS, lanes)).astype(jnp.bfloat16)


def layer_norm(tokens, gain, owners, capacity):
    rows, width = tokens.shape
    lanes = -(-owners.shape[0] // 128) * 128
    return pl.pallas_call(
        functools.partial(norm_kernel, capacity),
        out_shape=[
            jax.ShapeDtypeStruct((rows // 2, width), jnp.bfloat16),
            jax.ShapeDtypeStruct((rows // 2 + EXTRA_ROWS, width), jnp.bfloat16),
        ],
        scratch_shapes=[pltpu.VMEM((8, lanes), jnp.float32)],
        compiler_params=PARAMS,
        name="layer_norm",
    )(tokens, gain, owners[None, :])


def project_kernel(first, layout, weight_count, peers, capacity, meta, *refs):
    operands = 1 + max(entry[0] for pieces in layout for entry in pieces)
    tokens = refs[:operands]
    weights = refs[operands : operands + weight_count]
    cosine, sine = refs[operands + weight_count : operands + weight_count + 2]
    query_out, pair_out, send_out, blocks, weight, page_source, sems = refs[-7:]
    step = pl.program_id(0)
    steps = len(layout)
    rows = query_out.shape[0]
    width = query_out.shape[1]
    shard = weights[0].shape[0] // 2

    def arrivals(number):
        return [
            pltpu.make_async_copy(
                tokens[operand],
                blocks.at[number, pl.ds(offset, count), :],
                sems.at[number, place],
            )
            for place, (operand, offset, count) in enumerate(layout[number])
        ]

    @pl.when(step == 0)
    def _():
        for number in range(steps):
            for copy in arrivals(number):
                copy.start()
        for plane in range(weight_count):
            for low in range(2):
                row = pl.multiple_of((meta[1] ^ (2 * plane + low)) * shard, shard)
                for number in range(PARTS):
                    column = pl.multiple_of(meta[2 + number] * width, width)
                    weight[pl.ds(row, shard), number * width : (number + 1) * width] = weights[
                        plane
                    ][low * shard : (low + 1) * shard, pl.ds(column, width)]

    for number in range(steps):

        @pl.when(step == number)
        def _():
            for copy in arrivals(number):
                copy.wait()

    joined = jnp.dot(blocks[step, :rows, :], weight[...], preferred_element_type=jnp.float32)
    cosines = jnp.concatenate([cosine[...]] * 4, axis=0).T
    sines = jnp.concatenate([-sine[...], sine[...]] * 2, axis=0).T
    first_half = lax.rem(lax.broadcasted_iota(jnp.int32, (rows, width), 1), HEAD_DIM) < (
        HEAD_DIM // 2
    )

    def rotate(values):
        partner = jnp.where(
            first_half,
            pltpu.roll(values, width - HEAD_DIM // 2, 1),
            pltpu.roll(values, HEAD_DIM // 2, 1),
        )
        return (values * cosines + partner * sines).astype(jnp.bfloat16)

    query_out[...] = rotate(joined[:, :width])
    keys = rotate(joined[:, width : 2 * width])
    values = joined[:, 2 * width :].astype(jnp.bfloat16)
    pair_out[:, :width] = keys
    pair_out[:, width:] = values
    page_source[0] = keys.astype(jnp.float32)
    page_source[1] = values.astype(jnp.float32)

    pages = rows // PAGE
    slot_count = peers * capacity
    slots = blocks[step, rows : rows + EXTRA_ROWS, :128].astype(jnp.float32)[:1, :pages]
    chosen = (
        lax.broadcasted_iota(jnp.int32, (slot_count, pages), 0).astype(jnp.float32) == slots
    ).astype(jnp.bfloat16)
    for turn in range(PAGE):
        page_part = jnp.concatenate(
            [
                page_source[half, pl.ds(turn, pages, stride=PAGE), :].astype(jnp.bfloat16)
                for half in range(2)
            ],
            axis=1,
        )
        placed = jnp.dot(chosen, page_part, preferred_element_type=jnp.float32)
        columns = slice(turn * 2 * width, (turn + 1) * 2 * width)
        for peer in range(peers):
            send_out[peer, 0, :, columns] = placed[
                peer * capacity : (peer + 1) * capacity
            ].astype(jnp.bfloat16)


def project(meta, first, layout, operands, weights, cosine, sine, rows, blocks, peers, capacity, into):
    steps = len(layout)
    model_width = operands[0].shape[1]
    group_rows = rows * blocks
    width = weights[0].shape[1] // PARTS
    members = blocks // PAIR
    whole = lambda shape: pl.BlockSpec(shape, lambda i, m: (0,) * len(shape))
    place = lambda i, m: m[0] ^ (first + i)
    table = pl.BlockSpec((HEAD_DIM // 2, rows), lambda i, m: (0, place(i, m)))
    send_shape = (peers, members, capacity, 2 * PAGE * width)
    return pl.pallas_call(
        functools.partial(project_kernel, first, layout, len(weights), peers, capacity),
        grid_spec=pltpu.PrefetchScalarGridSpec(
            num_scalar_prefetch=1,
            grid=(steps,),
            in_specs=[pl.BlockSpec(memory_space=pl.ANY)] * len(operands)
            + [whole(weights[0].shape)] * len(weights)
            + [table, table]
            + [pl.BlockSpec(memory_space=pl.ANY)] * len(into),
            out_specs=[
                pl.BlockSpec((rows, width), lambda i, m: (place(i, m), 0)),
                pl.BlockSpec((rows, 2 * width), lambda i, m: (place(i, m), 0)),
                pl.BlockSpec(
                    (peers, 1) + send_shape[2:], lambda i, m: (0, place(i, m) % members, 0, 0)
                ),
            ],
            scratch_shapes=[
                pltpu.VMEM((steps, rows + EXTRA_ROWS, model_width), jnp.bfloat16),
                pltpu.VMEM((model_width, PARTS * width), jnp.bfloat16),
                pltpu.VMEM((2, rows, width), jnp.float32),
                pltpu.SemaphoreType.DMA((steps, 2)),
            ],
        ),
        out_shape=[
            jax.ShapeDtypeStruct((group_rows, width), jnp.bfloat16),
            jax.ShapeDtypeStruct((group_rows, 2 * width), jnp.bfloat16),
            jax.ShapeDtypeStruct(send_shape, jnp.bfloat16),
        ],
        input_output_aliases={
            1 + len(operands) + len(weights) + 2 + number: number for number in range(len(into))
        },
        compiler_params=PARAMS,
        cost_estimate=pl.CostEstimate(
            flops=2 * steps * rows * model_width * PARTS * width,
            bytes_accessed=(3 * steps) << 19,
            transcendentals=0,
        ),
        name="project",
    )(meta, *operands, *weights, cosine, sine, *into)


def mask_heads(queries, masked):
    head_of_lane = lax.broadcasted_iota(jnp.int32, queries.shape, 1) // HEAD_DIM
    for head in range(masked.shape[0]):
        masked[head] = jnp.where(head_of_lane == head, queries[...], jnp.zeros((), jnp.bfloat16))


def with_ones(values):
    turned = values.T
    ones = jnp.ones((ONES_ROWS, values.shape[0]), values.dtype)
    rows = []
    for head in range(values.shape[1] // HEAD_DIM):
        rows += [turned[head * HEAD_DIM : (head + 1) * HEAD_DIM], ones]
    return jnp.concatenate(rows, axis=0)


def sweep(begin, end, base, pairs, values_of, masked, starts, ends, total, peaks):
    width = pairs.shape[1] // 2
    held = pairs.shape[0] // TILE
    begin = jnp.maximum(begin, base)
    end = jnp.minimum(end, base + held)
    last = jnp.minimum(ends, end * TILE)

    def one(number, peaks):
        wanted = begin + number * (KEYS // TILE)
        block = jnp.minimum(wanted, base + held - KEYS // TILE)
        row = pl.multiple_of((block - base) * TILE, TILE)
        keys = pairs[pl.ds(row, KEYS), :width]
        values = values_of(row)
        index = block * TILE + lax.broadcasted_iota(jnp.int32, (KEYS, TILE), 0)
        allowed = (index >= jnp.maximum(starts, wanted * TILE)) & (index < last)
        new_peaks = []
        for head, old_peak in enumerate(peaks):
            scores = lax.dot_general(
                keys, masked[head], (((1,), (1,)), ((), ())), preferred_element_type=jnp.float32
            )
            scores = jnp.where(allowed, scores * SCALE, NEG_FILL)
            peak = jnp.maximum(old_peak, jnp.max(scores, axis=0, keepdims=True))
            fade = jnp.exp2(old_peak - peak)
            weights = jnp.exp2(scores - peak).astype(jnp.bfloat16)
            own = slice(head * HEAD_ROWS, (head + 1) * HEAD_ROWS)
            total[own, :] = total[own, :] * fade + jnp.dot(
                values[own, :], weights, preferred_element_type=jnp.float32
            )
            new_peaks.append(peak)
        return tuple(new_peaks)

    steps = jnp.maximum(end - begin + KEYS // TILE - 1, 0) // (KEYS // TILE)
    return lax.fori_loop(0, steps, one, peaks)


def attend_kernel(ranges, queries, starts, ends, pairs, total, peak_out, masked, values):
    step = pl.program_id(0)
    width = queries.shape[1]
    heads = width // HEAD_DIM
    per_span = SPAN // TILE

    @pl.when(step == 0)
    def _():
        for number in range(pairs.shape[0] // TILE):
            rows = slice(number * TILE, (number + 1) * TILE)
            values[:, rows] = with_ones(pairs[rows, width:])

    mask_heads(queries, masked)
    total[...] = jnp.zeros_like(total)
    peaks = sweep(
        ranges[2 * step],
        ranges[2 * step + 1],
        per_span,
        pairs,
        lambda row: values[:, pl.ds(row, KEYS)],
        masked,
        starts[...],
        ends[...],
        total.at[0],
        tuple(jnp.full((1, TILE), NEG_FILL, jnp.float32) for _ in range(heads)),
    )
    for head in range(heads):
        peak_out[0, head : head + 1, :] = peaks[head]


def finish_kernel(meta, queries, starts, ends, before, after, total, peak_in, *refs):
    outs = refs[:-3]
    masked, sums, mixed = refs[-3:]
    step = pl.program_id(0)
    width = queries.shape[1]
    heads = width // HEAD_DIM
    per_span = SPAN // TILE
    own_tiles = pl.num_programs(0)
    sums[...] = total[0]
    begin, end = meta[1 + 2 * step], meta[2 + 2 * step]

    @pl.when((begin < per_span) | (end > per_span + own_tiles))
    def _():
        mask_heads(queries, masked)
        peaks = tuple(peak_in[0, head : head + 1, :] for head in range(heads))
        for chunk, base in ((before, 0), (after, per_span + own_tiles)):
            peaks = sweep(
                begin,
                end,
                base,
                chunk,
                lambda row: with_ones(chunk[pl.ds(row, KEYS), width:]),
                masked,
                starts[...],
                ends[...],
                sums,
                peaks,
            )

    parts = []
    for head in range(heads):
        row = head * HEAD_ROWS
        parts.append(sums[row : row + HEAD_DIM, :] / sums[row + HEAD_DIM : row + HEAD_DIM + 1, :])
    tile_rows = pl.ds(pl.multiple_of(step * TILE, TILE), TILE)
    mixed[tile_rows, :] = jnp.concatenate(parts, axis=0).T.astype(jnp.bfloat16)

    @pl.when(step == own_tiles - 1)
    def _():
        rows = outs[0].shape[0]
        for distance, out in enumerate(outs):
            out[...] = mixed[pl.ds(pl.multiple_of((meta[0] ^ distance) * rows, 128), rows), :]


def attend_specs(width, held):
    spec = lambda shape, index: pl.BlockSpec(shape, lambda i, m: index(i))
    return [
        spec((TILE, width), lambda i: (i, 0)),
        spec((1, TILE), lambda i: (0, i)),
        spec((1, TILE), lambda i: (0, i)),
    ] + [spec((rows, 2 * width), lambda i: (0, 0)) for rows in held]


def attend_local(ranges, queries, starts, ends, pairs):
    group_rows, width = queries.shape
    heads = width // HEAD_DIM
    tiles = group_rows // TILE
    return pl.pallas_call(
        attend_kernel,
        grid_spec=pltpu.PrefetchScalarGridSpec(
            num_scalar_prefetch=1,
            grid=(tiles,),
            in_specs=attend_specs(width, (group_rows,)),
            out_specs=[
                pl.BlockSpec((1, heads * HEAD_ROWS, TILE), lambda i, m: (i, 0, 0)),
                pl.BlockSpec((1, 8, TILE), lambda i, m: (i, 0, 0)),
            ],
            scratch_shapes=[
                pltpu.VMEM((heads, TILE, width), jnp.bfloat16),
                pltpu.VMEM((heads * HEAD_ROWS, group_rows), jnp.bfloat16),
            ],
        ),
        out_shape=[
            jax.ShapeDtypeStruct((tiles, heads * HEAD_ROWS, TILE), jnp.float32),
            jax.ShapeDtypeStruct((tiles, 8, TILE), jnp.float32),
        ],
        compiler_params=PARAMS,
        cost_estimate=pl.CostEstimate(
            flops=16 * group_rows * 1024 * width,
            bytes_accessed=5 << 20,
            transcendentals=group_rows * 1024 * heads,
        ),
        name="attend_local",
    )(ranges, queries, starts, ends, pairs)


def attend_finish(meta, queries, starts, ends, before, after, total, peaks, rows):
    group_rows, width = queries.shape
    heads = width // HEAD_DIM
    tiles = group_rows // TILE
    members = group_rows // rows
    return pl.pallas_call(
        finish_kernel,
        grid_spec=pltpu.PrefetchScalarGridSpec(
            num_scalar_prefetch=1,
            grid=(tiles,),
            in_specs=attend_specs(width, (SPAN, SPAN))
            + [
                pl.BlockSpec((1,) + total.shape[1:], lambda i, m: (i, 0, 0)),
                pl.BlockSpec((1,) + peaks.shape[1:], lambda i, m: (i, 0, 0)),
            ],
            out_specs=[pl.BlockSpec((rows, width), lambda i, m: (0, 0))] * members,
            scratch_shapes=[
                pltpu.VMEM((heads, TILE, width), jnp.bfloat16),
                pltpu.VMEM(total.shape[1:], jnp.float32),
                pltpu.VMEM((group_rows, width), jnp.bfloat16),
            ],
        ),
        out_shape=[jax.ShapeDtypeStruct((rows, width), jnp.bfloat16)] * members,
        compiler_params=PARAMS,
        cost_estimate=pl.CostEstimate(
            flops=4 * group_rows * 1024 * width,
            bytes_accessed=5 << 20,
            transcendentals=group_rows * 256 * heads,
        ),
        name="attend_finish",
    )(meta, queries, starts, ends, before, after, total, peaks)


def output_kernel(members, meta, *refs):
    parts, weight, result, mixed = refs[:members], refs[members], refs[-2], refs[-1]
    width = parts[0].shape[1]

    @pl.when(pl.program_id(0) == 0)
    def _():
        for distance in range(members):
            source = meta[0] ^ distance
            head_pair = PAIR * (source % (members // PAIR)) + source // (members // PAIR)
            columns = pl.ds(pl.multiple_of(head_pair * width, width), width)
            mixed[:, columns] = parts[distance][...]

    result[...] = jnp.dot(
        mixed[...], weight[...], preferred_element_type=jnp.float32
    ).astype(jnp.bfloat16)


def output_projection(meta, parts, weight):
    rows, width = parts[0].shape
    depth = width * len(parts)
    tile = weight.shape[1]
    steps = weight.shape[0] // depth
    return pl.pallas_call(
        functools.partial(output_kernel, len(parts)),
        grid_spec=pltpu.PrefetchScalarGridSpec(
            num_scalar_prefetch=1,
            grid=(steps,),
            in_specs=[pl.BlockSpec((rows, width), lambda i, m: (0, 0))] * len(parts)
            + [pl.BlockSpec((depth, tile), lambda i, m: (i, 0))],
            out_specs=pl.BlockSpec((rows, tile), lambda i, m: (0, i)),
            scratch_shapes=[pltpu.VMEM((rows, depth), jnp.bfloat16)],
        ),
        out_shape=jax.ShapeDtypeStruct((rows, steps * tile), jnp.bfloat16),
        compiler_params=PARAMS,
        cost_estimate=pl.CostEstimate(
            flops=2 * rows * depth * steps * tile, bytes_accessed=4 << 20, transcendentals=0
        ),
        name="output_projection",
    )(meta, *parts, weight)


def unpack_kernel(own_row, other_row, pages):
    _, pair, members, capacity, part = own_row.shape
    width = part // (2 * PAGE)
    for source in range(pair):
        for low in range(pair):
            received = own_row if source == low else other_row
            for high in range(members):
                for turn in range(2 * PAGE):
                    start = (turn * pair * members + PAIR * high + low) * width
                    pages[source, :, start : start + width] = received[
                        0, low, high, :, turn * width : (turn + 1) * width
                    ]


def unpack(own_row, other_row):
    planes, pair, members, capacity, part = own_row.shape
    block = pl.BlockSpec((1,) + own_row.shape[1:], lambda i: (i, 0, 0, 0, 0))
    return pl.pallas_call(
        unpack_kernel,
        grid=(planes,),
        in_specs=[block, block],
        out_specs=pl.BlockSpec((pair, capacity, pair * members * part), lambda i: (i, 0, 0)),
        out_shape=jax.ShapeDtypeStruct(
            (planes * pair, capacity, pair * members * part), jnp.bfloat16
        ),
        compiler_params=pltpu.CompilerParams(vmem_limit_bytes=24 * 1024 * 1024),
        cost_estimate=pl.CostEstimate(flops=0, bytes_accessed=6 << 20, transcendentals=0),
        name="unpack",
    )(own_row, other_row)


def rope_tables(positions):
    half_dim = HEAD_DIM // 2
    inverse = 1.0 / ROPE_BASE ** (jnp.arange(half_dim, dtype=jnp.float32) * 2.0 / HEAD_DIM)
    angles = inverse[:, None] * positions.astype(jnp.float32)[None, :]
    return jnp.cos(angles), jnp.sin(angles)


def document_bounds(window_ids, rows, blocks):
    reach = SPAN + rows
    firsts = jnp.arange(blocks, dtype=jnp.int32)[:, None] * rows
    own = window_ids[SPAN : SPAN + rows * blocks].reshape(blocks, rows)
    behind = jnp.stack([window_ids[k * rows : k * rows + reach] for k in range(blocks)])
    ahead = jnp.stack(
        [window_ids[SPAN + k * rows : SPAN + k * rows + reach] for k in range(blocks)]
    )
    starts = jnp.sum((behind[:, None, :] < own[:, :, None]).astype(jnp.int32), axis=2) + firsts
    ends = (
        jnp.sum((ahead[:, None, :] <= own[:, :, None]).astype(jnp.int32), axis=2)
        + firsts
        + SPAN
    )
    return starts.reshape(-1), ends.reshape(-1)


def per_device(tokens, norm_gain, input_weight, output_weight, segment_ids, page_owner):
    rows, model_width = tokens.shape
    peers, members = lax.axis_size("tok"), lax.axis_size("grp")
    place, column = lax.axis_index("tok"), lax.axis_index("grp")
    low = place % PAIR
    blocks = PAIR * members
    member = low * members + column
    group_rows = rows * blocks
    width = model_width // blocks
    pages = rows // PAGE

    flat = peers * members
    owners = page_owner[:, 0]
    capacity = max(2, (2 * pages + peers - 1) // peers)
    halves = []
    for parity in range(PAIR):
        pieces = []
        for number in range(PARTS):
            start = number * PAIR * width
            choices = [input_weight[:, start : start + width], input_weight[:, start + width : start + 2 * width]]
            piece = jnp.where((low ^ parity) == 0, choices[0], choices[1])
            route = []
            for source in range(flat):
                row, column_from = divmod(source, members)
                target = (row ^ parity) * members + (PARTS * column_from + number) % members
                route.append((source, target))
            pieces.append(lax.ppermute(piece, ("tok", "grp"), route))
        halves.append(jnp.concatenate(pieces, axis=1))
    plane = jnp.concatenate(halves, axis=0)
    top, bottom = layer_norm(tokens, norm_gain[None, :], owners, capacity)
    top, bottom, plane = lax.optimization_barrier((top, bottom, plane))
    planes = {0: plane}
    bit = peers // 2
    while bit > 1:
        for distance in list(planes):
            planes[distance ^ bit] = flipped(planes[distance], "tok", bit)
        bit //= 2
    weights = [planes[distance] for distance in range(0, peers, 2)]

    across_top, along_bottom = flipped(top, "grp", 2), flipped(bottom, "tok", 1)
    across_bottom, along_top = flipped(bottom, "grp", 2), flipped(top, "tok", 1)
    near_blocks = [top, bottom, flipped(top, "grp", 1), flipped(bottom, "grp", 1)]
    near_blocks += [across_top, across_bottom]
    near_blocks += [flipped(across_top, "grp", 1), flipped(across_bottom, "grp", 1)]
    far_blocks = [along_top, along_bottom]
    far_blocks += [flipped(along_top, "grp", 1), flipped(along_bottom, "grp", 1)]
    half, held = rows // 2, rows + EXTRA_ROWS
    layout = [
        [(2 * number, 0, half), (2 * number + 1, half, held - half)] for number in range(4)
    ]

    last_weight = output_weight
    bit = PAIR
    while bit < peers:
        last_weight = doubled(last_weight, "tok", bit, 0)
        bit *= 2
    last_weight = last_weight.reshape((peers // PAIR,) + output_weight.shape)
    near_blocks, far_blocks, weights, last_weight = lax.optimization_barrier(
        (near_blocks, far_blocks, weights, last_weight)
    )
    corners = [
        flipped(near_blocks[4], "tok", 1),
        flipped(far_blocks[1], "grp", 2),
        flipped(near_blocks[6], "tok", 1),
        flipped(far_blocks[3], "grp", 2),
    ]
    last_weight = doubled(last_weight, "tok", 1, 1).reshape(model_width, output_weight.shape[1])

    first_row = place // PAIR * group_rows
    padded_ids = jnp.concatenate(
        [
            jnp.full((SPAN,), -1, jnp.int32),
            segment_ids,
            jnp.full((SPAN,), 1 << 30, jnp.int32),
        ]
    )
    window_ids = lax.dynamic_slice_in_dim(padded_ids, first_row, group_rows + 2 * SPAN, 0)
    starts, ends = document_bounds(window_ids, rows, blocks)
    positions = SPAN + jnp.arange(group_rows, dtype=jnp.int32) - starts
    cosine, sine = rope_tables(positions)
    ranges = jnp.stack(
        [starts[::TILE] // TILE, (ends[TILE - 1 :: TILE] + TILE - 1) // TILE], axis=1
    ).reshape(-1)

    order = [
        (number * members + column) % PARTS for number in range(PARTS)
    ]
    meta = jnp.stack([member, place] + order).astype(jnp.int32)
    sizes = (weights, cosine, sine, rows, blocks, peers, capacity)

    def to_owners(send):
        received = lax.all_to_all(
            send.reshape((flat,) + send.shape[2:]),
            ("tok", "grp"),
            split_axis=0,
            concat_axis=0,
            tiled=True,
        )
        return received.reshape((peers // PAIR, PAIR, members) + send.shape[2:])

    queries, pairs, send = project(meta, 0, layout, near_blocks, *sizes, ())
    send, corners, last_weight = lax.optimization_barrier((send, corners, last_weight))
    own_row = to_owners(send)
    queries, pairs, send = project(
        meta, 4, layout, far_blocks + corners, *sizes, (queries, pairs)
    )
    other_row = to_owners(send)
    before = shifted(pairs[group_rows - SPAN :], "tok", PAIR)
    after = shifted(pairs[:SPAN], "tok", -PAIR)
    last_weight = doubled(last_weight[None], "grp", 2, 0)

    bounds = (starts[None, :], ends[None, :])
    total, peaks = attend_local(ranges, queries, *bounds, pairs)
    last_weight, before, after, total, peaks = lax.optimization_barrier(
        (last_weight, before, after, total, peaks)
    )
    last_weight = doubled(last_weight, "grp", 1, 1).reshape(members * model_width, -1)
    own_member = member[None].astype(jnp.int32)
    mixed = attend_finish(
        jnp.concatenate([own_member, ranges]),
        queries,
        *bounds,
        before,
        after,
        total,
        peaks,
        rows,
    )
    parts = [mixed[0]] + [
        lax.ppermute(
            mixed[distance],
            ("tok", "grp"),
            [(source, source ^ distance) for source in range(flat)],
        )
        for distance in range(1, blocks)
    ]
    attended = output_projection(own_member, parts, last_weight)

    cache_pages = unpack(own_row, other_row).reshape(
        peers * capacity, 2 * PAGE * model_width
    )
    return attended, cache_pages


def solution(mesh):
    placed = (
        P(("tok", "grp"), None),
        P(),
        P("tok", "grp"),
        P("tok", "grp"),
        P(),
        P(("tok", "grp"), None),
    )
    return jax.shard_map(
        per_device,
        mesh=mesh,
        in_specs=placed,
        out_specs=(P(("tok", "grp"), None), P(("tok", "grp"), None)),
        check_vma=False,
    )
```

```python
import functools
import math

import jax
import jax.numpy as jnp
from jax import lax
from jax.experimental import pallas as pl
from jax.experimental.pallas import tpu as pltpu
from jax.sharding import PartitionSpec as P

H = 16
SPAN = 1024
PAGE = 4
HEAD_DIM = 64

NEG_FILL = -1e30
ROPE_BASE = 160000.0
EPSILON = 1e-05
TILE = 256
PARTS = 3
PAIR = 2
ONES_ROWS = 16
HEAD_ROWS = HEAD_DIM + ONES_ROWS
EXTRA_ROWS = 16
KEYS = 512
SCALE = HEAD_DIM ** (-0.5) * math.log2(math.e)
VMEM_LIMIT = 60 * 1024 * 1024
PARAMS = pltpu.CompilerParams(vmem_limit_bytes=VMEM_LIMIT)


def flipped(value, axis, bit):
    count = lax.axis_size(axis)
    return lax.ppermute(value, axis, [(source, source ^ bit) for source in range(count)])


def shifted(value, axis, steps):
    count = lax.axis_size(axis)
    initial, last = (max(0, -steps), min(count, count - steps))
    return lax.ppermute(value, axis, [(source, source + steps) for source in range(initial, last)])


def doubled(value, axis, bit, low):
    other = flipped(value, axis, bit)
    first = (lax.axis_index(axis) & bit) == 0
    pair = jnp.stack([jnp.where(first, value, other), jnp.where(first, other, value)], axis=low)
    return pair.reshape((-1,) + value.shape[1:])


def norm_kernel(capacity, tokens, gain, owner_row, top, bottom, owners):
    half = top.shape[0]
    rest = tokens.shape[0] - half
    values = tokens[...].astype(jnp.float32)
    centred = values - jnp.mean(values, axis=-1, keepdims=True)
    spread = jnp.mean(jnp.square(centred), axis=-1, keepdims=True)
    normed = (centred * lax.rsqrt(spread + EPSILON) * gain[...]).astype(jnp.bfloat16)
    top[...] = normed[:half]
    bottom[:rest, :] = normed[half:]
    pages = owner_row.shape[1]
    owners[...] = jnp.full(owners.shape, -1.0, jnp.float32)
    owners[:1, :pages] = owner_row[...].astype(jnp.float32)
    lanes = owners.shape[1]
    across = jnp.broadcast_to(owners[:1, :], (lanes, lanes))
    earlier = lax.broadcasted_iota(jnp.int32, (lanes, lanes), 0) < lax.broadcasted_iota(
        jnp.int32, (lanes, lanes), 1
    )
    same = (across.T == across) & earlier
    ranks = jnp.sum(jnp.where(same, 1.0, 0.0), axis=0, keepdims=True)
    slots = owners[:1, :] * capacity + ranks
    bottom[rest:, :] = jnp.zeros((EXTRA_ROWS, bottom.shape[1]), jnp.bfloat16)
    bottom[rest:, :lanes] = jnp.broadcast_to(slots, (EXTRA_ROWS, lanes)).astype(jnp.bfloat16)


def layer_norm(tokens, gain, owners, capacity):
    rows, width = tokens.shape
    lanes = -(-owners.shape[0] // 128) * 128
    return pl.pallas_call(
        functools.partial(norm_kernel, capacity),
        out_shape=[
            jax.ShapeDtypeStruct((rows // 2, width), jnp.bfloat16),
            jax.ShapeDtypeStruct((rows // 2 + EXTRA_ROWS, width), jnp.bfloat16),
        ],
        scratch_shapes=[pltpu.VMEM((8, lanes), jnp.float32)],
        compiler_params=PARAMS,
        name="layer_norm",
    )(tokens, gain, owners[None, :])


def project_kernel(first, layout, weight_count, peers, capacity, meta, *refs):
    operands = 1 + max(entry[0] for pieces in layout for entry in pieces)
    tokens = refs[:operands]
    weights = refs[operands : operands + weight_count]
    cosine, sine = refs[operands + weight_count : operands + weight_count + 2]
    query_out, pair_out, send_out, blocks, weight, page_source, sems = refs[-7:]
    step = pl.program_id(0)
    steps = len(layout)
    rows = query_out.shape[0]
    width = query_out.shape[1]
    shard = weights[0].shape[0] // 2

    def arrivals(number):
        return [
            pltpu.make_async_copy(
                tokens[operand],
                blocks.at[number, pl.ds(offset, count), :],
                sems.at[number, place],
            )
            for place, (operand, offset, count) in enumerate(layout[number])
        ]

    @pl.when(step == 0)
    def _():
        for number in range(steps):
            for copy in arrivals(number):
                copy.start()
        for plane in range(weight_count):
            for low in range(2):
                row = pl.multiple_of((meta[1] ^ (2 * plane + low)) * shard, shard)
                for number in range(PARTS):
                    column = pl.multiple_of(meta[2 + number] * width, width)
                    weight[pl.ds(row, shard), number * width : (number + 1) * width] = weights[
                        plane
                    ][low * shard : (low + 1) * shard, pl.ds(column, width)]

    for number in range(steps):

        @pl.when(step == number)
        def _():
            for copy in arrivals(number):
                copy.wait()

    joined = jnp.dot(blocks[step, :rows, :], weight[...], preferred_element_type=jnp.float32)
    cosines = jnp.concatenate([cosine[...]] * 4, axis=0).T
    sines = jnp.concatenate([-sine[...], sine[...]] * 2, axis=0).T
    first_half = lax.rem(lax.broadcasted_iota(jnp.int32, (rows, width), 1), HEAD_DIM) < (
        HEAD_DIM // 2
    )

    def rotate(values):
        partner = jnp.where(
            first_half,
            pltpu.roll(values, width - HEAD_DIM // 2, 1),
            pltpu.roll(values, HEAD_DIM // 2, 1),
        )
        return (values * cosines + partner * sines).astype(jnp.bfloat16)

    query_out[...] = rotate(joined[:, :width])
    keys = rotate(joined[:, width : 2 * width])
    values = joined[:, 2 * width :].astype(jnp.bfloat16)
    pair_out[:, :width] = keys
    pair_out[:, width:] = values
    page_source[0] = keys.astype(jnp.float32)
    page_source[1] = values.astype(jnp.float32)

    pages = rows // PAGE
    slot_count = peers * capacity
    slots = blocks[step, rows : rows + EXTRA_ROWS, :128].astype(jnp.float32)[:1, :pages]
    chosen = (
        lax.broadcasted_iota(jnp.int32, (slot_count, pages), 0).astype(jnp.float32) == slots
    ).astype(jnp.bfloat16)
    for turn in range(PAGE):
        page_part = jnp.concatenate(
            [
                page_source[half, pl.ds(turn, pages, stride=PAGE), :].astype(jnp.bfloat16)
                for half in range(2)
            ],
            axis=1,
        )
        placed = jnp.dot(chosen, page_part, preferred_element_type=jnp.float32)
        columns = slice(turn * 2 * width, (turn + 1) * 2 * width)
        for peer in range(peers):
            send_out[peer, 0, :, columns] = placed[
                peer * capacity : (peer + 1) * capacity
            ].astype(jnp.bfloat16)


def project(meta, first, layout, operands, weights, cosine, sine, rows, blocks, peers, capacity, into):
    steps = len(layout)
    model_width = operands[0].shape[1]
    group_rows = rows * blocks
    width = weights[0].shape[1] // PARTS
    members = blocks // PAIR
    whole = lambda shape: pl.BlockSpec(shape, lambda i, m: (0,) * len(shape))
    place = lambda i, m: m[0] ^ (first + i)
    table = pl.BlockSpec((HEAD_DIM // 2, rows), lambda i, m: (0, place(i, m)))
    send_shape = (peers, members, capacity, 2 * PAGE * width)
    return pl.pallas_call(
        functools.partial(project_kernel, first, layout, len(weights), peers, capacity),
        grid_spec=pltpu.PrefetchScalarGridSpec(
            num_scalar_prefetch=1,
            grid=(steps,),
            in_specs=[pl.BlockSpec(memory_space=pl.ANY)] * len(operands)
            + [whole(weights[0].shape)] * len(weights)
            + [table, table]
            + [pl.BlockSpec(memory_space=pl.ANY)] * len(into),
            out_specs=[
                pl.BlockSpec((rows, width), lambda i, m: (place(i, m), 0)),
                pl.BlockSpec((rows, 2 * width), lambda i, m: (place(i, m), 0)),
                pl.BlockSpec(
                    (peers, 1) + send_shape[2:], lambda i, m: (0, place(i, m) % members, 0, 0)
                ),
            ],
            scratch_shapes=[
                pltpu.VMEM((steps, rows + EXTRA_ROWS, model_width), jnp.bfloat16),
                pltpu.VMEM((model_width, PARTS * width), jnp.bfloat16),
                pltpu.VMEM((2, rows, width), jnp.float32),
                pltpu.SemaphoreType.DMA((steps, 2)),
            ],
        ),
        out_shape=[
            jax.ShapeDtypeStruct((group_rows, width), jnp.bfloat16),
            jax.ShapeDtypeStruct((group_rows, 2 * width), jnp.bfloat16),
            jax.ShapeDtypeStruct(send_shape, jnp.bfloat16),
        ],
        input_output_aliases={
            1 + len(operands) + len(weights) + 2 + number: number for number in range(len(into))
        },
        compiler_params=PARAMS,
        cost_estimate=pl.CostEstimate(
            flops=2 * steps * rows * model_width * PARTS * width,
            bytes_accessed=(3 * steps) << 19,
            transcendentals=0,
        ),
        name="project",
    )(meta, *operands, *weights, cosine, sine, *into)


def mask_heads(queries, masked):
    turned = queries[...].T
    head_of_row = lax.broadcasted_iota(jnp.int32, turned.shape, 0) // HEAD_DIM
    for head in range(masked.shape[0]):
        masked[head] = jnp.where(head_of_row == head, turned, jnp.zeros((), jnp.bfloat16))


def with_ones(values):
    turned = values.T
    ones = jnp.ones((ONES_ROWS, values.shape[0]), values.dtype)
    rows = []
    for head in range(values.shape[1] // HEAD_DIM):
        rows += [turned[head * HEAD_DIM : (head + 1) * HEAD_DIM], ones]
    return jnp.concatenate(rows, axis=0)


def sweep(begin, end, base, pairs, values_of, masked, starts, ends, total, peaks):
    width = pairs.shape[1] // 2
    held = pairs.shape[0] // TILE
    begin = jnp.maximum(begin, base)
    end = jnp.minimum(end, base + held)
    last = jnp.minimum(ends, end * TILE)

    def one(number, peaks):
        wanted = begin + number * (KEYS // TILE)
        block = jnp.minimum(wanted, base + held - KEYS // TILE)
        row = pl.multiple_of((block - base) * TILE, TILE)
        keys = pairs[pl.ds(row, KEYS), :width]
        values = values_of(row)
        index = block * TILE + lax.broadcasted_iota(jnp.int32, (KEYS, TILE), 0)
        allowed = (index >= jnp.maximum(starts, wanted * TILE)) & (index < last)
        new_peaks = []
        for head, old_peak in enumerate(peaks):
            scores = jnp.dot(keys, masked[head], preferred_element_type=jnp.float32)
            scores = jnp.where(allowed, scores * SCALE, NEG_FILL)
            peak = jnp.maximum(old_peak, jnp.max(scores, axis=0, keepdims=True))
            fade = jnp.exp2(old_peak - peak)
            weights = jnp.exp2(scores - peak).astype(jnp.bfloat16)
            own = slice(head * HEAD_ROWS, (head + 1) * HEAD_ROWS)
            total[own, :] = total[own, :] * fade + jnp.dot(
                values[own, :], weights, preferred_element_type=jnp.float32
            )
            new_peaks.append(peak)
        return tuple(new_peaks)

    steps = jnp.maximum(end - begin + KEYS // TILE - 1, 0) // (KEYS // TILE)
    return lax.fori_loop(0, steps, one, peaks)


def attend_kernel(ranges, queries, starts, ends, pairs, total, peak_out, masked, values):
    step = pl.program_id(0)
    width = queries.shape[1]
    heads = width // HEAD_DIM
    per_span = SPAN // TILE

    @pl.when(step == 0)
    def _():
        for number in range(pairs.shape[0] // TILE):
            rows = slice(number * TILE, (number + 1) * TILE)
            values[:, rows] = with_ones(pairs[rows, width:])

    mask_heads(queries, masked)
    total[...] = jnp.zeros_like(total)
    peaks = sweep(
        ranges[2 * step],
        ranges[2 * step + 1],
        per_span,
        pairs,
        lambda row: values[:, pl.ds(row, KEYS)],
        masked,
        starts[...],
        ends[...],
        total.at[0],
        tuple(jnp.full((1, TILE), NEG_FILL, jnp.float32) for _ in range(heads)),
    )
    for head in range(heads):
        peak_out[0, head : head + 1, :] = peaks[head]


def finish_kernel(meta, queries, starts, ends, before, after, total, peak_in, *refs):
    outs = refs[:-3]
    masked, sums, mixed = refs[-3:]
    step = pl.program_id(0)
    width = queries.shape[1]
    heads = width // HEAD_DIM
    per_span = SPAN // TILE
    own_tiles = pl.num_programs(0)
    sums[...] = total[0]
    begin, end = meta[1 + 2 * step], meta[2 + 2 * step]

    @pl.when((begin < per_span) | (end > per_span + own_tiles))
    def _():
        mask_heads(queries, masked)
        peaks = tuple(peak_in[0, head : head + 1, :] for head in range(heads))
        for chunk, base in ((before, 0), (after, per_span + own_tiles)):
            peaks = sweep(
                begin,
                end,
                base,
                chunk,
                lambda row: with_ones(chunk[pl.ds(row, KEYS), width:]),
                masked,
                starts[...],
                ends[...],
                sums,
                peaks,
            )

    parts = []
    for head in range(heads):
        row = head * HEAD_ROWS
        parts.append(sums[row : row + HEAD_DIM, :] / sums[row + HEAD_DIM : row + HEAD_DIM + 1, :])
    tile_rows = pl.ds(pl.multiple_of(step * TILE, TILE), TILE)
    mixed[tile_rows, :] = jnp.concatenate(parts, axis=0).T.astype(jnp.bfloat16)

    @pl.when(step == own_tiles - 1)
    def _():
        rows = outs[0].shape[0]
        for distance, out in enumerate(outs):
            out[...] = mixed[pl.ds(pl.multiple_of((meta[0] ^ distance) * rows, 128), rows), :]


def attend_specs(width, held):
    spec = lambda shape, index: pl.BlockSpec(shape, lambda i, m: index(i))
    return [
        spec((TILE, width), lambda i: (i, 0)),
        spec((1, TILE), lambda i: (0, i)),
        spec((1, TILE), lambda i: (0, i)),
    ] + [spec((rows, 2 * width), lambda i: (0, 0)) for rows in held]


def attend_local(ranges, queries, starts, ends, pairs):
    group_rows, width = queries.shape
    heads = width // HEAD_DIM
    tiles = group_rows // TILE
    return pl.pallas_call(
        attend_kernel,
        grid_spec=pltpu.PrefetchScalarGridSpec(
            num_scalar_prefetch=1,
            grid=(tiles,),
            in_specs=attend_specs(width, (group_rows,)),
            out_specs=[
                pl.BlockSpec((1, heads * HEAD_ROWS, TILE), lambda i, m: (i, 0, 0)),
                pl.BlockSpec((1, 8, TILE), lambda i, m: (i, 0, 0)),
            ],
            scratch_shapes=[
                pltpu.VMEM((heads, width, TILE), jnp.bfloat16),
                pltpu.VMEM((heads * HEAD_ROWS, group_rows), jnp.bfloat16),
            ],
        ),
        out_shape=[
            jax.ShapeDtypeStruct((tiles, heads * HEAD_ROWS, TILE), jnp.float32),
            jax.ShapeDtypeStruct((tiles, 8, TILE), jnp.float32),
        ],
        compiler_params=PARAMS,
        cost_estimate=pl.CostEstimate(
            flops=16 * group_rows * 1024 * width,
            bytes_accessed=5 << 20,
            transcendentals=group_rows * 1024 * heads,
        ),
        name="attend_local",
    )(ranges, queries, starts, ends, pairs)


def attend_finish(meta, queries, starts, ends, before, after, total, peaks, rows):
    group_rows, width = queries.shape
    heads = width // HEAD_DIM
    tiles = group_rows // TILE
    members = group_rows // rows
    return pl.pallas_call(
        finish_kernel,
        grid_spec=pltpu.PrefetchScalarGridSpec(
            num_scalar_prefetch=1,
            grid=(tiles,),
            in_specs=attend_specs(width, (SPAN, SPAN))
            + [
                pl.BlockSpec((1,) + total.shape[1:], lambda i, m: (i, 0, 0)),
                pl.BlockSpec((1,) + peaks.shape[1:], lambda i, m: (i, 0, 0)),
            ],
            out_specs=[pl.BlockSpec((rows, width), lambda i, m: (0, 0))] * members,
            scratch_shapes=[
                pltpu.VMEM((heads, width, TILE), jnp.bfloat16),
                pltpu.VMEM(total.shape[1:], jnp.float32),
                pltpu.VMEM((group_rows, width), jnp.bfloat16),
            ],
        ),
        out_shape=[jax.ShapeDtypeStruct((rows, width), jnp.bfloat16)] * members,
        compiler_params=PARAMS,
        cost_estimate=pl.CostEstimate(
            flops=4 * group_rows * 1024 * width,
            bytes_accessed=5 << 20,
            transcendentals=group_rows * 256 * heads,
        ),
        name="attend_finish",
    )(meta, queries, starts, ends, before, after, total, peaks)


def output_kernel(members, meta, *refs):
    parts, weight, result, mixed = refs[:members], refs[members], refs[-2], refs[-1]
    width = parts[0].shape[1]

    @pl.when(pl.program_id(0) == 0)
    def _():
        for distance in range(members):
            source = meta[0] ^ distance
            head_pair = PAIR * (source % (members // PAIR)) + source // (members // PAIR)
            columns = pl.ds(pl.multiple_of(head_pair * width, width), width)
            mixed[:, columns] = parts[distance][...]

    result[...] = jnp.dot(
        mixed[...], weight[...], preferred_element_type=jnp.float32
    ).astype(jnp.bfloat16)


def output_projection(meta, parts, weight):
    rows, width = parts[0].shape
    depth = width * len(parts)
    tile = weight.shape[1]
    steps = weight.shape[0] // depth
    return pl.pallas_call(
        functools.partial(output_kernel, len(parts)),
        grid_spec=pltpu.PrefetchScalarGridSpec(
            num_scalar_prefetch=1,
            grid=(steps,),
            in_specs=[pl.BlockSpec((rows, width), lambda i, m: (0, 0))] * len(parts)
            + [pl.BlockSpec((depth, tile), lambda i, m: (i, 0))],
            out_specs=pl.BlockSpec((rows, tile), lambda i, m: (0, i)),
            scratch_shapes=[pltpu.VMEM((rows, depth), jnp.bfloat16)],
        ),
        out_shape=jax.ShapeDtypeStruct((rows, steps * tile), jnp.bfloat16),
        compiler_params=PARAMS,
        cost_estimate=pl.CostEstimate(
            flops=2 * rows * depth * steps * tile, bytes_accessed=4 << 20, transcendentals=0
        ),
        name="output_projection",
    )(meta, *parts, weight)


def unpack_kernel(own_row, other_row, pages):
    _, pair, members, capacity, part = own_row.shape
    width = part // (2 * PAGE)
    for source in range(pair):
        for low in range(pair):
            received = own_row if source == low else other_row
            for high in range(members):
                for turn in range(2 * PAGE):
                    start = (turn * pair * members + PAIR * high + low) * width
                    pages[source, :, start : start + width] = received[
                        0, low, high, :, turn * width : (turn + 1) * width
                    ]


def unpack(own_row, other_row):
    planes, pair, members, capacity, part = own_row.shape
    block = pl.BlockSpec((1,) + own_row.shape[1:], lambda i: (i, 0, 0, 0, 0))
    return pl.pallas_call(
        unpack_kernel,
        grid=(planes,),
        in_specs=[block, block],
        out_specs=pl.BlockSpec((pair, capacity, pair * members * part), lambda i: (i, 0, 0)),
        out_shape=jax.ShapeDtypeStruct(
            (planes * pair, capacity, pair * members * part), jnp.bfloat16
        ),
        compiler_params=pltpu.CompilerParams(vmem_limit_bytes=24 * 1024 * 1024),
        cost_estimate=pl.CostEstimate(flops=0, bytes_accessed=6 << 20, transcendentals=0),
        name="unpack",
    )(own_row, other_row)


def rope_tables(positions):
    half_dim = HEAD_DIM // 2
    inverse = 1.0 / ROPE_BASE ** (jnp.arange(half_dim, dtype=jnp.float32) * 2.0 / HEAD_DIM)
    angles = inverse[:, None] * positions.astype(jnp.float32)[None, :]
    return jnp.cos(angles), jnp.sin(angles)


def document_bounds(window_ids, rows, blocks):
    reach = SPAN + rows
    firsts = jnp.arange(blocks, dtype=jnp.int32)[:, None] * rows
    own = window_ids[SPAN : SPAN + rows * blocks].reshape(blocks, rows)
    behind = jnp.stack([window_ids[k * rows : k * rows + reach] for k in range(blocks)])
    ahead = jnp.stack(
        [window_ids[SPAN + k * rows : SPAN + k * rows + reach] for k in range(blocks)]
    )
    starts = jnp.sum((behind[:, None, :] < own[:, :, None]).astype(jnp.int32), axis=2) + firsts
    ends = (
        jnp.sum((ahead[:, None, :] <= own[:, :, None]).astype(jnp.int32), axis=2)
        + firsts
        + SPAN
    )
    return starts.reshape(-1), ends.reshape(-1)


def per_device(tokens, norm_gain, input_weight, output_weight, segment_ids, page_owner):
    rows, model_width = tokens.shape
    peers, members = lax.axis_size("tok"), lax.axis_size("grp")
    place, column = lax.axis_index("tok"), lax.axis_index("grp")
    low = place % PAIR
    blocks = PAIR * members
    member = low * members + column
    group_rows = rows * blocks
    width = model_width // blocks
    pages = rows // PAGE

    flat = peers * members
    owners = page_owner[:, 0]
    capacity = max(2, (2 * pages + peers - 1) // peers)
    halves = []
    for parity in range(PAIR):
        pieces = []
        for number in range(PARTS):
            start = number * PAIR * width
            choices = [input_weight[:, start : start + width], input_weight[:, start + width : start + 2 * width]]
            piece = jnp.where((low ^ parity) == 0, choices[0], choices[1])
            route = []
            for source in range(flat):
                row, column_from = divmod(source, members)
                target = (row ^ parity) * members + (PARTS * column_from + number) % members
                route.append((source, target))
            pieces.append(lax.ppermute(piece, ("tok", "grp"), route))
        halves.append(jnp.concatenate(pieces, axis=1))
    plane = jnp.concatenate(halves, axis=0)
    top, bottom = layer_norm(tokens, norm_gain[None, :], owners, capacity)
    top, bottom, plane = lax.optimization_barrier((top, bottom, plane))
    across = [flipped(top, "grp", 2), flipped(bottom, "grp", 2)]
    along = [flipped(top, "tok", 1), flipped(bottom, "tok", 1)]
    sibling = [flipped(top, "grp", 1), flipped(bottom, "grp", 1)]
    planes = {0: plane}
    bit = peers // 2
    while bit > 1:
        for distance in list(planes):
            planes[distance ^ bit] = flipped(planes[distance], "tok", bit)
        bit //= 2
    last_weight = output_weight
    bit = PAIR
    while 2 * bit < peers:
        last_weight = doubled(last_weight, "tok", bit, 0)
        bit *= 2
    across, along, sibling, last_weight = lax.optimization_barrier(
        (across, along, sibling, last_weight)
    )
    corner = [flipped(across[0], "tok", 1), flipped(along[1], "grp", 2)]
    across_sibling = [flipped(block, "grp", 1) for block in across]
    along_sibling = [flipped(block, "grp", 1) for block in along]
    if bit < peers:
        last_weight = doubled(last_weight, "tok", bit, 0)
    last_weight = last_weight.reshape((peers // PAIR,) + output_weight.shape)
    weights = [planes[distance] for distance in range(0, peers, 2)]
    across_sibling, along_sibling, corner, weights, last_weight = lax.optimization_barrier(
        (across_sibling, along_sibling, corner, weights, last_weight)
    )
    corner_sibling = [flipped(block, "grp", 1) for block in corner]
    last_weight = doubled(last_weight, "tok", 1, 1).reshape(model_width, output_weight.shape[1])
    near_blocks = [top, bottom] + sibling + across + across_sibling
    far_blocks = along + along_sibling + corner
    half, held = rows // 2, rows + EXTRA_ROWS
    layout = [
        [(2 * number, 0, half), (2 * number + 1, half, held - half)] for number in range(4)
    ]

    first_row = place // PAIR * group_rows
    padded_ids = jnp.concatenate(
        [
            jnp.full((SPAN,), -1, jnp.int32),
            segment_ids,
            jnp.full((SPAN,), 1 << 30, jnp.int32),
        ]
    )
    window_ids = lax.dynamic_slice_in_dim(padded_ids, first_row, group_rows + 2 * SPAN, 0)
    starts, ends = document_bounds(window_ids, rows, blocks)
    positions = SPAN + jnp.arange(group_rows, dtype=jnp.int32) - starts
    cosine, sine = rope_tables(positions)
    ranges = jnp.stack(
        [starts[::TILE] // TILE, (ends[TILE - 1 :: TILE] + TILE - 1) // TILE], axis=1
    ).reshape(-1)

    order = [
        (number * members + column) % PARTS for number in range(PARTS)
    ]
    meta = jnp.stack([member, place] + order).astype(jnp.int32)
    sizes = (weights, cosine, sine, rows, blocks, peers, capacity)

    def to_owners(send):
        received = lax.all_to_all(
            send.reshape((flat,) + send.shape[2:]),
            ("tok", "grp"),
            split_axis=0,
            concat_axis=0,
            tiled=True,
        )
        return received.reshape((peers // PAIR, PAIR, members) + send.shape[2:])

    queries, pairs, send = project(meta, 0, layout, near_blocks, *sizes, ())
    send, corner_sibling, last_weight = lax.optimization_barrier(
        (send, corner_sibling, last_weight)
    )
    own_row = to_owners(send)
    queries, pairs, send = project(
        meta, 4, layout, far_blocks + corner_sibling, *sizes, (queries, pairs)
    )
    before = shifted(pairs[group_rows - SPAN :], "tok", PAIR)
    after = shifted(pairs[:SPAN], "tok", -PAIR)
    last_weight = doubled(last_weight[None], "grp", 2, 0)

    bounds = (starts[None, :], ends[None, :])
    total, peaks = attend_local(ranges, queries, *bounds, pairs)
    last_weight, before, after, total, peaks, send = lax.optimization_barrier(
        (last_weight, before, after, total, peaks, send)
    )
    other_row = to_owners(send)
    last_weight = doubled(last_weight, "grp", 1, 1).reshape(members * model_width, -1)
    own_member = member[None].astype(jnp.int32)
    mixed = attend_finish(
        jnp.concatenate([own_member, ranges]),
        queries,
        *bounds,
        before,
        after,
        total,
        peaks,
        rows,
    )
    parts = [mixed[0]] + [
        lax.ppermute(
            mixed[distance],
            ("tok", "grp"),
            [(source, source ^ distance) for source in range(flat)],
        )
        for distance in range(1, blocks)
    ]
    attended = output_projection(own_member, parts, last_weight)

    cache_pages = unpack(own_row, other_row).reshape(
        peers * capacity, 2 * PAGE * model_width
    )
    return attended, cache_pages


def solution(mesh):
    placed = (
        P(("tok", "grp"), None),
        P(),
        P("tok", "grp"),
        P("tok", "grp"),
        P(),
        P(("tok", "grp"), None),
    )
    return jax.shard_map(
        per_device,
        mesh=mesh,
        in_specs=placed,
        out_specs=(P(("tok", "grp"), None), P(("tok", "grp"), None)),
        check_vma=False,
    )
```

```python
import functools
import math

import jax
import jax.numpy as jnp
from jax import lax
from jax.experimental import pallas as pl
from jax.experimental.pallas import tpu as pltpu
from jax.sharding import PartitionSpec as P

H = 16
SPAN = 1024
PAGE = 4
HEAD_DIM = 64

NEG_FILL = -1e30
ROPE_BASE = 160000.0
EPSILON = 1e-05
TILE = 256
PARTS = 3
PAIR = 2
ONES_ROWS = 16
HEAD_ROWS = HEAD_DIM + ONES_ROWS
EXTRA_ROWS = 16
KEYS = 512
SCALE = HEAD_DIM ** (-0.5) * math.log2(math.e)
VMEM_LIMIT = 60 * 1024 * 1024
PARAMS = pltpu.CompilerParams(vmem_limit_bytes=VMEM_LIMIT)


def flipped(value, axis, bit):
    count = lax.axis_size(axis)
    return lax.ppermute(value, axis, [(source, source ^ bit) for source in range(count)])


def shifted(value, axis, steps):
    count = lax.axis_size(axis)
    initial, last = (max(0, -steps), min(count, count - steps))
    return lax.ppermute(value, axis, [(source, source + steps) for source in range(initial, last)])


def merged(value, other, axis, bit, low):
    first = (lax.axis_index(axis) & bit) == 0
    pair = jnp.stack([jnp.where(first, value, other), jnp.where(first, other, value)], axis=low)
    return pair.reshape((-1,) + value.shape[1:])


def norm_kernel(capacity, tokens, gain, owner_row, top, bottom, owners):
    half = top.shape[0]
    rest = tokens.shape[0] - half
    values = tokens[...].astype(jnp.float32)
    centred = values - jnp.mean(values, axis=-1, keepdims=True)
    spread = jnp.mean(jnp.square(centred), axis=-1, keepdims=True)
    normed = (centred * lax.rsqrt(spread + EPSILON) * gain[...]).astype(jnp.bfloat16)
    top[...] = normed[:half]
    bottom[:rest, :] = normed[half:]
    pages = owner_row.shape[1]
    owners[...] = jnp.full(owners.shape, -1.0, jnp.float32)
    owners[:1, :pages] = owner_row[...].astype(jnp.float32)
    lanes = owners.shape[1]
    across = jnp.broadcast_to(owners[:1, :], (lanes, lanes))
    earlier = lax.broadcasted_iota(jnp.int32, (lanes, lanes), 0) < lax.broadcasted_iota(
        jnp.int32, (lanes, lanes), 1
    )
    same = (across.T == across) & earlier
    ranks = jnp.sum(jnp.where(same, 1.0, 0.0), axis=0, keepdims=True)
    slots = owners[:1, :] * capacity + ranks
    bottom[rest:, :] = jnp.zeros((EXTRA_ROWS, bottom.shape[1]), jnp.bfloat16)
    bottom[rest:, :lanes] = jnp.broadcast_to(slots, (EXTRA_ROWS, lanes)).astype(jnp.bfloat16)


def layer_norm(tokens, gain, owners, capacity):
    rows, width = tokens.shape
    lanes = -(-owners.shape[0] // 128) * 128
    return pl.pallas_call(
        functools.partial(norm_kernel, capacity),
        out_shape=[
            jax.ShapeDtypeStruct((rows // 2, width), jnp.bfloat16),
            jax.ShapeDtypeStruct((rows // 2 + EXTRA_ROWS, width), jnp.bfloat16),
        ],
        scratch_shapes=[pltpu.VMEM((8, lanes), jnp.float32)],
        compiler_params=PARAMS,
        name="layer_norm",
    )(tokens, gain, owners[None, :])


def project_kernel(first, layout, weight_count, peers, capacity, meta, *refs):
    operands = 1 + max(entry[0] for pieces in layout for entry in pieces)
    tokens = refs[:operands]
    weights = refs[operands : operands + weight_count]
    cosine, sine = refs[operands + weight_count : operands + weight_count + 2]
    query_out, pair_out, send_out, blocks, weight, page_source, sems = refs[-7:]
    step = pl.program_id(0)
    steps = len(layout)
    rows = query_out.shape[0]
    width = query_out.shape[1]
    shard = weights[0].shape[0] // 2

    def arrivals(number):
        return [
            pltpu.make_async_copy(
                tokens[operand],
                blocks.at[number, pl.ds(offset, count), :],
                sems.at[number, place],
            )
            for place, (operand, offset, count) in enumerate(layout[number])
        ]

    @pl.when(step == 0)
    def _():
        for number in range(steps):
            for copy in arrivals(number):
                copy.start()
        for plane in range(weight_count):
            for low in range(2):
                row = pl.multiple_of((meta[1] ^ (2 * plane + low)) * shard, shard)
                for number in range(PARTS):
                    column = pl.multiple_of(meta[2 + number] * width, width)
                    weight[pl.ds(row, shard), number * width : (number + 1) * width] = weights[
                        plane
                    ][low * shard : (low + 1) * shard, pl.ds(column, width)]

    for number in range(steps):

        @pl.when(step == number)
        def _():
            for copy in arrivals(number):
                copy.wait()

    joined = jnp.dot(blocks[step, :rows, :], weight[...], preferred_element_type=jnp.float32)
    cosines = jnp.concatenate([cosine[...]] * 4, axis=0).T
    sines = jnp.concatenate([-sine[...], sine[...]] * 2, axis=0).T
    first_half = lax.rem(lax.broadcasted_iota(jnp.int32, (rows, width), 1), HEAD_DIM) < (
        HEAD_DIM // 2
    )

    def rotate(values):
        partner = jnp.where(
            first_half,
            pltpu.roll(values, width - HEAD_DIM // 2, 1),
            pltpu.roll(values, HEAD_DIM // 2, 1),
        )
        return (values * cosines + partner * sines).astype(jnp.bfloat16)

    query_out[...] = rotate(joined[:, :width])
    keys = rotate(joined[:, width : 2 * width])
    values = joined[:, 2 * width :].astype(jnp.bfloat16)
    pair_out[:, :width] = keys
    pair_out[:, width:] = values
    page_source[0] = keys.astype(jnp.float32)
    page_source[1] = values.astype(jnp.float32)

    pages = rows // PAGE
    slot_count = peers * capacity
    slots = blocks[step, rows : rows + EXTRA_ROWS, :128].astype(jnp.float32)[:1, :pages]
    chosen = (
        lax.broadcasted_iota(jnp.int32, (slot_count, pages), 0).astype(jnp.float32) == slots
    ).astype(jnp.bfloat16)
    for turn in range(PAGE):
        page_part = jnp.concatenate(
            [
                page_source[half, pl.ds(turn, pages, stride=PAGE), :].astype(jnp.bfloat16)
                for half in range(2)
            ],
            axis=1,
        )
        placed = jnp.dot(chosen, page_part, preferred_element_type=jnp.float32)
        columns = slice(turn * 2 * width, (turn + 1) * 2 * width)
        for peer in range(peers):
            send_out[peer, 0, :, columns] = placed[
                peer * capacity : (peer + 1) * capacity
            ].astype(jnp.bfloat16)


def project(meta, first, layout, operands, weights, cosine, sine, rows, blocks, peers, capacity, into):
    steps = len(layout)
    model_width = operands[0].shape[1]
    group_rows = rows * blocks
    width = weights[0].shape[1] // PARTS
    members = blocks // PAIR
    whole = lambda shape: pl.BlockSpec(shape, lambda i, m: (0,) * len(shape))
    place = lambda i, m: m[0] ^ (first + i)
    table = pl.BlockSpec((HEAD_DIM // 2, rows), lambda i, m: (0, place(i, m)))
    send_shape = (peers, members, capacity, 2 * PAGE * width)
    return pl.pallas_call(
        functools.partial(project_kernel, first, layout, len(weights), peers, capacity),
        grid_spec=pltpu.PrefetchScalarGridSpec(
            num_scalar_prefetch=1,
            grid=(steps,),
            in_specs=[pl.BlockSpec(memory_space=pl.ANY)] * len(operands)
            + [whole(weights[0].shape)] * len(weights)
            + [table, table]
            + [pl.BlockSpec(memory_space=pl.ANY)] * len(into),
            out_specs=[
                pl.BlockSpec((rows, width), lambda i, m: (place(i, m), 0)),
                pl.BlockSpec((rows, 2 * width), lambda i, m: (place(i, m), 0)),
                pl.BlockSpec(
                    (peers, 1) + send_shape[2:], lambda i, m: (0, place(i, m) % members, 0, 0)
                ),
            ],
            scratch_shapes=[
                pltpu.VMEM((steps, rows + EXTRA_ROWS, model_width), jnp.bfloat16),
                pltpu.VMEM((model_width, PARTS * width), jnp.bfloat16),
                pltpu.VMEM((2, rows, width), jnp.float32),
                pltpu.SemaphoreType.DMA((steps, 2)),
            ],
        ),
        out_shape=[
            jax.ShapeDtypeStruct((group_rows, width), jnp.bfloat16),
            jax.ShapeDtypeStruct((group_rows, 2 * width), jnp.bfloat16),
            jax.ShapeDtypeStruct(send_shape, jnp.bfloat16),
        ],
        input_output_aliases={
            1 + len(operands) + len(weights) + 2 + number: number for number in range(len(into))
        },
        compiler_params=PARAMS,
        cost_estimate=pl.CostEstimate(
            flops=2 * steps * rows * model_width * PARTS * width,
            bytes_accessed=(3 * steps) << 19,
            transcendentals=0,
        ),
        name="project",
    )(meta, *operands, *weights, cosine, sine, *into)


def mask_heads(queries, masked):
    turned = queries[...].T
    head_of_row = lax.broadcasted_iota(jnp.int32, turned.shape, 0) // HEAD_DIM
    for head in range(masked.shape[0]):
        masked[head] = jnp.where(head_of_row == head, turned, jnp.zeros((), jnp.bfloat16))


def with_ones(values):
    turned = values.T
    ones = jnp.ones((ONES_ROWS, values.shape[0]), values.dtype)
    rows = []
    for head in range(values.shape[1] // HEAD_DIM):
        rows += [turned[head * HEAD_DIM : (head + 1) * HEAD_DIM], ones]
    return jnp.concatenate(rows, axis=0)


def sweep(jobs, peaks):
    plans = []
    steps = 0
    for begin, end, base, pairs, values_of, masked, starts, ends, total in jobs:
        held = pairs.shape[0] // TILE
        begin, end = jnp.maximum(begin, base), jnp.minimum(end, base + held)
        last = jnp.minimum(ends, end * TILE)
        steps = jnp.maximum(steps, (end - begin + KEYS // TILE - 1) // (KEYS // TILE))
        plans.append((begin, base, held, pairs, values_of, masked, starts, last, total))

    def one(number, peaks):
        new_peaks = []
        for plan, old_peaks in zip(plans, peaks):
            begin, base, held, pairs, values_of, masked, starts, last, total = plan
            wanted = begin + number * (KEYS // TILE)
            block = jnp.minimum(wanted, base + held - KEYS // TILE)
            row = pl.multiple_of((block - base) * TILE, TILE)
            keys = pairs[pl.ds(row, KEYS), : pairs.shape[1] // 2]
            values = values_of(row)
            index = block * TILE + lax.broadcasted_iota(jnp.int32, (KEYS, TILE), 0)
            allowed = (index >= jnp.maximum(starts, wanted * TILE)) & (index < last)
            job_peaks = []
            for head, old_peak in enumerate(old_peaks):
                scores = jnp.dot(keys, masked[head], preferred_element_type=jnp.float32)
                scores = jnp.where(allowed, scores * SCALE, NEG_FILL)
                peak = jnp.maximum(old_peak, jnp.max(scores, axis=0, keepdims=True))
                fade = jnp.exp2(old_peak - peak)
                weights = jnp.exp2(scores - peak).astype(jnp.bfloat16)
                own = slice(head * HEAD_ROWS, (head + 1) * HEAD_ROWS)
                total[own, :] = total[own, :] * fade + jnp.dot(
                    values[own, :], weights, preferred_element_type=jnp.float32
                )
                job_peaks.append(peak)
            new_peaks.append(tuple(job_peaks))
        return tuple(new_peaks)

    return lax.fori_loop(0, steps, one, peaks)


def fresh_peaks(heads):
    return tuple(jnp.full((1, TILE), NEG_FILL, jnp.float32) for _ in range(heads))


def edge_kernel(meta, *refs):
    rows, pairs, outs, (masked, values) = refs[:6], refs[6], refs[7:11], refs[11:]
    step = pl.program_id(0)
    width = rows[0].shape[1]
    heads = width // HEAD_DIM
    edge = pl.num_programs(0)
    tiles = pairs.shape[0] // TILE

    @pl.when(step == 0)
    def _():
        for number in range(tiles):
            own = slice(number * TILE, (number + 1) * TILE)
            values[:, own] = with_ones(pairs[own, width:])

    jobs = []
    for side in range(2):
        tile = step + side * (tiles - edge)
        queries, starts, ends = rows[3 * side : 3 * side + 3]
        mask_heads(queries, masked.at[side])
        total = outs[side]
        total[...] = jnp.zeros_like(total)
        jobs.append(
            (
                meta[1 + 2 * tile],
                meta[2 + 2 * tile],
                edge,
                pairs,
                lambda row: values[:, pl.ds(row, KEYS)],
                masked.at[side],
                starts[...],
                ends[...],
                total.at[0],
            )
        )
    peaks = sweep(jobs, (fresh_peaks(heads), fresh_peaks(heads)))
    for side in range(2):
        for head in range(heads):
            outs[2 + side][0, head : head + 1, :] = peaks[side][head]


def finish_kernel(edge, meta, *refs):
    rows, pairs, halos, held, held_peaks = refs[:6], refs[6], refs[7:9], refs[9:11], refs[11:13]
    outs, (masked, sums, mixed) = refs[13:-3], refs[-3:]
    step = pl.program_id(0)
    width = rows[0].shape[1]
    heads = width // HEAD_DIM
    tiles = pairs.shape[0] // TILE
    places = tile_places(step, edge, tiles)

    def jobs_on(keys, bases):
        jobs = []
        for side in range(2):
            queries, starts, ends = rows[3 * side : 3 * side + 3]
            mask_heads(queries, masked.at[side])
            jobs.append(
                (
                    meta[1 + 2 * places[side]],
                    meta[2 + 2 * places[side]],
                    bases[side],
                    keys[side],
                    lambda row, held=keys[side]: with_ones(held[pl.ds(row, KEYS), width:]),
                    masked.at[side],
                    starts[...],
                    ends[...],
                    sums.at[side],
                )
            )
        return jobs

    @pl.when(step < edge)
    def _():
        for side in range(2):
            sums[side] = held[side][0]

    reaches_back = meta[1 + 2 * places[0]] < edge
    reaches_ahead = meta[2 + 2 * places[1]] > edge + tiles

    @pl.when((step < edge) & (reaches_back | reaches_ahead))
    def _():
        peaks = tuple(
            tuple(held_peaks[side][0, head : head + 1, :] for head in range(heads))
            for side in range(2)
        )
        sweep(jobs_on(halos, (0, edge + tiles)), peaks)

    @pl.when(step >= edge)
    def _():
        sums[...] = jnp.zeros_like(sums)
        sweep(jobs_on((pairs, pairs), (edge, edge)), (fresh_peaks(heads), fresh_peaks(heads)))

    for side in range(2):
        parts = []
        for head in range(heads):
            row = head * HEAD_ROWS
            parts.append(
                sums[side, row : row + HEAD_DIM, :]
                / sums[side, row + HEAD_DIM : row + HEAD_DIM + 1, :]
            )
        tile_rows = pl.ds(pl.multiple_of(places[side] * TILE, TILE), TILE)
        mixed[tile_rows, :] = jnp.concatenate(parts, axis=0).T.astype(jnp.bfloat16)

    @pl.when(step == pl.num_programs(0) - 1)
    def _():
        count = outs[0].shape[0]
        for distance, out in enumerate(outs):
            out[...] = mixed[pl.ds(pl.multiple_of((meta[0] ^ distance) * count, 128), count), :]


def tile_places(step, edge, tiles):
    middle = edge + 2 * (step - edge)
    return (
        jnp.where(step < edge, step, middle),
        jnp.where(step < edge, tiles - edge + step, middle + 1),
    )


def attend_specs(width, edge, tiles):
    specs = []
    for side in range(2):
        place = lambda i, side=side: tile_places(i, edge, tiles)[side]
        specs.append(pl.BlockSpec((TILE, width), lambda i, m, place=place: (place(i), 0)))
        specs += [pl.BlockSpec((1, TILE), lambda i, m, place=place: (0, place(i)))] * 2
    return specs + [pl.BlockSpec((tiles * TILE, 2 * width), lambda i, m: (0, 0))]


def attend_edges(meta, queries, starts, ends, pairs):
    group_rows, width = queries.shape
    heads = width // HEAD_DIM
    tiles, edge = group_rows // TILE, SPAN // TILE
    shapes = [(edge, heads * HEAD_ROWS, TILE)] * 2 + [(edge, 8, TILE)] * 2
    return pl.pallas_call(
        edge_kernel,
        grid_spec=pltpu.PrefetchScalarGridSpec(
            num_scalar_prefetch=1,
            grid=(edge,),
            in_specs=attend_specs(width, edge, tiles),
            out_specs=[pl.BlockSpec((1,) + shape[1:], lambda i, m: (i, 0, 0)) for shape in shapes],
            scratch_shapes=[
                pltpu.VMEM((2, heads, width, TILE), jnp.bfloat16),
                pltpu.VMEM((heads * HEAD_ROWS, group_rows), jnp.bfloat16),
            ],
        ),
        out_shape=[jax.ShapeDtypeStruct(shape, jnp.float32) for shape in shapes],
        compiler_params=PARAMS,
        cost_estimate=pl.CostEstimate(
            flops=16 * group_rows * 1024 * width,
            bytes_accessed=5 << 20,
            transcendentals=group_rows * 1024 * heads,
        ),
        name="attend_edges",
    )(meta, queries, starts, ends, queries, starts, ends, pairs)


def attend_finish(meta, queries, starts, ends, pairs, before, after, held, rows):
    group_rows, width = queries.shape
    heads = width // HEAD_DIM
    tiles, edge = group_rows // TILE, SPAN // TILE
    members = group_rows // rows
    return pl.pallas_call(
        functools.partial(finish_kernel, edge),
        grid_spec=pltpu.PrefetchScalarGridSpec(
            num_scalar_prefetch=1,
            grid=(edge + (tiles - 2 * edge) // 2,),
            in_specs=attend_specs(width, edge, tiles)
            + [pl.BlockSpec((SPAN, 2 * width), lambda i, m: (0, 0))] * 2
            + [
                pl.BlockSpec((1,) + part.shape[1:], lambda i, m: (jnp.minimum(i, edge - 1), 0, 0))
                for part in held
            ],
            out_specs=[pl.BlockSpec((rows, width), lambda i, m: (0, 0))] * members,
            scratch_shapes=[
                pltpu.VMEM((2, heads, width, TILE), jnp.bfloat16),
                pltpu.VMEM((2, heads * HEAD_ROWS, TILE), jnp.float32),
                pltpu.VMEM((group_rows, width), jnp.bfloat16),
            ],
        ),
        out_shape=[jax.ShapeDtypeStruct((rows, width), jnp.bfloat16)] * members,
        compiler_params=PARAMS,
        cost_estimate=pl.CostEstimate(
            flops=16 * group_rows * 1024 * width,
            bytes_accessed=5 << 20,
            transcendentals=group_rows * 1024 * heads,
        ),
        name="attend_finish",
    )(meta, queries, starts, ends, queries, starts, ends, pairs, before, after, *held)


def output_kernel(members, meta, *refs):
    parts, result, mixed = refs[:members], refs[-2], refs[-1]
    weights = refs[members:-2]
    step = pl.program_id(0)
    width = parts[0].shape[1]

    @pl.when(step == 0)
    def _():
        for distance in range(members):
            source = meta[0] ^ distance
            head_pair = PAIR * (source % (members // PAIR)) + source // (members // PAIR)
            columns = pl.ds(pl.multiple_of(head_pair * width, width), width)
            mixed[:, columns] = parts[distance][...]

    for distance, weight in enumerate(weights):

        @pl.when(step == distance)
        def _():
            result[...] = jnp.dot(
                mixed[...], weight[...], preferred_element_type=jnp.float32
            ).astype(jnp.bfloat16)


def output_projection(meta, parts, weights):
    rows, width = parts[0].shape
    depth, tile = weights[0].shape
    steps = len(weights)
    return pl.pallas_call(
        functools.partial(output_kernel, len(parts)),
        grid_spec=pltpu.PrefetchScalarGridSpec(
            num_scalar_prefetch=1,
            grid=(steps,),
            in_specs=[pl.BlockSpec((rows, width), lambda i, m: (0, 0))] * len(parts)
            + [pl.BlockSpec((depth, tile), lambda i, m: (0, 0))] * steps,
            out_specs=pl.BlockSpec((rows, tile), lambda i, m: (0, (m[0] % steps) ^ i)),
            scratch_shapes=[pltpu.VMEM((rows, depth), jnp.bfloat16)],
        ),
        out_shape=jax.ShapeDtypeStruct((rows, steps * tile), jnp.bfloat16),
        compiler_params=PARAMS,
        cost_estimate=pl.CostEstimate(
            flops=2 * rows * depth * steps * tile, bytes_accessed=4 << 20, transcendentals=0
        ),
        name="output_projection",
    )(meta, *parts, *weights)


def unpack_kernel(own_row, other_row, pages):
    _, pair, members, capacity, part = own_row.shape
    width = part // (2 * PAGE)
    for source in range(pair):
        for low in range(pair):
            received = own_row if source == low else other_row
            for high in range(members):
                for turn in range(2 * PAGE):
                    start = (turn * pair * members + PAIR * high + low) * width
                    pages[source, :, start : start + width] = received[
                        0, low, high, :, turn * width : (turn + 1) * width
                    ]


def unpack(own_row, other_row):
    planes, pair, members, capacity, part = own_row.shape
    block = pl.BlockSpec((1,) + own_row.shape[1:], lambda i: (i, 0, 0, 0, 0))
    return pl.pallas_call(
        unpack_kernel,
        grid=(planes,),
        in_specs=[block, block],
        out_specs=pl.BlockSpec((pair, capacity, pair * members * part), lambda i: (i, 0, 0)),
        out_shape=jax.ShapeDtypeStruct(
            (planes * pair, capacity, pair * members * part), jnp.bfloat16
        ),
        compiler_params=pltpu.CompilerParams(vmem_limit_bytes=24 * 1024 * 1024),
        cost_estimate=pl.CostEstimate(flops=0, bytes_accessed=6 << 20, transcendentals=0),
        name="unpack",
    )(own_row, other_row)


def rope_tables(positions):
    half_dim = HEAD_DIM // 2
    inverse = 1.0 / ROPE_BASE ** (jnp.arange(half_dim, dtype=jnp.float32) * 2.0 / HEAD_DIM)
    angles = inverse[:, None] * positions.astype(jnp.float32)[None, :]
    return jnp.cos(angles), jnp.sin(angles)


def document_bounds(window_ids, rows, blocks):
    reach = SPAN + rows
    firsts = jnp.arange(blocks, dtype=jnp.int32)[:, None] * rows
    own = window_ids[SPAN : SPAN + rows * blocks].reshape(blocks, rows)
    behind = jnp.stack([window_ids[k * rows : k * rows + reach] for k in range(blocks)])
    ahead = jnp.stack(
        [window_ids[SPAN + k * rows : SPAN + k * rows + reach] for k in range(blocks)]
    )
    starts = jnp.sum((behind[:, None, :] < own[:, :, None]).astype(jnp.int32), axis=2) + firsts
    ends = (
        jnp.sum((ahead[:, None, :] <= own[:, :, None]).astype(jnp.int32), axis=2)
        + firsts
        + SPAN
    )
    return starts.reshape(-1), ends.reshape(-1)


def per_device(tokens, norm_gain, input_weight, output_weight, segment_ids, page_owner):
    rows, model_width = tokens.shape
    peers, members = lax.axis_size("tok"), lax.axis_size("grp")
    place, column = lax.axis_index("tok"), lax.axis_index("grp")
    low = place % PAIR
    blocks = PAIR * members
    member = low * members + column
    group_rows = rows * blocks
    width = model_width // blocks
    pages = rows // PAGE

    flat = peers * members
    owners = page_owner[:, 0]
    capacity = max(2, (2 * pages + peers - 1) // peers)
    halves = []
    for parity in range(PAIR):
        pieces = []
        for number in range(PARTS):
            start = number * PAIR * width
            choices = [input_weight[:, start : start + width], input_weight[:, start + width : start + 2 * width]]
            piece = jnp.where((low ^ parity) == 0, choices[0], choices[1])
            route = []
            for source in range(flat):
                row, column_from = divmod(source, members)
                target = (row ^ parity) * members + (PARTS * column_from + number) % members
                route.append((source, target))
            pieces.append(lax.ppermute(piece, ("tok", "grp"), route))
        halves.append(jnp.concatenate(pieces, axis=1))
    plane = jnp.concatenate(halves, axis=0)
    top, bottom = layer_norm(tokens, norm_gain[None, :], owners, capacity)
    top, bottom, plane = lax.optimization_barrier((top, bottom, plane))
    across = [flipped(top, "grp", 2), flipped(bottom, "grp", 2)]
    along = [flipped(top, "tok", 1), flipped(bottom, "tok", 1)]
    sibling = [flipped(top, "grp", 1), flipped(bottom, "grp", 1)]
    planes = {0: plane}
    bit = peers // 2
    while bit > 1:
        planes[bit] = flipped(plane, "tok", bit)
        bit //= 2
    last_weight = output_weight
    bit = PAIR
    while 2 * bit < peers:
        last_weight = merged(last_weight, flipped(last_weight, "tok", bit), "tok", bit, 0)
        bit *= 2

    first_row = place // PAIR * group_rows
    segment_ids, last_weight = lax.optimization_barrier((segment_ids, last_weight))
    padded_ids = jnp.concatenate(
        [
            jnp.full((SPAN,), -1, jnp.int32),
            segment_ids,
            jnp.full((SPAN,), 1 << 30, jnp.int32),
        ]
    )
    window_ids = lax.dynamic_slice_in_dim(padded_ids, first_row, group_rows + 2 * SPAN, 0)
    starts, ends = document_bounds(window_ids, rows, blocks)
    positions = SPAN + jnp.arange(group_rows, dtype=jnp.int32) - starts
    cosine, sine = rope_tables(positions)
    ranges = jnp.stack(
        [starts[::TILE] // TILE, (ends[TILE - 1 :: TILE] + TILE - 1) // TILE], axis=1
    ).reshape(-1)
    own_member = member[None].astype(jnp.int32)
    tile_meta = jnp.concatenate([own_member, ranges])
    order = [(number * members + column) % PARTS for number in range(PARTS)]
    meta = jnp.stack([member, place] + order).astype(jnp.int32)
    bounds = (starts[None, :], ends[None, :])

    across, along, sibling, planes, last_weight, cosine, sine, tile_meta, meta, bounds = (
        lax.optimization_barrier(
            (across, along, sibling, planes, last_weight, cosine, sine, tile_meta, meta, bounds)
        )
    )
    corner = [flipped(across[0], "tok", 1), flipped(along[1], "grp", 2)]
    across_sibling = [flipped(block, "grp", 1) for block in across]
    along_sibling = [flipped(block, "grp", 1) for block in along]
    for distance in range(PAIR, peers, PAIR):
        if distance not in planes:
            step_bit = distance & -distance
            planes[distance] = flipped(planes[distance ^ step_bit], "tok", step_bit)
    if bit < peers:
        last_weight = merged(last_weight, flipped(last_weight, "tok", bit), "tok", bit, 0)
    last_weight = last_weight.reshape((peers // PAIR,) + output_weight.shape)
    weights = [planes[distance] for distance in range(0, peers, PAIR)]
    across_sibling, along_sibling, corner, weights, last_weight = lax.optimization_barrier(
        (across_sibling, along_sibling, corner, weights, last_weight)
    )
    corner_sibling = [flipped(block, "grp", 1) for block in corner]
    other_weight = flipped(last_weight, "tok", 1)
    near_blocks = [top, bottom] + sibling + across + across_sibling
    far_blocks = along + along_sibling + corner
    half, held = rows // 2, rows + EXTRA_ROWS
    layout = [
        [(2 * number, 0, half), (2 * number + 1, half, held - half)] for number in range(4)
    ]

    sizes = (weights, cosine, sine, rows, blocks, peers, capacity)

    def to_owners(send):
        received = lax.all_to_all(
            send.reshape((flat,) + send.shape[2:]),
            ("tok", "grp"),
            split_axis=0,
            concat_axis=0,
            tiled=True,
        )
        return received.reshape((peers // PAIR, PAIR, members) + send.shape[2:])

    queries, pairs, send = project(meta, 0, layout, near_blocks, *sizes, ())
    send, corner_sibling, other_weight = lax.optimization_barrier(
        (send, corner_sibling, other_weight)
    )
    own_row = to_owners(send)
    queries, pairs, send = project(
        meta, 4, layout, far_blocks + corner_sibling, *sizes, (queries, pairs)
    )
    before = shifted(pairs[group_rows - SPAN :], "tok", PAIR)
    after = shifted(pairs[:SPAN], "tok", -PAIR)
    columns = merged(last_weight, other_weight, "tok", 1, 1).reshape(model_width, -1)
    columns_across = flipped(columns, "grp", 2)

    edges = attend_edges(tile_meta, queries, *bounds, pairs)
    columns_across, before, after, edges, send = lax.optimization_barrier(
        (columns_across, before, after, edges, send)
    )
    other_row = to_owners(send)
    last_weights = [columns, flipped(columns, "grp", 1)]
    last_weights += [columns_across, flipped(columns_across, "grp", 1)]
    mixed = attend_finish(tile_meta, queries, *bounds, pairs, before, after, edges, rows)
    parts = [mixed[0]] + [
        lax.ppermute(
            mixed[distance],
            ("tok", "grp"),
            [(source, source ^ distance) for source in range(flat)],
        )
        for distance in range(1, blocks)
    ]
    attended = output_projection(own_member, parts, last_weights)

    cache_pages = unpack(own_row, other_row).reshape(
        peers * capacity, 2 * PAGE * model_width
    )
    return attended, cache_pages


def solution(mesh):
    placed = (
        P(("tok", "grp"), None),
        P(),
        P("tok", "grp"),
        P("tok", "grp"),
        P(),
        P(("tok", "grp"), None),
    )
    return jax.shard_map(
        per_device,
        mesh=mesh,
        in_specs=placed,
        out_specs=(P(("tok", "grp"), None), P(("tok", "grp"), None)),
        check_vma=False,
    )
```

```python
import functools
import math

import jax
import jax.numpy as jnp
from jax import lax
from jax.experimental import pallas as pl
from jax.experimental.pallas import tpu as pltpu
from jax.sharding import PartitionSpec as P

H = 16
SPAN = 1024
PAGE = 4
HEAD_DIM = 64

NEG_FILL = -1e30
ROPE_BASE = 160000.0
EPSILON = 1e-05
TILE = 256
PARTS = 3
PAIR = 2
ONES_ROWS = 16
HEAD_ROWS = HEAD_DIM + ONES_ROWS
EXTRA_ROWS = 16
KEYS = 512
SCALE = HEAD_DIM ** (-0.5) * math.log2(math.e)
VMEM_LIMIT = 60 * 1024 * 1024
PARAMS = pltpu.CompilerParams(vmem_limit_bytes=VMEM_LIMIT)


def flipped(value, axis, bit):
    count = lax.axis_size(axis)
    return lax.ppermute(value, axis, [(source, source ^ bit) for source in range(count)])


def shifted(value, axis, steps):
    count = lax.axis_size(axis)
    initial, last = (max(0, -steps), min(count, count - steps))
    return lax.ppermute(value, axis, [(source, source + steps) for source in range(initial, last)])


def merged(value, other, axis, bit, low):
    first = (lax.axis_index(axis) & bit) == 0
    pair = jnp.stack([jnp.where(first, value, other), jnp.where(first, other, value)], axis=low)
    return pair.reshape((-1,) + value.shape[1:])


def norm_kernel(capacity, tokens, gain, owner_row, normed, owners):
    rows = tokens.shape[0]
    values = tokens[...].astype(jnp.float32)
    centred = values - jnp.mean(values, axis=-1, keepdims=True)
    spread = jnp.mean(jnp.square(centred), axis=-1, keepdims=True)
    normed[:rows, :] = (centred * lax.rsqrt(spread + EPSILON) * gain[...]).astype(jnp.bfloat16)
    pages = owner_row.shape[1]
    owners[...] = jnp.full(owners.shape, -1.0, jnp.float32)
    owners[:1, :pages] = owner_row[...].astype(jnp.float32)
    lanes = owners.shape[1]
    across = jnp.broadcast_to(owners[:1, :], (lanes, lanes))
    earlier = lax.broadcasted_iota(jnp.int32, (lanes, lanes), 0) < lax.broadcasted_iota(
        jnp.int32, (lanes, lanes), 1
    )
    same = (across.T == across) & earlier
    ranks = jnp.sum(jnp.where(same, 1.0, 0.0), axis=0, keepdims=True)
    slots = owners[:1, :] * capacity + ranks
    normed[rows:, :] = jnp.zeros((EXTRA_ROWS, normed.shape[1]), jnp.bfloat16)
    normed[rows:, :lanes] = jnp.broadcast_to(slots, (EXTRA_ROWS, lanes)).astype(jnp.bfloat16)


def layer_norm(tokens, gain, owners, capacity):
    rows, width = tokens.shape
    lanes = -(-owners.shape[0] // 128) * 128
    return pl.pallas_call(
        functools.partial(norm_kernel, capacity),
        out_shape=jax.ShapeDtypeStruct((rows + EXTRA_ROWS, width), jnp.bfloat16),
        scratch_shapes=[pltpu.VMEM((8, lanes), jnp.float32)],
        compiler_params=PARAMS,
        name="layer_norm",
    )(tokens, gain, owners[None, :])


def project_kernel(first, layout, weight_count, peers, capacity, meta, *refs):
    operands = 1 + max(entry[0] for pieces in layout for entry in pieces)
    tokens = refs[:operands]
    weights = refs[operands : operands + weight_count]
    cosine, sine = refs[operands + weight_count : operands + weight_count + 2]
    query_out, pair_out, send_out, blocks, weight, page_source, sems = refs[-7:]
    step = pl.program_id(0)
    steps = len(layout)
    rows = query_out.shape[0]
    width = query_out.shape[1]
    shard = weights[0].shape[0] // 2

    def arrivals(number):
        return [
            pltpu.make_async_copy(
                tokens[operand],
                blocks.at[number, pl.ds(offset, count), :],
                sems.at[number, place],
            )
            for place, (operand, offset, count) in enumerate(layout[number])
        ]

    @pl.when(step == 0)
    def _():
        for number in range(steps):
            for copy in arrivals(number):
                copy.start()
        for plane in range(weight_count):
            for low in range(2):
                row = pl.multiple_of((meta[1] ^ (2 * plane + low)) * shard, shard)
                for number in range(PARTS):
                    column = pl.multiple_of(meta[2 + number] * width, width)
                    weight[pl.ds(row, shard), number * width : (number + 1) * width] = weights[
                        plane
                    ][low * shard : (low + 1) * shard, pl.ds(column, width)]

    for number in range(steps):

        @pl.when(step == number)
        def _():
            for copy in arrivals(number):
                copy.wait()

    joined = jnp.dot(blocks[step, :rows, :], weight[...], preferred_element_type=jnp.float32)
    cosines = jnp.concatenate([cosine[...]] * 4, axis=0).T
    sines = jnp.concatenate([-sine[...], sine[...]] * 2, axis=0).T
    first_half = lax.rem(lax.broadcasted_iota(jnp.int32, (rows, width), 1), HEAD_DIM) < (
        HEAD_DIM // 2
    )

    def rotate(values):
        partner = jnp.where(
            first_half,
            pltpu.roll(values, width - HEAD_DIM // 2, 1),
            pltpu.roll(values, HEAD_DIM // 2, 1),
        )
        return (values * cosines + partner * sines).astype(jnp.bfloat16)

    query_out[...] = rotate(joined[:, :width])
    keys = rotate(joined[:, width : 2 * width])
    values = joined[:, 2 * width :].astype(jnp.bfloat16)
    pair_out[:, :width] = keys
    pair_out[:, width:] = values
    page_source[0] = keys.astype(jnp.float32)
    page_source[1] = values.astype(jnp.float32)

    pages = rows // PAGE
    slot_count = peers * capacity
    slots = blocks[step, rows : rows + EXTRA_ROWS, :128].astype(jnp.float32)[:1, :pages]
    chosen = (
        lax.broadcasted_iota(jnp.int32, (slot_count, pages), 0).astype(jnp.float32) == slots
    ).astype(jnp.bfloat16)
    for turn in range(PAGE):
        page_part = jnp.concatenate(
            [
                page_source[half, pl.ds(turn, pages, stride=PAGE), :].astype(jnp.bfloat16)
                for half in range(2)
            ],
            axis=1,
        )
        placed = jnp.dot(chosen, page_part, preferred_element_type=jnp.float32)
        columns = slice(turn * 2 * width, (turn + 1) * 2 * width)
        for peer in range(peers):
            send_out[peer, 0, :, columns] = placed[
                peer * capacity : (peer + 1) * capacity
            ].astype(jnp.bfloat16)


def project(meta, first, layout, operands, weights, cosine, sine, rows, blocks, peers, capacity, into):
    steps = len(layout)
    model_width = operands[0].shape[1]
    group_rows = rows * blocks
    width = weights[0].shape[1] // PARTS
    members = blocks // PAIR
    whole = lambda shape: pl.BlockSpec(shape, lambda i, m: (0,) * len(shape))
    place = lambda i, m: m[0] ^ (first + i)
    table = pl.BlockSpec((HEAD_DIM // 2, rows), lambda i, m: (0, place(i, m)))
    send_shape = (peers, members, capacity, 2 * PAGE * width)
    return pl.pallas_call(
        functools.partial(project_kernel, first, layout, len(weights), peers, capacity),
        grid_spec=pltpu.PrefetchScalarGridSpec(
            num_scalar_prefetch=1,
            grid=(steps,),
            in_specs=[pl.BlockSpec(memory_space=pl.ANY)] * len(operands)
            + [whole(weights[0].shape)] * len(weights)
            + [table, table]
            + [pl.BlockSpec(memory_space=pl.ANY)] * len(into),
            out_specs=[
                pl.BlockSpec((rows, width), lambda i, m: (place(i, m), 0)),
                pl.BlockSpec((rows, 2 * width), lambda i, m: (place(i, m), 0)),
                pl.BlockSpec(
                    (peers, 1) + send_shape[2:], lambda i, m: (0, place(i, m) % members, 0, 0)
                ),
            ],
            scratch_shapes=[
                pltpu.VMEM((steps, rows + EXTRA_ROWS, model_width), jnp.bfloat16),
                pltpu.VMEM((model_width, PARTS * width), jnp.bfloat16),
                pltpu.VMEM((2, rows, width), jnp.float32),
                pltpu.SemaphoreType.DMA((steps, 2)),
            ],
        ),
        out_shape=[
            jax.ShapeDtypeStruct((group_rows, width), jnp.bfloat16),
            jax.ShapeDtypeStruct((group_rows, 2 * width), jnp.bfloat16),
            jax.ShapeDtypeStruct(send_shape, jnp.bfloat16),
        ],
        input_output_aliases={
            1 + len(operands) + len(weights) + 2 + number: number for number in range(len(into))
        },
        compiler_params=PARAMS,
        cost_estimate=pl.CostEstimate(
            flops=16 * steps * rows * model_width * PARTS * width,
            bytes_accessed=(3 * steps) << 19,
            transcendentals=0,
        ),
        name="project",
    )(meta, *operands, *weights, cosine, sine, *into)


def mask_heads(queries, masked):
    turned = queries[...].T
    head_of_row = lax.broadcasted_iota(jnp.int32, turned.shape, 0) // HEAD_DIM
    for head in range(masked.shape[0]):
        masked[head] = jnp.where(head_of_row == head, turned, jnp.zeros((), jnp.bfloat16))


def with_ones(values):
    turned = values.T
    ones = jnp.ones((ONES_ROWS, values.shape[0]), values.dtype)
    rows = []
    for head in range(values.shape[1] // HEAD_DIM):
        rows += [turned[head * HEAD_DIM : (head + 1) * HEAD_DIM], ones]
    return jnp.concatenate(rows, axis=0)


def sweep(jobs, peaks):
    plans = []
    steps = 0
    for begin, end, base, pairs, values_of, masked, starts, ends, total in jobs:
        held = pairs.shape[0] // TILE
        begin, end = jnp.maximum(begin, base), jnp.minimum(end, base + held)
        last = jnp.minimum(ends, end * TILE)
        steps = jnp.maximum(steps, (end - begin + KEYS // TILE - 1) // (KEYS // TILE))
        plans.append((begin, base, held, pairs, values_of, masked, starts, last, total))

    def one(number, peaks):
        new_peaks = []
        for plan, old_peaks in zip(plans, peaks):
            begin, base, held, pairs, values_of, masked, starts, last, total = plan
            wanted = begin + number * (KEYS // TILE)
            block = jnp.minimum(wanted, base + held - KEYS // TILE)
            row = pl.multiple_of((block - base) * TILE, TILE)
            keys = pairs[pl.ds(row, KEYS), : pairs.shape[1] // 2]
            values = values_of(row)
            index = block * TILE + lax.broadcasted_iota(jnp.int32, (KEYS, TILE), 0)
            allowed = (index >= jnp.maximum(starts, wanted * TILE)) & (index < last)
            job_peaks = []
            for head, old_peak in enumerate(old_peaks):
                scores = jnp.dot(keys, masked[head], preferred_element_type=jnp.float32)
                scores = jnp.where(allowed, scores * SCALE, NEG_FILL)
                peak = jnp.maximum(old_peak, jnp.max(scores, axis=0, keepdims=True))
                fade = jnp.exp2(old_peak - peak)
                weights = jnp.exp2(scores - peak).astype(jnp.bfloat16)
                own = slice(head * HEAD_ROWS, (head + 1) * HEAD_ROWS)
                total[own, :] = total[own, :] * fade + jnp.dot(
                    values[own, :], weights, preferred_element_type=jnp.float32
                )
                job_peaks.append(peak)
            new_peaks.append(tuple(job_peaks))
        return tuple(new_peaks)

    return lax.fori_loop(0, steps, one, peaks)


def fresh_peaks(heads):
    return tuple(jnp.full((1, TILE), NEG_FILL, jnp.float32) for _ in range(heads))


def edge_kernel(meta, *refs):
    rows, pairs, outs, (masked, values) = refs[:6], refs[6], refs[7:11], refs[11:]
    step = pl.program_id(0)
    width = rows[0].shape[1]
    heads = width // HEAD_DIM
    edge = pl.num_programs(0)
    tiles = pairs.shape[0] // TILE

    @pl.when(step == 0)
    def _():
        for number in range(tiles):
            own = slice(number * TILE, (number + 1) * TILE)
            values[:, own] = with_ones(pairs[own, width:])

    jobs = []
    for side in range(2):
        tile = step + side * (tiles - edge)
        queries, starts, ends = rows[3 * side : 3 * side + 3]
        mask_heads(queries, masked.at[side])
        total = outs[side]
        total[...] = jnp.zeros_like(total)
        jobs.append(
            (
                meta[1 + 2 * tile],
                meta[2 + 2 * tile],
                edge,
                pairs,
                lambda row: values[:, pl.ds(row, KEYS)],
                masked.at[side],
                starts[...],
                ends[...],
                total.at[0],
            )
        )
    peaks = sweep(jobs, (fresh_peaks(heads), fresh_peaks(heads)))
    for side in range(2):
        for head in range(heads):
            outs[2 + side][0, head : head + 1, :] = peaks[side][head]


def finish_kernel(edge, meta, *refs):
    rows, pairs, halos, held, held_peaks = refs[:6], refs[6], refs[7:9], refs[9:11], refs[11:13]
    outs, (masked, sums, mixed) = refs[13:-3], refs[-3:]
    step = pl.program_id(0)
    width = rows[0].shape[1]
    heads = width // HEAD_DIM
    tiles = pairs.shape[0] // TILE
    places = tile_places(step, edge, tiles)

    def jobs_on(keys, bases):
        jobs = []
        for side in range(2):
            queries, starts, ends = rows[3 * side : 3 * side + 3]
            mask_heads(queries, masked.at[side])
            jobs.append(
                (
                    meta[1 + 2 * places[side]],
                    meta[2 + 2 * places[side]],
                    bases[side],
                    keys[side],
                    lambda row, held=keys[side]: with_ones(held[pl.ds(row, KEYS), width:]),
                    masked.at[side],
                    starts[...],
                    ends[...],
                    sums.at[side],
                )
            )
        return jobs

    @pl.when(step < edge)
    def _():
        for side in range(2):
            sums[side] = held[side][0]

    reaches_back = meta[1 + 2 * places[0]] < edge
    reaches_ahead = meta[2 + 2 * places[1]] > edge + tiles

    @pl.when((step < edge) & (reaches_back | reaches_ahead))
    def _():
        peaks = tuple(
            tuple(held_peaks[side][0, head : head + 1, :] for head in range(heads))
            for side in range(2)
        )
        sweep(jobs_on(halos, (0, edge + tiles)), peaks)

    @pl.when(step >= edge)
    def _():
        sums[...] = jnp.zeros_like(sums)
        sweep(jobs_on((pairs, pairs), (edge, edge)), (fresh_peaks(heads), fresh_peaks(heads)))

    for side in range(2):
        parts = []
        for head in range(heads):
            row = head * HEAD_ROWS
            parts.append(
                sums[side, row : row + HEAD_DIM, :]
                / sums[side, row + HEAD_DIM : row + HEAD_DIM + 1, :]
            )
        tile_rows = pl.ds(pl.multiple_of(places[side] * TILE, TILE), TILE)
        mixed[tile_rows, :] = jnp.concatenate(parts, axis=0).T.astype(jnp.bfloat16)

    @pl.when(step == pl.num_programs(0) - 1)
    def _():
        count = outs[0].shape[0]
        for distance, out in enumerate(outs):
            out[...] = mixed[pl.ds(pl.multiple_of((meta[0] ^ distance) * count, 128), count), :]


def tile_places(step, edge, tiles):
    middle = edge + 2 * (step - edge)
    return (
        jnp.where(step < edge, step, middle),
        jnp.where(step < edge, tiles - edge + step, middle + 1),
    )


def attend_specs(width, edge, tiles):
    specs = []
    for side in range(2):
        place = lambda i, side=side: tile_places(i, edge, tiles)[side]
        specs.append(pl.BlockSpec((TILE, width), lambda i, m, place=place: (place(i), 0)))
        specs += [pl.BlockSpec((1, TILE), lambda i, m, place=place: (0, place(i)))] * 2
    return specs + [pl.BlockSpec((tiles * TILE, 2 * width), lambda i, m: (0, 0))]


def attend_edges(meta, queries, starts, ends, pairs):
    group_rows, width = queries.shape
    heads = width // HEAD_DIM
    tiles, edge = group_rows // TILE, SPAN // TILE
    shapes = [(edge, heads * HEAD_ROWS, TILE)] * 2 + [(edge, 8, TILE)] * 2
    return pl.pallas_call(
        edge_kernel,
        grid_spec=pltpu.PrefetchScalarGridSpec(
            num_scalar_prefetch=1,
            grid=(edge,),
            in_specs=attend_specs(width, edge, tiles),
            out_specs=[pl.BlockSpec((1,) + shape[1:], lambda i, m: (i, 0, 0)) for shape in shapes],
            scratch_shapes=[
                pltpu.VMEM((2, heads, width, TILE), jnp.bfloat16),
                pltpu.VMEM((heads * HEAD_ROWS, group_rows), jnp.bfloat16),
            ],
        ),
        out_shape=[jax.ShapeDtypeStruct(shape, jnp.float32) for shape in shapes],
        compiler_params=PARAMS,
        cost_estimate=pl.CostEstimate(
            flops=16 * group_rows * 1024 * width,
            bytes_accessed=5 << 20,
            transcendentals=group_rows * 1024 * heads,
        ),
        name="attend_edges",
    )(meta, queries, starts, ends, queries, starts, ends, pairs)


def attend_finish(meta, queries, starts, ends, pairs, before, after, held, rows):
    group_rows, width = queries.shape
    heads = width // HEAD_DIM
    tiles, edge = group_rows // TILE, SPAN // TILE
    members = group_rows // rows
    return pl.pallas_call(
        functools.partial(finish_kernel, edge),
        grid_spec=pltpu.PrefetchScalarGridSpec(
            num_scalar_prefetch=1,
            grid=(edge + (tiles - 2 * edge) // 2,),
            in_specs=attend_specs(width, edge, tiles)
            + [pl.BlockSpec((SPAN, 2 * width), lambda i, m: (0, 0))] * 2
            + [
                pl.BlockSpec((1,) + part.shape[1:], lambda i, m: (jnp.minimum(i, edge - 1), 0, 0))
                for part in held
            ],
            out_specs=[pl.BlockSpec((rows, width), lambda i, m: (0, 0))] * members,
            scratch_shapes=[
                pltpu.VMEM((2, heads, width, TILE), jnp.bfloat16),
                pltpu.VMEM((2, heads * HEAD_ROWS, TILE), jnp.float32),
                pltpu.VMEM((group_rows, width), jnp.bfloat16),
            ],
        ),
        out_shape=[jax.ShapeDtypeStruct((rows, width), jnp.bfloat16)] * members,
        compiler_params=PARAMS,
        cost_estimate=pl.CostEstimate(
            flops=16 * group_rows * 1024 * width,
            bytes_accessed=5 << 20,
            transcendentals=group_rows * 1024 * heads,
        ),
        name="attend_finish",
    )(meta, queries, starts, ends, queries, starts, ends, pairs, before, after, *held)


def output_kernel(members, meta, *refs):
    parts, result, mixed = refs[:members], refs[-2], refs[-1]
    weights = refs[members:-2]
    step = pl.program_id(0)
    width = parts[0].shape[1]

    @pl.when(step == 0)
    def _():
        for distance in range(members):
            source = meta[0] ^ distance
            head_pair = PAIR * (source % (members // PAIR)) + source // (members // PAIR)
            columns = pl.ds(pl.multiple_of(head_pair * width, width), width)
            mixed[:, columns] = parts[distance][...]

    for distance, weight in enumerate(weights):

        @pl.when(step == distance)
        def _():
            result[...] = jnp.dot(
                mixed[...], weight[...], preferred_element_type=jnp.float32
            ).astype(jnp.bfloat16)


def output_projection(meta, parts, weights):
    rows, width = parts[0].shape
    depth, tile = weights[0].shape
    steps = len(weights)
    return pl.pallas_call(
        functools.partial(output_kernel, len(parts)),
        grid_spec=pltpu.PrefetchScalarGridSpec(
            num_scalar_prefetch=1,
            grid=(steps,),
            in_specs=[pl.BlockSpec((rows, width), lambda i, m: (0, 0))] * len(parts)
            + [pl.BlockSpec((depth, tile), lambda i, m: (0, 0))] * steps,
            out_specs=pl.BlockSpec((rows, tile), lambda i, m: (0, (m[0] % steps) ^ i)),
            scratch_shapes=[pltpu.VMEM((rows, depth), jnp.bfloat16)],
        ),
        out_shape=jax.ShapeDtypeStruct((rows, steps * tile), jnp.bfloat16),
        compiler_params=PARAMS,
        cost_estimate=pl.CostEstimate(
            flops=2 * rows * depth * steps * tile, bytes_accessed=4 << 20, transcendentals=0
        ),
        name="output_projection",
    )(meta, *parts, *weights)


def unpack_kernel(own_row, other_row, pages):
    _, pair, members, capacity, part = own_row.shape
    width = part // (2 * PAGE)
    for source in range(pair):
        for low in range(pair):
            received = own_row if source == low else other_row
            for high in range(members):
                for turn in range(2 * PAGE):
                    start = (turn * pair * members + PAIR * high + low) * width
                    pages[source, :, start : start + width] = received[
                        0, low, high, :, turn * width : (turn + 1) * width
                    ]


def unpack(own_row, other_row):
    planes, pair, members, capacity, part = own_row.shape
    block = pl.BlockSpec((1,) + own_row.shape[1:], lambda i: (i, 0, 0, 0, 0))
    return pl.pallas_call(
        unpack_kernel,
        grid=(planes,),
        in_specs=[block, block],
        out_specs=pl.BlockSpec((pair, capacity, pair * members * part), lambda i: (i, 0, 0)),
        out_shape=jax.ShapeDtypeStruct(
            (planes * pair, capacity, pair * members * part), jnp.bfloat16
        ),
        compiler_params=pltpu.CompilerParams(vmem_limit_bytes=24 * 1024 * 1024),
        cost_estimate=pl.CostEstimate(flops=0, bytes_accessed=6 << 20, transcendentals=0),
        name="unpack",
    )(own_row, other_row)


def rope_tables(positions):
    half_dim = HEAD_DIM // 2
    inverse = 1.0 / ROPE_BASE ** (jnp.arange(half_dim, dtype=jnp.float32) * 2.0 / HEAD_DIM)
    angles = inverse[:, None] * positions.astype(jnp.float32)[None, :]
    return jnp.cos(angles), jnp.sin(angles)


def bounds_kernel(ids, starts, ends):
    shape = (8, ids.shape[1])
    width = ids.shape[1]
    own = jnp.broadcast_to(ids[...], shape)
    index = lax.broadcasted_iota(jnp.int32, shape, 1)
    first = jnp.where((own != pltpu.roll(own, 1, 1)) | (index == 0), index, 0)
    after = jnp.where((own != pltpu.roll(own, width - 1, 1)) | (index == width - 1), index + 1, width)
    shift = 1
    while shift < SPAN:
        first = jnp.maximum(first, jnp.where(index >= shift, pltpu.roll(first, shift, 1), 0))
        after = jnp.minimum(
            after, jnp.where(index < width - shift, pltpu.roll(after, width - shift, 1), width)
        )
        shift *= 2
    rows = starts.shape[1]
    starts[...] = first[:1, SPAN : SPAN + rows]
    ends[...] = after[:1, SPAN : SPAN + rows]


def document_bounds(window_ids, rows):
    return pl.pallas_call(
        bounds_kernel,
        out_shape=[jax.ShapeDtypeStruct((1, rows), jnp.int32)] * 2,
        compiler_params=PARAMS,
        cost_estimate=pl.CostEstimate(flops=1 << 34, bytes_accessed=0, transcendentals=0),
        name="document_bounds",
    )(window_ids[None, :])


def per_device(tokens, norm_gain, input_weight, output_weight, segment_ids, page_owner):
    rows, model_width = tokens.shape
    peers, members = lax.axis_size("tok"), lax.axis_size("grp")
    place, column = lax.axis_index("tok"), lax.axis_index("grp")
    low = place % PAIR
    blocks = PAIR * members
    member = low * members + column
    group_rows = rows * blocks
    width = model_width // blocks
    pages = rows // PAGE

    flat = peers * members
    owners = page_owner[:, 0]
    capacity = max(2, (2 * pages + peers - 1) // peers)
    halves = []
    for parity in range(PAIR):
        pieces = []
        for number in range(PARTS):
            start = number * PAIR * width
            choices = [input_weight[:, start : start + width], input_weight[:, start + width : start + 2 * width]]
            piece = jnp.where((low ^ parity) == 0, choices[0], choices[1])
            route = []
            for source in range(flat):
                row, column_from = divmod(source, members)
                target = (row ^ parity) * members + (PARTS * column_from + number) % members
                route.append((source, target))
            pieces.append(lax.ppermute(piece, ("tok", "grp"), route))
        halves.append(jnp.concatenate(pieces, axis=1))
    plane = jnp.concatenate(halves, axis=0)
    own = layer_norm(tokens, norm_gain[None, :], owners, capacity)
    own, plane = lax.optimization_barrier((own, plane))

    across, along = flipped(own, "grp", 2), flipped(own, "tok", 1)
    sibling = flipped(own, "grp", 1)
    planes = {0: plane}
    bit = peers // 2
    while bit > 1:
        planes[bit] = flipped(plane, "tok", bit)
        bit //= 2

    last_weight = output_weight
    bit = PAIR
    while 2 * bit < peers:
        last_weight = merged(last_weight, flipped(last_weight, "tok", bit), "tok", bit, 0)
        bit *= 2

    first_row = place // PAIR * group_rows
    padded_ids = jnp.concatenate(
        [
            jnp.full((SPAN,), -1, jnp.int32),
            segment_ids,
            jnp.full((SPAN,), 1 << 30, jnp.int32),
        ]
    )
    window_ids = lax.dynamic_slice_in_dim(padded_ids, first_row, group_rows + 2 * SPAN, 0)
    window_ids, plane = lax.optimization_barrier((window_ids, plane))
    bounds = document_bounds(window_ids, group_rows)
    starts, ends = bounds[0][0], bounds[1][0]
    positions = SPAN + jnp.arange(group_rows, dtype=jnp.int32) - starts
    order = [(number * members + column) % PARTS for number in range(PARTS)]
    meta = jnp.stack([member, place] + order).astype(jnp.int32)
    cosine, sine = rope_tables(positions)
    across, along, sibling, planes, last_weight, cosine, sine, meta = lax.optimization_barrier(
        (across, along, sibling, planes, last_weight, cosine, sine, meta)
    )
    other_planes = flipped(last_weight, "tok", bit)

    half, held = rows // 2, rows + EXTRA_ROWS
    corner = [flipped(across[:half], "tok", 1), flipped(along[half:], "grp", 2)]
    across_sibling = flipped(across, "grp", 1)
    along_sibling = flipped(along, "grp", 1)
    for distance in range(PAIR, peers, PAIR):
        if distance not in planes:
            step_bit = distance & -distance
            planes[distance] = flipped(planes[distance ^ step_bit], "tok", step_bit)
    weights = [planes[distance] for distance in range(0, peers, PAIR)]
    across_sibling, weights = lax.optimization_barrier((across_sibling, weights))
    near_blocks = [own, sibling, across, across_sibling]
    near_layout = [[(number, 0, held)] for number in range(4)]
    far_layout = [[(0, 0, held)], [(1, 0, held)]]
    far_layout += [[(number, 0, half), (number + 1, half, held - half)] for number in (2, 4)]

    sizes = (weights, cosine, sine, rows, blocks, peers, capacity)

    def to_owners(send):
        received = lax.all_to_all(
            send.reshape((flat,) + send.shape[2:]),
            ("tok", "grp"),
            split_axis=0,
            concat_axis=0,
            tiled=True,
        )
        return received.reshape((peers // PAIR, PAIR, members) + send.shape[2:])

    queries, pairs, send = project(meta, 0, near_layout, near_blocks, *sizes, ())
    send, corner, along_sibling, other_planes = lax.optimization_barrier(
        (send, corner, along_sibling, other_planes)
    )
    own_row = to_owners(send)
    corner_sibling = [flipped(block, "grp", 1) for block in corner]
    far_blocks = [along, along_sibling] + corner + corner_sibling
    queries, pairs, send = project(meta, 4, far_layout, far_blocks, *sizes, (queries, pairs))
    before = shifted(pairs[group_rows - SPAN :], "tok", PAIR)
    after = shifted(pairs[:SPAN], "tok", -PAIR)
    last_weight = merged(last_weight, other_planes, "tok", bit, 0)
    last_weight = last_weight.reshape((peers // PAIR,) + output_weight.shape)
    other_weight = flipped(last_weight, "tok", 1)

    own_member = member[None].astype(jnp.int32)
    ranges = jnp.stack(
        [starts[::TILE] // TILE, (ends[TILE - 1 :: TILE] + TILE - 1) // TILE], axis=1
    ).reshape(-1)
    tile_meta = jnp.concatenate([own_member, ranges])
    edges = attend_edges(tile_meta, queries, *bounds, pairs)
    other_weight, before, after, edges, send = lax.optimization_barrier(
        (other_weight, before, after, edges, send)
    )
    other_row = to_owners(send)
    columns = merged(last_weight, other_weight, "tok", 1, 1).reshape(model_width, -1)
    columns_across = flipped(columns, "grp", 2)
    mixed = attend_finish(tile_meta, queries, *bounds, pairs, before, after, edges, rows)
    mixed, columns_across = lax.optimization_barrier((mixed, columns_across))
    last_weights = [columns, flipped(columns, "grp", 1)]
    last_weights += [columns_across, flipped(columns_across, "grp", 1)]
    parts = [mixed[0]] + [
        lax.ppermute(
            mixed[distance],
            ("tok", "grp"),
            [(source, source ^ distance) for source in range(flat)],
        )
        for distance in range(1, blocks)
    ]
    attended = output_projection(own_member, parts, last_weights)

    cache_pages = unpack(own_row, other_row).reshape(
        peers * capacity, 2 * PAGE * model_width
    )
    return attended, cache_pages


def solution(mesh):
    placed = (
        P(("tok", "grp"), None),
        P(),
        P("tok", "grp"),
        P("tok", "grp"),
        P(),
        P(("tok", "grp"), None),
    )
    return jax.shard_map(
        per_device,
        mesh=mesh,
        in_specs=placed,
        out_specs=(P(("tok", "grp"), None), P(("tok", "grp"), None)),
        check_vma=False,
    )
```

```python
import functools
import math

import jax
import jax.numpy as jnp
from jax import lax
from jax.experimental import pallas as pl
from jax.experimental.pallas import tpu as pltpu
from jax.sharding import PartitionSpec as P

H = 16
SPAN = 1024
PAGE = 4
HEAD_DIM = 64

NEG_FILL = -1e30
ROPE_BASE = 160000.0
EPSILON = 1e-05
TILE = 256
PARTS = 3
PAIR = 2
ONES_ROWS = 16
HEAD_ROWS = HEAD_DIM + ONES_ROWS
EXTRA_ROWS = 16
KEYS = 512
SCALE = HEAD_DIM ** (-0.5) * math.log2(math.e)
VMEM_LIMIT = 60 * 1024 * 1024
PARAMS = pltpu.CompilerParams(vmem_limit_bytes=VMEM_LIMIT)


def flipped(value, axis, bit):
    count = lax.axis_size(axis)
    return lax.ppermute(value, axis, [(source, source ^ bit) for source in range(count)])


def shifted(value, axis, steps):
    count = lax.axis_size(axis)
    initial, last = (max(0, -steps), min(count, count - steps))
    return lax.ppermute(value, axis, [(source, source + steps) for source in range(initial, last)])


def norm_kernel(capacity, tokens, gain, owner_row, normed, owners):
    rows = tokens.shape[0]
    values = tokens[...].astype(jnp.float32)
    centred = values - jnp.mean(values, axis=-1, keepdims=True)
    spread = jnp.mean(jnp.square(centred), axis=-1, keepdims=True)
    normed[:rows, :] = (centred * lax.rsqrt(spread + EPSILON) * gain[...]).astype(jnp.bfloat16)
    pages = owner_row.shape[1]
    owners[...] = jnp.full(owners.shape, -1.0, jnp.float32)
    owners[:1, :pages] = owner_row[...].astype(jnp.float32)
    lanes = owners.shape[1]
    across = jnp.broadcast_to(owners[:1, :], (lanes, lanes))
    earlier = lax.broadcasted_iota(jnp.int32, (lanes, lanes), 0) < lax.broadcasted_iota(
        jnp.int32, (lanes, lanes), 1
    )
    same = (across.T == across) & earlier
    ranks = jnp.sum(jnp.where(same, 1.0, 0.0), axis=0, keepdims=True)
    slots = owners[:1, :] * capacity + ranks
    normed[rows:, :] = jnp.zeros((EXTRA_ROWS, normed.shape[1]), jnp.bfloat16)
    normed[rows:, :lanes] = jnp.broadcast_to(slots, (EXTRA_ROWS, lanes)).astype(jnp.bfloat16)


def layer_norm(tokens, gain, owners, capacity):
    rows, width = tokens.shape
    lanes = -(-owners.shape[0] // 128) * 128
    return pl.pallas_call(
        functools.partial(norm_kernel, capacity),
        out_shape=jax.ShapeDtypeStruct((rows + EXTRA_ROWS, width), jnp.bfloat16),
        scratch_shapes=[pltpu.VMEM((8, lanes), jnp.float32)],
        compiler_params=PARAMS,
        name="layer_norm",
    )(tokens, gain, owners[None, :])


def project_kernel(first, layout, weight_count, peers, capacity, meta, *refs):
    operands = 1 + max(entry[0] for pieces in layout for entry in pieces)
    tokens = refs[:operands]
    weights = refs[operands : operands + weight_count]
    cosine, sine = refs[operands + weight_count : operands + weight_count + 2]
    query_out, pair_out, send_out, blocks, weight, page_source, sems = refs[-7:]
    step = pl.program_id(0)
    steps = len(layout)
    rows = query_out.shape[0]
    width = query_out.shape[1]
    shard = weights[0].shape[0] // 2

    def arrivals(number):
        return [
            pltpu.make_async_copy(
                tokens[operand],
                blocks.at[number, pl.ds(offset, count), :],
                sems.at[number, place],
            )
            for place, (operand, offset, count) in enumerate(layout[number])
        ]

    @pl.when(step == 0)
    def _():
        for number in range(steps):
            for copy in arrivals(number):
                copy.start()
        for plane in range(weight_count):
            for low in range(2):
                row = pl.multiple_of((meta[1] ^ (2 * plane + low)) * shard, shard)
                for number in range(PARTS):
                    column = pl.multiple_of(meta[2 + number] * width, width)
                    weight[pl.ds(row, shard), number * width : (number + 1) * width] = weights[
                        plane
                    ][low * shard : (low + 1) * shard, pl.ds(column, width)]

    for number in range(steps):

        @pl.when(step == number)
        def _():
            for copy in arrivals(number):
                copy.wait()

    joined = jnp.dot(blocks[step, :rows, :], weight[...], preferred_element_type=jnp.float32)
    cosines = jnp.concatenate([cosine[...]] * 4, axis=0).T
    sines = jnp.concatenate([-sine[...], sine[...]] * 2, axis=0).T
    first_half = lax.rem(lax.broadcasted_iota(jnp.int32, (rows, width), 1), HEAD_DIM) < (
        HEAD_DIM // 2
    )

    def rotate(values):
        partner = jnp.where(
            first_half,
            pltpu.roll(values, width - HEAD_DIM // 2, 1),
            pltpu.roll(values, HEAD_DIM // 2, 1),
        )
        return (values * cosines + partner * sines).astype(jnp.bfloat16)

    query_out[...] = rotate(joined[:, :width])
    keys = rotate(joined[:, width : 2 * width])
    values = joined[:, 2 * width :].astype(jnp.bfloat16)
    pair_out[:, :width] = keys
    pair_out[:, width:] = values
    page_source[0] = keys.astype(jnp.float32)
    page_source[1] = values.astype(jnp.float32)

    pages = rows // PAGE
    slot_count = peers * capacity
    slots = blocks[step, rows : rows + EXTRA_ROWS, :128].astype(jnp.float32)[:1, :pages]
    chosen = (
        lax.broadcasted_iota(jnp.int32, (slot_count, pages), 0).astype(jnp.float32) == slots
    ).astype(jnp.bfloat16)
    for turn in range(PAGE):
        page_part = jnp.concatenate(
            [
                page_source[half, pl.ds(turn, pages, stride=PAGE), :].astype(jnp.bfloat16)
                for half in range(2)
            ],
            axis=1,
        )
        placed = jnp.dot(chosen, page_part, preferred_element_type=jnp.float32)
        columns = slice(turn * 2 * width, (turn + 1) * 2 * width)
        for peer in range(peers):
            send_out[peer, 0, :, columns] = placed[
                peer * capacity : (peer + 1) * capacity
            ].astype(jnp.bfloat16)


def project(meta, first, layout, operands, weights, cosine, sine, rows, blocks, peers, capacity, into):
    steps = len(layout)
    model_width = operands[0].shape[1]
    group_rows = rows * blocks
    width = model_width // blocks
    members = blocks // PAIR
    whole = lambda shape: pl.BlockSpec(shape, lambda i, m: (0,) * len(shape))
    place = lambda i, m: m[0] ^ (first + i)
    table = pl.BlockSpec((HEAD_DIM // 2, rows), lambda i, m: (0, place(i, m)))
    send_shape = (peers, members, capacity, 2 * PAGE * width)
    return pl.pallas_call(
        functools.partial(project_kernel, first, layout, len(weights), peers, capacity),
        grid_spec=pltpu.PrefetchScalarGridSpec(
            num_scalar_prefetch=1,
            grid=(steps,),
            in_specs=[pl.BlockSpec(memory_space=pl.ANY)] * len(operands)
            + [whole(weights[0].shape)] * len(weights)
            + [table, table]
            + [pl.BlockSpec(memory_space=pl.ANY)] * len(into),
            out_specs=[
                pl.BlockSpec((rows, width), lambda i, m: (place(i, m), 0)),
                pl.BlockSpec((rows, 2 * width), lambda i, m: (place(i, m), 0)),
                pl.BlockSpec(
                    (peers, 1) + send_shape[2:], lambda i, m: (0, place(i, m) % members, 0, 0)
                ),
            ],
            scratch_shapes=[
                pltpu.VMEM((steps, rows + EXTRA_ROWS, model_width), jnp.bfloat16),
                pltpu.VMEM((model_width, PARTS * width), jnp.bfloat16),
                pltpu.VMEM((2, rows, width), jnp.float32),
                pltpu.SemaphoreType.DMA((steps, 2)),
            ],
        ),
        out_shape=[
            jax.ShapeDtypeStruct((group_rows, width), jnp.bfloat16),
            jax.ShapeDtypeStruct((group_rows, 2 * width), jnp.bfloat16),
            jax.ShapeDtypeStruct(send_shape, jnp.bfloat16),
        ],
        input_output_aliases={
            1 + len(operands) + len(weights) + 2 + number: number for number in range(len(into))
        },
        compiler_params=PARAMS,
        cost_estimate=pl.CostEstimate(
            flops=16 * steps * rows * model_width * PARTS * width,
            bytes_accessed=(3 * steps) << 19,
            transcendentals=0,
        ),
        name="project",
    )(meta, *operands, *weights, cosine, sine, *into)


def mask_heads(queries, masked):
    turned = queries[...].T
    head_of_row = lax.broadcasted_iota(jnp.int32, turned.shape, 0) // HEAD_DIM
    for head in range(masked.shape[0]):
        masked[head] = jnp.where(head_of_row == head, turned, jnp.zeros((), jnp.bfloat16))


def with_ones(values):
    turned = values.T
    ones = jnp.ones((ONES_ROWS, values.shape[0]), values.dtype)
    rows = []
    for head in range(values.shape[1] // HEAD_DIM):
        rows += [turned[head * HEAD_DIM : (head + 1) * HEAD_DIM], ones]
    return jnp.concatenate(rows, axis=0)


def sweep(jobs, peaks):
    plans = []
    steps = 0
    for begin, end, base, pairs, values_of, masked, starts, ends, total in jobs:
        held = pairs.shape[0] // TILE
        begin, end = jnp.maximum(begin, base), jnp.minimum(end, base + held)
        last = jnp.minimum(ends, end * TILE)
        steps = jnp.maximum(steps, (end - begin + KEYS // TILE - 1) // (KEYS // TILE))
        plans.append((begin, base, held, pairs, values_of, masked, starts, last, total))

    def one(number, peaks):
        new_peaks = []
        for plan, old_peaks in zip(plans, peaks):
            begin, base, held, pairs, values_of, masked, starts, last, total = plan
            wanted = begin + number * (KEYS // TILE)
            block = jnp.minimum(wanted, base + held - KEYS // TILE)
            row = pl.multiple_of((block - base) * TILE, TILE)
            keys = pairs[pl.ds(row, KEYS), : pairs.shape[1] // 2]
            values = values_of(row)
            index = block * TILE + lax.broadcasted_iota(jnp.int32, (KEYS, TILE), 0)
            allowed = (index >= jnp.maximum(starts, wanted * TILE)) & (index < last)
            job_peaks = []
            for head, old_peak in enumerate(old_peaks):
                scores = jnp.dot(keys, masked[head], preferred_element_type=jnp.float32)
                scores = jnp.where(allowed, scores * SCALE, NEG_FILL)
                peak = jnp.maximum(old_peak, jnp.max(scores, axis=0, keepdims=True))
                fade = jnp.exp2(old_peak - peak)
                weights = jnp.exp2(scores - peak).astype(jnp.bfloat16)
                own = slice(head * HEAD_ROWS, (head + 1) * HEAD_ROWS)
                total[own, :] = total[own, :] * fade + jnp.dot(
                    values[own, :], weights, preferred_element_type=jnp.float32
                )
                job_peaks.append(peak)
            new_peaks.append(tuple(job_peaks))
        return tuple(new_peaks)

    return lax.fori_loop(0, steps, one, peaks)


def fresh_peaks(heads):
    return tuple(jnp.full((1, TILE), NEG_FILL, jnp.float32) for _ in range(heads))


def edge_kernel(meta, ranges, *refs):
    rows, pairs, outs, (masked, values) = refs[:6], refs[6], refs[7:11], refs[11:]
    step = pl.program_id(0)
    width = rows[0].shape[1]
    heads = width // HEAD_DIM
    edge = pl.num_programs(0)
    tiles = pairs.shape[0] // TILE

    @pl.when(step == 0)
    def _():
        for number in range(tiles):
            own = slice(number * TILE, (number + 1) * TILE)
            values[:, own] = with_ones(pairs[own, width:])

    jobs = []
    for side in range(2):
        tile = step + side * (tiles - edge)
        queries, starts, ends = rows[3 * side : 3 * side + 3]
        mask_heads(queries, masked.at[side])
        total = outs[side]
        total[...] = jnp.zeros_like(total)
        jobs.append(
            (
                ranges[0, 2 * tile],
                ranges[0, 2 * tile + 1],
                edge,
                pairs,
                lambda row: values[:, pl.ds(row, KEYS)],
                masked.at[side],
                starts[...],
                ends[...],
                total.at[0],
            )
        )
    peaks = sweep(jobs, (fresh_peaks(heads), fresh_peaks(heads)))
    for side in range(2):
        for head in range(heads):
            outs[2 + side][0, head : head + 1, :] = peaks[side][head]


def finish_kernel(edge, meta, ranges, *refs):
    rows, pairs, halos, held, held_peaks = refs[:6], refs[6], refs[7:9], refs[9:11], refs[11:13]
    outs, (masked, sums, mixed) = refs[13:-3], refs[-3:]
    step = pl.program_id(0)
    width = rows[0].shape[1]
    heads = width // HEAD_DIM
    tiles = pairs.shape[0] // TILE
    places = tile_places(step, edge, tiles)

    def jobs_on(keys, bases):
        jobs = []
        for side in range(2):
            queries, starts, ends = rows[3 * side : 3 * side + 3]
            mask_heads(queries, masked.at[side])
            jobs.append(
                (
                    ranges[0, 2 * places[side]],
                    ranges[0, 2 * places[side] + 1],
                    bases[side],
                    keys[side],
                    lambda row, held=keys[side]: with_ones(held[pl.ds(row, KEYS), width:]),
                    masked.at[side],
                    starts[...],
                    ends[...],
                    sums.at[side],
                )
            )
        return jobs

    @pl.when(step < edge)
    def _():
        for side in range(2):
            sums[side] = held[side][0]

    reaches_back = ranges[0, 2 * places[0]] < edge
    reaches_ahead = ranges[0, 2 * places[1] + 1] > edge + tiles

    @pl.when((step < edge) & (reaches_back | reaches_ahead))
    def _():
        peaks = tuple(
            tuple(held_peaks[side][0, head : head + 1, :] for head in range(heads))
            for side in range(2)
        )
        sweep(jobs_on(halos, (0, edge + tiles)), peaks)

    @pl.when(step >= edge)
    def _():
        sums[...] = jnp.zeros_like(sums)
        sweep(jobs_on((pairs, pairs), (edge, edge)), (fresh_peaks(heads), fresh_peaks(heads)))

    for side in range(2):
        parts = []
        for head in range(heads):
            row = head * HEAD_ROWS
            parts.append(
                sums[side, row : row + HEAD_DIM, :]
                / sums[side, row + HEAD_DIM : row + HEAD_DIM + 1, :]
            )
        tile_rows = pl.ds(pl.multiple_of(places[side] * TILE, TILE), TILE)
        mixed[tile_rows, :] = jnp.concatenate(parts, axis=0).T.astype(jnp.bfloat16)

    @pl.when(step == pl.num_programs(0) - 1)
    def _():
        count = outs[0].shape[0]
        for distance, out in enumerate(outs):
            out[...] = mixed[pl.ds(pl.multiple_of((meta[0] ^ distance) * count, 128), count), :]


def tile_places(step, edge, tiles):
    middle = edge + 2 * (step - edge)
    return (
        jnp.where(step < edge, step, middle),
        jnp.where(step < edge, tiles - edge + step, middle + 1),
    )


def attend_specs(width, edge, tiles):
    specs = []
    for side in range(2):
        place = lambda i, side=side: tile_places(i, edge, tiles)[side]
        specs.append(pl.BlockSpec((TILE, width), lambda i, m, r, place=place: (place(i), 0)))
        specs += [pl.BlockSpec((1, TILE), lambda i, m, r, place=place: (0, place(i)))] * 2
    return specs + [pl.BlockSpec((tiles * TILE, 2 * width), lambda i, m, r: (0, 0))]


def attend_edges(meta, ranges, queries, starts, ends, pairs):
    group_rows, width = queries.shape
    heads = width // HEAD_DIM
    tiles, edge = group_rows // TILE, SPAN // TILE
    shapes = [(edge, heads * HEAD_ROWS, TILE)] * 2 + [(edge, 8, TILE)] * 2
    return pl.pallas_call(
        edge_kernel,
        grid_spec=pltpu.PrefetchScalarGridSpec(
            num_scalar_prefetch=2,
            grid=(edge,),
            in_specs=attend_specs(width, edge, tiles),
            out_specs=[pl.BlockSpec((1,) + shape[1:], lambda i, m, r: (i, 0, 0)) for shape in shapes],
            scratch_shapes=[
                pltpu.VMEM((2, heads, width, TILE), jnp.bfloat16),
                pltpu.VMEM((heads * HEAD_ROWS, group_rows), jnp.bfloat16),
            ],
        ),
        out_shape=[jax.ShapeDtypeStruct(shape, jnp.float32) for shape in shapes],
        compiler_params=PARAMS,
        cost_estimate=pl.CostEstimate(
            flops=16 * group_rows * 1024 * width,
            bytes_accessed=5 << 20,
            transcendentals=group_rows * 1024 * heads,
        ),
        name="attend_edges",
    )(meta, ranges, queries, starts, ends, queries, starts, ends, pairs)


def attend_finish(meta, ranges, queries, starts, ends, pairs, before, after, held, rows):
    group_rows, width = queries.shape
    heads = width // HEAD_DIM
    tiles, edge = group_rows // TILE, SPAN // TILE
    members = group_rows // rows
    return pl.pallas_call(
        functools.partial(finish_kernel, edge),
        grid_spec=pltpu.PrefetchScalarGridSpec(
            num_scalar_prefetch=2,
            grid=(edge + (tiles - 2 * edge) // 2,),
            in_specs=attend_specs(width, edge, tiles)
            + [pl.BlockSpec((SPAN, 2 * width), lambda i, m, r: (0, 0))] * 2
            + [
                pl.BlockSpec((1,) + part.shape[1:], lambda i, m, r: (jnp.minimum(i, edge - 1), 0, 0))
                for part in held
            ],
            out_specs=[pl.BlockSpec((rows, width), lambda i, m, r: (0, 0))] * members,
            scratch_shapes=[
                pltpu.VMEM((2, heads, width, TILE), jnp.bfloat16),
                pltpu.VMEM((2, heads * HEAD_ROWS, TILE), jnp.float32),
                pltpu.VMEM((group_rows, width), jnp.bfloat16),
            ],
        ),
        out_shape=[jax.ShapeDtypeStruct((rows, width), jnp.bfloat16)] * members,
        compiler_params=PARAMS,
        cost_estimate=pl.CostEstimate(
            flops=16 * group_rows * 1024 * width,
            bytes_accessed=5 << 20,
            transcendentals=group_rows * 1024 * heads,
        ),
        name="attend_finish",
    )(meta, ranges, queries, starts, ends, queries, starts, ends, pairs, before, after, *held)


def output_kernel(members, meta, *refs):
    parts, weights, result, mixed = refs[:members], refs[members:-2], refs[-2], refs[-1]
    width = parts[0].shape[1]
    tile = weights[0].shape[1]
    for distance in range(members):
        source = meta[0] ^ distance
        head_pair = PAIR * (source % (members // PAIR)) + source // (members // PAIR)
        columns = pl.ds(pl.multiple_of((head_pair ^ meta[1]) * width, width), width)
        mixed[:, columns] = parts[distance][...]
    for distance, weight in enumerate(weights):
        columns = pl.ds(pl.multiple_of((meta[0] % len(weights) ^ distance) * tile, tile), tile)
        result[:, columns] = jnp.dot(
            mixed[...], weight[...], preferred_element_type=jnp.float32
        ).astype(jnp.bfloat16)


def output_projection(meta, parts, weights):
    rows, width = parts[0].shape
    depth, tile = weights[0].shape
    whole = lambda shape: pl.BlockSpec(shape, lambda i, m: (0, 0))
    return pl.pallas_call(
        functools.partial(output_kernel, len(parts)),
        grid_spec=pltpu.PrefetchScalarGridSpec(
            num_scalar_prefetch=1,
            grid=(1,),
            in_specs=[whole(parts[0].shape)] * len(parts) + [whole((depth, tile))] * len(weights),
            out_specs=whole((rows, len(weights) * tile)),
            scratch_shapes=[pltpu.VMEM((rows, depth), jnp.bfloat16)],
        ),
        out_shape=jax.ShapeDtypeStruct((rows, len(weights) * tile), jnp.bfloat16),
        compiler_params=PARAMS,
        cost_estimate=pl.CostEstimate(
            flops=2 * rows * depth * len(weights) * tile,
            bytes_accessed=4 << 20,
            transcendentals=0,
        ),
        name="output_projection",
    )(meta, *parts, *weights)


def unpack_kernel(own_row, other_row, pages):
    _, pair, members, capacity, part = own_row.shape
    width = part // (2 * PAGE)
    for source in range(pair):
        for low in range(pair):
            received = own_row if source == low else other_row
            for high in range(members):
                for turn in range(2 * PAGE):
                    start = (turn * pair * members + PAIR * high + low) * width
                    pages[source, :, start : start + width] = received[
                        0, low, high, :, turn * width : (turn + 1) * width
                    ]


def unpack(own_row, other_row):
    planes, pair, members, capacity, part = own_row.shape
    block = pl.BlockSpec((1,) + own_row.shape[1:], lambda i: (i, 0, 0, 0, 0))
    return pl.pallas_call(
        unpack_kernel,
        grid=(planes,),
        in_specs=[block, block],
        out_specs=pl.BlockSpec((pair, capacity, pair * members * part), lambda i: (i, 0, 0)),
        out_shape=jax.ShapeDtypeStruct(
            (planes * pair, capacity, pair * members * part), jnp.bfloat16
        ),
        compiler_params=pltpu.CompilerParams(vmem_limit_bytes=24 * 1024 * 1024),
        cost_estimate=pl.CostEstimate(flops=0, bytes_accessed=6 << 20, transcendentals=0),
        name="unpack",
    )(own_row, other_row)


def rope_tables(positions):
    half_dim = HEAD_DIM // 2
    inverse = 1.0 / ROPE_BASE ** (jnp.arange(half_dim, dtype=jnp.float32) * 2.0 / HEAD_DIM)
    angles = inverse[:, None] * positions.astype(jnp.float32)[None, :]
    return jnp.cos(angles), jnp.sin(angles)


def bounds_kernel(ids, starts, ends, ranges):
    shape = (8, ids.shape[1])
    width = ids.shape[1]
    own = jnp.broadcast_to(ids[...], shape)
    index = lax.broadcasted_iota(jnp.int32, shape, 1)
    first = jnp.where((own != pltpu.roll(own, 1, 1)) | (index == 0), index, 0)
    after = jnp.where((own != pltpu.roll(own, width - 1, 1)) | (index == width - 1), index + 1, width)
    shift = 1
    while shift < SPAN:
        first = jnp.maximum(first, jnp.where(index >= shift, pltpu.roll(first, shift, 1), 0))
        after = jnp.minimum(
            after, jnp.where(index < width - shift, pltpu.roll(after, width - shift, 1), width)
        )
        shift *= 2
    rows = starts.shape[1]
    starts[...] = first[:1, SPAN : SPAN + rows]
    ends[...] = after[:1, SPAN : SPAN + rows]
    lane = lax.broadcasted_iota(jnp.int32, (rows, ranges.shape[1]), 0)
    entry = lax.broadcasted_iota(jnp.int32, (rows, ranges.shape[1]), 1)
    own_lane = entry // 2 * TILE + lax.rem(entry, 2) * (TILE - 1)
    chosen = jnp.where(lane == own_lane, 1.0, 0.0)
    odd = lax.rem(entry, 2) == 1
    begin = (first[:, SPAN : SPAN + rows] // TILE).astype(jnp.bfloat16)
    end = ((after[:, SPAN : SPAN + rows] + TILE - 1) // TILE).astype(jnp.bfloat16)
    from_begin = jnp.where(odd, 0.0, chosen).astype(jnp.bfloat16)
    from_end = jnp.where(odd, chosen, 0.0).astype(jnp.bfloat16)
    found = jnp.dot(begin, from_begin, preferred_element_type=jnp.float32) + jnp.dot(
        end, from_end, preferred_element_type=jnp.float32
    )
    ranges[...] = found[:1].astype(jnp.int32)


def document_bounds(window_ids, rows):
    return pl.pallas_call(
        bounds_kernel,
        out_shape=[jax.ShapeDtypeStruct((1, rows), jnp.int32)] * 2
        + [jax.ShapeDtypeStruct((1, 128), jnp.int32)],
        compiler_params=PARAMS,
        cost_estimate=pl.CostEstimate(flops=1 << 34, bytes_accessed=0, transcendentals=0),
        name="document_bounds",
    )(window_ids[None, :])


def per_device(tokens, norm_gain, input_weight, output_weight, segment_ids, page_owner):
    rows, model_width = tokens.shape
    peers, members = lax.axis_size("tok"), lax.axis_size("grp")
    place, column = lax.axis_index("tok"), lax.axis_index("grp")
    low = place % PAIR
    blocks = PAIR * members
    member = low * members + column
    group_rows = rows * blocks
    width = model_width // blocks
    pages = rows // PAGE

    flat = peers * members
    owners = page_owner[:, 0]
    capacity = max(2, (2 * pages + peers - 1) // peers)
    halves = []
    for parity in range(PAIR):
        pieces = []
        for number in range(PARTS):
            start = number * PAIR * width
            choices = [input_weight[:, start : start + width], input_weight[:, start + width : start + 2 * width]]
            piece = jnp.where((low ^ parity) == 0, choices[0], choices[1])
            route = []
            for source in range(flat):
                row, column_from = divmod(source, members)
                target = (row ^ parity) * members + (PARTS * column_from + number) % members
                route.append((source, target))
            pieces.append(lax.ppermute(piece, ("tok", "grp"), route))
        pieces.append(flipped(output_weight, "tok", 1) if parity else output_weight)
        halves.append(jnp.concatenate(pieces, axis=1))
    plane = jnp.concatenate(halves, axis=0)
    own = layer_norm(tokens, norm_gain[None, :], owners, capacity)
    own, plane = lax.optimization_barrier((own, plane))

    across, along = flipped(own, "grp", 2), flipped(own, "tok", 1)
    sibling = flipped(own, "grp", 1)
    planes = {0: plane}
    bit = peers // 2
    while bit > 1:
        planes[bit] = flipped(plane, "tok", bit)
        bit //= 2
    for distance in range(PAIR, peers, PAIR):
        if distance not in planes:
            step_bit = distance & -distance
            planes[distance] = flipped(planes[distance ^ step_bit], "tok", step_bit)
    weights = [planes[distance] for distance in range(0, peers, PAIR)]

    first_row = place // PAIR * group_rows
    padded_ids = jnp.concatenate(
        [
            jnp.full((SPAN,), -1, jnp.int32),
            segment_ids,
            jnp.full((SPAN,), 1 << 30, jnp.int32),
        ]
    )
    window_ids = lax.dynamic_slice_in_dim(padded_ids, first_row, group_rows + 2 * SPAN, 0)
    window_ids, plane = lax.optimization_barrier((window_ids, plane))
    *bounds, ranges = document_bounds(window_ids, group_rows)
    positions = SPAN + jnp.arange(group_rows, dtype=jnp.int32) - bounds[0][0]
    order = [(number * members + column) % PARTS for number in range(PARTS)]
    meta = jnp.stack([member, place] + order).astype(jnp.int32)
    cosine, sine = rope_tables(positions)
    across, along, sibling, weights, cosine, sine, meta = lax.optimization_barrier(
        (across, along, sibling, weights, cosine, sine, meta)
    )

    half, held = rows // 2, rows + EXTRA_ROWS
    corner = [flipped(across[:half], "tok", 1), flipped(along[half:], "grp", 2)]
    across_sibling = flipped(across, "grp", 1)
    along_sibling = flipped(along, "grp", 1)
    near_blocks = [own, sibling, across, across_sibling]
    near_layout = [[(number, 0, held)] for number in range(4)]
    far_layout = [[(0, 0, held)], [(1, 0, held)]]
    far_layout += [[(number, 0, half), (number + 1, half, held - half)] for number in (2, 4)]

    sizes = (weights, cosine, sine, rows, blocks, peers, capacity)

    def to_owners(send):
        received = lax.all_to_all(
            send.reshape((flat,) + send.shape[2:]),
            ("tok", "grp"),
            split_axis=0,
            concat_axis=0,
            tiled=True,
        )
        return received.reshape((peers // PAIR, PAIR, members) + send.shape[2:])

    queries, pairs, send = project(meta, 0, near_layout, near_blocks, *sizes, ())
    send, corner, along_sibling = lax.optimization_barrier((send, corner, along_sibling))
    own_row = to_owners(send)
    corner_sibling = [flipped(block, "grp", 1) for block in corner]
    far_blocks = [along, along_sibling] + corner + corner_sibling
    columns = jnp.concatenate([held_rows[:, PARTS * width :] for held_rows in weights], axis=0)
    row_order = place
    if output_weight.shape[0] != width:
        shards = columns.reshape((peers,) + output_weight.shape)
        columns = shards[jnp.arange(peers) ^ place].reshape(columns.shape)
        row_order = jnp.zeros_like(place)
    queries, pairs, send = project(meta, 4, far_layout, far_blocks, *sizes, (queries, pairs))
    before = shifted(pairs[group_rows - SPAN :], "tok", PAIR)
    after = shifted(pairs[:SPAN], "tok", -PAIR)
    columns_across = flipped(columns, "grp", 2)

    edges = attend_edges(meta, ranges, queries, *bounds, pairs)
    send, edges = lax.optimization_barrier((send, edges))
    other_row = to_owners(send)
    before, after, edges, columns_across = lax.optimization_barrier(
        (before, after, edges, columns_across)
    )
    mixed = attend_finish(meta, ranges, queries, *bounds, pairs, before, after, edges, rows)
    last_weights = [columns, flipped(columns, "grp", 1)]
    last_weights += [columns_across, flipped(columns_across, "grp", 1)]
    parts = [mixed[0]] + [
        lax.ppermute(
            mixed[distance],
            ("tok", "grp"),
            [(source, source ^ distance) for source in range(flat)],
        )
        for distance in range(1, blocks)
    ]
    cache_pages = unpack(own_row, other_row).reshape(
        peers * capacity, 2 * PAGE * model_width
    )
    parts, cache_pages = lax.optimization_barrier((parts, cache_pages))
    output_meta = jnp.stack([member, row_order]).astype(jnp.int32)
    attended = output_projection(output_meta, parts, last_weights)
    return attended, cache_pages


def solution(mesh):
    placed = (
        P(("tok", "grp"), None),
        P(),
        P("tok", "grp"),
        P("tok", "grp"),
        P(),
        P(("tok", "grp"), None),
    )
    return jax.shard_map(
        per_device,
        mesh=mesh,
        in_specs=placed,
        out_specs=(P(("tok", "grp"), None), P(("tok", "grp"), None)),
        check_vma=False,
    )
```

```python
import functools
import math

import jax
import jax.numpy as jnp
from jax import lax
from jax.experimental import pallas as pl
from jax.experimental.pallas import tpu as pltpu
from jax.sharding import PartitionSpec as P

H = 16
SPAN = 1024
PAGE = 4
HEAD_DIM = 64

NEG_FILL = -1e30
ROPE_BASE = 160000.0
EPSILON = 1e-05
TILE = 256
PARTS = 3
PAIR = 2
ONES_ROWS = 16
HEAD_ROWS = HEAD_DIM + ONES_ROWS
EXTRA_ROWS = 16
KEYS = 512
SCALE = HEAD_DIM ** (-0.5) * math.log2(math.e)
VMEM_LIMIT = 60 * 1024 * 1024
PARAMS = pltpu.CompilerParams(vmem_limit_bytes=VMEM_LIMIT)


def flipped(value, axis, bit):
    count = lax.axis_size(axis)
    return lax.ppermute(value, axis, [(source, source ^ bit) for source in range(count)])


def shifted(value, axis, steps):
    count = lax.axis_size(axis)
    initial, last = (max(0, -steps), min(count, count - steps))
    return lax.ppermute(value, axis, [(source, source + steps) for source in range(initial, last)])


def norm_kernel(capacity, tokens, gain, owner_row, normed, owners):
    rows = tokens.shape[0]
    values = tokens[...].astype(jnp.float32)
    centred = values - jnp.mean(values, axis=-1, keepdims=True)
    spread = jnp.mean(jnp.square(centred), axis=-1, keepdims=True)
    normed[:rows, :] = (centred * lax.rsqrt(spread + EPSILON) * gain[...]).astype(jnp.bfloat16)
    pages = owner_row.shape[1]
    owners[...] = jnp.full(owners.shape, -1.0, jnp.float32)
    owners[:1, :pages] = owner_row[...].astype(jnp.float32)
    lanes = owners.shape[1]
    across = jnp.broadcast_to(owners[:1, :], (lanes, lanes))
    earlier = lax.broadcasted_iota(jnp.int32, (lanes, lanes), 0) < lax.broadcasted_iota(
        jnp.int32, (lanes, lanes), 1
    )
    same = (across.T == across) & earlier
    ranks = jnp.sum(jnp.where(same, 1.0, 0.0), axis=0, keepdims=True)
    slots = owners[:1, :] * capacity + ranks
    normed[rows:, :] = jnp.zeros((EXTRA_ROWS, normed.shape[1]), jnp.bfloat16)
    normed[rows:, :lanes] = jnp.broadcast_to(slots, (EXTRA_ROWS, lanes)).astype(jnp.bfloat16)


def layer_norm(tokens, gain, owners, capacity):
    rows, width = tokens.shape
    lanes = -(-owners.shape[0] // 128) * 128
    return pl.pallas_call(
        functools.partial(norm_kernel, capacity),
        out_shape=jax.ShapeDtypeStruct((rows + EXTRA_ROWS, width), jnp.bfloat16),
        scratch_shapes=[pltpu.VMEM((8, lanes), jnp.float32)],
        compiler_params=PARAMS,
        name="layer_norm",
    )(tokens, gain, owners[None, :])


def project_kernel(first, layout, weight_count, peers, capacity, meta, *refs):
    operands = 1 + max(entry[0] for pieces in layout for entry in pieces)
    tokens = refs[:operands]
    weights = refs[operands : operands + weight_count]
    cosine, sine = refs[operands + weight_count : operands + weight_count + 2]
    query_out, pair_out, send_out, blocks, weight, page_source, sems = refs[-7:]
    step = pl.program_id(0)
    steps = len(layout)
    rows = query_out.shape[0]
    width = query_out.shape[1]
    shard = weights[0].shape[0] // 2

    def arrivals(number):
        return [
            pltpu.make_async_copy(
                tokens[operand],
                blocks.at[number, pl.ds(offset, count), :],
                sems.at[number, place],
            )
            for place, (operand, offset, count) in enumerate(layout[number])
        ]

    @pl.when(step == 0)
    def _():
        for number in range(steps):
            for copy in arrivals(number):
                copy.start()
        for plane in range(weight_count):
            for low in range(2):
                row = pl.multiple_of((meta[1] ^ (2 * plane + low)) * shard, shard)
                for number in range(PARTS):
                    column = pl.multiple_of(meta[2 + number] * width, width)
                    weight[pl.ds(row, shard), number * width : (number + 1) * width] = weights[
                        plane
                    ][low * shard : (low + 1) * shard, pl.ds(column, width)]

    for number in range(steps):

        @pl.when(step == number)
        def _():
            for copy in arrivals(number):
                copy.wait()

    joined = jnp.dot(blocks[step, :rows, :], weight[...], preferred_element_type=jnp.float32)
    cosines = jnp.concatenate([cosine[...]] * 4, axis=0).T
    sines = jnp.concatenate([-sine[...], sine[...]] * 2, axis=0).T
    first_half = lax.rem(lax.broadcasted_iota(jnp.int32, (rows, width), 1), HEAD_DIM) < (
        HEAD_DIM // 2
    )

    def rotate(values):
        partner = jnp.where(
            first_half,
            pltpu.roll(values, width - HEAD_DIM // 2, 1),
            pltpu.roll(values, HEAD_DIM // 2, 1),
        )
        return (values * cosines + partner * sines).astype(jnp.bfloat16)

    query_out[...] = rotate(joined[:, :width])
    keys = rotate(joined[:, width : 2 * width])
    values = joined[:, 2 * width :].astype(jnp.bfloat16)
    pair_out[:, :width] = keys
    pair_out[:, width:] = values
    page_source[0] = keys.astype(jnp.float32)
    page_source[1] = values.astype(jnp.float32)

    pages = rows // PAGE
    slot_count = peers * capacity
    slots = blocks[step, rows : rows + EXTRA_ROWS, :128].astype(jnp.float32)[:1, :pages]
    chosen = (
        lax.broadcasted_iota(jnp.int32, (slot_count, pages), 0).astype(jnp.float32) == slots
    ).astype(jnp.bfloat16)
    for turn in range(PAGE):
        page_part = jnp.concatenate(
            [
                page_source[half, pl.ds(turn, pages, stride=PAGE), :].astype(jnp.bfloat16)
                for half in range(2)
            ],
            axis=1,
        )
        placed = jnp.dot(chosen, page_part, preferred_element_type=jnp.float32)
        columns = slice(turn * 2 * width, (turn + 1) * 2 * width)
        for peer in range(peers):
            send_out[peer, 0, :, columns] = placed[
                peer * capacity : (peer + 1) * capacity
            ].astype(jnp.bfloat16)


def project(meta, first, layout, operands, weights, cosine, sine, rows, blocks, peers, capacity, into):
    steps = len(layout)
    model_width = operands[0].shape[1]
    group_rows = rows * blocks
    width = model_width // blocks
    members = blocks // PAIR
    whole = lambda shape: pl.BlockSpec(shape, lambda i, m: (0,) * len(shape))
    place = lambda i, m: m[0] ^ (first + i)
    table = pl.BlockSpec((HEAD_DIM // 2, rows), lambda i, m: (0, place(i, m)))
    send_shape = (peers, members, capacity, 2 * PAGE * width)
    return pl.pallas_call(
        functools.partial(project_kernel, first, layout, len(weights), peers, capacity),
        grid_spec=pltpu.PrefetchScalarGridSpec(
            num_scalar_prefetch=1,
            grid=(steps,),
            in_specs=[pl.BlockSpec(memory_space=pl.ANY)] * len(operands)
            + [whole(weights[0].shape)] * len(weights)
            + [table, table]
            + [pl.BlockSpec(memory_space=pl.ANY)] * len(into),
            out_specs=[
                pl.BlockSpec((rows, width), lambda i, m: (place(i, m), 0)),
                pl.BlockSpec((rows, 2 * width), lambda i, m: (place(i, m), 0)),
                pl.BlockSpec(
                    (peers, 1) + send_shape[2:], lambda i, m: (0, place(i, m) % members, 0, 0)
                ),
            ],
            scratch_shapes=[
                pltpu.VMEM((steps, rows + EXTRA_ROWS, model_width), jnp.bfloat16),
                pltpu.VMEM((model_width, PARTS * width), jnp.bfloat16),
                pltpu.VMEM((2, rows, width), jnp.float32),
                pltpu.SemaphoreType.DMA((steps, 2)),
            ],
        ),
        out_shape=[
            jax.ShapeDtypeStruct((group_rows, width), jnp.bfloat16),
            jax.ShapeDtypeStruct((group_rows, 2 * width), jnp.bfloat16),
            jax.ShapeDtypeStruct(send_shape, jnp.bfloat16),
        ],
        input_output_aliases={
            1 + len(operands) + len(weights) + 2 + number: number for number in range(len(into))
        },
        compiler_params=PARAMS,
        cost_estimate=pl.CostEstimate(
            flops=16 * steps * rows * model_width * PARTS * width,
            bytes_accessed=(3 * steps) << 19,
            transcendentals=0,
        ),
        name="project",
    )(meta, *operands, *weights, cosine, sine, *into)


def mask_heads(queries, masked):
    turned = queries[...].T
    head_of_row = lax.broadcasted_iota(jnp.int32, turned.shape, 0) // HEAD_DIM
    for head in range(masked.shape[0]):
        masked[head] = jnp.where(head_of_row == head, turned, jnp.zeros((), jnp.bfloat16))


def with_ones(values):
    turned = values.T
    ones = jnp.ones((ONES_ROWS, values.shape[0]), values.dtype)
    rows = []
    for head in range(values.shape[1] // HEAD_DIM):
        rows += [turned[head * HEAD_DIM : (head + 1) * HEAD_DIM], ones]
    return jnp.concatenate(rows, axis=0)


def sweep(jobs, peaks):
    plans = []
    steps = 0
    for begin, end, base, pairs, values_of, masked, starts, ends, total in jobs:
        held = pairs.shape[0] // TILE
        begin, end = jnp.maximum(begin, base), jnp.minimum(end, base + held)
        last = jnp.minimum(ends, end * TILE)
        steps = jnp.maximum(steps, (end - begin + KEYS // TILE - 1) // (KEYS // TILE))
        plans.append((begin, base, held, pairs, values_of, masked, starts, last, total))

    def one(number, peaks):
        new_peaks = []
        for plan, old_peaks in zip(plans, peaks):
            begin, base, held, pairs, values_of, masked, starts, last, total = plan
            wanted = begin + number * (KEYS // TILE)
            block = jnp.minimum(wanted, base + held - KEYS // TILE)
            row = pl.multiple_of((block - base) * TILE, TILE)
            keys = pairs[pl.ds(row, KEYS), : pairs.shape[1] // 2]
            values = values_of(row)
            index = block * TILE + lax.broadcasted_iota(jnp.int32, (KEYS, TILE), 0)
            allowed = (index >= jnp.maximum(starts, wanted * TILE)) & (index < last)
            job_peaks = []
            for head, old_peak in enumerate(old_peaks):
                scores = jnp.dot(keys, masked[head], preferred_element_type=jnp.float32)
                scores = jnp.where(allowed, scores * SCALE, NEG_FILL)
                peak = jnp.maximum(old_peak, jnp.max(scores, axis=0, keepdims=True))
                fade = jnp.exp2(old_peak - peak)
                weights = jnp.exp2(scores - peak).astype(jnp.bfloat16)
                own = slice(head * HEAD_ROWS, (head + 1) * HEAD_ROWS)
                total[own, :] = total[own, :] * fade + jnp.dot(
                    values[own, :], weights, preferred_element_type=jnp.float32
                )
                job_peaks.append(peak)
            new_peaks.append(tuple(job_peaks))
        return tuple(new_peaks)

    return lax.fori_loop(0, steps, one, peaks)


def fresh_peaks(heads):
    return tuple(jnp.full((1, TILE), NEG_FILL, jnp.float32) for _ in range(heads))


def edge_kernel(meta, ranges, *refs):
    rows, pairs, outs, (masked, values) = refs[:6], refs[6], refs[7:11], refs[11:]
    step = pl.program_id(0)
    width = rows[0].shape[1]
    heads = width // HEAD_DIM
    edge = pl.num_programs(0)
    tiles = pairs.shape[0] // TILE

    @pl.when(step == 0)
    def _():
        for number in range(tiles):
            own = slice(number * TILE, (number + 1) * TILE)
            values[:, own] = with_ones(pairs[own, width:])

    jobs = []
    for side in range(2):
        tile = step + side * (tiles - edge)
        queries, starts, ends = rows[3 * side : 3 * side + 3]
        mask_heads(queries, masked.at[side])
        total = outs[side]
        total[...] = jnp.zeros_like(total)
        jobs.append(
            (
                ranges[0, 2 * tile],
                ranges[0, 2 * tile + 1],
                edge,
                pairs,
                lambda row: values[:, pl.ds(row, KEYS)],
                masked.at[side],
                starts[...],
                ends[...],
                total.at[0],
            )
        )
    peaks = sweep(jobs, (fresh_peaks(heads), fresh_peaks(heads)))
    for side in range(2):
        for head in range(heads):
            outs[2 + side][0, head : head + 1, :] = peaks[side][head]


def finish_kernel(edge, meta, ranges, *refs):
    rows, pairs, halos, held, held_peaks = refs[:6], refs[6], refs[7:9], refs[9:11], refs[11:13]
    outs, (masked, sums, mixed) = refs[13:-3], refs[-3:]
    step = pl.program_id(0)
    width = rows[0].shape[1]
    heads = width // HEAD_DIM
    tiles = pairs.shape[0] // TILE
    places = tile_places(step, edge, tiles)

    def jobs_on(keys, bases):
        jobs = []
        for side in range(2):
            queries, starts, ends = rows[3 * side : 3 * side + 3]
            mask_heads(queries, masked.at[side])
            jobs.append(
                (
                    ranges[0, 2 * places[side]],
                    ranges[0, 2 * places[side] + 1],
                    bases[side],
                    keys[side],
                    lambda row, held=keys[side]: with_ones(held[pl.ds(row, KEYS), width:]),
                    masked.at[side],
                    starts[...],
                    ends[...],
                    sums.at[side],
                )
            )
        return jobs

    @pl.when(step < edge)
    def _():
        for side in range(2):
            sums[side] = held[side][0]

    reaches_back = ranges[0, 2 * places[0]] < edge
    reaches_ahead = ranges[0, 2 * places[1] + 1] > edge + tiles

    @pl.when((step < edge) & (reaches_back | reaches_ahead))
    def _():
        peaks = tuple(
            tuple(held_peaks[side][0, head : head + 1, :] for head in range(heads))
            for side in range(2)
        )
        sweep(jobs_on(halos, (0, edge + tiles)), peaks)

    @pl.when(step >= edge)
    def _():
        sums[...] = jnp.zeros_like(sums)
        sweep(jobs_on((pairs, pairs), (edge, edge)), (fresh_peaks(heads), fresh_peaks(heads)))

    for side in range(2):
        parts = []
        for head in range(heads):
            row = head * HEAD_ROWS
            parts.append(
                sums[side, row : row + HEAD_DIM, :]
                / sums[side, row + HEAD_DIM : row + HEAD_DIM + 1, :]
            )
        tile_rows = pl.ds(pl.multiple_of(places[side] * TILE, TILE), TILE)
        mixed[tile_rows, :] = jnp.concatenate(parts, axis=0).T.astype(jnp.bfloat16)

    @pl.when(step == pl.num_programs(0) - 1)
    def _():
        count = outs[0].shape[0]
        for distance, out in enumerate(outs):
            out[...] = mixed[pl.ds(pl.multiple_of((meta[0] ^ distance) * count, 128), count), :]


def tile_places(step, edge, tiles):
    middle = edge + 2 * (step - edge)
    return (
        jnp.where(step < edge, step, middle),
        jnp.where(step < edge, tiles - edge + step, middle + 1),
    )


def attend_specs(width, edge, tiles):
    specs = []
    for side in range(2):
        place = lambda i, side=side: tile_places(i, edge, tiles)[side]
        specs.append(pl.BlockSpec((TILE, width), lambda i, m, r, place=place: (place(i), 0)))
        specs += [pl.BlockSpec((1, TILE), lambda i, m, r, place=place: (0, place(i)))] * 2
    return specs + [pl.BlockSpec((tiles * TILE, 2 * width), lambda i, m, r: (0, 0))]


def attend_edges(meta, ranges, queries, starts, ends, pairs):
    group_rows, width = queries.shape
    heads = width // HEAD_DIM
    tiles, edge = group_rows // TILE, SPAN // TILE
    shapes = [(edge, heads * HEAD_ROWS, TILE)] * 2 + [(edge, 8, TILE)] * 2
    return pl.pallas_call(
        edge_kernel,
        grid_spec=pltpu.PrefetchScalarGridSpec(
            num_scalar_prefetch=2,
            grid=(edge,),
            in_specs=attend_specs(width, edge, tiles),
            out_specs=[pl.BlockSpec((1,) + shape[1:], lambda i, m, r: (i, 0, 0)) for shape in shapes],
            scratch_shapes=[
                pltpu.VMEM((2, heads, width, TILE), jnp.bfloat16),
                pltpu.VMEM((heads * HEAD_ROWS, group_rows), jnp.bfloat16),
            ],
        ),
        out_shape=[jax.ShapeDtypeStruct(shape, jnp.float32) for shape in shapes],
        compiler_params=PARAMS,
        cost_estimate=pl.CostEstimate(
            flops=1 << 35,
            bytes_accessed=5 << 20,
            transcendentals=group_rows * 1024 * heads,
        ),
        name="attend_edges",
    )(meta, ranges, queries, starts, ends, queries, starts, ends, pairs)


def attend_finish(meta, ranges, queries, starts, ends, pairs, before, after, held, rows):
    group_rows, width = queries.shape
    heads = width // HEAD_DIM
    tiles, edge = group_rows // TILE, SPAN // TILE
    members = group_rows // rows
    return pl.pallas_call(
        functools.partial(finish_kernel, edge),
        grid_spec=pltpu.PrefetchScalarGridSpec(
            num_scalar_prefetch=2,
            grid=(edge + (tiles - 2 * edge) // 2,),
            in_specs=attend_specs(width, edge, tiles)
            + [pl.BlockSpec((SPAN, 2 * width), lambda i, m, r: (0, 0))] * 2
            + [
                pl.BlockSpec((1,) + part.shape[1:], lambda i, m, r: (jnp.minimum(i, edge - 1), 0, 0))
                for part in held
            ],
            out_specs=[pl.BlockSpec((rows, width), lambda i, m, r: (0, 0))] * members,
            scratch_shapes=[
                pltpu.VMEM((2, heads, width, TILE), jnp.bfloat16),
                pltpu.VMEM((2, heads * HEAD_ROWS, TILE), jnp.float32),
                pltpu.VMEM((group_rows, width), jnp.bfloat16),
            ],
        ),
        out_shape=[jax.ShapeDtypeStruct((rows, width), jnp.bfloat16)] * members,
        compiler_params=PARAMS,
        cost_estimate=pl.CostEstimate(
            flops=1 << 37,
            bytes_accessed=5 << 20,
            transcendentals=group_rows * 1024 * heads,
        ),
        name="attend_finish",
    )(meta, ranges, queries, starts, ends, queries, starts, ends, pairs, before, after, *held)


def output_kernel(members, meta, *refs):
    parts, weights, result, mixed = refs[:members], refs[members:-2], refs[-2], refs[-1]
    width = parts[0].shape[1]
    tile = weights[0].shape[1]
    for distance in range(members):
        source = meta[0] ^ distance
        head_pair = PAIR * (source % (members // PAIR)) + source // (members // PAIR)
        columns = pl.ds(pl.multiple_of((head_pair ^ meta[1]) * width, width), width)
        mixed[:, columns] = parts[distance][...]
    for distance, weight in enumerate(weights):
        columns = pl.ds(pl.multiple_of((meta[0] % len(weights) ^ distance) * tile, tile), tile)
        result[:, columns] = jnp.dot(
            mixed[...], weight[...], preferred_element_type=jnp.float32
        ).astype(jnp.bfloat16)


def output_projection(meta, parts, weights):
    rows, width = parts[0].shape
    depth, tile = weights[0].shape
    whole = lambda shape: pl.BlockSpec(shape, lambda i, m: (0, 0))
    return pl.pallas_call(
        functools.partial(output_kernel, len(parts)),
        grid_spec=pltpu.PrefetchScalarGridSpec(
            num_scalar_prefetch=1,
            grid=(1,),
            in_specs=[whole(parts[0].shape)] * len(parts) + [whole((depth, tile))] * len(weights),
            out_specs=whole((rows, len(weights) * tile)),
            scratch_shapes=[pltpu.VMEM((rows, depth), jnp.bfloat16)],
        ),
        out_shape=jax.ShapeDtypeStruct((rows, len(weights) * tile), jnp.bfloat16),
        compiler_params=PARAMS,
        cost_estimate=pl.CostEstimate(
            flops=2 * rows * depth * len(weights) * tile,
            bytes_accessed=4 << 20,
            transcendentals=0,
        ),
        name="output_projection",
    )(meta, *parts, *weights)


def unpack_kernel(own_row, other_row, pages):
    _, pair, members, capacity, part = own_row.shape
    width = part // (2 * PAGE)
    for source in range(pair):
        for low in range(pair):
            received = own_row if source == low else other_row
            for high in range(members):
                for turn in range(2 * PAGE):
                    start = (turn * pair * members + PAIR * high + low) * width
                    pages[source, :, start : start + width] = received[
                        0, low, high, :, turn * width : (turn + 1) * width
                    ]


def unpack(own_row, other_row):
    planes, pair, members, capacity, part = own_row.shape
    block = pl.BlockSpec((1,) + own_row.shape[1:], lambda i: (i, 0, 0, 0, 0))
    return pl.pallas_call(
        unpack_kernel,
        grid=(planes,),
        in_specs=[block, block],
        out_specs=pl.BlockSpec((pair, capacity, pair * members * part), lambda i: (i, 0, 0)),
        out_shape=jax.ShapeDtypeStruct(
            (planes * pair, capacity, pair * members * part), jnp.bfloat16
        ),
        compiler_params=pltpu.CompilerParams(vmem_limit_bytes=24 * 1024 * 1024),
        cost_estimate=pl.CostEstimate(flops=0, bytes_accessed=6 << 20, transcendentals=0),
        name="unpack",
    )(own_row, other_row)


def rope_tables(positions):
    half_dim = HEAD_DIM // 2
    inverse = 1.0 / ROPE_BASE ** (jnp.arange(half_dim, dtype=jnp.float32) * 2.0 / HEAD_DIM)
    angles = inverse[:, None] * positions.astype(jnp.float32)[None, :]
    return jnp.cos(angles), jnp.sin(angles)


def bounds_kernel(ids, starts, ends, ranges):
    shape = (8, ids.shape[1])
    width = ids.shape[1]
    own = jnp.broadcast_to(ids[...], shape)
    index = lax.broadcasted_iota(jnp.int32, shape, 1)
    first = jnp.where((own != pltpu.roll(own, 1, 1)) | (index == 0), index, 0)
    after = jnp.where((own != pltpu.roll(own, width - 1, 1)) | (index == width - 1), index + 1, width)
    shift = 1
    while shift < SPAN:
        first = jnp.maximum(first, jnp.where(index >= shift, pltpu.roll(first, shift, 1), 0))
        after = jnp.minimum(
            after, jnp.where(index < width - shift, pltpu.roll(after, width - shift, 1), width)
        )
        shift *= 2
    rows = starts.shape[1]
    starts[...] = first[:1, SPAN : SPAN + rows]
    ends[...] = after[:1, SPAN : SPAN + rows]
    lane = lax.broadcasted_iota(jnp.int32, (rows, ranges.shape[1]), 0)
    entry = lax.broadcasted_iota(jnp.int32, (rows, ranges.shape[1]), 1)
    own_lane = entry // 2 * TILE + lax.rem(entry, 2) * (TILE - 1)
    chosen = jnp.where(lane == own_lane, 1.0, 0.0)
    odd = lax.rem(entry, 2) == 1
    begin = (first[:, SPAN : SPAN + rows] // TILE).astype(jnp.bfloat16)
    end = ((after[:, SPAN : SPAN + rows] + TILE - 1) // TILE).astype(jnp.bfloat16)
    from_begin = jnp.where(odd, 0.0, chosen).astype(jnp.bfloat16)
    from_end = jnp.where(odd, chosen, 0.0).astype(jnp.bfloat16)
    found = jnp.dot(begin, from_begin, preferred_element_type=jnp.float32) + jnp.dot(
        end, from_end, preferred_element_type=jnp.float32
    )
    ranges[...] = found[:1].astype(jnp.int32)


def document_bounds(window_ids, rows):
    return pl.pallas_call(
        bounds_kernel,
        out_shape=[jax.ShapeDtypeStruct((1, rows), jnp.int32)] * 2
        + [jax.ShapeDtypeStruct((1, 128), jnp.int32)],
        compiler_params=PARAMS,
        cost_estimate=pl.CostEstimate(flops=1 << 34, bytes_accessed=0, transcendentals=0),
        name="document_bounds",
    )(window_ids[None, :])


def per_device(tokens, norm_gain, input_weight, output_weight, segment_ids, page_owner):
    rows, model_width = tokens.shape
    peers, members = lax.axis_size("tok"), lax.axis_size("grp")
    place, column = lax.axis_index("tok"), lax.axis_index("grp")
    low = place % PAIR
    blocks = PAIR * members
    member = low * members + column
    group_rows = rows * blocks
    width = model_width // blocks
    pages = rows // PAGE

    flat = peers * members
    owners = page_owner[:, 0]
    capacity = max(2, (2 * pages + peers - 1) // peers)
    halves = []
    for parity in range(PAIR):
        pieces = []
        for number in range(PARTS):
            start = number * PAIR * width
            choices = [input_weight[:, start : start + width], input_weight[:, start + width : start + 2 * width]]
            piece = jnp.where((low ^ parity) == 0, choices[0], choices[1])
            route = []
            for source in range(flat):
                row, column_from = divmod(source, members)
                target = (row ^ parity) * members + (PARTS * column_from + number) % members
                route.append((source, target))
            pieces.append(lax.ppermute(piece, ("tok", "grp"), route))
        halves.append(jnp.concatenate(pieces, axis=1))
    plane = jnp.concatenate(halves, axis=0)
    last_rows = jnp.concatenate([output_weight, flipped(output_weight, "tok", 1)], axis=0)
    own = layer_norm(tokens, norm_gain[None, :], owners, capacity)
    own, plane, last_rows = lax.optimization_barrier((own, plane, last_rows))

    across, along = flipped(own, "grp", 2), flipped(own, "tok", 1)
    sibling = flipped(own, "grp", 1)
    planes = {0: plane}
    bit = peers // 2
    while bit > 1:
        planes[bit] = flipped(plane, "tok", bit)
        bit //= 2
    for distance in range(PAIR, peers, PAIR):
        if distance not in planes:
            step_bit = distance & -distance
            planes[distance] = flipped(planes[distance ^ step_bit], "tok", step_bit)
    weights = [planes[distance] for distance in range(0, peers, PAIR)]

    first_row = place // PAIR * group_rows
    padded_ids = jnp.concatenate(
        [
            jnp.full((SPAN,), -1, jnp.int32),
            segment_ids,
            jnp.full((SPAN,), 1 << 30, jnp.int32),
        ]
    )
    window_ids = lax.dynamic_slice_in_dim(padded_ids, first_row, group_rows + 2 * SPAN, 0)
    window_ids, plane = lax.optimization_barrier((window_ids, plane))
    *bounds, ranges = document_bounds(window_ids, group_rows)
    positions = SPAN + jnp.arange(group_rows, dtype=jnp.int32) - bounds[0][0]
    order = [(number * members + column) % PARTS for number in range(PARTS)]
    meta = jnp.stack([member, place] + order).astype(jnp.int32)
    cosine, sine = rope_tables(positions)
    across, along, sibling, weights, last_rows, cosine, sine, meta = lax.optimization_barrier(
        (across, along, sibling, weights, last_rows, cosine, sine, meta)
    )

    half, held = rows // 2, rows + EXTRA_ROWS
    corner = [flipped(across[:half], "tok", 1), flipped(along[half:], "grp", 2)]
    across_sibling = flipped(across, "grp", 1)
    along_sibling = flipped(along, "grp", 1)
    last_planes = [
        flipped(last_rows, "tok", distance) for distance in range(PAIR, peers, PAIR)
    ]
    near_blocks = [own, sibling, across, across_sibling]
    near_layout = [[(number, 0, held)] for number in range(4)]
    far_layout = [[(0, 0, held)], [(1, 0, held)]]
    far_layout += [[(number, 0, half), (number + 1, half, held - half)] for number in (2, 4)]

    sizes = (weights, cosine, sine, rows, blocks, peers, capacity)

    def to_owners(send):
        received = lax.all_to_all(
            send.reshape((flat,) + send.shape[2:]),
            ("tok", "grp"),
            split_axis=0,
            concat_axis=0,
            tiled=True,
        )
        return received.reshape((peers // PAIR, PAIR, members) + send.shape[2:])

    queries, pairs, send = project(meta, 0, near_layout, near_blocks, *sizes, ())
    send, corner, along_sibling, last_planes = lax.optimization_barrier(
        (send, corner, along_sibling, last_planes)
    )
    own_row = to_owners(send)
    corner_sibling = [flipped(block, "grp", 1) for block in corner]
    far_blocks = [along, along_sibling] + corner + corner_sibling
    columns = jnp.concatenate([last_rows] + last_planes, axis=0)
    row_order = place
    if output_weight.shape[0] != width:
        shards = columns.reshape((peers,) + output_weight.shape)
        columns = shards[jnp.arange(peers) ^ place].reshape(columns.shape)
        row_order = jnp.zeros_like(place)
    queries, pairs, send = project(meta, 4, far_layout, far_blocks, *sizes, (queries, pairs))
    before = shifted(pairs[group_rows - SPAN :], "tok", PAIR)
    after = shifted(pairs[:SPAN], "tok", -PAIR)
    columns_across = flipped(columns, "grp", 2)

    edges = attend_edges(meta, ranges, queries, *bounds, pairs)
    send, edges = lax.optimization_barrier((send, edges))
    other_row = to_owners(send)
    before, after, edges, columns_across = lax.optimization_barrier(
        (before, after, edges, columns_across)
    )
    mixed = attend_finish(meta, ranges, queries, *bounds, pairs, before, after, edges, rows)
    last_weights = [columns, flipped(columns, "grp", 1)]
    last_weights += [columns_across, flipped(columns_across, "grp", 1)]
    parts = [mixed[0]] + [
        lax.ppermute(
            mixed[distance],
            ("tok", "grp"),
            [(source, source ^ distance) for source in range(flat)],
        )
        for distance in range(1, blocks)
    ]
    cache_pages = unpack(own_row, other_row).reshape(
        peers * capacity, 2 * PAGE * model_width
    )
    parts, cache_pages = lax.optimization_barrier((parts, cache_pages))
    output_meta = jnp.stack([member, row_order]).astype(jnp.int32)
    attended = output_projection(output_meta, parts, last_weights)
    return attended, cache_pages


def solution(mesh):
    placed = (
        P(("tok", "grp"), None),
        P(),
        P("tok", "grp"),
        P("tok", "grp"),
        P(),
        P(("tok", "grp"), None),
    )
    return jax.shard_map(
        per_device,
        mesh=mesh,
        in_specs=placed,
        out_specs=(P(("tok", "grp"), None), P(("tok", "grp"), None)),
        check_vma=False,
    )
```

```python
import functools
import math

import jax
import jax.numpy as jnp
from jax import lax
from jax.experimental import pallas as pl
from jax.experimental.pallas import tpu as pltpu
from jax.sharding import PartitionSpec as P

H = 16
SPAN = 1024
PAGE = 4
HEAD_DIM = 64

NEG_FILL = -1e30
ROPE_BASE = 160000.0
EPSILON = 1e-05
TILE = 256
PARTS = 3
PAIR = 2
ONES_ROWS = 16
HEAD_ROWS = HEAD_DIM + ONES_ROWS
EXTRA_ROWS = 16
KEYS = 512
SCALE = HEAD_DIM ** (-0.5) * math.log2(math.e)
VMEM_LIMIT = 60 * 1024 * 1024
PARAMS = pltpu.CompilerParams(vmem_limit_bytes=VMEM_LIMIT)


def flipped(value, axis, bit):
    count = lax.axis_size(axis)
    return lax.ppermute(value, axis, [(source, source ^ bit) for source in range(count)])


def shifted(value, axis, steps):
    count = lax.axis_size(axis)
    initial, last = (max(0, -steps), min(count, count - steps))
    return lax.ppermute(value, axis, [(source, source + steps) for source in range(initial, last)])


def norm_kernel(capacity, tokens, gain, owner_row, normed, owners):
    rows = tokens.shape[0]
    values = tokens[...].astype(jnp.float32)
    centred = values - jnp.mean(values, axis=-1, keepdims=True)
    spread = jnp.mean(jnp.square(centred), axis=-1, keepdims=True)
    normed[:rows, :] = (centred * lax.rsqrt(spread + EPSILON) * gain[...]).astype(jnp.bfloat16)
    pages = owner_row.shape[1]
    owners[...] = jnp.full(owners.shape, -1.0, jnp.float32)
    owners[:1, :pages] = owner_row[...].astype(jnp.float32)
    lanes = owners.shape[1]
    across = jnp.broadcast_to(owners[:1, :], (lanes, lanes))
    earlier = lax.broadcasted_iota(jnp.int32, (lanes, lanes), 0) < lax.broadcasted_iota(
        jnp.int32, (lanes, lanes), 1
    )
    same = (across.T == across) & earlier
    ranks = jnp.sum(jnp.where(same, 1.0, 0.0), axis=0, keepdims=True)
    slots = owners[:1, :] * capacity + ranks
    normed[rows:, :] = jnp.zeros((EXTRA_ROWS, normed.shape[1]), jnp.bfloat16)
    normed[rows:, :lanes] = jnp.broadcast_to(slots, (EXTRA_ROWS, lanes)).astype(jnp.bfloat16)


def layer_norm(tokens, gain, owners, capacity):
    rows, width = tokens.shape
    lanes = -(-owners.shape[0] // 128) * 128
    return pl.pallas_call(
        functools.partial(norm_kernel, capacity),
        out_shape=jax.ShapeDtypeStruct((rows + EXTRA_ROWS, width), jnp.bfloat16),
        scratch_shapes=[pltpu.VMEM((8, lanes), jnp.float32)],
        compiler_params=PARAMS,
        name="layer_norm",
    )(tokens, gain, owners[None, :])


def project_kernel(first, layout, weight_count, peers, capacity, meta, *refs):
    operands = 1 + max(entry[0] for pieces in layout for entry in pieces)
    tokens = refs[:operands]
    weights = refs[operands : operands + weight_count]
    cosine, sine = refs[operands + weight_count : operands + weight_count + 2]
    query_out, pair_out, send_out, blocks, weight, page_source, sems = refs[-7:]
    step = pl.program_id(0)
    steps = len(layout)
    rows = query_out.shape[0]
    width = query_out.shape[1]
    shard = weights[0].shape[0] // 2

    def arrivals(number):
        return [
            pltpu.make_async_copy(
                tokens[operand],
                blocks.at[number, pl.ds(offset, count), :],
                sems.at[number, place],
            )
            for place, (operand, offset, count) in enumerate(layout[number])
        ]

    @pl.when(step == 0)
    def _():
        for number in range(steps):
            for copy in arrivals(number):
                copy.start()
        for plane in range(weight_count):
            for low in range(2):
                row = pl.multiple_of((meta[1] ^ (2 * plane + low)) * shard, shard)
                for number in range(PARTS):
                    column = pl.multiple_of(meta[2 + number] * width, width)
                    weight[pl.ds(row, shard), number * width : (number + 1) * width] = weights[
                        plane
                    ][low * shard : (low + 1) * shard, pl.ds(column, width)]

    for number in range(steps):

        @pl.when(step == number)
        def _():
            for copy in arrivals(number):
                copy.wait()

    joined = jnp.dot(blocks[step, :rows, :], weight[...], preferred_element_type=jnp.float32)
    cosines = jnp.concatenate([cosine[...]] * 4, axis=0).T
    sines = jnp.concatenate([-sine[...], sine[...]] * 2, axis=0).T
    first_half = lax.rem(lax.broadcasted_iota(jnp.int32, (rows, width), 1), HEAD_DIM) < (
        HEAD_DIM // 2
    )

    def rotate(values):
        partner = jnp.where(
            first_half,
            pltpu.roll(values, width - HEAD_DIM // 2, 1),
            pltpu.roll(values, HEAD_DIM // 2, 1),
        )
        return (values * cosines + partner * sines).astype(jnp.bfloat16)

    query_out[...] = rotate(joined[:, :width])
    keys = rotate(joined[:, width : 2 * width])
    values = joined[:, 2 * width :].astype(jnp.bfloat16)
    pair_out[:, :width] = keys
    pair_out[:, width:] = values
    page_source[0] = keys.astype(jnp.float32)
    page_source[1] = values.astype(jnp.float32)

    pages = rows // PAGE
    slot_count = peers * capacity
    slots = blocks[step, rows : rows + EXTRA_ROWS, :128].astype(jnp.float32)[:1, :pages]
    chosen = (
        lax.broadcasted_iota(jnp.int32, (slot_count, pages), 0).astype(jnp.float32) == slots
    ).astype(jnp.bfloat16)
    for turn in range(PAGE):
        page_part = jnp.concatenate(
            [
                page_source[half, pl.ds(turn, pages, stride=PAGE), :].astype(jnp.bfloat16)
                for half in range(2)
            ],
            axis=1,
        )
        placed = jnp.dot(chosen, page_part, preferred_element_type=jnp.float32)
        columns = slice(turn * 2 * width, (turn + 1) * 2 * width)
        for peer in range(peers):
            send_out[peer, 0, :, columns] = placed[
                peer * capacity : (peer + 1) * capacity
            ].astype(jnp.bfloat16)


def project(meta, first, layout, operands, weights, cosine, sine, rows, blocks, peers, capacity, into):
    steps = len(layout)
    model_width = operands[0].shape[1]
    group_rows = rows * blocks
    width = model_width // blocks
    members = blocks // PAIR
    whole = lambda shape: pl.BlockSpec(shape, lambda i, m: (0,) * len(shape))
    place = lambda i, m: m[0] ^ (first + i)
    table = pl.BlockSpec((HEAD_DIM // 2, rows), lambda i, m: (0, place(i, m)))
    send_shape = (peers, members, capacity, 2 * PAGE * width)
    return pl.pallas_call(
        functools.partial(project_kernel, first, layout, len(weights), peers, capacity),
        grid_spec=pltpu.PrefetchScalarGridSpec(
            num_scalar_prefetch=1,
            grid=(steps,),
            in_specs=[pl.BlockSpec(memory_space=pl.ANY)] * len(operands)
            + [whole(weights[0].shape)] * len(weights)
            + [table, table]
            + [pl.BlockSpec(memory_space=pl.ANY)] * len(into),
            out_specs=[
                pl.BlockSpec((rows, width), lambda i, m: (place(i, m), 0)),
                pl.BlockSpec((rows, 2 * width), lambda i, m: (place(i, m), 0)),
                pl.BlockSpec(
                    (peers, 1) + send_shape[2:], lambda i, m: (0, place(i, m) % members, 0, 0)
                ),
            ],
            scratch_shapes=[
                pltpu.VMEM((steps, rows + EXTRA_ROWS, model_width), jnp.bfloat16),
                pltpu.VMEM((model_width, PARTS * width), jnp.bfloat16),
                pltpu.VMEM((2, rows, width), jnp.float32),
                pltpu.SemaphoreType.DMA((steps, 2)),
            ],
        ),
        out_shape=[
            jax.ShapeDtypeStruct((group_rows, width), jnp.bfloat16),
            jax.ShapeDtypeStruct((group_rows, 2 * width), jnp.bfloat16),
            jax.ShapeDtypeStruct(send_shape, jnp.bfloat16),
        ],
        input_output_aliases={
            1 + len(operands) + len(weights) + 2 + number: number for number in range(len(into))
        },
        compiler_params=PARAMS,
        cost_estimate=pl.CostEstimate(
            flops=16 * steps * rows * model_width * PARTS * width,
            bytes_accessed=(3 * steps) << 19,
            transcendentals=0,
        ),
        name="project",
    )(meta, *operands, *weights, cosine, sine, *into)


def mask_heads(queries, masked):
    turned = queries[...].T
    head_of_row = lax.broadcasted_iota(jnp.int32, turned.shape, 0) // HEAD_DIM
    for head in range(masked.shape[0]):
        masked[head] = jnp.where(head_of_row == head, turned, jnp.zeros((), jnp.bfloat16))


def with_ones(values):
    turned = values.T
    ones = jnp.ones((ONES_ROWS, values.shape[0]), values.dtype)
    rows = []
    for head in range(values.shape[1] // HEAD_DIM):
        rows += [turned[head * HEAD_DIM : (head + 1) * HEAD_DIM], ones]
    return jnp.concatenate(rows, axis=0)


def sweep(jobs, peaks):
    plans = []
    steps = 0
    for begin, end, base, pairs, values_of, masked, starts, ends, total in jobs:
        held = pairs.shape[0] // TILE
        begin, end = jnp.maximum(begin, base), jnp.minimum(end, base + held)
        last = jnp.minimum(ends, end * TILE)
        steps = jnp.maximum(steps, (end - begin + KEYS // TILE - 1) // (KEYS // TILE))
        plans.append((begin, base, held, pairs, values_of, masked, starts, last, total))

    def one(number, peaks):
        new_peaks = []
        for plan, old_peaks in zip(plans, peaks):
            begin, base, held, pairs, values_of, masked, starts, last, total = plan
            wanted = begin + number * (KEYS // TILE)
            block = jnp.minimum(wanted, base + held - KEYS // TILE)
            row = pl.multiple_of((block - base) * TILE, TILE)
            keys = pairs[pl.ds(row, KEYS), : pairs.shape[1] // 2]
            values = values_of(row)
            index = block * TILE + lax.broadcasted_iota(jnp.int32, (KEYS, TILE), 0)
            allowed = (index >= jnp.maximum(starts, wanted * TILE)) & (index < last)
            job_peaks = []
            for head, old_peak in enumerate(old_peaks):
                scores = jnp.dot(keys, masked[head], preferred_element_type=jnp.float32)
                scores = jnp.where(allowed, scores * SCALE, NEG_FILL)
                peak = jnp.maximum(old_peak, jnp.max(scores, axis=0, keepdims=True))
                fade = jnp.exp2(old_peak - peak)
                weights = jnp.exp2(scores - peak).astype(jnp.bfloat16)
                own = slice(head * HEAD_ROWS, (head + 1) * HEAD_ROWS)
                total[own, :] = total[own, :] * fade + jnp.dot(
                    values[own, :], weights, preferred_element_type=jnp.float32
                )
                job_peaks.append(peak)
            new_peaks.append(tuple(job_peaks))
        return tuple(new_peaks)

    return lax.fori_loop(0, steps, one, peaks)


def fresh_peaks(heads):
    return tuple(jnp.full((1, TILE), NEG_FILL, jnp.float32) for _ in range(heads))


def edge_kernel(meta, ranges, *refs):
    rows, pairs, outs, (masked, values) = refs[:6], refs[6], refs[7:11], refs[11:]
    step = pl.program_id(0)
    width = rows[0].shape[1]
    heads = width // HEAD_DIM
    edge = pl.num_programs(0)
    tiles = pairs.shape[0] // TILE

    @pl.when(step == 0)
    def _():
        for number in range(tiles):
            own = slice(number * TILE, (number + 1) * TILE)
            values[:, own] = with_ones(pairs[own, width:])

    jobs = []
    for side in range(2):
        tile = step + side * (tiles - edge)
        queries, starts, ends = rows[3 * side : 3 * side + 3]
        mask_heads(queries, masked.at[side])
        total = outs[side]
        total[...] = jnp.zeros_like(total)
        jobs.append(
            (
                ranges[0, 2 * tile],
                ranges[0, 2 * tile + 1],
                edge,
                pairs,
                lambda row: values[:, pl.ds(row, KEYS)],
                masked.at[side],
                starts[...],
                ends[...],
                total.at[0],
            )
        )
    peaks = sweep(jobs, (fresh_peaks(heads), fresh_peaks(heads)))
    for side in range(2):
        for head in range(heads):
            outs[2 + side][0, head : head + 1, :] = peaks[side][head]


def finish_kernel(edge, meta, ranges, *refs):
    rows, pairs, halos, held, held_peaks = refs[:6], refs[6], refs[7:9], refs[9:11], refs[11:13]
    outs, (masked, sums, mixed) = refs[13:-3], refs[-3:]
    step = pl.program_id(0)
    width = rows[0].shape[1]
    heads = width // HEAD_DIM
    tiles = pairs.shape[0] // TILE
    places = tile_places(step, edge, tiles)

    def jobs_on(keys, bases):
        jobs = []
        for side in range(2):
            queries, starts, ends = rows[3 * side : 3 * side + 3]
            mask_heads(queries, masked.at[side])
            jobs.append(
                (
                    ranges[0, 2 * places[side]],
                    ranges[0, 2 * places[side] + 1],
                    bases[side],
                    keys[side],
                    lambda row, held=keys[side]: with_ones(held[pl.ds(row, KEYS), width:]),
                    masked.at[side],
                    starts[...],
                    ends[...],
                    sums.at[side],
                )
            )
        return jobs

    @pl.when(step < edge)
    def _():
        for side in range(2):
            sums[side] = held[side][0]

    reaches_back = ranges[0, 2 * places[0]] < edge
    reaches_ahead = ranges[0, 2 * places[1] + 1] > edge + tiles

    @pl.when((step < edge) & (reaches_back | reaches_ahead))
    def _():
        peaks = tuple(
            tuple(held_peaks[side][0, head : head + 1, :] for head in range(heads))
            for side in range(2)
        )
        sweep(jobs_on(halos, (0, edge + tiles)), peaks)

    @pl.when(step >= edge)
    def _():
        sums[...] = jnp.zeros_like(sums)
        sweep(jobs_on((pairs, pairs), (edge, edge)), (fresh_peaks(heads), fresh_peaks(heads)))

    for side in range(2):
        parts = []
        for head in range(heads):
            row = head * HEAD_ROWS
            parts.append(
                sums[side, row : row + HEAD_DIM, :]
                / sums[side, row + HEAD_DIM : row + HEAD_DIM + 1, :]
            )
        tile_rows = pl.ds(pl.multiple_of(places[side] * TILE, TILE), TILE)
        mixed[tile_rows, :] = jnp.concatenate(parts, axis=0).T.astype(jnp.bfloat16)

    @pl.when(step == pl.num_programs(0) - 1)
    def _():
        count = outs[0].shape[0]
        for distance, out in enumerate(outs):
            out[...] = mixed[pl.ds(pl.multiple_of((meta[0] ^ distance) * count, 128), count), :]


def tile_places(step, edge, tiles):
    middle = edge + 2 * (step - edge)
    return (
        jnp.where(step < edge, step, middle),
        jnp.where(step < edge, tiles - edge + step, middle + 1),
    )


def attend_specs(width, edge, tiles):
    specs = []
    for side in range(2):
        place = lambda i, side=side: tile_places(i, edge, tiles)[side]
        specs.append(pl.BlockSpec((TILE, width), lambda i, m, r, place=place: (place(i), 0)))
        specs += [pl.BlockSpec((1, TILE), lambda i, m, r, place=place: (0, place(i)))] * 2
    return specs + [pl.BlockSpec((tiles * TILE, 2 * width), lambda i, m, r: (0, 0))]


def attend_edges(meta, ranges, queries, starts, ends, pairs):
    group_rows, width = queries.shape
    heads = width // HEAD_DIM
    tiles, edge = group_rows // TILE, SPAN // TILE
    shapes = [(edge, heads * HEAD_ROWS, TILE)] * 2 + [(edge, 8, TILE)] * 2
    return pl.pallas_call(
        edge_kernel,
        grid_spec=pltpu.PrefetchScalarGridSpec(
            num_scalar_prefetch=2,
            grid=(edge,),
            in_specs=attend_specs(width, edge, tiles),
            out_specs=[pl.BlockSpec((1,) + shape[1:], lambda i, m, r: (i, 0, 0)) for shape in shapes],
            scratch_shapes=[
                pltpu.VMEM((2, heads, width, TILE), jnp.bfloat16),
                pltpu.VMEM((heads * HEAD_ROWS, group_rows), jnp.bfloat16),
            ],
        ),
        out_shape=[jax.ShapeDtypeStruct(shape, jnp.float32) for shape in shapes],
        compiler_params=PARAMS,
        cost_estimate=pl.CostEstimate(
            flops=16 * group_rows * 1024 * width,
            bytes_accessed=5 << 20,
            transcendentals=group_rows * 1024 * heads,
        ),
        name="attend_edges",
    )(meta, ranges, queries, starts, ends, queries, starts, ends, pairs)


def attend_finish(meta, ranges, queries, starts, ends, pairs, before, after, held, rows):
    group_rows, width = queries.shape
    heads = width // HEAD_DIM
    tiles, edge = group_rows // TILE, SPAN // TILE
    members = group_rows // rows
    return pl.pallas_call(
        functools.partial(finish_kernel, edge),
        grid_spec=pltpu.PrefetchScalarGridSpec(
            num_scalar_prefetch=2,
            grid=(edge + (tiles - 2 * edge) // 2,),
            in_specs=attend_specs(width, edge, tiles)
            + [pl.BlockSpec((SPAN, 2 * width), lambda i, m, r: (0, 0))] * 2
            + [
                pl.BlockSpec((1,) + part.shape[1:], lambda i, m, r: (jnp.minimum(i, edge - 1), 0, 0))
                for part in held
            ],
            out_specs=[pl.BlockSpec((rows, width), lambda i, m, r: (0, 0))] * members,
            scratch_shapes=[
                pltpu.VMEM((2, heads, width, TILE), jnp.bfloat16),
                pltpu.VMEM((2, heads * HEAD_ROWS, TILE), jnp.float32),
                pltpu.VMEM((group_rows, width), jnp.bfloat16),
            ],
        ),
        out_shape=[jax.ShapeDtypeStruct((rows, width), jnp.bfloat16)] * members,
        compiler_params=PARAMS,
        cost_estimate=pl.CostEstimate(
            flops=16 * group_rows * 1024 * width,
            bytes_accessed=5 << 20,
            transcendentals=group_rows * 1024 * heads,
        ),
        name="attend_finish",
    )(meta, ranges, queries, starts, ends, queries, starts, ends, pairs, before, after, *held)


def output_kernel(members, meta, *refs):
    parts, weights, result, mixed = refs[:members], refs[members:-2], refs[-2], refs[-1]
    width = parts[0].shape[1]
    tile = weights[0].shape[1]
    for distance in range(members):
        source = meta[0] ^ distance
        head_pair = PAIR * (source % (members // PAIR)) + source // (members // PAIR)
        columns = pl.ds(pl.multiple_of((head_pair ^ meta[1]) * width, width), width)
        mixed[:, columns] = parts[distance][...]
    for distance, weight in enumerate(weights):
        columns = pl.ds(pl.multiple_of((meta[0] % len(weights) ^ distance) * tile, tile), tile)
        result[:, columns] = jnp.dot(
            mixed[...], weight[...], preferred_element_type=jnp.float32
        ).astype(jnp.bfloat16)


def output_projection(meta, parts, weights):
    rows, width = parts[0].shape
    depth, tile = weights[0].shape
    whole = lambda shape: pl.BlockSpec(shape, lambda i, m: (0, 0))
    return pl.pallas_call(
        functools.partial(output_kernel, len(parts)),
        grid_spec=pltpu.PrefetchScalarGridSpec(
            num_scalar_prefetch=1,
            grid=(1,),
            in_specs=[whole(parts[0].shape)] * len(parts) + [whole((depth, tile))] * len(weights),
            out_specs=whole((rows, len(weights) * tile)),
            scratch_shapes=[pltpu.VMEM((rows, depth), jnp.bfloat16)],
        ),
        out_shape=jax.ShapeDtypeStruct((rows, len(weights) * tile), jnp.bfloat16),
        compiler_params=PARAMS,
        cost_estimate=pl.CostEstimate(
            flops=2 * rows * depth * len(weights) * tile,
            bytes_accessed=4 << 20,
            transcendentals=0,
        ),
        name="output_projection",
    )(meta, *parts, *weights)


def unpack_kernel(own_row, other_row, pages):
    _, pair, members, capacity, part = own_row.shape
    width = part // (2 * PAGE)
    for source in range(pair):
        for low in range(pair):
            received = own_row if source == low else other_row
            for high in range(members):
                for turn in range(2 * PAGE):
                    start = (turn * pair * members + PAIR * high + low) * width
                    pages[source, :, start : start + width] = received[
                        0, low, high, :, turn * width : (turn + 1) * width
                    ]


def unpack(own_row, other_row):
    planes, pair, members, capacity, part = own_row.shape
    block = pl.BlockSpec((1,) + own_row.shape[1:], lambda i: (i, 0, 0, 0, 0))
    return pl.pallas_call(
        unpack_kernel,
        grid=(planes,),
        in_specs=[block, block],
        out_specs=pl.BlockSpec((pair, capacity, pair * members * part), lambda i: (i, 0, 0)),
        out_shape=jax.ShapeDtypeStruct(
            (planes * pair, capacity, pair * members * part), jnp.bfloat16
        ),
        compiler_params=pltpu.CompilerParams(vmem_limit_bytes=24 * 1024 * 1024),
        cost_estimate=pl.CostEstimate(flops=0, bytes_accessed=6 << 20, transcendentals=0),
        name="unpack",
    )(own_row, other_row)


def rope_tables(positions):
    half_dim = HEAD_DIM // 2
    inverse = 1.0 / ROPE_BASE ** (jnp.arange(half_dim, dtype=jnp.float32) * 2.0 / HEAD_DIM)
    angles = inverse[:, None] * positions.astype(jnp.float32)[None, :]
    return jnp.cos(angles), jnp.sin(angles)


def bounds_kernel(ids, starts, ends, ranges):
    shape = (8, ids.shape[1])
    width = ids.shape[1]
    own = jnp.broadcast_to(ids[...], shape)
    index = lax.broadcasted_iota(jnp.int32, shape, 1)
    first = jnp.where((own != pltpu.roll(own, 1, 1)) | (index == 0), index, 0)
    after = jnp.where((own != pltpu.roll(own, width - 1, 1)) | (index == width - 1), index + 1, width)
    shift = 1
    while shift < SPAN:
        first = jnp.maximum(first, jnp.where(index >= shift, pltpu.roll(first, shift, 1), 0))
        after = jnp.minimum(
            after, jnp.where(index < width - shift, pltpu.roll(after, width - shift, 1), width)
        )
        shift *= 2
    rows = starts.shape[1]
    starts[...] = first[:1, SPAN : SPAN + rows]
    ends[...] = after[:1, SPAN : SPAN + rows]
    lane = lax.broadcasted_iota(jnp.int32, (rows, ranges.shape[1]), 0)
    entry = lax.broadcasted_iota(jnp.int32, (rows, ranges.shape[1]), 1)
    own_lane = entry // 2 * TILE + lax.rem(entry, 2) * (TILE - 1)
    chosen = jnp.where(lane == own_lane, 1.0, 0.0)
    odd = lax.rem(entry, 2) == 1
    begin = (first[:, SPAN : SPAN + rows] // TILE).astype(jnp.bfloat16)
    end = ((after[:, SPAN : SPAN + rows] + TILE - 1) // TILE).astype(jnp.bfloat16)
    from_begin = jnp.where(odd, 0.0, chosen).astype(jnp.bfloat16)
    from_end = jnp.where(odd, chosen, 0.0).astype(jnp.bfloat16)
    found = jnp.dot(begin, from_begin, preferred_element_type=jnp.float32) + jnp.dot(
        end, from_end, preferred_element_type=jnp.float32
    )
    ranges[...] = found[:1].astype(jnp.int32)


def document_bounds(window_ids, rows):
    return pl.pallas_call(
        bounds_kernel,
        out_shape=[jax.ShapeDtypeStruct((1, rows), jnp.int32)] * 2
        + [jax.ShapeDtypeStruct((1, 128), jnp.int32)],
        compiler_params=PARAMS,
        cost_estimate=pl.CostEstimate(flops=1 << 34, bytes_accessed=0, transcendentals=0),
        name="document_bounds",
    )(window_ids[None, :])


def per_device(tokens, norm_gain, input_weight, output_weight, segment_ids, page_owner):
    rows, model_width = tokens.shape
    peers, members = lax.axis_size("tok"), lax.axis_size("grp")
    place, column = lax.axis_index("tok"), lax.axis_index("grp")
    low = place % PAIR
    blocks = PAIR * members
    member = low * members + column
    group_rows = rows * blocks
    width = model_width // blocks
    pages = rows // PAGE

    flat = peers * members
    owners = page_owner[:, 0]
    capacity = max(2, (2 * pages + peers - 1) // peers)
    halves = []
    for parity in range(PAIR):
        pieces = []
        for number in range(PARTS):
            start = number * PAIR * width
            choices = [input_weight[:, start : start + width], input_weight[:, start + width : start + 2 * width]]
            piece = jnp.where((low ^ parity) == 0, choices[0], choices[1])
            route = []
            for source in range(flat):
                row, column_from = divmod(source, members)
                target = (row ^ parity) * members + (PARTS * column_from + number) % members
                route.append((source, target))
            pieces.append(lax.ppermute(piece, ("tok", "grp"), route))
        pieces.append(flipped(output_weight, "tok", 1) if parity else output_weight)
        halves.append(jnp.concatenate(pieces, axis=1))
    plane = jnp.concatenate(halves, axis=0)
    own = layer_norm(tokens, norm_gain[None, :], owners, capacity)
    own, plane = lax.optimization_barrier((own, plane))

    across, along = flipped(own, "grp", 2), flipped(own, "tok", 1)
    sibling = flipped(own, "grp", 1)
    planes = {0: plane}
    bit = peers // 2
    while bit > 1:
        planes[bit] = flipped(plane, "tok", bit)
        bit //= 2
    for distance in range(PAIR, peers, PAIR):
        if distance not in planes:
            step_bit = distance & -distance
            planes[distance] = flipped(planes[distance ^ step_bit], "tok", step_bit)
    weights = [planes[distance] for distance in range(0, peers, PAIR)]

    first_row = place // PAIR * group_rows
    padded_ids = jnp.concatenate(
        [
            jnp.full((SPAN,), -1, jnp.int32),
            segment_ids,
            jnp.full((SPAN,), 1 << 30, jnp.int32),
        ]
    )
    window_ids = lax.dynamic_slice_in_dim(padded_ids, first_row, group_rows + 2 * SPAN, 0)
    window_ids, plane = lax.optimization_barrier((window_ids, plane))
    *bounds, ranges = document_bounds(window_ids, group_rows)
    positions = SPAN + jnp.arange(group_rows, dtype=jnp.int32) - bounds[0][0]
    order = [(number * members + column) % PARTS for number in range(PARTS)]
    meta = jnp.stack([member, place] + order).astype(jnp.int32)
    cosine, sine = rope_tables(positions)
    across, along, sibling, weights, cosine, sine, meta = lax.optimization_barrier(
        (across, along, sibling, weights, cosine, sine, meta)
    )

    half, held = rows // 2, rows + EXTRA_ROWS
    corner = [flipped(across[:half], "tok", 1), flipped(along[half:], "grp", 2)]
    across_sibling = flipped(across, "grp", 1)
    along_sibling = flipped(along, "grp", 1)
    near_blocks = [own, sibling, across, across_sibling]
    near_layout = [[(number, 0, held)] for number in range(4)]
    far_layout = [[(0, 0, held)], [(1, 0, held)]]
    far_layout += [[(number, 0, half), (number + 1, half, held - half)] for number in (2, 4)]

    sizes = (weights, cosine, sine, rows, blocks, peers, capacity)

    def to_owners(send):
        received = lax.all_to_all(
            send.reshape((flat,) + send.shape[2:]),
            ("tok", "grp"),
            split_axis=0,
            concat_axis=0,
            tiled=True,
        )
        return received.reshape((peers // PAIR, PAIR, members) + send.shape[2:])

    queries, pairs, send = project(meta, 0, near_layout, near_blocks, *sizes, ())
    send, corner, along_sibling = lax.optimization_barrier((send, corner, along_sibling))
    own_row = to_owners(send)
    corner_sibling = [flipped(block, "grp", 1) for block in corner]
    far_blocks = [along, along_sibling] + corner + corner_sibling
    columns = jnp.concatenate([held_rows[:, PARTS * width :] for held_rows in weights], axis=0)
    row_order = place
    if output_weight.shape[0] != width:
        shards = columns.reshape((peers,) + output_weight.shape)
        columns = shards[jnp.arange(peers) ^ place].reshape(columns.shape)
        row_order = jnp.zeros_like(place)
    queries, pairs, send = project(meta, 4, far_layout, far_blocks, *sizes, (queries, pairs))
    before = shifted(pairs[group_rows - SPAN :], "tok", PAIR)
    after = shifted(pairs[:SPAN], "tok", -PAIR)
    columns_across = flipped(columns, "grp", 2)

    edges = attend_edges(meta, ranges, queries, *bounds, pairs)
    before, after, edges, columns_across, send = lax.optimization_barrier(
        (before, after, edges, columns_across, send)
    )
    other_row = to_owners(send)
    mixed = attend_finish(meta, ranges, queries, *bounds, pairs, before, after, edges, rows)
    last_weights = [columns, flipped(columns, "grp", 1)]
    last_weights += [columns_across, flipped(columns_across, "grp", 1)]
    parts = [mixed[0]] + [
        lax.ppermute(
            mixed[distance],
            ("tok", "grp"),
            [(source, source ^ distance) for source in range(flat)],
        )
        for distance in range(1, blocks)
    ]
    output_meta = jnp.stack([member, row_order]).astype(jnp.int32)
    attended = output_projection(output_meta, parts, last_weights)
    cache_pages = unpack(own_row, other_row).reshape(
        peers * capacity, 2 * PAGE * model_width
    )
    return attended, cache_pages


def solution(mesh):
    placed = (
        P(("tok", "grp"), None),
        P(),
        P("tok", "grp"),
        P("tok", "grp"),
        P(),
        P(("tok", "grp"), None),
    )
    return jax.shard_map(
        per_device,
        mesh=mesh,
        in_specs=placed,
        out_specs=(P(("tok", "grp"), None), P(("tok", "grp"), None)),
        check_vma=False,
    )
```

```python
import functools
import math

import jax
import jax.numpy as jnp
from jax import lax
from jax.experimental import pallas as pl
from jax.experimental.pallas import tpu as pltpu
from jax.sharding import PartitionSpec as P

H = 16
SPAN = 1024
PAGE = 4
HEAD_DIM = 64

NEG_FILL = -1e30
ROPE_BASE = 160000.0
EPSILON = 1e-05
TILE = 256
PARTS = 3
PAIR = 2
ONES_ROWS = 16
HEAD_ROWS = HEAD_DIM + ONES_ROWS
EXTRA_ROWS = 16
KEYS = 512
SCALE = HEAD_DIM ** (-0.5) * math.log2(math.e)
VMEM_LIMIT = 60 * 1024 * 1024
PARAMS = pltpu.CompilerParams(vmem_limit_bytes=VMEM_LIMIT)


def flipped(value, axis, bit):
    count = lax.axis_size(axis)
    return lax.ppermute(value, axis, [(source, source ^ bit) for source in range(count)])


def shifted(value, axis, steps):
    count = lax.axis_size(axis)
    initial, last = (max(0, -steps), min(count, count - steps))
    return lax.ppermute(value, axis, [(source, source + steps) for source in range(initial, last)])


def norm_kernel(capacity, tokens, gain, owner_row, normed, owners):
    rows = tokens.shape[0]
    values = tokens[...].astype(jnp.float32)
    centred = values - jnp.mean(values, axis=-1, keepdims=True)
    spread = jnp.mean(jnp.square(centred), axis=-1, keepdims=True)
    normed[:rows, :] = (centred * lax.rsqrt(spread + EPSILON) * gain[...]).astype(jnp.bfloat16)
    pages = owner_row.shape[1]
    owners[...] = jnp.full(owners.shape, -1.0, jnp.float32)
    owners[:1, :pages] = owner_row[...].astype(jnp.float32)
    lanes = owners.shape[1]
    across = jnp.broadcast_to(owners[:1, :], (lanes, lanes))
    earlier = lax.broadcasted_iota(jnp.int32, (lanes, lanes), 0) < lax.broadcasted_iota(
        jnp.int32, (lanes, lanes), 1
    )
    same = (across.T == across) & earlier
    ranks = jnp.sum(jnp.where(same, 1.0, 0.0), axis=0, keepdims=True)
    slots = owners[:1, :] * capacity + ranks
    normed[rows:, :] = jnp.zeros((EXTRA_ROWS, normed.shape[1]), jnp.bfloat16)
    normed[rows:, :lanes] = jnp.broadcast_to(slots, (EXTRA_ROWS, lanes)).astype(jnp.bfloat16)


def layer_norm(tokens, gain, owners, capacity):
    rows, width = tokens.shape
    lanes = -(-owners.shape[0] // 128) * 128
    return pl.pallas_call(
        functools.partial(norm_kernel, capacity),
        out_shape=jax.ShapeDtypeStruct((rows + EXTRA_ROWS, width), jnp.bfloat16),
        scratch_shapes=[pltpu.VMEM((8, lanes), jnp.float32)],
        compiler_params=PARAMS,
        name="layer_norm",
    )(tokens, gain, owners[None, :])


def project_kernel(first, layout, weight_count, peers, capacity, meta, *refs):
    operands = 1 + max(entry[0] for pieces in layout for entry in pieces)
    tokens = refs[:operands]
    weights = refs[operands : operands + weight_count]
    cosine, sine = refs[operands + weight_count : operands + weight_count + 2]
    query_out, pair_out, send_out, blocks, weight, page_source, sems = refs[-7:]
    step = pl.program_id(0)
    steps = len(layout)
    rows = query_out.shape[0]
    width = query_out.shape[1]
    shard = weights[0].shape[0] // 2

    def arrivals(number):
        return [
            pltpu.make_async_copy(
                tokens[operand],
                blocks.at[number, pl.ds(offset, count), :],
                sems.at[number, place],
            )
            for place, (operand, offset, count) in enumerate(layout[number])
        ]

    @pl.when(step == 0)
    def _():
        for number in range(steps):
            for copy in arrivals(number):
                copy.start()
        for plane in range(weight_count):
            for low in range(2):
                row = pl.multiple_of((meta[1] ^ (2 * plane + low)) * shard, shard)
                for number in range(PARTS):
                    column = pl.multiple_of(meta[2 + number] * width, width)
                    weight[pl.ds(row, shard), number * width : (number + 1) * width] = weights[
                        plane
                    ][low * shard : (low + 1) * shard, pl.ds(column, width)]

    for number in range(steps):

        @pl.when(step == number)
        def _():
            for copy in arrivals(number):
                copy.wait()

    joined = jnp.dot(blocks[step, :rows, :], weight[...], preferred_element_type=jnp.float32)
    cosines = jnp.concatenate([cosine[...]] * 4, axis=0).T
    sines = jnp.concatenate([-sine[...], sine[...]] * 2, axis=0).T
    first_half = lax.rem(lax.broadcasted_iota(jnp.int32, (rows, width), 1), HEAD_DIM) < (
        HEAD_DIM // 2
    )

    def rotate(values):
        partner = jnp.where(
            first_half,
            pltpu.roll(values, width - HEAD_DIM // 2, 1),
            pltpu.roll(values, HEAD_DIM // 2, 1),
        )
        return (values * cosines + partner * sines).astype(jnp.bfloat16)

    query_out[...] = rotate(joined[:, :width])
    keys = rotate(joined[:, width : 2 * width])
    values = joined[:, 2 * width :].astype(jnp.bfloat16)
    pair_out[:, :width] = keys
    pair_out[:, width:] = values
    page_source[0] = keys.astype(jnp.float32)
    page_source[1] = values.astype(jnp.float32)

    pages = rows // PAGE
    slot_count = peers * capacity
    slots = blocks[step, rows : rows + EXTRA_ROWS, :128].astype(jnp.float32)[:1, :pages]
    chosen = (
        lax.broadcasted_iota(jnp.int32, (slot_count, pages), 0).astype(jnp.float32) == slots
    ).astype(jnp.bfloat16)
    for turn in range(PAGE):
        page_part = jnp.concatenate(
            [
                page_source[half, pl.ds(turn, pages, stride=PAGE), :].astype(jnp.bfloat16)
                for half in range(2)
            ],
            axis=1,
        )
        placed = jnp.dot(chosen, page_part, preferred_element_type=jnp.float32)
        columns = slice(turn * 2 * width, (turn + 1) * 2 * width)
        for peer in range(peers):
            send_out[peer, 0, :, columns] = placed[
                peer * capacity : (peer + 1) * capacity
            ].astype(jnp.bfloat16)


def project(meta, first, layout, operands, weights, cosine, sine, rows, blocks, peers, capacity, into):
    steps = len(layout)
    model_width = operands[0].shape[1]
    group_rows = rows * blocks
    width = model_width // blocks
    members = blocks // PAIR
    whole = lambda shape: pl.BlockSpec(shape, lambda i, m: (0,) * len(shape))
    place = lambda i, m: m[0] ^ (first + i)
    table = pl.BlockSpec((HEAD_DIM // 2, rows), lambda i, m: (0, place(i, m)))
    send_shape = (peers, members, capacity, 2 * PAGE * width)
    return pl.pallas_call(
        functools.partial(project_kernel, first, layout, len(weights), peers, capacity),
        grid_spec=pltpu.PrefetchScalarGridSpec(
            num_scalar_prefetch=1,
            grid=(steps,),
            in_specs=[pl.BlockSpec(memory_space=pl.ANY)] * len(operands)
            + [whole(weights[0].shape)] * len(weights)
            + [table, table]
            + [pl.BlockSpec(memory_space=pl.ANY)] * len(into),
            out_specs=[
                pl.BlockSpec((rows, width), lambda i, m: (place(i, m), 0)),
                pl.BlockSpec((rows, 2 * width), lambda i, m: (place(i, m), 0)),
                pl.BlockSpec(
                    (peers, 1) + send_shape[2:], lambda i, m: (0, place(i, m) % members, 0, 0)
                ),
            ],
            scratch_shapes=[
                pltpu.VMEM((steps, rows + EXTRA_ROWS, model_width), jnp.bfloat16),
                pltpu.VMEM((model_width, PARTS * width), jnp.bfloat16),
                pltpu.VMEM((2, rows, width), jnp.float32),
                pltpu.SemaphoreType.DMA((steps, 2)),
            ],
        ),
        out_shape=[
            jax.ShapeDtypeStruct((group_rows, width), jnp.bfloat16),
            jax.ShapeDtypeStruct((group_rows, 2 * width), jnp.bfloat16),
            jax.ShapeDtypeStruct(send_shape, jnp.bfloat16),
        ],
        input_output_aliases={
            1 + len(operands) + len(weights) + 2 + number: number for number in range(len(into))
        },
        compiler_params=PARAMS,
        cost_estimate=pl.CostEstimate(
            flops=16 * steps * rows * model_width * PARTS * width,
            bytes_accessed=(3 * steps) << 19,
            transcendentals=0,
        ),
        name="project",
    )(meta, *operands, *weights, cosine, sine, *into)


def mask_heads(queries, masked):
    turned = queries[...].T
    head_of_row = lax.broadcasted_iota(jnp.int32, turned.shape, 0) // HEAD_DIM
    for head in range(masked.shape[0]):
        masked[head] = jnp.where(head_of_row == head, turned, jnp.zeros((), jnp.bfloat16))


def with_ones(values):
    turned = values.T
    ones = jnp.ones((ONES_ROWS, values.shape[0]), values.dtype)
    rows = []
    for head in range(values.shape[1] // HEAD_DIM):
        rows += [turned[head * HEAD_DIM : (head + 1) * HEAD_DIM], ones]
    return jnp.concatenate(rows, axis=0)


def sweep(jobs, peaks):
    plans = []
    steps = 0
    for begin, end, base, pairs, values_of, masked, starts, ends, total in jobs:
        held = pairs.shape[0] // TILE
        begin, end = jnp.maximum(begin, base), jnp.minimum(end, base + held)
        last = jnp.minimum(ends, end * TILE)
        steps = jnp.maximum(steps, (end - begin + KEYS // TILE - 1) // (KEYS // TILE))
        plans.append((begin, base, held, pairs, values_of, masked, starts, last, total))

    def one(number, peaks):
        new_peaks = []
        for plan, old_peaks in zip(plans, peaks):
            begin, base, held, pairs, values_of, masked, starts, last, total = plan
            wanted = begin + number * (KEYS // TILE)
            block = jnp.minimum(wanted, base + held - KEYS // TILE)
            row = pl.multiple_of((block - base) * TILE, TILE)
            keys = pairs[pl.ds(row, KEYS), : pairs.shape[1] // 2]
            values = values_of(row)
            index = block * TILE + lax.broadcasted_iota(jnp.int32, (KEYS, TILE), 0)
            allowed = (index >= jnp.maximum(starts, wanted * TILE)) & (index < last)
            job_peaks = []
            for head, old_peak in enumerate(old_peaks):
                scores = jnp.dot(keys, masked[head], preferred_element_type=jnp.float32)
                scores = jnp.where(allowed, scores * SCALE, NEG_FILL)
                peak = jnp.maximum(old_peak, jnp.max(scores, axis=0, keepdims=True))
                fade = jnp.exp2(old_peak - peak)
                weights = jnp.exp2(scores - peak).astype(jnp.bfloat16)
                own = slice(head * HEAD_ROWS, (head + 1) * HEAD_ROWS)
                total[own, :] = total[own, :] * fade + jnp.dot(
                    values[own, :], weights, preferred_element_type=jnp.float32
                )
                job_peaks.append(peak)
            new_peaks.append(tuple(job_peaks))
        return tuple(new_peaks)

    return lax.fori_loop(0, steps, one, peaks)


def fresh_peaks(heads):
    return tuple(jnp.full((1, TILE), NEG_FILL, jnp.float32) for _ in range(heads))


def edge_kernel(edge, meta, ranges, *refs):
    rows, pairs, outs, (masked, values) = refs[:6], refs[6], refs[7:11], refs[11:]
    step = pl.program_id(0)
    width = rows[0].shape[1]
    heads = width // HEAD_DIM
    tiles = pairs.shape[0] // TILE

    @pl.when(step == 0)
    def _():
        for number in range(tiles):
            own = slice(number * TILE, (number + 1) * TILE)
            values[:, own] = with_ones(pairs[own, width:])

    jobs = []
    for side in range(2):
        tile = step + side * (tiles - edge)
        queries, starts, ends = rows[3 * side : 3 * side + 3]
        mask_heads(queries, masked.at[side])
        total = outs[side]
        total[...] = jnp.zeros_like(total)
        jobs.append(
            (
                ranges[0, 2 * tile],
                ranges[0, 2 * tile + 1],
                edge,
                pairs,
                lambda row: values[:, pl.ds(row, KEYS)],
                masked.at[side],
                starts[...],
                ends[...],
                total.at[0],
            )
        )
    peaks = sweep(jobs, (fresh_peaks(heads), fresh_peaks(heads)))
    for side in range(2):
        for head in range(heads):
            outs[2 + side][0, head : head + 1, :] = peaks[side][head]


def finish_kernel(edge, meta, ranges, *refs):
    rows, pairs, halos, held, held_peaks = refs[:6], refs[6], refs[7:9], refs[9:11], refs[11:13]
    outs, (masked, sums, peaks_held, mixed) = refs[13:-4], refs[-4:]
    held_steps = edge // 2
    step = pl.program_id(0)
    width = rows[0].shape[1]
    heads = width // HEAD_DIM
    tiles = pairs.shape[0] // TILE
    places = tile_places(step, edge, tiles)

    def jobs_on(keys, bases):
        jobs = []
        for side in range(2):
            queries, starts, ends = rows[3 * side : 3 * side + 3]
            mask_heads(queries, masked.at[side])
            jobs.append(
                (
                    ranges[0, 2 * places[side]],
                    ranges[0, 2 * places[side] + 1],
                    bases[side],
                    keys[side],
                    lambda row, held=keys[side]: with_ones(held[pl.ds(row, KEYS), width:]),
                    masked.at[side],
                    starts[...],
                    ends[...],
                    sums.at[side],
                )
            )
        return jobs

    @pl.when(step < held_steps)
    def _():
        for side in range(2):
            sums[side] = held[side][0]
            peaks_held[side] = held_peaks[side][0]

    @pl.when(step >= held_steps)
    def _():
        sums[...] = jnp.zeros_like(sums)
        peaks = sweep(jobs_on((pairs, pairs), (edge, edge)), (fresh_peaks(heads),) * 2)
        for side in range(2):
            for head in range(heads):
                peaks_held[side, head : head + 1, :] = peaks[side][head]

    reaches_back = ranges[0, 2 * places[0]] < edge
    reaches_ahead = ranges[0, 2 * places[1] + 1] > edge + tiles

    @pl.when((step < edge) & (reaches_back | reaches_ahead))
    def _():
        peaks = tuple(
            tuple(peaks_held[side, head : head + 1, :] for head in range(heads))
            for side in range(2)
        )
        sweep(jobs_on(halos, (0, edge + tiles)), peaks)

    for side in range(2):
        parts = []
        for head in range(heads):
            row = head * HEAD_ROWS
            parts.append(
                sums[side, row : row + HEAD_DIM, :]
                / sums[side, row + HEAD_DIM : row + HEAD_DIM + 1, :]
            )
        tile_rows = pl.ds(pl.multiple_of(places[side] * TILE, TILE), TILE)
        mixed[tile_rows, :] = jnp.concatenate(parts, axis=0).T.astype(jnp.bfloat16)

    @pl.when(step == pl.num_programs(0) - 1)
    def _():
        count = outs[0].shape[0]
        for distance, out in enumerate(outs):
            out[...] = mixed[pl.ds(pl.multiple_of((meta[0] ^ distance) * count, 128), count), :]


def tile_places(step, edge, tiles):
    middle = edge + 2 * (step - edge)
    return (
        jnp.where(step < edge, step, middle),
        jnp.where(step < edge, tiles - edge + step, middle + 1),
    )


def attend_specs(width, edge, tiles):
    specs = []
    for side in range(2):
        place = lambda i, side=side: tile_places(i, edge, tiles)[side]
        specs.append(pl.BlockSpec((TILE, width), lambda i, m, r, place=place: (place(i), 0)))
        specs += [pl.BlockSpec((1, TILE), lambda i, m, r, place=place: (0, place(i)))] * 2
    return specs + [pl.BlockSpec((tiles * TILE, 2 * width), lambda i, m, r: (0, 0))]


def attend_edges(meta, ranges, queries, starts, ends, pairs):
    group_rows, width = queries.shape
    heads = width // HEAD_DIM
    tiles, edge = group_rows // TILE, SPAN // TILE
    steps = edge // 2
    shapes = [(steps, heads * HEAD_ROWS, TILE)] * 2 + [(steps, 8, TILE)] * 2
    return pl.pallas_call(
        functools.partial(edge_kernel, edge),
        grid_spec=pltpu.PrefetchScalarGridSpec(
            num_scalar_prefetch=2,
            grid=(steps,),
            in_specs=attend_specs(width, edge, tiles),
            out_specs=[pl.BlockSpec((1,) + shape[1:], lambda i, m, r: (i, 0, 0)) for shape in shapes],
            scratch_shapes=[
                pltpu.VMEM((2, heads, width, TILE), jnp.bfloat16),
                pltpu.VMEM((heads * HEAD_ROWS, group_rows), jnp.bfloat16),
            ],
        ),
        out_shape=[jax.ShapeDtypeStruct(shape, jnp.float32) for shape in shapes],
        compiler_params=PARAMS,
        cost_estimate=pl.CostEstimate(
            flops=16 * group_rows * 1024 * width,
            bytes_accessed=5 << 20,
            transcendentals=group_rows * 1024 * heads,
        ),
        name="attend_edges",
    )(meta, ranges, queries, starts, ends, queries, starts, ends, pairs)


def attend_finish(meta, ranges, queries, starts, ends, pairs, before, after, held, rows):
    group_rows, width = queries.shape
    heads = width // HEAD_DIM
    tiles, edge = group_rows // TILE, SPAN // TILE
    members = group_rows // rows
    return pl.pallas_call(
        functools.partial(finish_kernel, edge),
        grid_spec=pltpu.PrefetchScalarGridSpec(
            num_scalar_prefetch=2,
            grid=(edge + (tiles - 2 * edge) // 2,),
            in_specs=attend_specs(width, edge, tiles)
            + [pl.BlockSpec((SPAN, 2 * width), lambda i, m, r: (0, 0))] * 2
            + [
                pl.BlockSpec(
                    (1,) + part.shape[1:], lambda i, m, r: (jnp.minimum(i, edge // 2 - 1), 0, 0)
                )
                for part in held
            ],
            out_specs=[pl.BlockSpec((rows, width), lambda i, m, r: (0, 0))] * members,
            scratch_shapes=[
                pltpu.VMEM((2, heads, width, TILE), jnp.bfloat16),
                pltpu.VMEM((2, heads * HEAD_ROWS, TILE), jnp.float32),
                pltpu.VMEM((2, 8, TILE), jnp.float32),
                pltpu.VMEM((group_rows, width), jnp.bfloat16),
            ],
        ),
        out_shape=[jax.ShapeDtypeStruct((rows, width), jnp.bfloat16)] * members,
        compiler_params=PARAMS,
        cost_estimate=pl.CostEstimate(
            flops=16 * group_rows * 1024 * width,
            bytes_accessed=5 << 20,
            transcendentals=group_rows * 1024 * heads,
        ),
        name="attend_finish",
    )(meta, ranges, queries, starts, ends, queries, starts, ends, pairs, before, after, *held)


def output_kernel(members, meta, *refs):
    parts, weights, result, mixed = refs[:members], refs[members:-2], refs[-2], refs[-1]
    width = parts[0].shape[1]
    tile = weights[0].shape[1]
    for distance in range(members):
        source = meta[0] ^ distance
        head_pair = PAIR * (source % (members // PAIR)) + source // (members // PAIR)
        shard = head_pair ^ meta[1]
        shard = jnp.where(meta[1] < 0, head_pair, shard // PAIR + shard % PAIR * (members // PAIR))
        columns = pl.ds(pl.multiple_of(shard * width, width), width)
        mixed[:, columns] = parts[distance][...]
    for distance, weight in enumerate(weights):
        columns = pl.ds(pl.multiple_of((meta[0] % len(weights) ^ distance) * tile, tile), tile)
        result[:, columns] = jnp.dot(
            mixed[...], weight[...], preferred_element_type=jnp.float32
        ).astype(jnp.bfloat16)


def output_projection(meta, parts, weights):
    rows, width = parts[0].shape
    depth, tile = weights[0].shape
    whole = lambda shape: pl.BlockSpec(shape, lambda i, m: (0, 0))
    return pl.pallas_call(
        functools.partial(output_kernel, len(parts)),
        grid_spec=pltpu.PrefetchScalarGridSpec(
            num_scalar_prefetch=1,
            grid=(1,),
            in_specs=[whole(parts[0].shape)] * len(parts) + [whole((depth, tile))] * len(weights),
            out_specs=whole((rows, len(weights) * tile)),
            scratch_shapes=[pltpu.VMEM((rows, depth), jnp.bfloat16)],
        ),
        out_shape=jax.ShapeDtypeStruct((rows, len(weights) * tile), jnp.bfloat16),
        compiler_params=PARAMS,
        cost_estimate=pl.CostEstimate(
            flops=2 * rows * depth * len(weights) * tile,
            bytes_accessed=4 << 20,
            transcendentals=0,
        ),
        name="output_projection",
    )(meta, *parts, *weights)


def unpack_kernel(own_row, other_row, pages):
    _, pair, members, capacity, part = own_row.shape
    width = part // (2 * PAGE)
    for source in range(pair):
        for low in range(pair):
            received = own_row if source == low else other_row
            for high in range(members):
                for turn in range(2 * PAGE):
                    start = (turn * pair * members + PAIR * high + low) * width
                    pages[source, :, start : start + width] = received[
                        0, low, high, :, turn * width : (turn + 1) * width
                    ]


def unpack(own_row, other_row):
    planes, pair, members, capacity, part = own_row.shape
    block = pl.BlockSpec((1,) + own_row.shape[1:], lambda i: (i, 0, 0, 0, 0))
    return pl.pallas_call(
        unpack_kernel,
        grid=(planes,),
        in_specs=[block, block],
        out_specs=pl.BlockSpec((pair, capacity, pair * members * part), lambda i: (i, 0, 0)),
        out_shape=jax.ShapeDtypeStruct(
            (planes * pair, capacity, pair * members * part), jnp.bfloat16
        ),
        compiler_params=pltpu.CompilerParams(vmem_limit_bytes=24 * 1024 * 1024),
        cost_estimate=pl.CostEstimate(flops=0, bytes_accessed=6 << 20, transcendentals=0),
        name="unpack",
    )(own_row, other_row)


def rope_tables(positions):
    half_dim = HEAD_DIM // 2
    inverse = 1.0 / ROPE_BASE ** (jnp.arange(half_dim, dtype=jnp.float32) * 2.0 / HEAD_DIM)
    angles = inverse[:, None] * positions.astype(jnp.float32)[None, :]
    return jnp.cos(angles), jnp.sin(angles)


def bounds_kernel(ids, starts, ends, ranges):
    shape = (8, ids.shape[1])
    width = ids.shape[1]
    own = jnp.broadcast_to(ids[...], shape)
    index = lax.broadcasted_iota(jnp.int32, shape, 1)
    first = jnp.where((own != pltpu.roll(own, 1, 1)) | (index == 0), index, 0)
    after = jnp.where((own != pltpu.roll(own, width - 1, 1)) | (index == width - 1), index + 1, width)
    shift = 1
    while shift < SPAN:
        first = jnp.maximum(first, jnp.where(index >= shift, pltpu.roll(first, shift, 1), 0))
        after = jnp.minimum(
            after, jnp.where(index < width - shift, pltpu.roll(after, width - shift, 1), width)
        )
        shift *= 2
    rows = starts.shape[1]
    starts[...] = first[:1, SPAN : SPAN + rows]
    ends[...] = after[:1, SPAN : SPAN + rows]
    lane = lax.broadcasted_iota(jnp.int32, (rows, ranges.shape[1]), 0)
    entry = lax.broadcasted_iota(jnp.int32, (rows, ranges.shape[1]), 1)
    own_lane = entry // 2 * TILE + lax.rem(entry, 2) * (TILE - 1)
    chosen = jnp.where(lane == own_lane, 1.0, 0.0)
    odd = lax.rem(entry, 2) == 1
    begin = (first[:, SPAN : SPAN + rows] // TILE).astype(jnp.bfloat16)
    end = ((after[:, SPAN : SPAN + rows] + TILE - 1) // TILE).astype(jnp.bfloat16)
    from_begin = jnp.where(odd, 0.0, chosen).astype(jnp.bfloat16)
    from_end = jnp.where(odd, chosen, 0.0).astype(jnp.bfloat16)
    found = jnp.dot(begin, from_begin, preferred_element_type=jnp.float32) + jnp.dot(
        end, from_end, preferred_element_type=jnp.float32
    )
    ranges[...] = found[:1].astype(jnp.int32)


def document_bounds(window_ids, rows):
    return pl.pallas_call(
        bounds_kernel,
        out_shape=[jax.ShapeDtypeStruct((1, rows), jnp.int32)] * 2
        + [jax.ShapeDtypeStruct((1, 128), jnp.int32)],
        compiler_params=PARAMS,
        cost_estimate=pl.CostEstimate(flops=1 << 34, bytes_accessed=0, transcendentals=0),
        name="document_bounds",
    )(window_ids[None, :])


def per_device(tokens, norm_gain, input_weight, output_weight, segment_ids, page_owner):
    rows, model_width = tokens.shape
    peers, members = lax.axis_size("tok"), lax.axis_size("grp")
    place, column = lax.axis_index("tok"), lax.axis_index("grp")
    low = place % PAIR
    blocks = PAIR * members
    member = low * members + column
    group_rows = rows * blocks
    width = model_width // blocks
    pages = rows // PAGE

    flat = peers * members
    owners = page_owner[:, 0]
    capacity = max(2, (2 * pages + peers - 1) // peers)
    halves = []
    for parity in range(PAIR):
        pieces = []
        for number in range(PARTS):
            start = number * PAIR * width
            choices = [input_weight[:, start : start + width], input_weight[:, start + width : start + 2 * width]]
            piece = jnp.where((low ^ parity) == 0, choices[0], choices[1])
            route = []
            for source in range(flat):
                row, column_from = divmod(source, members)
                target = (row ^ parity) * members + (PARTS * column_from + number) % members
                route.append((source, target))
            pieces.append(lax.ppermute(piece, ("tok", "grp"), route))
        halves.append(jnp.concatenate(pieces, axis=1))
    plane = jnp.concatenate(halves, axis=0)
    own = layer_norm(tokens, norm_gain[None, :], owners, capacity)
    own, plane = lax.optimization_barrier((own, plane))

    across, along = flipped(own, "grp", 2), flipped(own, "tok", 1)
    sibling = flipped(own, "grp", 1)
    planes = {0: plane}
    bit = peers // 2
    while bit > 1:
        planes[bit] = flipped(plane, "tok", bit)
        bit //= 2
    for distance in range(PAIR, peers, PAIR):
        if distance not in planes:
            step_bit = distance & -distance
            planes[distance] = flipped(planes[distance ^ step_bit], "tok", step_bit)
    weights = [planes[distance] for distance in range(0, peers, PAIR)]

    first_row = place // PAIR * group_rows
    padded_ids = jnp.concatenate(
        [
            jnp.full((SPAN,), -1, jnp.int32),
            segment_ids,
            jnp.full((SPAN,), 1 << 30, jnp.int32),
        ]
    )
    window_ids = lax.dynamic_slice_in_dim(padded_ids, first_row, group_rows + 2 * SPAN, 0)
    window_ids, plane = lax.optimization_barrier((window_ids, plane))
    *bounds, ranges = document_bounds(window_ids, group_rows)
    positions = SPAN + jnp.arange(group_rows, dtype=jnp.int32) - bounds[0][0]
    order = [(number * members + column) % PARTS for number in range(PARTS)]
    meta = jnp.stack([member, place] + order).astype(jnp.int32)
    cosine, sine = rope_tables(positions)
    last_rows = output_weight
    bit = PAIR
    while 4 * bit < peers:
        last_rows = jnp.concatenate([last_rows, flipped(last_rows, "tok", bit)], axis=0)
        bit *= 2
    other_rows = flipped(last_rows, "tok", bit)
    across, along, sibling, weights, last_rows, other_rows, cosine, sine, meta = (
        lax.optimization_barrier(
            (across, along, sibling, weights, last_rows, other_rows, cosine, sine, meta)
        )
    )
    last_rows = jnp.concatenate([last_rows, other_rows], axis=0)

    half, held = rows // 2, rows + EXTRA_ROWS
    corner = [flipped(across[:half], "tok", 1), flipped(along[half:], "grp", 2)]
    across_sibling = flipped(across, "grp", 1)
    along_sibling = flipped(along, "grp", 1)
    other_rows = flipped(last_rows, "tok", peers // 2)
    near_blocks = [own, sibling, across, across_sibling]
    near_layout = [[(number, 0, held)] for number in range(4)]
    far_layout = [[(0, 0, held)], [(1, 0, held)]]
    far_layout += [[(number, 0, half), (number + 1, half, held - half)] for number in (2, 4)]

    sizes = (weights, cosine, sine, rows, blocks, peers, capacity)

    def to_owners(send):
        received = lax.all_to_all(
            send.reshape((flat,) + send.shape[2:]),
            ("tok", "grp"),
            split_axis=0,
            concat_axis=0,
            tiled=True,
        )
        return received.reshape((peers // PAIR, PAIR, members) + send.shape[2:])

    queries, pairs, send = project(meta, 0, near_layout, near_blocks, *sizes, ())
    send, corner, along_sibling, last_rows, other_rows = lax.optimization_barrier(
        (send, corner, along_sibling, last_rows, other_rows)
    )
    own_row = to_owners(send)
    corner_sibling = [flipped(block, "grp", 1) for block in corner]
    far_blocks = [along, along_sibling] + corner + corner_sibling
    last_rows = jnp.concatenate([last_rows, other_rows], axis=0)
    queries, pairs, send = project(meta, 4, far_layout, far_blocks, *sizes, (queries, pairs))
    before = shifted(pairs[group_rows - SPAN :], "tok", PAIR)
    after = shifted(pairs[:SPAN], "tok", -PAIR)
    other_rows = flipped(last_rows, "tok", 1)

    edges = attend_edges(meta, ranges, queries, *bounds, pairs)
    before, after, edges, last_rows, other_rows, send = lax.optimization_barrier(
        (before, after, edges, last_rows, other_rows, send)
    )
    other_row = to_owners(send)
    columns = jnp.concatenate([last_rows, other_rows], axis=0)
    row_order = place
    if output_weight.shape[0] != width:
        wanted = jnp.arange(peers) ^ place
        shards = columns.reshape((peers,) + output_weight.shape)
        columns = shards[wanted // PAIR + wanted % PAIR * (peers // PAIR)].reshape(columns.shape)
        row_order = jnp.full_like(place, -1)
    columns_across = flipped(columns, "grp", 2)
    mixed = attend_finish(meta, ranges, queries, *bounds, pairs, before, after, edges, rows)
    last_weights = [columns, flipped(columns, "grp", 1)]
    last_weights += [columns_across, flipped(columns_across, "grp", 1)]
    parts = [mixed[0]] + [
        lax.ppermute(
            mixed[distance],
            ("tok", "grp"),
            [(source, source ^ distance) for source in range(flat)],
        )
        for distance in range(1, blocks)
    ]
    output_meta = jnp.stack([member, row_order]).astype(jnp.int32)
    attended = output_projection(output_meta, parts, last_weights)
    cache_pages = unpack(own_row, other_row).reshape(
        peers * capacity, 2 * PAGE * model_width
    )
    return attended, cache_pages


def solution(mesh):
    placed = (
        P(("tok", "grp"), None),
        P(),
        P("tok", "grp"),
        P("tok", "grp"),
        P(),
        P(("tok", "grp"), None),
    )
    return jax.shard_map(
        per_device,
        mesh=mesh,
        in_specs=placed,
        out_specs=(P(("tok", "grp"), None), P(("tok", "grp"), None)),
        check_vma=False,
    )
```

```python
import functools
import math

import jax
import jax.numpy as jnp
from jax import lax
from jax.experimental import pallas as pl
from jax.experimental.pallas import tpu as pltpu
from jax.sharding import PartitionSpec as P

H = 16
SPAN = 1024
PAGE = 4
HEAD_DIM = 64

NEG_FILL = -1e30
ROPE_BASE = 160000.0
EPSILON = 1e-05
TILE = 256
PARTS = 3
PAIR = 2
ONES_ROWS = 16
HEAD_ROWS = HEAD_DIM + ONES_ROWS
EXTRA_ROWS = 16
KEYS = 512
SCALE = HEAD_DIM ** (-0.5) * math.log2(math.e)
VMEM_LIMIT = 60 * 1024 * 1024
PARAMS = pltpu.CompilerParams(vmem_limit_bytes=VMEM_LIMIT)


def flipped(value, axis, bit):
    count = lax.axis_size(axis)
    return lax.ppermute(value, axis, [(source, source ^ bit) for source in range(count)])


def shifted(value, axis, steps):
    count = lax.axis_size(axis)
    initial, last = (max(0, -steps), min(count, count - steps))
    return lax.ppermute(value, axis, [(source, source + steps) for source in range(initial, last)])


def norm_kernel(capacity, tokens, gain, owner_row, normed, owners):
    rows = tokens.shape[0]
    values = tokens[...].astype(jnp.float32)
    centred = values - jnp.mean(values, axis=-1, keepdims=True)
    spread = jnp.mean(jnp.square(centred), axis=-1, keepdims=True)
    normed[:rows, :] = (centred * lax.rsqrt(spread + EPSILON) * gain[...]).astype(jnp.bfloat16)
    pages = owner_row.shape[1]
    owners[...] = jnp.full(owners.shape, -1.0, jnp.float32)
    owners[:1, :pages] = owner_row[...].astype(jnp.float32)
    lanes = owners.shape[1]
    across = jnp.broadcast_to(owners[:1, :], (lanes, lanes))
    earlier = lax.broadcasted_iota(jnp.int32, (lanes, lanes), 0) < lax.broadcasted_iota(
        jnp.int32, (lanes, lanes), 1
    )
    same = (across.T == across) & earlier
    ranks = jnp.sum(jnp.where(same, 1.0, 0.0), axis=0, keepdims=True)
    slots = owners[:1, :] * capacity + ranks
    normed[rows:, :] = jnp.zeros((EXTRA_ROWS, normed.shape[1]), jnp.bfloat16)
    normed[rows:, :lanes] = jnp.broadcast_to(slots, (EXTRA_ROWS, lanes)).astype(jnp.bfloat16)


def layer_norm(tokens, gain, owners, capacity):
    rows, width = tokens.shape
    lanes = -(-owners.shape[0] // 128) * 128
    return pl.pallas_call(
        functools.partial(norm_kernel, capacity),
        out_shape=jax.ShapeDtypeStruct((rows + EXTRA_ROWS, width), jnp.bfloat16),
        scratch_shapes=[pltpu.VMEM((8, lanes), jnp.float32)],
        compiler_params=PARAMS,
        name="layer_norm",
    )(tokens, gain, owners[None, :])


def project_kernel(first, layout, weight_count, peers, capacity, meta, *refs):
    operands = 1 + max(entry[0] for pieces in layout for entry in pieces)
    tokens = refs[:operands]
    weights = refs[operands : operands + weight_count]
    cosine, sine = refs[operands + weight_count : operands + weight_count + 2]
    query_out, pair_out, send_out, blocks, weight, page_source, sems = refs[-7:]
    step = pl.program_id(0)
    steps = len(layout)
    rows = query_out.shape[0]
    width = query_out.shape[1]
    shard = weights[0].shape[0] // 2

    def arrivals(number):
        return [
            pltpu.make_async_copy(
                tokens[operand],
                blocks.at[number, pl.ds(offset, count), :],
                sems.at[number, place],
            )
            for place, (operand, offset, count) in enumerate(layout[number])
        ]

    @pl.when(step == 0)
    def _():
        for number in range(steps):
            for copy in arrivals(number):
                copy.start()
        for plane in range(weight_count):
            for low in range(2):
                row = pl.multiple_of((meta[1] ^ (2 * plane + low)) * shard, shard)
                for number in range(PARTS):
                    column = pl.multiple_of(meta[2 + number] * width, width)
                    weight[pl.ds(row, shard), number * width : (number + 1) * width] = weights[
                        plane
                    ][low * shard : (low + 1) * shard, pl.ds(column, width)]

    for number in range(steps):

        @pl.when(step == number)
        def _():
            for copy in arrivals(number):
                copy.wait()

    joined = jnp.dot(blocks[step, :rows, :], weight[...], preferred_element_type=jnp.float32)
    cosines = jnp.concatenate([cosine[...]] * 4, axis=0).T
    sines = jnp.concatenate([-sine[...], sine[...]] * 2, axis=0).T
    first_half = lax.rem(lax.broadcasted_iota(jnp.int32, (rows, width), 1), HEAD_DIM) < (
        HEAD_DIM // 2
    )

    def rotate(values):
        partner = jnp.where(
            first_half,
            pltpu.roll(values, width - HEAD_DIM // 2, 1),
            pltpu.roll(values, HEAD_DIM // 2, 1),
        )
        return (values * cosines + partner * sines).astype(jnp.bfloat16)

    query_out[...] = rotate(joined[:, :width])
    keys = rotate(joined[:, width : 2 * width])
    values = joined[:, 2 * width :].astype(jnp.bfloat16)
    pair_out[:, :width] = keys
    pair_out[:, width:] = values
    page_source[0] = keys.astype(jnp.float32)
    page_source[1] = values.astype(jnp.float32)

    pages = rows // PAGE
    slot_count = peers * capacity
    slots = blocks[step, rows : rows + EXTRA_ROWS, :128].astype(jnp.float32)[:1, :pages]
    chosen = (
        lax.broadcasted_iota(jnp.int32, (slot_count, pages), 0).astype(jnp.float32) == slots
    ).astype(jnp.bfloat16)
    for turn in range(PAGE):
        page_part = jnp.concatenate(
            [
                page_source[half, pl.ds(turn, pages, stride=PAGE), :].astype(jnp.bfloat16)
                for half in range(2)
            ],
            axis=1,
        )
        placed = jnp.dot(chosen, page_part, preferred_element_type=jnp.float32)
        columns = slice(turn * 2 * width, (turn + 1) * 2 * width)
        for peer in range(peers):
            send_out[peer, 0, :, columns] = placed[
                peer * capacity : (peer + 1) * capacity
            ].astype(jnp.bfloat16)


def project(meta, first, layout, operands, weights, cosine, sine, rows, blocks, peers, capacity, into):
    steps = len(layout)
    model_width = operands[0].shape[1]
    group_rows = rows * blocks
    width = model_width // blocks
    members = blocks // PAIR
    whole = lambda shape: pl.BlockSpec(shape, lambda i, m: (0,) * len(shape))
    place = lambda i, m: m[0] ^ (first + i)
    table = pl.BlockSpec((HEAD_DIM // 2, rows), lambda i, m: (0, place(i, m)))
    send_shape = (peers, members, capacity, 2 * PAGE * width)
    return pl.pallas_call(
        functools.partial(project_kernel, first, layout, len(weights), peers, capacity),
        grid_spec=pltpu.PrefetchScalarGridSpec(
            num_scalar_prefetch=1,
            grid=(steps,),
            in_specs=[pl.BlockSpec(memory_space=pl.ANY)] * len(operands)
            + [whole(weights[0].shape)] * len(weights)
            + [table, table]
            + [pl.BlockSpec(memory_space=pl.ANY)] * len(into),
            out_specs=[
                pl.BlockSpec((rows, width), lambda i, m: (place(i, m), 0)),
                pl.BlockSpec((rows, 2 * width), lambda i, m: (place(i, m), 0)),
                pl.BlockSpec(
                    (peers, 1) + send_shape[2:], lambda i, m: (0, place(i, m) % members, 0, 0)
                ),
            ],
            scratch_shapes=[
                pltpu.VMEM((steps, rows + EXTRA_ROWS, model_width), jnp.bfloat16),
                pltpu.VMEM((model_width, PARTS * width), jnp.bfloat16),
                pltpu.VMEM((2, rows, width), jnp.float32),
                pltpu.SemaphoreType.DMA((steps, 2)),
            ],
        ),
        out_shape=[
            jax.ShapeDtypeStruct((group_rows, width), jnp.bfloat16),
            jax.ShapeDtypeStruct((group_rows, 2 * width), jnp.bfloat16),
            jax.ShapeDtypeStruct(send_shape, jnp.bfloat16),
        ],
        input_output_aliases={
            1 + len(operands) + len(weights) + 2 + number: number for number in range(len(into))
        },
        compiler_params=PARAMS,
        cost_estimate=pl.CostEstimate(
            flops=16 * steps * rows * model_width * PARTS * width,
            bytes_accessed=(3 * steps) << 19,
            transcendentals=0,
        ),
        name="project",
    )(meta, *operands, *weights, cosine, sine, *into)


def mask_heads(queries, masked):
    turned = queries[...].T
    head_of_row = lax.broadcasted_iota(jnp.int32, turned.shape, 0) // HEAD_DIM
    for head in range(masked.shape[0]):
        masked[head] = jnp.where(head_of_row == head, turned, jnp.zeros((), jnp.bfloat16))


def with_ones(values):
    turned = values.T
    ones = jnp.ones((ONES_ROWS, values.shape[0]), values.dtype)
    rows = []
    for head in range(values.shape[1] // HEAD_DIM):
        rows += [turned[head * HEAD_DIM : (head + 1) * HEAD_DIM], ones]
    return jnp.concatenate(rows, axis=0)


def sweep(jobs, peaks):
    plans = []
    steps = 0
    for begin, end, base, pairs, values_of, masked, starts, ends, total in jobs:
        held = pairs.shape[0] // TILE
        begin, end = jnp.maximum(begin, base), jnp.minimum(end, base + held)
        last = jnp.minimum(ends, end * TILE)
        steps = jnp.maximum(steps, (end - begin + KEYS // TILE - 1) // (KEYS // TILE))
        plans.append((begin, base, held, pairs, values_of, masked, starts, last, total))

    def one(number, peaks):
        new_peaks = []
        for plan, old_peaks in zip(plans, peaks):
            begin, base, held, pairs, values_of, masked, starts, last, total = plan
            wanted = begin + number * (KEYS // TILE)
            block = jnp.minimum(wanted, base + held - KEYS // TILE)
            row = pl.multiple_of((block - base) * TILE, TILE)
            keys = pairs[pl.ds(row, KEYS), : pairs.shape[1] // 2]
            values = values_of(row)
            index = block * TILE + lax.broadcasted_iota(jnp.int32, (KEYS, TILE), 0)
            allowed = (index >= jnp.maximum(starts, wanted * TILE)) & (index < last)
            job_peaks = []
            for head, old_peak in enumerate(old_peaks):
                scores = jnp.dot(keys, masked[head], preferred_element_type=jnp.float32)
                scores = jnp.where(allowed, scores * SCALE, NEG_FILL)
                peak = jnp.maximum(old_peak, jnp.max(scores, axis=0, keepdims=True))
                fade = jnp.exp2(old_peak - peak)
                weights = jnp.exp2(scores - peak).astype(jnp.bfloat16)
                own = slice(head * HEAD_ROWS, (head + 1) * HEAD_ROWS)
                total[own, :] = total[own, :] * fade + jnp.dot(
                    values[own, :], weights, preferred_element_type=jnp.float32
                )
                job_peaks.append(peak)
            new_peaks.append(tuple(job_peaks))
        return tuple(new_peaks)

    return lax.fori_loop(0, steps, one, peaks)


def fresh_peaks(heads):
    return tuple(jnp.full((1, TILE), NEG_FILL, jnp.float32) for _ in range(heads))


def edge_kernel(edge, meta, ranges, *refs):
    rows, pairs, outs, (masked, values) = refs[:6], refs[6], refs[7:11], refs[11:]
    step = pl.program_id(0)
    width = rows[0].shape[1]
    heads = width // HEAD_DIM
    tiles = pairs.shape[0] // TILE

    @pl.when(step == 0)
    def _():
        for number in range(tiles):
            own = slice(number * TILE, (number + 1) * TILE)
            values[:, own] = with_ones(pairs[own, width:])

    jobs = []
    for side in range(2):
        tile = step + side * (tiles - edge)
        queries, starts, ends = rows[3 * side : 3 * side + 3]
        mask_heads(queries, masked.at[side])
        total = outs[side]
        total[...] = jnp.zeros_like(total)
        jobs.append(
            (
                ranges[0, 2 * tile],
                ranges[0, 2 * tile + 1],
                edge,
                pairs,
                lambda row: values[:, pl.ds(row, KEYS)],
                masked.at[side],
                starts[...],
                ends[...],
                total.at[0],
            )
        )
    peaks = sweep(jobs, (fresh_peaks(heads), fresh_peaks(heads)))
    for side in range(2):
        for head in range(heads):
            outs[2 + side][0, head : head + 1, :] = peaks[side][head]


def finish_kernel(edge, meta, ranges, *refs):
    rows, pairs, halos, held, held_peaks = refs[:6], refs[6], refs[7:9], refs[9:11], refs[11:13]
    outs, (masked, sums, peaks_held, mixed) = refs[13:-4], refs[-4:]
    held_steps = edge
    step = pl.program_id(0)
    width = rows[0].shape[1]
    heads = width // HEAD_DIM
    tiles = pairs.shape[0] // TILE
    places = tile_places(step, edge, tiles)

    def jobs_on(keys, bases):
        jobs = []
        for side in range(2):
            queries, starts, ends = rows[3 * side : 3 * side + 3]
            mask_heads(queries, masked.at[side])
            jobs.append(
                (
                    ranges[0, 2 * places[side]],
                    ranges[0, 2 * places[side] + 1],
                    bases[side],
                    keys[side],
                    lambda row, held=keys[side]: with_ones(held[pl.ds(row, KEYS), width:]),
                    masked.at[side],
                    starts[...],
                    ends[...],
                    sums.at[side],
                )
            )
        return jobs

    @pl.when(step < held_steps)
    def _():
        for side in range(2):
            sums[side] = held[side][0]
            peaks_held[side] = held_peaks[side][0]

    @pl.when(step >= held_steps)
    def _():
        sums[...] = jnp.zeros_like(sums)
        peaks = sweep(jobs_on((pairs, pairs), (edge, edge)), (fresh_peaks(heads),) * 2)
        for side in range(2):
            for head in range(heads):
                peaks_held[side, head : head + 1, :] = peaks[side][head]

    reaches_back = ranges[0, 2 * places[0]] < edge
    reaches_ahead = ranges[0, 2 * places[1] + 1] > edge + tiles

    @pl.when((step < edge) & (reaches_back | reaches_ahead))
    def _():
        peaks = tuple(
            tuple(peaks_held[side, head : head + 1, :] for head in range(heads))
            for side in range(2)
        )
        sweep(jobs_on(halos, (0, edge + tiles)), peaks)

    for side in range(2):
        parts = []
        for head in range(heads):
            row = head * HEAD_ROWS
            parts.append(
                sums[side, row : row + HEAD_DIM, :]
                / sums[side, row + HEAD_DIM : row + HEAD_DIM + 1, :]
            )
        tile_rows = pl.ds(pl.multiple_of(places[side] * TILE, TILE), TILE)
        mixed[tile_rows, :] = jnp.concatenate(parts, axis=0).T.astype(jnp.bfloat16)

    @pl.when(step == pl.num_programs(0) - 1)
    def _():
        count = outs[0].shape[0]
        for distance, out in enumerate(outs):
            out[...] = mixed[pl.ds(pl.multiple_of((meta[0] ^ distance) * count, 128), count), :]


def tile_places(step, edge, tiles):
    middle = edge + 2 * (step - edge)
    return (
        jnp.where(step < edge, step, middle),
        jnp.where(step < edge, tiles - edge + step, middle + 1),
    )


def attend_specs(width, edge, tiles):
    specs = []
    for side in range(2):
        place = lambda i, side=side: tile_places(i, edge, tiles)[side]
        specs.append(pl.BlockSpec((TILE, width), lambda i, m, r, place=place: (place(i), 0)))
        specs += [pl.BlockSpec((1, TILE), lambda i, m, r, place=place: (0, place(i)))] * 2
    return specs + [pl.BlockSpec((tiles * TILE, 2 * width), lambda i, m, r: (0, 0))]


def attend_edges(meta, ranges, queries, starts, ends, pairs):
    group_rows, width = queries.shape
    heads = width // HEAD_DIM
    tiles, edge = group_rows // TILE, SPAN // TILE
    steps = edge
    shapes = [(steps, heads * HEAD_ROWS, TILE)] * 2 + [(steps, 8, TILE)] * 2
    return pl.pallas_call(
        functools.partial(edge_kernel, edge),
        grid_spec=pltpu.PrefetchScalarGridSpec(
            num_scalar_prefetch=2,
            grid=(steps,),
            in_specs=attend_specs(width, edge, tiles),
            out_specs=[pl.BlockSpec((1,) + shape[1:], lambda i, m, r: (i, 0, 0)) for shape in shapes],
            scratch_shapes=[
                pltpu.VMEM((2, heads, width, TILE), jnp.bfloat16),
                pltpu.VMEM((heads * HEAD_ROWS, group_rows), jnp.bfloat16),
            ],
        ),
        out_shape=[jax.ShapeDtypeStruct(shape, jnp.float32) for shape in shapes],
        compiler_params=PARAMS,
        cost_estimate=pl.CostEstimate(
            flops=16 * group_rows * 1024 * width,
            bytes_accessed=5 << 20,
            transcendentals=group_rows * 1024 * heads,
        ),
        name="attend_edges",
    )(meta, ranges, queries, starts, ends, queries, starts, ends, pairs)


def attend_finish(meta, ranges, queries, starts, ends, pairs, before, after, held, rows):
    group_rows, width = queries.shape
    heads = width // HEAD_DIM
    tiles, edge = group_rows // TILE, SPAN // TILE
    members = group_rows // rows
    return pl.pallas_call(
        functools.partial(finish_kernel, edge),
        grid_spec=pltpu.PrefetchScalarGridSpec(
            num_scalar_prefetch=2,
            grid=(edge + (tiles - 2 * edge) // 2,),
            in_specs=attend_specs(width, edge, tiles)
            + [pl.BlockSpec((SPAN, 2 * width), lambda i, m, r: (0, 0))] * 2
            + [
                pl.BlockSpec(
                    (1,) + part.shape[1:], lambda i, m, r: (jnp.minimum(i, edge - 1), 0, 0)
                )
                for part in held
            ],
            out_specs=[pl.BlockSpec((rows, width), lambda i, m, r: (0, 0))] * members,
            scratch_shapes=[
                pltpu.VMEM((2, heads, width, TILE), jnp.bfloat16),
                pltpu.VMEM((2, heads * HEAD_ROWS, TILE), jnp.float32),
                pltpu.VMEM((2, 8, TILE), jnp.float32),
                pltpu.VMEM((group_rows, width), jnp.bfloat16),
            ],
        ),
        out_shape=[jax.ShapeDtypeStruct((rows, width), jnp.bfloat16)] * members,
        compiler_params=PARAMS,
        cost_estimate=pl.CostEstimate(
            flops=16 * group_rows * 1024 * width,
            bytes_accessed=5 << 20,
            transcendentals=group_rows * 1024 * heads,
        ),
        name="attend_finish",
    )(meta, ranges, queries, starts, ends, queries, starts, ends, pairs, before, after, *held)


def output_kernel(members, meta, *refs):
    parts, weights, result, mixed = refs[:members], refs[members:-2], refs[-2], refs[-1]
    width = parts[0].shape[1]
    tile = weights[0].shape[1]
    for distance in range(members):
        source = meta[0] ^ distance
        head_pair = PAIR * (source % (members // PAIR)) + source // (members // PAIR)
        shard = head_pair ^ meta[1]
        shard = jnp.where(meta[1] < 0, head_pair, shard // PAIR + shard % PAIR * (members // PAIR))
        columns = pl.ds(pl.multiple_of(shard * width, width), width)
        mixed[:, columns] = parts[distance][...]
    for distance, weight in enumerate(weights):
        columns = pl.ds(pl.multiple_of((meta[0] % len(weights) ^ distance) * tile, tile), tile)
        result[:, columns] = jnp.dot(
            mixed[...], weight[...], preferred_element_type=jnp.float32
        ).astype(jnp.bfloat16)


def output_projection(meta, parts, weights):
    rows, width = parts[0].shape
    depth, tile = weights[0].shape
    whole = lambda shape: pl.BlockSpec(shape, lambda i, m: (0, 0))
    return pl.pallas_call(
        functools.partial(output_kernel, len(parts)),
        grid_spec=pltpu.PrefetchScalarGridSpec(
            num_scalar_prefetch=1,
            grid=(1,),
            in_specs=[whole(parts[0].shape)] * len(parts) + [whole((depth, tile))] * len(weights),
            out_specs=whole((rows, len(weights) * tile)),
            scratch_shapes=[pltpu.VMEM((rows, depth), jnp.bfloat16)],
        ),
        out_shape=jax.ShapeDtypeStruct((rows, len(weights) * tile), jnp.bfloat16),
        compiler_params=PARAMS,
        cost_estimate=pl.CostEstimate(
            flops=2 * rows * depth * len(weights) * tile,
            bytes_accessed=4 << 20,
            transcendentals=0,
        ),
        name="output_projection",
    )(meta, *parts, *weights)


def unpack_kernel(own_row, other_row, pages):
    _, pair, members, capacity, part = own_row.shape
    width = part // (2 * PAGE)
    for source in range(pair):
        for low in range(pair):
            received = own_row if source == low else other_row
            for high in range(members):
                for turn in range(2 * PAGE):
                    start = (turn * pair * members + PAIR * high + low) * width
                    pages[source, :, start : start + width] = received[
                        0, low, high, :, turn * width : (turn + 1) * width
                    ]


def unpack(own_row, other_row):
    planes, pair, members, capacity, part = own_row.shape
    block = pl.BlockSpec((1,) + own_row.shape[1:], lambda i: (i, 0, 0, 0, 0))
    return pl.pallas_call(
        unpack_kernel,
        grid=(planes,),
        in_specs=[block, block],
        out_specs=pl.BlockSpec((pair, capacity, pair * members * part), lambda i: (i, 0, 0)),
        out_shape=jax.ShapeDtypeStruct(
            (planes * pair, capacity, pair * members * part), jnp.bfloat16
        ),
        compiler_params=pltpu.CompilerParams(vmem_limit_bytes=24 * 1024 * 1024),
        cost_estimate=pl.CostEstimate(flops=0, bytes_accessed=6 << 20, transcendentals=0),
        name="unpack",
    )(own_row, other_row)


def rope_tables(positions):
    half_dim = HEAD_DIM // 2
    inverse = 1.0 / ROPE_BASE ** (jnp.arange(half_dim, dtype=jnp.float32) * 2.0 / HEAD_DIM)
    angles = inverse[:, None] * positions.astype(jnp.float32)[None, :]
    return jnp.cos(angles), jnp.sin(angles)


def bounds_kernel(ids, starts, ends, ranges):
    shape = (8, ids.shape[1])
    width = ids.shape[1]
    own = jnp.broadcast_to(ids[...], shape)
    index = lax.broadcasted_iota(jnp.int32, shape, 1)
    first = jnp.where((own != pltpu.roll(own, 1, 1)) | (index == 0), index, 0)
    after = jnp.where((own != pltpu.roll(own, width - 1, 1)) | (index == width - 1), index + 1, width)
    shift = 1
    while shift < SPAN:
        first = jnp.maximum(first, jnp.where(index >= shift, pltpu.roll(first, shift, 1), 0))
        after = jnp.minimum(
            after, jnp.where(index < width - shift, pltpu.roll(after, width - shift, 1), width)
        )
        shift *= 2
    rows = starts.shape[1]
    starts[...] = first[:1, SPAN : SPAN + rows]
    ends[...] = after[:1, SPAN : SPAN + rows]
    lane = lax.broadcasted_iota(jnp.int32, (rows, ranges.shape[1]), 0)
    entry = lax.broadcasted_iota(jnp.int32, (rows, ranges.shape[1]), 1)
    own_lane = entry // 2 * TILE + lax.rem(entry, 2) * (TILE - 1)
    chosen = jnp.where(lane == own_lane, 1.0, 0.0)
    odd = lax.rem(entry, 2) == 1
    begin = (first[:, SPAN : SPAN + rows] // TILE).astype(jnp.bfloat16)
    end = ((after[:, SPAN : SPAN + rows] + TILE - 1) // TILE).astype(jnp.bfloat16)
    from_begin = jnp.where(odd, 0.0, chosen).astype(jnp.bfloat16)
    from_end = jnp.where(odd, chosen, 0.0).astype(jnp.bfloat16)
    found = jnp.dot(begin, from_begin, preferred_element_type=jnp.float32) + jnp.dot(
        end, from_end, preferred_element_type=jnp.float32
    )
    ranges[...] = found[:1].astype(jnp.int32)


def document_bounds(window_ids, rows):
    return pl.pallas_call(
        bounds_kernel,
        out_shape=[jax.ShapeDtypeStruct((1, rows), jnp.int32)] * 2
        + [jax.ShapeDtypeStruct((1, 128), jnp.int32)],
        compiler_params=PARAMS,
        cost_estimate=pl.CostEstimate(flops=1 << 34, bytes_accessed=0, transcendentals=0),
        name="document_bounds",
    )(window_ids[None, :])


def per_device(tokens, norm_gain, input_weight, output_weight, segment_ids, page_owner):
    rows, model_width = tokens.shape
    peers, members = lax.axis_size("tok"), lax.axis_size("grp")
    place, column = lax.axis_index("tok"), lax.axis_index("grp")
    low = place % PAIR
    blocks = PAIR * members
    member = low * members + column
    group_rows = rows * blocks
    width = model_width // blocks
    pages = rows // PAGE

    flat = peers * members
    owners = page_owner[:, 0]
    capacity = max(2, (2 * pages + peers - 1) // peers)
    halves = []
    for parity in range(PAIR):
        pieces = []
        for number in range(PARTS):
            start = number * PAIR * width
            choices = [input_weight[:, start : start + width], input_weight[:, start + width : start + 2 * width]]
            piece = jnp.where((low ^ parity) == 0, choices[0], choices[1])
            route = []
            for source in range(flat):
                row, column_from = divmod(source, members)
                target = (row ^ parity) * members + (PARTS * column_from + number) % members
                route.append((source, target))
            pieces.append(lax.ppermute(piece, ("tok", "grp"), route))
        halves.append(jnp.concatenate(pieces, axis=1))
    plane = jnp.concatenate(halves, axis=0)
    own = layer_norm(tokens, norm_gain[None, :], owners, capacity)
    own, plane = lax.optimization_barrier((own, plane))

    across, along = flipped(own, "grp", 2), flipped(own, "tok", 1)
    sibling = flipped(own, "grp", 1)
    planes = {0: plane}
    bit = peers // 2
    while bit > 1:
        planes[bit] = flipped(plane, "tok", bit)
        bit //= 2
    for distance in range(PAIR, peers, PAIR):
        if distance not in planes:
            step_bit = distance & -distance
            planes[distance] = flipped(planes[distance ^ step_bit], "tok", step_bit)
    weights = [planes[distance] for distance in range(0, peers, PAIR)]

    first_row = place // PAIR * group_rows
    padded_ids = jnp.concatenate(
        [
            jnp.full((SPAN,), -1, jnp.int32),
            segment_ids,
            jnp.full((SPAN,), 1 << 30, jnp.int32),
        ]
    )
    window_ids = lax.dynamic_slice_in_dim(padded_ids, first_row, group_rows + 2 * SPAN, 0)
    window_ids, plane = lax.optimization_barrier((window_ids, plane))
    *bounds, ranges = document_bounds(window_ids, group_rows)
    positions = SPAN + jnp.arange(group_rows, dtype=jnp.int32) - bounds[0][0]
    order = [(number * members + column) % PARTS for number in range(PARTS)]
    meta = jnp.stack([member, place] + order).astype(jnp.int32)
    cosine, sine = rope_tables(positions)
    last_rows = output_weight
    bit = PAIR
    while 4 * bit < peers:
        last_rows = jnp.concatenate([last_rows, flipped(last_rows, "tok", bit)], axis=0)
        bit *= 2
    other_rows = flipped(last_rows, "tok", bit)
    across, along, sibling, weights, last_rows, other_rows, cosine, sine, meta = (
        lax.optimization_barrier(
            (across, along, sibling, weights, last_rows, other_rows, cosine, sine, meta)
        )
    )
    last_rows = jnp.concatenate([last_rows, other_rows], axis=0)

    half, held = rows // 2, rows + EXTRA_ROWS
    corner = [flipped(across[:half], "tok", 1), flipped(along[half:], "grp", 2)]
    across_sibling = flipped(across, "grp", 1)
    along_sibling = flipped(along, "grp", 1)
    other_rows = flipped(last_rows, "tok", peers // 2)
    near_blocks = [own, sibling, across, across_sibling]
    near_layout = [[(number, 0, held)] for number in range(4)]
    far_layout = [[(0, 0, held)], [(1, 0, held)]]
    far_layout += [[(number, 0, half), (number + 1, half, held - half)] for number in (2, 4)]

    sizes = (weights, cosine, sine, rows, blocks, peers, capacity)

    def to_owners(send):
        received = lax.all_to_all(
            send.reshape((flat,) + send.shape[2:]),
            ("tok", "grp"),
            split_axis=0,
            concat_axis=0,
            tiled=True,
        )
        return received.reshape((peers // PAIR, PAIR, members) + send.shape[2:])

    queries, pairs, send = project(meta, 0, near_layout, near_blocks, *sizes, ())
    send, corner, along_sibling, last_rows, other_rows = lax.optimization_barrier(
        (send, corner, along_sibling, last_rows, other_rows)
    )
    own_row = to_owners(send)
    corner_sibling = [flipped(block, "grp", 1) for block in corner]
    far_blocks = [along, along_sibling] + corner + corner_sibling
    last_rows = jnp.concatenate([last_rows, other_rows], axis=0)
    queries, pairs, send = project(meta, 4, far_layout, far_blocks, *sizes, (queries, pairs))
    before = shifted(pairs[group_rows - SPAN :], "tok", PAIR)
    after = shifted(pairs[:SPAN], "tok", -PAIR)
    other_rows = flipped(last_rows, "tok", 1)
    across_rows = flipped(last_rows, "grp", 2)
    corner_rows = lax.ppermute(
        last_rows,
        ("tok", "grp"),
        [(source, source ^ (members + 2)) for source in range(flat)],
    )

    edges = attend_edges(meta, ranges, queries, *bounds, pairs)
    before, after, edges, last_rows, other_rows, across_rows, corner_rows, send = (
        lax.optimization_barrier(
            (before, after, edges, last_rows, other_rows, across_rows, corner_rows, send)
        )
    )
    other_row = to_owners(send)
    columns = [
        jnp.concatenate([last_rows, other_rows], axis=0),
        jnp.concatenate([across_rows, corner_rows], axis=0),
    ]
    row_order = place
    if output_weight.shape[0] != width:
        wanted = jnp.arange(peers) ^ place
        wanted = wanted // PAIR + wanted % PAIR * (peers // PAIR)
        shards = (peers,) + output_weight.shape
        columns = [part.reshape(shards)[wanted].reshape(part.shape) for part in columns]
        row_order = jnp.full_like(place, -1)
    mixed = attend_finish(meta, ranges, queries, *bounds, pairs, before, after, edges, rows)
    siblings = [flipped(part, "grp", 1) for part in columns]
    last_weights = [columns[0], siblings[0], columns[1], siblings[1]]
    parts = [mixed[0]] + [
        lax.ppermute(
            mixed[distance],
            ("tok", "grp"),
            [(source, source ^ distance) for source in range(flat)],
        )
        for distance in range(1, blocks)
    ]
    output_meta = jnp.stack([member, row_order]).astype(jnp.int32)
    attended = output_projection(output_meta, parts, last_weights)
    cache_pages = unpack(own_row, other_row).reshape(
        peers * capacity, 2 * PAGE * model_width
    )
    return attended, cache_pages


def solution(mesh):
    placed = (
        P(("tok", "grp"), None),
        P(),
        P("tok", "grp"),
        P("tok", "grp"),
        P(),
        P(("tok", "grp"), None),
    )
    return jax.shard_map(
        per_device,
        mesh=mesh,
        in_specs=placed,
        out_specs=(P(("tok", "grp"), None), P(("tok", "grp"), None)),
        check_vma=False,
    )
```

```python
import functools

import jax
import jax.numpy as jnp
from jax import lax
from jax.experimental import pallas as pl
from jax.experimental.pallas import tpu as pltpu
from jax.sharding import PartitionSpec as P

H = 16
SPAN = 1024
PAGE = 4
HEAD_DIM = 64

NEG_FILL = -1e30
ROPE_BASE = 160000.0
EPSILON = 1e-05
TILE = 256
PARTS = 3
PAIR = 2
ONES_ROWS = 16
HEAD_ROWS = HEAD_DIM + ONES_ROWS
EXTRA_ROWS = 16
KEYS = 512
SCALE = HEAD_DIM ** (-0.5)
VMEM_LIMIT = 60 * 1024 * 1024
PARAMS = pltpu.CompilerParams(vmem_limit_bytes=VMEM_LIMIT)


def flipped(value, axis, bit):
    count = lax.axis_size(axis)
    return lax.ppermute(value, axis, [(source, source ^ bit) for source in range(count)])


def shifted(value, axis, steps):
    count = lax.axis_size(axis)
    initial, last = (max(0, -steps), min(count, count - steps))
    return lax.ppermute(value, axis, [(source, source + steps) for source in range(initial, last)])


def norm_kernel(capacity, tokens, gain, owner_row, normed, owners):
    rows = tokens.shape[0]
    values = tokens[...].astype(jnp.float32)
    centred = values - jnp.mean(values, axis=-1, keepdims=True)
    spread = jnp.mean(jnp.square(centred), axis=-1, keepdims=True)
    normed[:rows, :] = (centred * lax.rsqrt(spread + EPSILON) * gain[...]).astype(jnp.bfloat16)
    pages = owner_row.shape[1]
    owners[...] = jnp.full(owners.shape, -1.0, jnp.float32)
    owners[:1, :pages] = owner_row[...].astype(jnp.float32)
    lanes = owners.shape[1]
    across = jnp.broadcast_to(owners[:1, :], (lanes, lanes))
    earlier = lax.broadcasted_iota(jnp.int32, (lanes, lanes), 0) < lax.broadcasted_iota(
        jnp.int32, (lanes, lanes), 1
    )
    same = (across.T == across) & earlier
    ranks = jnp.sum(jnp.where(same, 1.0, 0.0), axis=0, keepdims=True)
    slots = owners[:1, :] * capacity + ranks
    normed[rows:, :] = jnp.zeros((EXTRA_ROWS, normed.shape[1]), jnp.bfloat16)
    normed[rows:, :lanes] = jnp.broadcast_to(slots, (EXTRA_ROWS, lanes)).astype(jnp.bfloat16)


def layer_norm(tokens, gain, owners, capacity):
    rows, width = tokens.shape
    lanes = -(-owners.shape[0] // 128) * 128
    return pl.pallas_call(
        functools.partial(norm_kernel, capacity),
        out_shape=jax.ShapeDtypeStruct((rows + EXTRA_ROWS, width), jnp.bfloat16),
        scratch_shapes=[pltpu.VMEM((8, lanes), jnp.float32)],
        compiler_params=PARAMS,
        name="layer_norm",
    )(tokens, gain, owners[None, :])


def project_kernel(first, layout, weight_count, peers, capacity, meta, *refs):
    operands = 1 + max(entry[0] for pieces in layout for entry in pieces)
    tokens = refs[:operands]
    weights = refs[operands : operands + weight_count]
    cosine, sine = refs[operands + weight_count : operands + weight_count + 2]
    query_out, pair_out, send_out, blocks, weight, page_source, sems = refs[-7:]
    step = pl.program_id(0)
    steps = len(layout)
    rows = query_out.shape[0]
    width = query_out.shape[1]
    shard = weights[0].shape[0] // 2

    def arrivals(number):
        return [
            pltpu.make_async_copy(
                tokens[operand],
                blocks.at[number, pl.ds(offset, count), :],
                sems.at[number, place],
            )
            for place, (operand, offset, count) in enumerate(layout[number])
        ]

    @pl.when(step == 0)
    def _():
        for number in range(steps):
            for copy in arrivals(number):
                copy.start()
        for plane in range(weight_count):
            for low in range(2):
                row = pl.multiple_of((meta[1] ^ (2 * plane + low)) * shard, shard)
                for number in range(PARTS):
                    column = pl.multiple_of(meta[2 + number] * width, width)
                    weight[pl.ds(row, shard), number * width : (number + 1) * width] = weights[
                        plane
                    ][low * shard : (low + 1) * shard, pl.ds(column, width)]

    for number in range(steps):

        @pl.when(step == number)
        def _():
            for copy in arrivals(number):
                copy.wait()

    joined = jnp.dot(blocks[step, :rows, :], weight[...], preferred_element_type=jnp.float32)
    cosines = jnp.concatenate([cosine[...]] * 4, axis=0).T
    sines = jnp.concatenate([-sine[...], sine[...]] * 2, axis=0).T
    first_half = lax.rem(lax.broadcasted_iota(jnp.int32, (rows, width), 1), HEAD_DIM) < (
        HEAD_DIM // 2
    )

    def rotate(values):
        partner = jnp.where(
            first_half,
            pltpu.roll(values, width - HEAD_DIM // 2, 1),
            pltpu.roll(values, HEAD_DIM // 2, 1),
        )
        return (values * cosines + partner * sines).astype(jnp.bfloat16)

    query_out[...] = rotate(joined[:, :width]) * jnp.asarray(SCALE, jnp.bfloat16)
    keys = rotate(joined[:, width : 2 * width])
    values = joined[:, 2 * width :].astype(jnp.bfloat16)
    pair_out[:, :width] = keys
    pair_out[:, width:] = values
    page_source[0] = keys.astype(jnp.float32)
    page_source[1] = values.astype(jnp.float32)

    pages = rows // PAGE
    slot_count = peers * capacity
    slots = blocks[step, rows : rows + EXTRA_ROWS, :128].astype(jnp.float32)[:1, :pages]
    chosen = (
        lax.broadcasted_iota(jnp.int32, (slot_count, pages), 0).astype(jnp.float32) == slots
    ).astype(jnp.bfloat16)
    for turn in range(PAGE):
        page_part = jnp.concatenate(
            [
                page_source[half, pl.ds(turn, pages, stride=PAGE), :].astype(jnp.bfloat16)
                for half in range(2)
            ],
            axis=1,
        )
        placed = jnp.dot(chosen, page_part, preferred_element_type=jnp.float32)
        columns = slice(turn * 2 * width, (turn + 1) * 2 * width)
        for peer in range(peers):
            send_out[peer, 0, :, columns] = placed[
                peer * capacity : (peer + 1) * capacity
            ].astype(jnp.bfloat16)


def project(meta, first, layout, operands, weights, cosine, sine, rows, blocks, peers, capacity, into):
    steps = len(layout)
    model_width = operands[0].shape[1]
    group_rows = rows * blocks
    width = model_width // blocks
    members = blocks // PAIR
    whole = lambda shape: pl.BlockSpec(shape, lambda i, m: (0,) * len(shape))
    place = lambda i, m: m[0] ^ (first + i)
    table = pl.BlockSpec((HEAD_DIM // 2, rows), lambda i, m: (0, place(i, m)))
    send_shape = (peers, members, capacity, 2 * PAGE * width)
    return pl.pallas_call(
        functools.partial(project_kernel, first, layout, len(weights), peers, capacity),
        grid_spec=pltpu.PrefetchScalarGridSpec(
            num_scalar_prefetch=1,
            grid=(steps,),
            in_specs=[pl.BlockSpec(memory_space=pl.ANY)] * len(operands)
            + [whole(weights[0].shape)] * len(weights)
            + [table, table]
            + [pl.BlockSpec(memory_space=pl.ANY)] * len(into),
            out_specs=[
                pl.BlockSpec((rows, width), lambda i, m: (place(i, m), 0)),
                pl.BlockSpec((rows, 2 * width), lambda i, m: (place(i, m), 0)),
                pl.BlockSpec(
                    (peers, 1) + send_shape[2:], lambda i, m: (0, place(i, m) % members, 0, 0)
                ),
            ],
            scratch_shapes=[
                pltpu.VMEM((steps, rows + EXTRA_ROWS, model_width), jnp.bfloat16),
                pltpu.VMEM((model_width, PARTS * width), jnp.bfloat16),
                pltpu.VMEM((2, rows, width), jnp.float32),
                pltpu.SemaphoreType.DMA((steps, 2)),
            ],
        ),
        out_shape=[
            jax.ShapeDtypeStruct((group_rows, width), jnp.bfloat16),
            jax.ShapeDtypeStruct((group_rows, 2 * width), jnp.bfloat16),
            jax.ShapeDtypeStruct(send_shape, jnp.bfloat16),
        ],
        input_output_aliases={
            1 + len(operands) + len(weights) + 2 + number: number for number in range(len(into))
        },
        compiler_params=PARAMS,
        cost_estimate=pl.CostEstimate(
            flops=16 * steps * rows * model_width * PARTS * width,
            bytes_accessed=(3 * steps) << 19,
            transcendentals=0,
        ),
        name="project",
    )(meta, *operands, *weights, cosine, sine, *into)


def mask_heads(queries, masked):
    turned = queries[...].T
    head_of_row = lax.broadcasted_iota(jnp.int32, turned.shape, 0) // HEAD_DIM
    for head in range(masked.shape[0]):
        masked[head] = jnp.where(head_of_row == head, turned, jnp.zeros((), jnp.bfloat16))


def with_ones(values):
    turned = values.T
    ones = jnp.ones((ONES_ROWS, values.shape[0]), values.dtype)
    rows = []
    for head in range(values.shape[1] // HEAD_DIM):
        rows += [turned[head * HEAD_DIM : (head + 1) * HEAD_DIM], ones]
    return jnp.concatenate(rows, axis=0)


def sweep(jobs, peaks):
    plans = []
    steps = 0
    for begin, end, base, pairs, values_of, masked, starts, ends, total in jobs:
        held = pairs.shape[0] // TILE
        begin, end = jnp.maximum(begin, base), jnp.minimum(end, base + held)
        last = jnp.minimum(ends, end * TILE)
        steps = jnp.maximum(steps, (end - begin + KEYS // TILE - 1) // (KEYS // TILE))
        plans.append((begin, base, held, pairs, values_of, masked, starts, last, total))

    key_rows = lax.broadcasted_iota(jnp.int32, (KEYS, TILE), 0)

    def one(number, peaks):
        new_peaks = []
        for plan, old_peaks in zip(plans, peaks):
            begin, base, held, pairs, values_of, masked, starts, last, total = plan
            wanted = begin + number * (KEYS // TILE)
            block = jnp.minimum(wanted, base + held - KEYS // TILE)
            row = pl.multiple_of((block - base) * TILE, TILE)
            keys = pairs[pl.ds(row, KEYS), : pairs.shape[1] // 2]
            values = values_of(row)
            first_key = block * TILE
            allowed = (key_rows >= jnp.maximum(starts, wanted * TILE) - first_key) & (
                key_rows < last - first_key
            )
            job_peaks = []
            for head, old_peak in enumerate(old_peaks):
                scores = jnp.dot(keys, masked[head], preferred_element_type=jnp.float32)
                scores = jnp.where(allowed, scores, NEG_FILL)
                peak = jnp.maximum(old_peak, jnp.max(scores, axis=0, keepdims=True))
                fade = jnp.exp(old_peak - peak)
                weights = jnp.exp(scores - peak).astype(jnp.bfloat16)
                own = slice(head * HEAD_ROWS, (head + 1) * HEAD_ROWS)
                total[own, :] = total[own, :] * fade + jnp.dot(
                    values[own, :], weights, preferred_element_type=jnp.float32
                )
                job_peaks.append(peak)
            new_peaks.append(tuple(job_peaks))
        return tuple(new_peaks)

    return lax.fori_loop(0, steps, one, peaks)


def fresh_peaks(heads):
    return tuple(jnp.full((1, TILE), NEG_FILL, jnp.float32) for _ in range(heads))


def edge_kernel(edge, meta, ranges, *refs):
    rows, pairs, outs, (masked, values) = refs[:6], refs[6], refs[7:11], refs[11:]
    step = pl.program_id(0)
    width = rows[0].shape[1]
    heads = width // HEAD_DIM
    tiles = pairs.shape[0] // TILE

    @pl.when(step == 0)
    def _():
        for number in range(tiles):
            own = slice(number * TILE, (number + 1) * TILE)
            values[:, own] = with_ones(pairs[own, width:])

    jobs = []
    for side in range(2):
        tile = step + side * (tiles - edge)
        queries, starts, ends = rows[3 * side : 3 * side + 3]
        mask_heads(queries, masked.at[side])
        total = outs[side]
        total[...] = jnp.zeros_like(total)
        jobs.append(
            (
                ranges[0, 2 * tile],
                ranges[0, 2 * tile + 1],
                edge,
                pairs,
                lambda row: values[:, pl.ds(row, KEYS)],
                masked.at[side],
                starts[...],
                ends[...],
                total.at[0],
            )
        )
    peaks = sweep(jobs, (fresh_peaks(heads), fresh_peaks(heads)))
    for side in range(2):
        for head in range(heads):
            outs[2 + side][0, head : head + 1, :] = peaks[side][head]


def finish_kernel(edge, meta, ranges, *refs):
    rows, pairs, halos, held, held_peaks = refs[:6], refs[6], refs[7:9], refs[9:11], refs[11:13]
    outs, (masked, sums, peaks_held, mixed) = refs[13:-4], refs[-4:]
    held_steps = edge
    step = pl.program_id(0)
    width = rows[0].shape[1]
    heads = width // HEAD_DIM
    tiles = pairs.shape[0] // TILE
    places = tile_places(step, edge, tiles)

    def jobs_on(keys, bases):
        jobs = []
        for side in range(2):
            queries, starts, ends = rows[3 * side : 3 * side + 3]
            mask_heads(queries, masked.at[side])
            jobs.append(
                (
                    ranges[0, 2 * places[side]],
                    ranges[0, 2 * places[side] + 1],
                    bases[side],
                    keys[side],
                    lambda row, held=keys[side]: with_ones(held[pl.ds(row, KEYS), width:]),
                    masked.at[side],
                    starts[...],
                    ends[...],
                    sums.at[side],
                )
            )
        return jobs

    @pl.when(step < held_steps)
    def _():
        for side in range(2):
            sums[side] = held[side][0]
            peaks_held[side] = held_peaks[side][0]

    @pl.when(step >= held_steps)
    def _():
        sums[...] = jnp.zeros_like(sums)
        peaks = sweep(jobs_on((pairs, pairs), (edge, edge)), (fresh_peaks(heads),) * 2)
        for side in range(2):
            for head in range(heads):
                peaks_held[side, head : head + 1, :] = peaks[side][head]

    reaches_back = ranges[0, 2 * places[0]] < edge
    reaches_ahead = ranges[0, 2 * places[1] + 1] > edge + tiles

    @pl.when((step < edge) & (reaches_back | reaches_ahead))
    def _():
        peaks = tuple(
            tuple(peaks_held[side, head : head + 1, :] for head in range(heads))
            for side in range(2)
        )
        sweep(jobs_on(halos, (0, edge + tiles)), peaks)

    for side in range(2):
        parts = []
        for head in range(heads):
            row = head * HEAD_ROWS
            parts.append(
                sums[side, row : row + HEAD_DIM, :]
                / sums[side, row + HEAD_DIM : row + HEAD_DIM + 1, :]
            )
        tile_rows = pl.ds(pl.multiple_of(places[side] * TILE, TILE), TILE)
        mixed[tile_rows, :] = jnp.concatenate(parts, axis=0).T.astype(jnp.bfloat16)

    @pl.when(step == pl.num_programs(0) - 1)
    def _():
        count = outs[0].shape[0]
        for distance, out in enumerate(outs):
            out[...] = mixed[pl.ds(pl.multiple_of((meta[0] ^ distance) * count, 128), count), :]


def tile_places(step, edge, tiles):
    middle = edge + 2 * (step - edge)
    return (
        jnp.where(step < edge, step, middle),
        jnp.where(step < edge, tiles - edge + step, middle + 1),
    )


def attend_specs(width, edge, tiles):
    specs = []
    for side in range(2):
        place = lambda i, side=side: tile_places(i, edge, tiles)[side]
        specs.append(pl.BlockSpec((TILE, width), lambda i, m, r, place=place: (place(i), 0)))
        specs += [pl.BlockSpec((1, TILE), lambda i, m, r, place=place: (0, place(i)))] * 2
    return specs + [pl.BlockSpec((tiles * TILE, 2 * width), lambda i, m, r: (0, 0))]


def attend_edges(meta, ranges, queries, starts, ends, pairs):
    group_rows, width = queries.shape
    heads = width // HEAD_DIM
    tiles, edge = group_rows // TILE, SPAN // TILE
    steps = edge
    shapes = [(steps, heads * HEAD_ROWS, TILE)] * 2 + [(steps, 8, TILE)] * 2
    return pl.pallas_call(
        functools.partial(edge_kernel, edge),
        grid_spec=pltpu.PrefetchScalarGridSpec(
            num_scalar_prefetch=2,
            grid=(steps,),
            in_specs=attend_specs(width, edge, tiles),
            out_specs=[pl.BlockSpec((1,) + shape[1:], lambda i, m, r: (i, 0, 0)) for shape in shapes],
            scratch_shapes=[
                pltpu.VMEM((2, heads, width, TILE), jnp.bfloat16),
                pltpu.VMEM((heads * HEAD_ROWS, group_rows), jnp.bfloat16),
            ],
        ),
        out_shape=[jax.ShapeDtypeStruct(shape, jnp.float32) for shape in shapes],
        compiler_params=PARAMS,
        cost_estimate=pl.CostEstimate(
            flops=16 * group_rows * 1024 * width,
            bytes_accessed=5 << 20,
            transcendentals=group_rows * 1024 * heads,
        ),
        name="attend_edges",
    )(meta, ranges, queries, starts, ends, queries, starts, ends, pairs)


def attend_finish(meta, ranges, queries, starts, ends, pairs, before, after, held, rows):
    group_rows, width = queries.shape
    heads = width // HEAD_DIM
    tiles, edge = group_rows // TILE, SPAN // TILE
    members = group_rows // rows
    return pl.pallas_call(
        functools.partial(finish_kernel, edge),
        grid_spec=pltpu.PrefetchScalarGridSpec(
            num_scalar_prefetch=2,
            grid=(edge + (tiles - 2 * edge) // 2,),
            in_specs=attend_specs(width, edge, tiles)
            + [pl.BlockSpec((SPAN, 2 * width), lambda i, m, r: (0, 0))] * 2
            + [
                pl.BlockSpec(
                    (1,) + part.shape[1:], lambda i, m, r: (jnp.minimum(i, edge - 1), 0, 0)
                )
                for part in held
            ],
            out_specs=[pl.BlockSpec((rows, width), lambda i, m, r: (0, 0))] * members,
            scratch_shapes=[
                pltpu.VMEM((2, heads, width, TILE), jnp.bfloat16),
                pltpu.VMEM((2, heads * HEAD_ROWS, TILE), jnp.float32),
                pltpu.VMEM((2, 8, TILE), jnp.float32),
                pltpu.VMEM((group_rows, width), jnp.bfloat16),
            ],
        ),
        out_shape=[jax.ShapeDtypeStruct((rows, width), jnp.bfloat16)] * members,
        compiler_params=PARAMS,
        cost_estimate=pl.CostEstimate(
            flops=16 * group_rows * 1024 * width,
            bytes_accessed=5 << 20,
            transcendentals=group_rows * 1024 * heads,
        ),
        name="attend_finish",
    )(meta, ranges, queries, starts, ends, queries, starts, ends, pairs, before, after, *held)


def output_kernel(members, meta, *refs):
    parts, weights, result, mixed = refs[:members], refs[members:-2], refs[-2], refs[-1]
    width = parts[0].shape[1]
    tile = weights[0].shape[1]
    for distance in range(members):
        source = meta[0] ^ distance
        head_pair = PAIR * (source % (members // PAIR)) + source // (members // PAIR)
        shard = head_pair ^ meta[1]
        shard = jnp.where(meta[1] < 0, head_pair, shard // PAIR + shard % PAIR * (members // PAIR))
        columns = pl.ds(pl.multiple_of(shard * width, width), width)
        mixed[:, columns] = parts[distance][...]
    half = weights[0].shape[0]
    for distance in range(len(weights) // 2):
        columns = pl.ds(pl.multiple_of((meta[0] % (len(weights) // 2) ^ distance) * tile, tile), tile)
        result[:, columns] = (
            jnp.dot(
                mixed[:, :half], weights[2 * distance][...], preferred_element_type=jnp.float32
            )
            + jnp.dot(
                mixed[:, half:], weights[2 * distance + 1][...], preferred_element_type=jnp.float32
            )
        ).astype(jnp.bfloat16)


def output_projection(meta, parts, weights):
    rows, width = parts[0].shape
    half, tile = weights[0].shape
    depth = 2 * half
    columns = len(weights) // 2 * tile
    whole = lambda shape: pl.BlockSpec(shape, lambda i, m: (0, 0))
    return pl.pallas_call(
        functools.partial(output_kernel, len(parts)),
        grid_spec=pltpu.PrefetchScalarGridSpec(
            num_scalar_prefetch=1,
            grid=(1,),
            in_specs=[whole(parts[0].shape)] * len(parts) + [whole((half, tile))] * len(weights),
            out_specs=whole((rows, columns)),
            scratch_shapes=[pltpu.VMEM((rows, depth), jnp.bfloat16)],
        ),
        out_shape=jax.ShapeDtypeStruct((rows, columns), jnp.bfloat16),
        compiler_params=PARAMS,
        cost_estimate=pl.CostEstimate(
            flops=2 * rows * depth * columns,
            bytes_accessed=4 << 20,
            transcendentals=0,
        ),
        name="output_projection",
    )(meta, *parts, *weights)


def unpack_kernel(own_row, other_row, pages):
    _, pair, members, capacity, part = own_row.shape
    width = part // (2 * PAGE)
    for source in range(pair):
        for low in range(pair):
            received = own_row if source == low else other_row
            for high in range(members):
                for turn in range(2 * PAGE):
                    start = (turn * pair * members + PAIR * high + low) * width
                    pages[source, :, start : start + width] = received[
                        0, low, high, :, turn * width : (turn + 1) * width
                    ]


def unpack(own_row, other_row):
    planes, pair, members, capacity, part = own_row.shape
    block = pl.BlockSpec((1,) + own_row.shape[1:], lambda i: (i, 0, 0, 0, 0))
    return pl.pallas_call(
        unpack_kernel,
        grid=(planes,),
        in_specs=[block, block],
        out_specs=pl.BlockSpec((pair, capacity, pair * members * part), lambda i: (i, 0, 0)),
        out_shape=jax.ShapeDtypeStruct(
            (planes * pair, capacity, pair * members * part), jnp.bfloat16
        ),
        compiler_params=pltpu.CompilerParams(vmem_limit_bytes=24 * 1024 * 1024),
        cost_estimate=pl.CostEstimate(flops=0, bytes_accessed=6 << 20, transcendentals=0),
        name="unpack",
    )(own_row, other_row)


def rope_tables(positions):
    half_dim = HEAD_DIM // 2
    inverse = 1.0 / ROPE_BASE ** (jnp.arange(half_dim, dtype=jnp.float32) * 2.0 / HEAD_DIM)
    angles = inverse[:, None] * positions.astype(jnp.float32)[None, :]
    return jnp.cos(angles), jnp.sin(angles)


def bounds_kernel(ids, starts, ends, ranges):
    shape = (8, ids.shape[1])
    width = ids.shape[1]
    own = jnp.broadcast_to(ids[...], shape)
    index = lax.broadcasted_iota(jnp.int32, shape, 1)
    first = jnp.where((own != pltpu.roll(own, 1, 1)) | (index == 0), index, 0)
    after = jnp.where((own != pltpu.roll(own, width - 1, 1)) | (index == width - 1), index + 1, width)
    shift = 1
    while shift < SPAN:
        first = jnp.maximum(first, jnp.where(index >= shift, pltpu.roll(first, shift, 1), 0))
        after = jnp.minimum(
            after, jnp.where(index < width - shift, pltpu.roll(after, width - shift, 1), width)
        )
        shift *= 2
    rows = starts.shape[1]
    starts[...] = first[:1, SPAN : SPAN + rows]
    ends[...] = after[:1, SPAN : SPAN + rows]
    lane = lax.broadcasted_iota(jnp.int32, (rows, ranges.shape[1]), 0)
    entry = lax.broadcasted_iota(jnp.int32, (rows, ranges.shape[1]), 1)
    own_lane = entry // 2 * TILE + lax.rem(entry, 2) * (TILE - 1)
    chosen = jnp.where(lane == own_lane, 1.0, 0.0)
    odd = lax.rem(entry, 2) == 1
    begin = (first[:, SPAN : SPAN + rows] // TILE).astype(jnp.bfloat16)
    end = ((after[:, SPAN : SPAN + rows] + TILE - 1) // TILE).astype(jnp.bfloat16)
    from_begin = jnp.where(odd, 0.0, chosen).astype(jnp.bfloat16)
    from_end = jnp.where(odd, chosen, 0.0).astype(jnp.bfloat16)
    found = jnp.dot(begin, from_begin, preferred_element_type=jnp.float32) + jnp.dot(
        end, from_end, preferred_element_type=jnp.float32
    )
    ranges[...] = found[:1].astype(jnp.int32)


def document_bounds(window_ids, rows):
    return pl.pallas_call(
        bounds_kernel,
        out_shape=[jax.ShapeDtypeStruct((1, rows), jnp.int32)] * 2
        + [jax.ShapeDtypeStruct((1, 128), jnp.int32)],
        compiler_params=PARAMS,
        cost_estimate=pl.CostEstimate(flops=1 << 34, bytes_accessed=0, transcendentals=0),
        name="document_bounds",
    )(window_ids[None, :])


def per_device(tokens, norm_gain, input_weight, output_weight, segment_ids, page_owner):
    rows, model_width = tokens.shape
    peers, members = lax.axis_size("tok"), lax.axis_size("grp")
    place, column = lax.axis_index("tok"), lax.axis_index("grp")
    low = place % PAIR
    blocks = PAIR * members
    member = low * members + column
    group_rows = rows * blocks
    width = model_width // blocks
    pages = rows // PAGE

    flat = peers * members
    owners = page_owner[:, 0]
    capacity = max(2, (2 * pages + peers - 1) // peers)
    halves = []
    for parity in range(PAIR):
        pieces = []
        for number in range(PARTS):
            start = number * PAIR * width
            choices = [input_weight[:, start : start + width], input_weight[:, start + width : start + 2 * width]]
            piece = jnp.where((low ^ parity) == 0, choices[0], choices[1])
            route = []
            for source in range(flat):
                row, column_from = divmod(source, members)
                target = (row ^ parity) * members + (PARTS * column_from + number) % members
                route.append((source, target))
            pieces.append(lax.ppermute(piece, ("tok", "grp"), route))
        halves.append(jnp.concatenate(pieces, axis=1))
    plane = jnp.concatenate(halves, axis=0)
    own = layer_norm(tokens, norm_gain[None, :], owners, capacity)
    own, plane = lax.optimization_barrier((own, plane))

    across, along = flipped(own, "grp", 2), flipped(own, "tok", 1)
    sibling = flipped(own, "grp", 1)
    planes = {0: plane}
    bit = peers // 2
    while bit > 1:
        planes[bit] = flipped(plane, "tok", bit)
        bit //= 2
    for distance in range(PAIR, peers, PAIR):
        if distance not in planes:
            step_bit = distance & -distance
            planes[distance] = flipped(planes[distance ^ step_bit], "tok", step_bit)
    weights = [planes[distance] for distance in range(0, peers, PAIR)]

    first_row = place // PAIR * group_rows
    padded_ids = jnp.concatenate(
        [
            jnp.full((SPAN,), -1, jnp.int32),
            segment_ids,
            jnp.full((SPAN,), 1 << 30, jnp.int32),
        ]
    )
    window_ids = lax.dynamic_slice_in_dim(padded_ids, first_row, group_rows + 2 * SPAN, 0)
    window_ids, plane = lax.optimization_barrier((window_ids, plane))
    *bounds, ranges = document_bounds(window_ids, group_rows)
    positions = SPAN + jnp.arange(group_rows, dtype=jnp.int32) - bounds[0][0]
    order = [(number * members + column) % PARTS for number in range(PARTS)]
    meta = jnp.stack([member, place] + order).astype(jnp.int32)
    cosine, sine = rope_tables(positions)
    last_rows = output_weight
    bit = PAIR
    while 4 * bit < peers:
        last_rows = jnp.concatenate([last_rows, flipped(last_rows, "tok", bit)], axis=0)
        bit *= 2
    other_rows = flipped(last_rows, "tok", bit)
    across, along, sibling, weights, last_rows, other_rows, cosine, sine, meta = (
        lax.optimization_barrier(
            (across, along, sibling, weights, last_rows, other_rows, cosine, sine, meta)
        )
    )
    last_rows = jnp.concatenate([last_rows, other_rows], axis=0)

    half, held = rows // 2, rows + EXTRA_ROWS
    corner = [flipped(across[:half], "tok", 1), flipped(along[half:], "grp", 2)]
    across_sibling = flipped(across, "grp", 1)
    along_sibling = flipped(along, "grp", 1)
    other_rows = flipped(last_rows, "tok", peers // 2)
    near_blocks = [own, sibling, across, across_sibling]
    near_layout = [[(number, 0, held)] for number in range(4)]
    far_layout = [[(0, 0, held)], [(1, 0, held)]]
    far_layout += [[(number, 0, half), (number + 1, half, held - half)] for number in (2, 4)]

    sizes = (weights, cosine, sine, rows, blocks, peers, capacity)

    def to_owners(send):
        received = lax.all_to_all(
            send.reshape((flat,) + send.shape[2:]),
            ("tok", "grp"),
            split_axis=0,
            concat_axis=0,
            tiled=True,
        )
        return received.reshape((peers // PAIR, PAIR, members) + send.shape[2:])

    queries, pairs, send = project(meta, 0, near_layout, near_blocks, *sizes, ())
    send, corner, along_sibling, last_rows, other_rows = lax.optimization_barrier(
        (send, corner, along_sibling, last_rows, other_rows)
    )
    own_row = to_owners(send)
    corner_sibling = [flipped(block, "grp", 1) for block in corner]
    far_blocks = [along, along_sibling] + corner + corner_sibling
    last_rows = jnp.concatenate([last_rows, other_rows], axis=0)
    queries, pairs, send = project(meta, 4, far_layout, far_blocks, *sizes, (queries, pairs))
    before = shifted(pairs[group_rows - SPAN :], "tok", PAIR)
    after = shifted(pairs[:SPAN], "tok", -PAIR)
    other_rows = flipped(last_rows, "tok", 1)
    across_rows = flipped(last_rows, "grp", 2)
    corner_rows = lax.ppermute(
        last_rows,
        ("tok", "grp"),
        [(source, source ^ (members + 2)) for source in range(flat)],
    )

    edges = attend_edges(meta, ranges, queries, *bounds, pairs)
    before, after, edges, last_rows, other_rows, across_rows, corner_rows, send = (
        lax.optimization_barrier(
            (before, after, edges, last_rows, other_rows, across_rows, corner_rows, send)
        )
    )
    other_row = to_owners(send)
    columns = [last_rows, other_rows, across_rows, corner_rows]
    row_order = place
    if output_weight.shape[0] != width:
        wanted = jnp.arange(peers) ^ place
        wanted = wanted // PAIR + wanted % PAIR * (peers // PAIR)
        shards = (peers,) + output_weight.shape
        whole = [jnp.concatenate(columns[k : k + 2], axis=0) for k in (0, 2)]
        whole = [part.reshape(shards)[wanted].reshape(part.shape) for part in whole]
        columns = [part for both in whole for part in jnp.split(both, 2, axis=0)]
        row_order = jnp.full_like(place, -1)
    mixed = attend_finish(meta, ranges, queries, *bounds, pairs, before, after, edges, rows)
    siblings = [flipped(part, "grp", 1) for part in columns]
    last_weights = columns[:2] + siblings[:2] + columns[2:] + siblings[2:]
    parts = [mixed[0]] + [
        lax.ppermute(
            mixed[distance],
            ("tok", "grp"),
            [(source, source ^ distance) for source in range(flat)],
        )
        for distance in range(1, blocks)
    ]
    output_meta = jnp.stack([member, row_order]).astype(jnp.int32)
    attended = output_projection(output_meta, parts, last_weights)
    cache_pages = unpack(own_row, other_row).reshape(
        peers * capacity, 2 * PAGE * model_width
    )
    return attended, cache_pages


def solution(mesh):
    placed = (
        P(("tok", "grp"), None),
        P(),
        P("tok", "grp"),
        P("tok", "grp"),
        P(),
        P(("tok", "grp"), None),
    )
    return jax.shard_map(
        per_device,
        mesh=mesh,
        in_specs=placed,
        out_specs=(P(("tok", "grp"), None), P(("tok", "grp"), None)),
        check_vma=False,
    )
```

```python
import functools

import jax
import jax.numpy as jnp
from jax import lax
from jax.experimental import pallas as pl
from jax.experimental.pallas import tpu as pltpu
from jax.sharding import PartitionSpec as P

H = 16
SPAN = 1024
PAGE = 4
HEAD_DIM = 64

NEG_FILL = -1e30
ROPE_BASE = 160000.0
EPSILON = 1e-05
TILE = 256
PARTS = 3
PAIR = 2
ONES_ROWS = 16
HEAD_ROWS = HEAD_DIM + ONES_ROWS
EXTRA_ROWS = 16
KEYS = 512
SCALE = HEAD_DIM ** (-0.5)
VMEM_LIMIT = 60 * 1024 * 1024
PARAMS = pltpu.CompilerParams(vmem_limit_bytes=VMEM_LIMIT)


def flipped(value, axis, bit):
    count = lax.axis_size(axis)
    return lax.ppermute(value, axis, [(source, source ^ bit) for source in range(count)])


def shifted(value, axis, steps):
    count = lax.axis_size(axis)
    initial, last = (max(0, -steps), min(count, count - steps))
    return lax.ppermute(value, axis, [(source, source + steps) for source in range(initial, last)])


def norm_kernel(capacity, tokens, gain, owner_row, normed, owners):
    rows = tokens.shape[0]
    values = tokens[...].astype(jnp.float32)
    centred = values - jnp.mean(values, axis=-1, keepdims=True)
    spread = jnp.mean(jnp.square(centred), axis=-1, keepdims=True)
    normed[:rows, :] = (centred * lax.rsqrt(spread + EPSILON) * gain[...]).astype(jnp.bfloat16)
    pages = owner_row.shape[1]
    owners[...] = jnp.full(owners.shape, -1.0, jnp.float32)
    owners[:1, :pages] = owner_row[...].astype(jnp.float32)
    lanes = owners.shape[1]
    across = jnp.broadcast_to(owners[:1, :], (lanes, lanes))
    earlier = lax.broadcasted_iota(jnp.int32, (lanes, lanes), 0) < lax.broadcasted_iota(
        jnp.int32, (lanes, lanes), 1
    )
    same = (across.T == across) & earlier
    ranks = jnp.sum(jnp.where(same, 1.0, 0.0), axis=0, keepdims=True)
    slots = owners[:1, :] * capacity + ranks
    normed[rows:, :] = jnp.zeros((EXTRA_ROWS, normed.shape[1]), jnp.bfloat16)
    normed[rows:, :lanes] = jnp.broadcast_to(slots, (EXTRA_ROWS, lanes)).astype(jnp.bfloat16)


def layer_norm(tokens, gain, owners, capacity):
    rows, width = tokens.shape
    lanes = -(-owners.shape[0] // 128) * 128
    return pl.pallas_call(
        functools.partial(norm_kernel, capacity),
        out_shape=jax.ShapeDtypeStruct((rows + EXTRA_ROWS, width), jnp.bfloat16),
        scratch_shapes=[pltpu.VMEM((8, lanes), jnp.float32)],
        compiler_params=PARAMS,
        name="layer_norm",
    )(tokens, gain, owners[None, :])


def project_kernel(first, layout, weight_count, peers, capacity, meta, *refs):
    operands = 1 + max(entry[0] for pieces in layout for entry in pieces)
    tokens = refs[:operands]
    weights = refs[operands : operands + weight_count]
    cosine, sine = refs[operands + weight_count : operands + weight_count + 2]
    query_out, pair_out, send_out, blocks, weight, page_source, sems = refs[-7:]
    step = pl.program_id(0)
    steps = len(layout)
    rows = query_out.shape[0]
    width = query_out.shape[1]
    shard = weights[0].shape[0] // 2

    def arrivals(number):
        return [
            pltpu.make_async_copy(
                tokens[operand],
                blocks.at[number, pl.ds(offset, count), :],
                sems.at[number, place],
            )
            for place, (operand, offset, count) in enumerate(layout[number])
        ]

    @pl.when(step == 0)
    def _():
        for number in range(steps):
            for copy in arrivals(number):
                copy.start()
        for plane in range(weight_count):
            for low in range(2):
                row = pl.multiple_of((meta[1] ^ (2 * plane + low)) * shard, shard)
                for number in range(PARTS):
                    column = pl.multiple_of(meta[2 + number] * width, width)
                    weight[pl.ds(row, shard), number * width : (number + 1) * width] = weights[
                        plane
                    ][low * shard : (low + 1) * shard, pl.ds(column, width)]

    for number in range(steps):

        @pl.when(step == number)
        def _():
            for copy in arrivals(number):
                copy.wait()

    joined = jnp.dot(blocks[step, :rows, :], weight[...], preferred_element_type=jnp.float32)
    cosines = jnp.concatenate([cosine[...]] * 4, axis=0).T
    sines = jnp.concatenate([-sine[...], sine[...]] * 2, axis=0).T
    first_half = lax.rem(lax.broadcasted_iota(jnp.int32, (rows, width), 1), HEAD_DIM) < (
        HEAD_DIM // 2
    )

    def rotate(values):
        partner = jnp.where(
            first_half,
            pltpu.roll(values, width - HEAD_DIM // 2, 1),
            pltpu.roll(values, HEAD_DIM // 2, 1),
        )
        return (values * cosines + partner * sines).astype(jnp.bfloat16)

    query_out[...] = rotate(joined[:, :width]) * jnp.asarray(SCALE, jnp.bfloat16)
    keys = rotate(joined[:, width : 2 * width])
    values = joined[:, 2 * width :].astype(jnp.bfloat16)
    pair_out[:, :width] = keys
    pair_out[:, width:] = values
    page_source[0] = keys.astype(jnp.float32)
    page_source[1] = values.astype(jnp.float32)

    pages = rows // PAGE
    slot_count = peers * capacity
    slots = blocks[step, rows : rows + EXTRA_ROWS, :128].astype(jnp.float32)[:1, :pages]
    chosen = (
        lax.broadcasted_iota(jnp.int32, (slot_count, pages), 0).astype(jnp.float32) == slots
    ).astype(jnp.bfloat16)
    for turn in range(PAGE):
        page_part = jnp.concatenate(
            [
                page_source[half, pl.ds(turn, pages, stride=PAGE), :].astype(jnp.bfloat16)
                for half in range(2)
            ],
            axis=1,
        )
        placed = jnp.dot(chosen, page_part, preferred_element_type=jnp.float32)
        columns = slice(turn * 2 * width, (turn + 1) * 2 * width)
        for peer in range(peers):
            send_out[peer, 0, :, columns] = placed[
                peer * capacity : (peer + 1) * capacity
            ].astype(jnp.bfloat16)


def project(meta, first, layout, operands, weights, cosine, sine, rows, blocks, peers, capacity, into):
    steps = len(layout)
    model_width = operands[0].shape[1]
    group_rows = rows * blocks
    width = model_width // blocks
    members = blocks // PAIR
    whole = lambda shape: pl.BlockSpec(shape, lambda i, m: (0,) * len(shape))
    place = lambda i, m: m[0] ^ (first + i)
    table = pl.BlockSpec((HEAD_DIM // 2, rows), lambda i, m: (0, place(i, m)))
    send_shape = (peers, members, capacity, 2 * PAGE * width)
    return pl.pallas_call(
        functools.partial(project_kernel, first, layout, len(weights), peers, capacity),
        grid_spec=pltpu.PrefetchScalarGridSpec(
            num_scalar_prefetch=1,
            grid=(steps,),
            in_specs=[pl.BlockSpec(memory_space=pl.ANY)] * len(operands)
            + [whole(weights[0].shape)] * len(weights)
            + [table, table]
            + [pl.BlockSpec(memory_space=pl.ANY)] * len(into),
            out_specs=[
                pl.BlockSpec((rows, width), lambda i, m: (place(i, m), 0)),
                pl.BlockSpec((rows, 2 * width), lambda i, m: (place(i, m), 0)),
                pl.BlockSpec(
                    (peers, 1) + send_shape[2:], lambda i, m: (0, place(i, m) % members, 0, 0)
                ),
            ],
            scratch_shapes=[
                pltpu.VMEM((steps, rows + EXTRA_ROWS, model_width), jnp.bfloat16),
                pltpu.VMEM((model_width, PARTS * width), jnp.bfloat16),
                pltpu.VMEM((2, rows, width), jnp.float32),
                pltpu.SemaphoreType.DMA((steps, 2)),
            ],
        ),
        out_shape=[
            jax.ShapeDtypeStruct((group_rows, width), jnp.bfloat16),
            jax.ShapeDtypeStruct((group_rows, 2 * width), jnp.bfloat16),
            jax.ShapeDtypeStruct(send_shape, jnp.bfloat16),
        ],
        input_output_aliases={
            1 + len(operands) + len(weights) + 2 + number: number for number in range(len(into))
        },
        compiler_params=PARAMS,
        cost_estimate=pl.CostEstimate(
            flops=16 * steps * rows * model_width * PARTS * width,
            bytes_accessed=(3 * steps) << 19,
            transcendentals=0,
        ),
        name="project",
    )(meta, *operands, *weights, cosine, sine, *into)


def mask_heads(queries, masked):
    turned = queries[...].T
    head_of_row = lax.broadcasted_iota(jnp.int32, turned.shape, 0) // HEAD_DIM
    for head in range(masked.shape[0]):
        masked[head] = jnp.where(head_of_row == head, turned, jnp.zeros((), jnp.bfloat16))


def with_ones(values):
    turned = values.T
    ones = jnp.ones((ONES_ROWS, values.shape[0]), values.dtype)
    rows = []
    for head in range(values.shape[1] // HEAD_DIM):
        rows += [turned[head * HEAD_DIM : (head + 1) * HEAD_DIM], ones]
    return jnp.concatenate(rows, axis=0)


def sweep(jobs, peaks):
    plans = []
    steps = 0
    for begin, end, base, pairs, values_of, masked, starts, ends, total in jobs:
        held = pairs.shape[0] // TILE
        begin, end = jnp.maximum(begin, base), jnp.minimum(end, base + held)
        last = jnp.minimum(ends, end * TILE)
        steps = jnp.maximum(steps, (end - begin + KEYS // TILE - 1) // (KEYS // TILE))
        plans.append((begin, base, held, pairs, values_of, masked, starts, last, total))

    key_rows = lax.broadcasted_iota(jnp.int32, (KEYS, TILE), 0)

    def one(number, peaks):
        units = []
        for place, plan in enumerate(plans):
            begin, base, held, pairs, values_of, masked, starts, last, total = plan
            wanted = begin + number * (KEYS // TILE)
            block = jnp.minimum(wanted, base + held - KEYS // TILE)
            row = pl.multiple_of((block - base) * TILE, TILE)
            keys = pairs[pl.ds(row, KEYS), : pairs.shape[1] // 2]
            values = values_of(row)
            first_key = block * TILE
            allowed = (key_rows >= jnp.maximum(starts, wanted * TILE) - first_key) & (
                key_rows < last - first_key
            )
            units += [
                (place, head, keys, values, masked, allowed, total)
                for head in range(len(peaks[place]))
            ]

        def products(unit):
            place, head, keys, values, masked, allowed, total = unit
            return jnp.dot(keys, masked[head], preferred_element_type=jnp.float32)

        new_peaks = [[] for _ in plans]
        ahead = products(units[0])
        for number, unit in enumerate(units):
            place, head, keys, values, masked, allowed, total = unit
            scores = ahead
            if number + 1 < len(units):
                ahead = products(units[number + 1])
            scores = jnp.where(allowed, scores, NEG_FILL)
            old_peak = peaks[place][head]
            peak = jnp.maximum(old_peak, jnp.max(scores, axis=0, keepdims=True))
            fade = jnp.exp(old_peak - peak)
            weights = jnp.exp(scores - peak).astype(jnp.bfloat16)
            own = slice(head * HEAD_ROWS, (head + 1) * HEAD_ROWS)
            total[own, :] = total[own, :] * fade + jnp.dot(
                values[own, :], weights, preferred_element_type=jnp.float32
            )
            new_peaks[place].append(peak)
        return tuple(tuple(job_peaks) for job_peaks in new_peaks)

    return lax.fori_loop(0, steps, one, peaks)


def fresh_peaks(heads):
    return tuple(jnp.full((1, TILE), NEG_FILL, jnp.float32) for _ in range(heads))


def edge_kernel(edge, meta, ranges, *refs):
    rows, pairs, outs, (masked, values) = refs[:6], refs[6], refs[7:11], refs[11:]
    step = pl.program_id(0)
    width = rows[0].shape[1]
    heads = width // HEAD_DIM
    tiles = pairs.shape[0] // TILE

    @pl.when(step == 0)
    def _():
        for number in range(tiles):
            own = slice(number * TILE, (number + 1) * TILE)
            values[:, own] = with_ones(pairs[own, width:])

    jobs = []
    for side in range(2):
        tile = step + side * (tiles - edge)
        queries, starts, ends = rows[3 * side : 3 * side + 3]
        mask_heads(queries, masked.at[side])
        total = outs[side]
        total[...] = jnp.zeros_like(total)
        jobs.append(
            (
                ranges[0, 2 * tile],
                ranges[0, 2 * tile + 1],
                edge,
                pairs,
                lambda row: values[:, pl.ds(row, KEYS)],
                masked.at[side],
                starts[...],
                ends[...],
                total.at[0],
            )
        )
    peaks = sweep(jobs, (fresh_peaks(heads), fresh_peaks(heads)))
    for side in range(2):
        for head in range(heads):
            outs[2 + side][0, head : head + 1, :] = peaks[side][head]


def finish_kernel(edge, meta, ranges, *refs):
    rows, pairs, halos, held, held_peaks = refs[:6], refs[6], refs[7:9], refs[9:11], refs[11:13]
    outs, (masked, sums, peaks_held, mixed) = refs[13:-4], refs[-4:]
    held_steps = edge
    step = pl.program_id(0)
    width = rows[0].shape[1]
    heads = width // HEAD_DIM
    tiles = pairs.shape[0] // TILE
    places = tile_places(step, edge, tiles)

    def jobs_on(keys, bases):
        jobs = []
        for side in range(2):
            queries, starts, ends = rows[3 * side : 3 * side + 3]
            mask_heads(queries, masked.at[side])
            jobs.append(
                (
                    ranges[0, 2 * places[side]],
                    ranges[0, 2 * places[side] + 1],
                    bases[side],
                    keys[side],
                    lambda row, held=keys[side]: with_ones(held[pl.ds(row, KEYS), width:]),
                    masked.at[side],
                    starts[...],
                    ends[...],
                    sums.at[side],
                )
            )
        return jobs

    @pl.when(step < held_steps)
    def _():
        for side in range(2):
            sums[side] = held[side][0]
            peaks_held[side] = held_peaks[side][0]

    @pl.when(step >= held_steps)
    def _():
        sums[...] = jnp.zeros_like(sums)
        peaks = sweep(jobs_on((pairs, pairs), (edge, edge)), (fresh_peaks(heads),) * 2)
        for side in range(2):
            for head in range(heads):
                peaks_held[side, head : head + 1, :] = peaks[side][head]

    reaches_back = ranges[0, 2 * places[0]] < edge
    reaches_ahead = ranges[0, 2 * places[1] + 1] > edge + tiles

    @pl.when((step < edge) & (reaches_back | reaches_ahead))
    def _():
        peaks = tuple(
            tuple(peaks_held[side, head : head + 1, :] for head in range(heads))
            for side in range(2)
        )
        sweep(jobs_on(halos, (0, edge + tiles)), peaks)

    for side in range(2):
        parts = []
        for head in range(heads):
            row = head * HEAD_ROWS
            parts.append(
                sums[side, row : row + HEAD_DIM, :]
                / sums[side, row + HEAD_DIM : row + HEAD_DIM + 1, :]
            )
        tile_rows = pl.ds(pl.multiple_of(places[side] * TILE, TILE), TILE)
        mixed[tile_rows, :] = jnp.concatenate(parts, axis=0).T.astype(jnp.bfloat16)

    @pl.when(step == pl.num_programs(0) - 1)
    def _():
        count = outs[0].shape[0]
        for distance, out in enumerate(outs):
            out[...] = mixed[pl.ds(pl.multiple_of((meta[0] ^ distance) * count, 128), count), :]


def tile_places(step, edge, tiles):
    middle = edge + 2 * (step - edge)
    return (
        jnp.where(step < edge, step, middle),
        jnp.where(step < edge, tiles - edge + step, middle + 1),
    )


def attend_specs(width, edge, tiles):
    specs = []
    for side in range(2):
        place = lambda i, side=side: tile_places(i, edge, tiles)[side]
        specs.append(pl.BlockSpec((TILE, width), lambda i, m, r, place=place: (place(i), 0)))
        specs += [pl.BlockSpec((1, TILE), lambda i, m, r, place=place: (0, place(i)))] * 2
    return specs + [pl.BlockSpec((tiles * TILE, 2 * width), lambda i, m, r: (0, 0))]


def attend_edges(meta, ranges, queries, starts, ends, pairs):
    group_rows, width = queries.shape
    heads = width // HEAD_DIM
    tiles, edge = group_rows // TILE, SPAN // TILE
    steps = edge
    shapes = [(steps, heads * HEAD_ROWS, TILE)] * 2 + [(steps, 8, TILE)] * 2
    return pl.pallas_call(
        functools.partial(edge_kernel, edge),
        grid_spec=pltpu.PrefetchScalarGridSpec(
            num_scalar_prefetch=2,
            grid=(steps,),
            in_specs=attend_specs(width, edge, tiles),
            out_specs=[pl.BlockSpec((1,) + shape[1:], lambda i, m, r: (i, 0, 0)) for shape in shapes],
            scratch_shapes=[
                pltpu.VMEM((2, heads, width, TILE), jnp.bfloat16),
                pltpu.VMEM((heads * HEAD_ROWS, group_rows), jnp.bfloat16),
            ],
        ),
        out_shape=[jax.ShapeDtypeStruct(shape, jnp.float32) for shape in shapes],
        compiler_params=PARAMS,
        cost_estimate=pl.CostEstimate(
            flops=16 * group_rows * 1024 * width,
            bytes_accessed=5 << 20,
            transcendentals=group_rows * 1024 * heads,
        ),
        name="attend_edges",
    )(meta, ranges, queries, starts, ends, queries, starts, ends, pairs)


def attend_finish(meta, ranges, queries, starts, ends, pairs, before, after, held, rows):
    group_rows, width = queries.shape
    heads = width // HEAD_DIM
    tiles, edge = group_rows // TILE, SPAN // TILE
    members = group_rows // rows
    return pl.pallas_call(
        functools.partial(finish_kernel, edge),
        grid_spec=pltpu.PrefetchScalarGridSpec(
            num_scalar_prefetch=2,
            grid=(edge + (tiles - 2 * edge) // 2,),
            in_specs=attend_specs(width, edge, tiles)
            + [pl.BlockSpec((SPAN, 2 * width), lambda i, m, r: (0, 0))] * 2
            + [
                pl.BlockSpec(
                    (1,) + part.shape[1:], lambda i, m, r: (jnp.minimum(i, edge - 1), 0, 0)
                )
                for part in held
            ],
            out_specs=[pl.BlockSpec((rows, width), lambda i, m, r: (0, 0))] * members,
            scratch_shapes=[
                pltpu.VMEM((2, heads, width, TILE), jnp.bfloat16),
                pltpu.VMEM((2, heads * HEAD_ROWS, TILE), jnp.float32),
                pltpu.VMEM((2, 8, TILE), jnp.float32),
                pltpu.VMEM((group_rows, width), jnp.bfloat16),
            ],
        ),
        out_shape=[jax.ShapeDtypeStruct((rows, width), jnp.bfloat16)] * members,
        compiler_params=PARAMS,
        cost_estimate=pl.CostEstimate(
            flops=16 * group_rows * 1024 * width,
            bytes_accessed=5 << 20,
            transcendentals=group_rows * 1024 * heads,
        ),
        name="attend_finish",
    )(meta, ranges, queries, starts, ends, queries, starts, ends, pairs, before, after, *held)


def output_kernel(members, meta, *refs):
    parts, weights, result, mixed = refs[:members], refs[members:-2], refs[-2], refs[-1]
    width = parts[0].shape[1]
    tile = weights[0].shape[1]
    for distance in range(members):
        source = meta[0] ^ distance
        head_pair = PAIR * (source % (members // PAIR)) + source // (members // PAIR)
        shard = head_pair ^ meta[1]
        shard = jnp.where(meta[1] < 0, head_pair, shard // PAIR + shard % PAIR * (members // PAIR))
        columns = pl.ds(pl.multiple_of(shard * width, width), width)
        mixed[:, columns] = parts[distance][...]
    for distance, weight in enumerate(weights):
        columns = pl.ds(pl.multiple_of((meta[0] % len(weights) ^ distance) * tile, tile), tile)
        result[:, columns] = jnp.dot(
            mixed[...], weight[...], preferred_element_type=jnp.float32
        ).astype(jnp.bfloat16)


def output_projection(meta, parts, weights):
    rows, width = parts[0].shape
    depth, tile = weights[0].shape
    whole = lambda shape: pl.BlockSpec(shape, lambda i, m: (0, 0))
    return pl.pallas_call(
        functools.partial(output_kernel, len(parts)),
        grid_spec=pltpu.PrefetchScalarGridSpec(
            num_scalar_prefetch=1,
            grid=(1,),
            in_specs=[whole(parts[0].shape)] * len(parts) + [whole((depth, tile))] * len(weights),
            out_specs=whole((rows, len(weights) * tile)),
            scratch_shapes=[pltpu.VMEM((rows, depth), jnp.bfloat16)],
        ),
        out_shape=jax.ShapeDtypeStruct((rows, len(weights) * tile), jnp.bfloat16),
        compiler_params=PARAMS,
        cost_estimate=pl.CostEstimate(
            flops=2 * rows * depth * len(weights) * tile,
            bytes_accessed=4 << 20,
            transcendentals=0,
        ),
        name="output_projection",
    )(meta, *parts, *weights)


def unpack_kernel(own_row, other_row, pages):
    _, pair, members, capacity, part = own_row.shape
    width = part // (2 * PAGE)
    for source in range(pair):
        for low in range(pair):
            received = own_row if source == low else other_row
            for high in range(members):
                for turn in range(2 * PAGE):
                    start = (turn * pair * members + PAIR * high + low) * width
                    pages[source, :, start : start + width] = received[
                        0, low, high, :, turn * width : (turn + 1) * width
                    ]


def unpack(own_row, other_row):
    planes, pair, members, capacity, part = own_row.shape
    block = pl.BlockSpec((1,) + own_row.shape[1:], lambda i: (i, 0, 0, 0, 0))
    return pl.pallas_call(
        unpack_kernel,
        grid=(planes,),
        in_specs=[block, block],
        out_specs=pl.BlockSpec((pair, capacity, pair * members * part), lambda i: (i, 0, 0)),
        out_shape=jax.ShapeDtypeStruct(
            (planes * pair, capacity, pair * members * part), jnp.bfloat16
        ),
        compiler_params=pltpu.CompilerParams(vmem_limit_bytes=24 * 1024 * 1024),
        cost_estimate=pl.CostEstimate(flops=0, bytes_accessed=6 << 20, transcendentals=0),
        name="unpack",
    )(own_row, other_row)


def rope_tables(positions):
    half_dim = HEAD_DIM // 2
    inverse = 1.0 / ROPE_BASE ** (jnp.arange(half_dim, dtype=jnp.float32) * 2.0 / HEAD_DIM)
    angles = inverse[:, None] * positions.astype(jnp.float32)[None, :]
    return jnp.cos(angles), jnp.sin(angles)


def bounds_kernel(ids, starts, ends, ranges):
    shape = (8, ids.shape[1])
    width = ids.shape[1]
    own = jnp.broadcast_to(ids[...], shape)
    index = lax.broadcasted_iota(jnp.int32, shape, 1)
    first = jnp.where((own != pltpu.roll(own, 1, 1)) | (index == 0), index, 0)
    after = jnp.where((own != pltpu.roll(own, width - 1, 1)) | (index == width - 1), index + 1, width)
    shift = 1
    while shift < SPAN:
        first = jnp.maximum(first, jnp.where(index >= shift, pltpu.roll(first, shift, 1), 0))
        after = jnp.minimum(
            after, jnp.where(index < width - shift, pltpu.roll(after, width - shift, 1), width)
        )
        shift *= 2
    rows = starts.shape[1]
    starts[...] = first[:1, SPAN : SPAN + rows]
    ends[...] = after[:1, SPAN : SPAN + rows]
    lane = lax.broadcasted_iota(jnp.int32, (rows, ranges.shape[1]), 0)
    entry = lax.broadcasted_iota(jnp.int32, (rows, ranges.shape[1]), 1)
    own_lane = entry // 2 * TILE + lax.rem(entry, 2) * (TILE - 1)
    chosen = jnp.where(lane == own_lane, 1.0, 0.0)
    odd = lax.rem(entry, 2) == 1
    begin = (first[:, SPAN : SPAN + rows] // TILE).astype(jnp.bfloat16)
    end = ((after[:, SPAN : SPAN + rows] + TILE - 1) // TILE).astype(jnp.bfloat16)
    from_begin = jnp.where(odd, 0.0, chosen).astype(jnp.bfloat16)
    from_end = jnp.where(odd, chosen, 0.0).astype(jnp.bfloat16)
    found = jnp.dot(begin, from_begin, preferred_element_type=jnp.float32) + jnp.dot(
        end, from_end, preferred_element_type=jnp.float32
    )
    ranges[...] = found[:1].astype(jnp.int32)


def document_bounds(window_ids, rows):
    return pl.pallas_call(
        bounds_kernel,
        out_shape=[jax.ShapeDtypeStruct((1, rows), jnp.int32)] * 2
        + [jax.ShapeDtypeStruct((1, 128), jnp.int32)],
        compiler_params=PARAMS,
        cost_estimate=pl.CostEstimate(flops=1 << 34, bytes_accessed=0, transcendentals=0),
        name="document_bounds",
    )(window_ids[None, :])


def per_device(tokens, norm_gain, input_weight, output_weight, segment_ids, page_owner):
    rows, model_width = tokens.shape
    peers, members = lax.axis_size("tok"), lax.axis_size("grp")
    place, column = lax.axis_index("tok"), lax.axis_index("grp")
    low = place % PAIR
    blocks = PAIR * members
    member = low * members + column
    group_rows = rows * blocks
    width = model_width // blocks
    pages = rows // PAGE

    flat = peers * members
    owners = page_owner[:, 0]
    capacity = max(2, (2 * pages + peers - 1) // peers)
    halves = []
    for parity in range(PAIR):
        pieces = []
        for number in range(PARTS):
            start = number * PAIR * width
            choices = [input_weight[:, start : start + width], input_weight[:, start + width : start + 2 * width]]
            piece = jnp.where((low ^ parity) == 0, choices[0], choices[1])
            route = []
            for source in range(flat):
                row, column_from = divmod(source, members)
                target = (row ^ parity) * members + (PARTS * column_from + number) % members
                route.append((source, target))
            pieces.append(lax.ppermute(piece, ("tok", "grp"), route))
        halves.append(jnp.concatenate(pieces, axis=1))
    plane = jnp.concatenate(halves, axis=0)
    own = layer_norm(tokens, norm_gain[None, :], owners, capacity)
    own, plane = lax.optimization_barrier((own, plane))

    across, along = flipped(own, "grp", 2), flipped(own, "tok", 1)
    sibling = flipped(own, "grp", 1)
    planes = {0: plane}
    bit = peers // 2
    while bit > 1:
        planes[bit] = flipped(plane, "tok", bit)
        bit //= 2
    for distance in range(PAIR, peers, PAIR):
        if distance not in planes:
            step_bit = distance & -distance
            planes[distance] = flipped(planes[distance ^ step_bit], "tok", step_bit)
    weights = [planes[distance] for distance in range(0, peers, PAIR)]

    first_row = place // PAIR * group_rows
    padded_ids = jnp.concatenate(
        [
            jnp.full((SPAN,), -1, jnp.int32),
            segment_ids,
            jnp.full((SPAN,), 1 << 30, jnp.int32),
        ]
    )
    window_ids = lax.dynamic_slice_in_dim(padded_ids, first_row, group_rows + 2 * SPAN, 0)
    window_ids, plane = lax.optimization_barrier((window_ids, plane))
    *bounds, ranges = document_bounds(window_ids, group_rows)
    positions = SPAN + jnp.arange(group_rows, dtype=jnp.int32) - bounds[0][0]
    order = [(number * members + column) % PARTS for number in range(PARTS)]
    meta = jnp.stack([member, place] + order).astype(jnp.int32)
    cosine, sine = rope_tables(positions)
    last_rows = output_weight
    bit = PAIR
    while 4 * bit < peers:
        last_rows = jnp.concatenate([last_rows, flipped(last_rows, "tok", bit)], axis=0)
        bit *= 2
    other_rows = flipped(last_rows, "tok", bit)
    across, along, sibling, weights, last_rows, other_rows, cosine, sine, meta = (
        lax.optimization_barrier(
            (across, along, sibling, weights, last_rows, other_rows, cosine, sine, meta)
        )
    )
    last_rows = jnp.concatenate([last_rows, other_rows], axis=0)

    half, held = rows // 2, rows + EXTRA_ROWS
    corner = [flipped(across[:half], "tok", 1), flipped(along[half:], "grp", 2)]
    across_sibling = flipped(across, "grp", 1)
    along_sibling = flipped(along, "grp", 1)
    other_rows = flipped(last_rows, "tok", peers // 2)
    near_blocks = [own, sibling, across, across_sibling]
    near_layout = [[(number, 0, held)] for number in range(4)]
    far_layout = [[(0, 0, held)], [(1, 0, held)]]
    far_layout += [[(number, 0, half), (number + 1, half, held - half)] for number in (2, 4)]

    sizes = (weights, cosine, sine, rows, blocks, peers, capacity)

    def to_owners(send):
        received = lax.all_to_all(
            send.reshape((flat,) + send.shape[2:]),
            ("tok", "grp"),
            split_axis=0,
            concat_axis=0,
            tiled=True,
        )
        return received.reshape((peers // PAIR, PAIR, members) + send.shape[2:])

    queries, pairs, send = project(meta, 0, near_layout, near_blocks, *sizes, ())
    send, corner, along_sibling, last_rows, other_rows = lax.optimization_barrier(
        (send, corner, along_sibling, last_rows, other_rows)
    )
    own_row = to_owners(send)
    corner_sibling = [flipped(block, "grp", 1) for block in corner]
    far_blocks = [along, along_sibling] + corner + corner_sibling
    last_rows = jnp.concatenate([last_rows, other_rows], axis=0)
    queries, pairs, send = project(meta, 4, far_layout, far_blocks, *sizes, (queries, pairs))
    before = shifted(pairs[group_rows - SPAN :], "tok", PAIR)
    after = shifted(pairs[:SPAN], "tok", -PAIR)
    other_rows = flipped(last_rows, "tok", 1)
    across_rows = flipped(last_rows, "grp", 2)
    corner_rows = lax.ppermute(
        last_rows,
        ("tok", "grp"),
        [(source, source ^ (members + 2)) for source in range(flat)],
    )

    edges = attend_edges(meta, ranges, queries, *bounds, pairs)
    before, after, edges, last_rows, other_rows, across_rows, corner_rows, send = (
        lax.optimization_barrier(
            (before, after, edges, last_rows, other_rows, across_rows, corner_rows, send)
        )
    )
    other_row = to_owners(send)
    columns = [
        jnp.concatenate([last_rows, other_rows], axis=0),
        jnp.concatenate([across_rows, corner_rows], axis=0),
    ]
    row_order = place
    if output_weight.shape[0] != width:
        wanted = jnp.arange(peers) ^ place
        wanted = wanted // PAIR + wanted % PAIR * (peers // PAIR)
        shards = (peers,) + output_weight.shape
        columns = [part.reshape(shards)[wanted].reshape(part.shape) for part in columns]
        row_order = jnp.full_like(place, -1)
    mixed = attend_finish(meta, ranges, queries, *bounds, pairs, before, after, edges, rows)
    siblings = [flipped(part, "grp", 1) for part in columns]
    last_weights = [columns[0], siblings[0], columns[1], siblings[1]]
    parts = [mixed[0]] + [
        lax.ppermute(
            mixed[distance],
            ("tok", "grp"),
            [(source, source ^ distance) for source in range(flat)],
        )
        for distance in range(1, blocks)
    ]
    output_meta = jnp.stack([member, row_order]).astype(jnp.int32)
    attended = output_projection(output_meta, parts, last_weights)
    cache_pages = unpack(own_row, other_row).reshape(
        peers * capacity, 2 * PAGE * model_width
    )
    return attended, cache_pages


def solution(mesh):
    placed = (
        P(("tok", "grp"), None),
        P(),
        P("tok", "grp"),
        P("tok", "grp"),
        P(),
        P(("tok", "grp"), None),
    )
    return jax.shard_map(
        per_device,
        mesh=mesh,
        in_specs=placed,
        out_specs=(P(("tok", "grp"), None), P(("tok", "grp"), None)),
        check_vma=False,
    )
```

```python
import functools

import jax
import jax.numpy as jnp
from jax import lax
from jax.experimental import pallas as pl
from jax.experimental.pallas import tpu as pltpu
from jax.sharding import PartitionSpec as P

H = 16
SPAN = 1024
PAGE = 4
HEAD_DIM = 64

NEG_FILL = -1e30
ROPE_BASE = 160000.0
EPSILON = 1e-05
TILE = 256
PARTS = 3
PAIR = 2
ONES_ROWS = 16
HEAD_ROWS = HEAD_DIM + ONES_ROWS
EXTRA_ROWS = 16
KEYS = 512
SCALE = HEAD_DIM ** (-0.5)
VMEM_LIMIT = 60 * 1024 * 1024
PARAMS = pltpu.CompilerParams(vmem_limit_bytes=VMEM_LIMIT)


def flipped(value, axis, bit):
    count = lax.axis_size(axis)
    return lax.ppermute(value, axis, [(source, source ^ bit) for source in range(count)])


def shifted(value, axis, steps):
    count = lax.axis_size(axis)
    initial, last = (max(0, -steps), min(count, count - steps))
    return lax.ppermute(value, axis, [(source, source + steps) for source in range(initial, last)])


def norm_kernel(capacity, tokens, gain, owner_row, normed, owners):
    rows = tokens.shape[0]
    values = tokens[...].astype(jnp.float32)
    centred = values - jnp.mean(values, axis=-1, keepdims=True)
    spread = jnp.mean(jnp.square(centred), axis=-1, keepdims=True)
    normed[:rows, :] = (centred * lax.rsqrt(spread + EPSILON) * gain[...]).astype(jnp.bfloat16)
    pages = owner_row.shape[1]
    owners[...] = jnp.full(owners.shape, -1.0, jnp.float32)
    owners[:1, :pages] = owner_row[...].astype(jnp.float32)
    lanes = owners.shape[1]
    across = jnp.broadcast_to(owners[:1, :], (lanes, lanes))
    earlier = lax.broadcasted_iota(jnp.int32, (lanes, lanes), 0) < lax.broadcasted_iota(
        jnp.int32, (lanes, lanes), 1
    )
    same = (across.T == across) & earlier
    ranks = jnp.sum(jnp.where(same, 1.0, 0.0), axis=0, keepdims=True)
    slots = owners[:1, :] * capacity + ranks
    normed[rows:, :] = jnp.zeros((EXTRA_ROWS, normed.shape[1]), jnp.bfloat16)
    normed[rows:, :lanes] = jnp.broadcast_to(slots, (EXTRA_ROWS, lanes)).astype(jnp.bfloat16)


def layer_norm(tokens, gain, owners, capacity):
    rows, width = tokens.shape
    lanes = -(-owners.shape[0] // 128) * 128
    return pl.pallas_call(
        functools.partial(norm_kernel, capacity),
        out_shape=jax.ShapeDtypeStruct((rows + EXTRA_ROWS, width), jnp.bfloat16),
        scratch_shapes=[pltpu.VMEM((8, lanes), jnp.float32)],
        compiler_params=PARAMS,
        name="layer_norm",
    )(tokens, gain, owners[None, :])


def project_kernel(first, layout, weight_count, peers, capacity, meta, *refs):
    operands = 1 + max(entry[0] for pieces in layout for entry in pieces)
    tokens = refs[:operands]
    weights = refs[operands : operands + weight_count]
    cosine, sine = refs[operands + weight_count : operands + weight_count + 2]
    query_out, pair_out, send_out, blocks, weight, page_source, sems = refs[-7:]
    step = pl.program_id(0)
    steps = len(layout)
    rows = query_out.shape[0]
    width = query_out.shape[1]
    shard = weights[0].shape[0] // 2

    def arrivals(number):
        return [
            pltpu.make_async_copy(
                tokens[operand],
                blocks.at[number, pl.ds(offset, count), :],
                sems.at[number, place],
            )
            for place, (operand, offset, count) in enumerate(layout[number])
        ]

    @pl.when(step == 0)
    def _():
        for number in range(steps):
            for copy in arrivals(number):
                copy.start()
        for plane in range(weight_count):
            for low in range(2):
                row = pl.multiple_of((meta[1] ^ (2 * plane + low)) * shard, shard)
                for number in range(PARTS):
                    column = pl.multiple_of(meta[2 + number] * width, width)
                    weight[pl.ds(row, shard), number * width : (number + 1) * width] = weights[
                        plane
                    ][low * shard : (low + 1) * shard, pl.ds(column, width)]

    for number in range(steps):

        @pl.when(step == number)
        def _():
            for copy in arrivals(number):
                copy.wait()

    joined = jnp.dot(blocks[step, :rows, :], weight[...], preferred_element_type=jnp.float32)
    cosines = jnp.concatenate([cosine[...]] * 4, axis=0).T
    sines = jnp.concatenate([-sine[...], sine[...]] * 2, axis=0).T
    first_half = lax.rem(lax.broadcasted_iota(jnp.int32, (rows, width), 1), HEAD_DIM) < (
        HEAD_DIM // 2
    )

    def rotate(values):
        partner = jnp.where(
            first_half,
            pltpu.roll(values, width - HEAD_DIM // 2, 1),
            pltpu.roll(values, HEAD_DIM // 2, 1),
        )
        return (values * cosines + partner * sines).astype(jnp.bfloat16)

    query_out[...] = rotate(joined[:, :width]) * jnp.asarray(SCALE, jnp.bfloat16)
    keys = rotate(joined[:, width : 2 * width])
    values = joined[:, 2 * width :].astype(jnp.bfloat16)
    pair_out[:, :width] = keys
    pair_out[:, width:] = values
    page_source[0] = keys.astype(jnp.float32)
    page_source[1] = values.astype(jnp.float32)

    pages = rows // PAGE
    slot_count = peers * capacity
    slots = blocks[step, rows : rows + EXTRA_ROWS, :128].astype(jnp.float32)[:1, :pages]
    chosen = (
        lax.broadcasted_iota(jnp.int32, (slot_count, pages), 0).astype(jnp.float32) == slots
    ).astype(jnp.bfloat16)
    for turn in range(PAGE):
        page_part = jnp.concatenate(
            [
                page_source[half, pl.ds(turn, pages, stride=PAGE), :].astype(jnp.bfloat16)
                for half in range(2)
            ],
            axis=1,
        )
        placed = jnp.dot(chosen, page_part, preferred_element_type=jnp.float32)
        columns = slice(turn * 2 * width, (turn + 1) * 2 * width)
        for peer in range(peers):
            send_out[peer, 0, :, columns] = placed[
                peer * capacity : (peer + 1) * capacity
            ].astype(jnp.bfloat16)


def project(meta, first, layout, operands, weights, cosine, sine, rows, blocks, peers, capacity, into):
    steps = len(layout)
    model_width = operands[0].shape[1]
    group_rows = rows * blocks
    width = model_width // blocks
    members = blocks // PAIR
    whole = lambda shape: pl.BlockSpec(shape, lambda i, m: (0,) * len(shape))
    place = lambda i, m: m[0] ^ (first + i)
    table = pl.BlockSpec((HEAD_DIM // 2, rows), lambda i, m: (0, place(i, m)))
    send_shape = (peers, members, capacity, 2 * PAGE * width)
    return pl.pallas_call(
        functools.partial(project_kernel, first, layout, len(weights), peers, capacity),
        grid_spec=pltpu.PrefetchScalarGridSpec(
            num_scalar_prefetch=1,
            grid=(steps,),
            in_specs=[pl.BlockSpec(memory_space=pl.ANY)] * len(operands)
            + [whole(weights[0].shape)] * len(weights)
            + [table, table]
            + [pl.BlockSpec(memory_space=pl.ANY)] * len(into),
            out_specs=[
                pl.BlockSpec((rows, width), lambda i, m: (place(i, m), 0)),
                pl.BlockSpec((rows, 2 * width), lambda i, m: (place(i, m), 0)),
                pl.BlockSpec(
                    (peers, 1) + send_shape[2:], lambda i, m: (0, place(i, m) % members, 0, 0)
                ),
            ],
            scratch_shapes=[
                pltpu.VMEM((steps, rows + EXTRA_ROWS, model_width), jnp.bfloat16),
                pltpu.VMEM((model_width, PARTS * width), jnp.bfloat16),
                pltpu.VMEM((2, rows, width), jnp.float32),
                pltpu.SemaphoreType.DMA((steps, 2)),
            ],
        ),
        out_shape=[
            jax.ShapeDtypeStruct((group_rows, width), jnp.bfloat16),
            jax.ShapeDtypeStruct((group_rows, 2 * width), jnp.bfloat16),
            jax.ShapeDtypeStruct(send_shape, jnp.bfloat16),
        ],
        input_output_aliases={
            1 + len(operands) + len(weights) + 2 + number: number for number in range(len(into))
        },
        compiler_params=PARAMS,
        cost_estimate=pl.CostEstimate(
            flops=16 * steps * rows * model_width * PARTS * width,
            bytes_accessed=(3 * steps) << 19,
            transcendentals=0,
        ),
        name="project",
    )(meta, *operands, *weights, cosine, sine, *into)


def mask_heads(queries, masked):
    turned = queries[...].T
    head_of_row = lax.broadcasted_iota(jnp.int32, turned.shape, 0) // HEAD_DIM
    for head in range(masked.shape[0]):
        masked[head] = jnp.where(head_of_row == head, turned, jnp.zeros((), jnp.bfloat16))


def with_ones(values):
    turned = values.T
    ones = jnp.ones((ONES_ROWS, values.shape[0]), values.dtype)
    rows = []
    for head in range(values.shape[1] // HEAD_DIM):
        rows += [turned[head * HEAD_DIM : (head + 1) * HEAD_DIM], ones]
    return jnp.concatenate(rows, axis=0)


def sweep(jobs, peaks):
    plans = []
    steps = 0
    for begin, end, base, pairs, values_of, masked, starts, ends, total in jobs:
        held = pairs.shape[0] // TILE
        begin, end = jnp.maximum(begin, base), jnp.minimum(end, base + held)
        last = jnp.minimum(ends, end * TILE)
        steps = jnp.maximum(steps, (end - begin + KEYS // TILE - 1) // (KEYS // TILE))
        plans.append((begin, base, held, pairs, values_of, masked, starts, last, total))

    key_rows = lax.broadcasted_iota(jnp.int32, (KEYS, TILE), 0)

    def one(number, peaks):
        units = []
        for place, plan in enumerate(plans):
            begin, base, held, pairs, values_of, masked, starts, last, total = plan
            wanted = begin + number * (KEYS // TILE)
            block = jnp.minimum(wanted, base + held - KEYS // TILE)
            row = pl.multiple_of((block - base) * TILE, TILE)
            keys = pairs[pl.ds(row, KEYS), : pairs.shape[1] // 2]
            values = values_of(row)
            first_key = block * TILE
            allowed = (key_rows >= jnp.maximum(starts, wanted * TILE) - first_key) & (
                key_rows < last - first_key
            )
            units += [
                (place, head, keys, values, masked, allowed, total)
                for head in range(len(peaks[place]))
            ]

        def products(unit):
            place, head, keys, values, masked, allowed, total = unit
            return jnp.dot(keys, masked[head], preferred_element_type=jnp.float32)

        new_peaks = [[] for _ in plans]
        ahead = products(units[0])
        for number, unit in enumerate(units):
            place, head, keys, values, masked, allowed, total = unit
            scores = ahead
            if number + 1 < len(units):
                ahead = products(units[number + 1])
            scores = jnp.where(allowed, scores, NEG_FILL)
            old_peak = peaks[place][head]
            peak = jnp.maximum(old_peak, jnp.max(scores, axis=0, keepdims=True))
            fade = jnp.exp(old_peak - peak)
            weights = jnp.exp(scores - peak).astype(jnp.bfloat16)
            own = slice(head * HEAD_ROWS, (head + 1) * HEAD_ROWS)
            total[own, :] = total[own, :] * fade + jnp.dot(
                values[own, :], weights, preferred_element_type=jnp.float32
            )
            new_peaks[place].append(peak)
        return tuple(tuple(job_peaks) for job_peaks in new_peaks)

    return lax.fori_loop(0, steps, one, peaks)


def fresh_peaks(heads):
    return tuple(jnp.full((1, TILE), NEG_FILL, jnp.float32) for _ in range(heads))


def edge_kernel(edge, meta, ranges, *refs):
    rows, pairs, outs, (masked, values) = refs[:6], refs[6], refs[7:11], refs[11:]
    step = pl.program_id(0)
    width = rows[0].shape[1]
    heads = width // HEAD_DIM
    tiles = pairs.shape[0] // TILE

    @pl.when(step == 0)
    def _():
        for number in range(tiles):
            own = slice(number * TILE, (number + 1) * TILE)
            values[:, own] = with_ones(pairs[own, width:])

    jobs = []
    places = tile_places(step, edge, tiles)
    for side in range(2):
        tile = places[side]
        queries, starts, ends = rows[3 * side : 3 * side + 3]
        mask_heads(queries, masked.at[side])
        total = outs[side]
        total[...] = jnp.zeros_like(total)
        jobs.append(
            (
                ranges[0, 2 * tile],
                ranges[0, 2 * tile + 1],
                edge,
                pairs,
                lambda row: values[:, pl.ds(row, KEYS)],
                masked.at[side],
                starts[...],
                ends[...],
                total.at[0],
            )
        )
    peaks = sweep(jobs, (fresh_peaks(heads), fresh_peaks(heads)))
    for side in range(2):
        for head in range(heads):
            outs[2 + side][0, head : head + 1, :] = peaks[side][head]


def finish_kernel(edge, meta, ranges, *refs):
    rows, pairs, halos, held, held_peaks = refs[:6], refs[6], refs[7:9], refs[9:11], refs[11:13]
    outs, (masked, sums, peaks_held, mixed) = refs[13:-4], refs[-4:]
    held_steps = edge + 1
    step = pl.program_id(0)
    width = rows[0].shape[1]
    heads = width // HEAD_DIM
    tiles = pairs.shape[0] // TILE
    places = tile_places(step, edge, tiles)

    def jobs_on(keys, bases):
        jobs = []
        for side in range(2):
            queries, starts, ends = rows[3 * side : 3 * side + 3]
            mask_heads(queries, masked.at[side])
            jobs.append(
                (
                    ranges[0, 2 * places[side]],
                    ranges[0, 2 * places[side] + 1],
                    bases[side],
                    keys[side],
                    lambda row, held=keys[side]: with_ones(held[pl.ds(row, KEYS), width:]),
                    masked.at[side],
                    starts[...],
                    ends[...],
                    sums.at[side],
                )
            )
        return jobs

    @pl.when(step < held_steps)
    def _():
        for side in range(2):
            sums[side] = held[side][0]
            peaks_held[side] = held_peaks[side][0]

    @pl.when(step >= held_steps)
    def _():
        sums[...] = jnp.zeros_like(sums)
        peaks = sweep(jobs_on((pairs, pairs), (edge, edge)), (fresh_peaks(heads),) * 2)
        for side in range(2):
            for head in range(heads):
                peaks_held[side, head : head + 1, :] = peaks[side][head]

    reaches_back = ranges[0, 2 * places[0]] < edge
    reaches_ahead = ranges[0, 2 * places[1] + 1] > edge + tiles

    @pl.when((step < edge) & (reaches_back | reaches_ahead))
    def _():
        peaks = tuple(
            tuple(peaks_held[side, head : head + 1, :] for head in range(heads))
            for side in range(2)
        )
        sweep(jobs_on(halos, (0, edge + tiles)), peaks)

    for side in range(2):
        parts = []
        for head in range(heads):
            row = head * HEAD_ROWS
            parts.append(
                sums[side, row : row + HEAD_DIM, :]
                / sums[side, row + HEAD_DIM : row + HEAD_DIM + 1, :]
            )
        tile_rows = pl.ds(pl.multiple_of(places[side] * TILE, TILE), TILE)
        mixed[tile_rows, :] = jnp.concatenate(parts, axis=0).T.astype(jnp.bfloat16)

    @pl.when(step == pl.num_programs(0) - 1)
    def _():
        count = outs[0].shape[0]
        for distance, out in enumerate(outs):
            out[...] = mixed[pl.ds(pl.multiple_of((meta[0] ^ distance) * count, 128), count), :]


def tile_places(step, edge, tiles):
    middle = edge + 2 * (step - edge)
    return (
        jnp.where(step < edge, step, middle),
        jnp.where(step < edge, tiles - edge + step, middle + 1),
    )


def attend_specs(width, edge, tiles):
    specs = []
    for side in range(2):
        place = lambda i, side=side: tile_places(i, edge, tiles)[side]
        specs.append(pl.BlockSpec((TILE, width), lambda i, m, r, place=place: (place(i), 0)))
        specs += [pl.BlockSpec((1, TILE), lambda i, m, r, place=place: (0, place(i)))] * 2
    return specs + [pl.BlockSpec((tiles * TILE, 2 * width), lambda i, m, r: (0, 0))]


def attend_edges(meta, ranges, queries, starts, ends, pairs):
    group_rows, width = queries.shape
    heads = width // HEAD_DIM
    tiles, edge = group_rows // TILE, SPAN // TILE
    steps = edge + 1
    shapes = [(steps, heads * HEAD_ROWS, TILE)] * 2 + [(steps, 8, TILE)] * 2
    return pl.pallas_call(
        functools.partial(edge_kernel, edge),
        grid_spec=pltpu.PrefetchScalarGridSpec(
            num_scalar_prefetch=2,
            grid=(steps,),
            in_specs=attend_specs(width, edge, tiles),
            out_specs=[pl.BlockSpec((1,) + shape[1:], lambda i, m, r: (i, 0, 0)) for shape in shapes],
            scratch_shapes=[
                pltpu.VMEM((2, heads, width, TILE), jnp.bfloat16),
                pltpu.VMEM((heads * HEAD_ROWS, group_rows), jnp.bfloat16),
            ],
        ),
        out_shape=[jax.ShapeDtypeStruct(shape, jnp.float32) for shape in shapes],
        compiler_params=PARAMS,
        cost_estimate=pl.CostEstimate(
            flops=16 * group_rows * 1024 * width,
            bytes_accessed=5 << 20,
            transcendentals=group_rows * 1024 * heads,
        ),
        name="attend_edges",
    )(meta, ranges, queries, starts, ends, queries, starts, ends, pairs)


def attend_finish(meta, ranges, queries, starts, ends, pairs, before, after, held, rows):
    group_rows, width = queries.shape
    heads = width // HEAD_DIM
    tiles, edge = group_rows // TILE, SPAN // TILE
    members = group_rows // rows
    return pl.pallas_call(
        functools.partial(finish_kernel, edge),
        grid_spec=pltpu.PrefetchScalarGridSpec(
            num_scalar_prefetch=2,
            grid=(edge + (tiles - 2 * edge) // 2,),
            in_specs=attend_specs(width, edge, tiles)
            + [pl.BlockSpec((SPAN, 2 * width), lambda i, m, r: (0, 0))] * 2
            + [
                pl.BlockSpec(
                    (1,) + part.shape[1:], lambda i, m, r: (jnp.minimum(i, edge), 0, 0)
                )
                for part in held
            ],
            out_specs=[pl.BlockSpec((rows, width), lambda i, m, r: (0, 0))] * members,
            scratch_shapes=[
                pltpu.VMEM((2, heads, width, TILE), jnp.bfloat16),
                pltpu.VMEM((2, heads * HEAD_ROWS, TILE), jnp.float32),
                pltpu.VMEM((2, 8, TILE), jnp.float32),
                pltpu.VMEM((group_rows, width), jnp.bfloat16),
            ],
        ),
        out_shape=[jax.ShapeDtypeStruct((rows, width), jnp.bfloat16)] * members,
        compiler_params=PARAMS,
        cost_estimate=pl.CostEstimate(
            flops=16 * group_rows * 1024 * width,
            bytes_accessed=5 << 20,
            transcendentals=group_rows * 1024 * heads,
        ),
        name="attend_finish",
    )(meta, ranges, queries, starts, ends, queries, starts, ends, pairs, before, after, *held)


def output_kernel(members, meta, *refs):
    parts, weights, result, mixed = refs[:members], refs[members:-2], refs[-2], refs[-1]
    width = parts[0].shape[1]
    tile = weights[0].shape[1]
    for distance in range(members):
        source = meta[0] ^ distance
        head_pair = PAIR * (source % (members // PAIR)) + source // (members // PAIR)
        shard = head_pair ^ meta[1]
        shard = jnp.where(meta[1] < 0, head_pair, shard // PAIR + shard % PAIR * (members // PAIR))
        columns = pl.ds(pl.multiple_of(shard * width, width), width)
        mixed[:, columns] = parts[distance][...]
    depth = mixed.shape[1]
    groups = len(weights) * (weights[0].shape[0] // depth)
    for distance in range(groups):
        columns = pl.ds(pl.multiple_of((meta[0] % groups ^ distance) * tile, tile), tile)
        start = distance // len(weights) * depth
        result[:, columns] = jnp.dot(
            mixed[...],
            weights[distance % len(weights)][start : start + depth, :],
            preferred_element_type=jnp.float32,
        ).astype(jnp.bfloat16)


def output_projection(meta, parts, weights):
    rows, width = parts[0].shape
    depth, tile = width * len(parts), weights[0].shape[1]
    columns = sum(weight.shape[0] for weight in weights) // depth * tile
    whole = lambda shape: pl.BlockSpec(shape, lambda i, m: (0, 0))
    return pl.pallas_call(
        functools.partial(output_kernel, len(parts)),
        grid_spec=pltpu.PrefetchScalarGridSpec(
            num_scalar_prefetch=1,
            grid=(1,),
            in_specs=[whole(parts[0].shape)] * len(parts)
            + [whole(weight.shape) for weight in weights],
            out_specs=whole((rows, columns)),
            scratch_shapes=[pltpu.VMEM((rows, depth), jnp.bfloat16)],
        ),
        out_shape=jax.ShapeDtypeStruct((rows, columns), jnp.bfloat16),
        compiler_params=PARAMS,
        cost_estimate=pl.CostEstimate(
            flops=2 * rows * depth * columns,
            bytes_accessed=4 << 20,
            transcendentals=0,
        ),
        name="output_projection",
    )(meta, *parts, *weights)


def unpack_kernel(own_row, other_row, pages):
    _, pair, members, capacity, part = own_row.shape
    width = part // (2 * PAGE)
    for source in range(pair):
        for low in range(pair):
            received = own_row if source == low else other_row
            for high in range(members):
                for turn in range(2 * PAGE):
                    start = (turn * pair * members + PAIR * high + low) * width
                    pages[source, :, start : start + width] = received[
                        0, low, high, :, turn * width : (turn + 1) * width
                    ]


def unpack(own_row, other_row):
    planes, pair, members, capacity, part = own_row.shape
    block = pl.BlockSpec((1,) + own_row.shape[1:], lambda i: (i, 0, 0, 0, 0))
    return pl.pallas_call(
        unpack_kernel,
        grid=(planes,),
        in_specs=[block, block],
        out_specs=pl.BlockSpec((pair, capacity, pair * members * part), lambda i: (i, 0, 0)),
        out_shape=jax.ShapeDtypeStruct(
            (planes * pair, capacity, pair * members * part), jnp.bfloat16
        ),
        compiler_params=pltpu.CompilerParams(vmem_limit_bytes=24 * 1024 * 1024),
        cost_estimate=pl.CostEstimate(flops=0, bytes_accessed=6 << 20, transcendentals=0),
        name="unpack",
    )(own_row, other_row)


def rope_tables(positions):
    half_dim = HEAD_DIM // 2
    inverse = 1.0 / ROPE_BASE ** (jnp.arange(half_dim, dtype=jnp.float32) * 2.0 / HEAD_DIM)
    angles = inverse[:, None] * positions.astype(jnp.float32)[None, :]
    return jnp.cos(angles), jnp.sin(angles)


def bounds_kernel(ids, starts, ends, ranges):
    shape = (8, ids.shape[1])
    width = ids.shape[1]
    own = jnp.broadcast_to(ids[...], shape)
    index = lax.broadcasted_iota(jnp.int32, shape, 1)
    first = jnp.where((own != pltpu.roll(own, 1, 1)) | (index == 0), index, 0)
    after = jnp.where((own != pltpu.roll(own, width - 1, 1)) | (index == width - 1), index + 1, width)
    shift = 1
    while shift < SPAN:
        first = jnp.maximum(first, jnp.where(index >= shift, pltpu.roll(first, shift, 1), 0))
        after = jnp.minimum(
            after, jnp.where(index < width - shift, pltpu.roll(after, width - shift, 1), width)
        )
        shift *= 2
    rows = starts.shape[1]
    starts[...] = first[:1, SPAN : SPAN + rows]
    ends[...] = after[:1, SPAN : SPAN + rows]
    lane = lax.broadcasted_iota(jnp.int32, (rows, ranges.shape[1]), 0)
    entry = lax.broadcasted_iota(jnp.int32, (rows, ranges.shape[1]), 1)
    own_lane = entry // 2 * TILE + lax.rem(entry, 2) * (TILE - 1)
    chosen = jnp.where(lane == own_lane, 1.0, 0.0)
    odd = lax.rem(entry, 2) == 1
    begin = (first[:, SPAN : SPAN + rows] // TILE).astype(jnp.bfloat16)
    end = ((after[:, SPAN : SPAN + rows] + TILE - 1) // TILE).astype(jnp.bfloat16)
    from_begin = jnp.where(odd, 0.0, chosen).astype(jnp.bfloat16)
    from_end = jnp.where(odd, chosen, 0.0).astype(jnp.bfloat16)
    found = jnp.dot(begin, from_begin, preferred_element_type=jnp.float32) + jnp.dot(
        end, from_end, preferred_element_type=jnp.float32
    )
    ranges[...] = found[:1].astype(jnp.int32)


def document_bounds(window_ids, rows):
    return pl.pallas_call(
        bounds_kernel,
        out_shape=[jax.ShapeDtypeStruct((1, rows), jnp.int32)] * 2
        + [jax.ShapeDtypeStruct((1, 128), jnp.int32)],
        compiler_params=PARAMS,
        cost_estimate=pl.CostEstimate(flops=1 << 34, bytes_accessed=0, transcendentals=0),
        name="document_bounds",
    )(window_ids[None, :])


def per_device(tokens, norm_gain, input_weight, output_weight, segment_ids, page_owner):
    rows, model_width = tokens.shape
    peers, members = lax.axis_size("tok"), lax.axis_size("grp")
    place, column = lax.axis_index("tok"), lax.axis_index("grp")
    low = place % PAIR
    blocks = PAIR * members
    member = low * members + column
    group_rows = rows * blocks
    width = model_width // blocks
    pages = rows // PAGE

    flat = peers * members
    owners = page_owner[:, 0]
    capacity = max(2, (2 * pages + peers - 1) // peers)
    halves = []
    for parity in range(PAIR):
        pieces = []
        for number in range(PARTS):
            start = number * PAIR * width
            choices = [input_weight[:, start : start + width], input_weight[:, start + width : start + 2 * width]]
            piece = jnp.where((low ^ parity) == 0, choices[0], choices[1])
            route = []
            for source in range(flat):
                row, column_from = divmod(source, members)
                target = (row ^ parity) * members + (PARTS * column_from + number) % members
                route.append((source, target))
            pieces.append(lax.ppermute(piece, ("tok", "grp"), route))
        halves.append(jnp.concatenate(pieces, axis=1))
    plane = jnp.concatenate(halves, axis=0)
    own = layer_norm(tokens, norm_gain[None, :], owners, capacity)
    own, plane = lax.optimization_barrier((own, plane))

    across, along = flipped(own, "grp", 2), flipped(own, "tok", 1)
    sibling = flipped(own, "grp", 1)
    planes = {0: plane}
    bit = peers // 2
    while bit > 1:
        planes[bit] = flipped(plane, "tok", bit)
        bit //= 2
    for distance in range(PAIR, peers, PAIR):
        if distance not in planes:
            step_bit = distance & -distance
            planes[distance] = flipped(planes[distance ^ step_bit], "tok", step_bit)
    weights = [planes[distance] for distance in range(0, peers, PAIR)]

    first_row = place // PAIR * group_rows
    padded_ids = jnp.concatenate(
        [
            jnp.full((SPAN,), -1, jnp.int32),
            segment_ids,
            jnp.full((SPAN,), 1 << 30, jnp.int32),
        ]
    )
    window_ids = lax.dynamic_slice_in_dim(padded_ids, first_row, group_rows + 2 * SPAN, 0)
    window_ids, plane = lax.optimization_barrier((window_ids, plane))
    *bounds, ranges = document_bounds(window_ids, group_rows)
    positions = SPAN + jnp.arange(group_rows, dtype=jnp.int32) - bounds[0][0]
    order = [(number * members + column) % PARTS for number in range(PARTS)]
    meta = jnp.stack([member, place] + order).astype(jnp.int32)
    cosine, sine = rope_tables(positions)
    last_rows = output_weight
    bit = PAIR
    while 4 * bit < peers:
        last_rows = jnp.concatenate([last_rows, flipped(last_rows, "tok", bit)], axis=0)
        bit *= 2
    other_rows = flipped(last_rows, "tok", bit)
    across, along, sibling, weights, last_rows, other_rows, cosine, sine, meta = (
        lax.optimization_barrier(
            (across, along, sibling, weights, last_rows, other_rows, cosine, sine, meta)
        )
    )
    last_rows = jnp.concatenate([last_rows, other_rows], axis=0)

    half, held = rows // 2, rows + EXTRA_ROWS
    corner = [flipped(across[:half], "tok", 1), flipped(along[half:], "grp", 2)]
    across_sibling = flipped(across, "grp", 1)
    along_sibling = flipped(along, "grp", 1)
    other_rows = flipped(last_rows, "tok", peers // 2)
    near_blocks = [own, sibling, across, across_sibling]
    near_layout = [[(number, 0, held)] for number in range(4)]
    far_layout = [[(0, 0, held)], [(1, 0, held)]]
    far_layout += [[(number, 0, half), (number + 1, half, held - half)] for number in (2, 4)]

    sizes = (weights, cosine, sine, rows, blocks, peers, capacity)

    def to_owners(send):
        received = lax.all_to_all(
            send.reshape((flat,) + send.shape[2:]),
            ("tok", "grp"),
            split_axis=0,
            concat_axis=0,
            tiled=True,
        )
        return received.reshape((peers // PAIR, PAIR, members) + send.shape[2:])

    queries, pairs, send = project(meta, 0, near_layout, near_blocks, *sizes, ())
    send, corner, along_sibling, last_rows, other_rows = lax.optimization_barrier(
        (send, corner, along_sibling, last_rows, other_rows)
    )
    own_row = to_owners(send)
    corner_sibling = [flipped(block, "grp", 1) for block in corner]
    far_blocks = [along, along_sibling] + corner + corner_sibling
    last_rows = jnp.concatenate([last_rows, other_rows], axis=0)
    queries, pairs, send = project(meta, 4, far_layout, far_blocks, *sizes, (queries, pairs))
    before = shifted(pairs[group_rows - SPAN :], "tok", PAIR)
    after = shifted(pairs[:SPAN], "tok", -PAIR)
    other_rows = flipped(last_rows, "tok", 1)
    across_rows = flipped(last_rows, "grp", 2)
    corner_rows = lax.ppermute(
        last_rows,
        ("tok", "grp"),
        [(source, source ^ (members + 2)) for source in range(flat)],
    )

    edges = attend_edges(meta, ranges, queries, *bounds, pairs)
    before, after, edges, last_rows, other_rows, across_rows, corner_rows, send = (
        lax.optimization_barrier(
            (before, after, edges, last_rows, other_rows, across_rows, corner_rows, send)
        )
    )
    other_row = to_owners(send)
    columns = jnp.concatenate([last_rows, other_rows, across_rows, corner_rows], axis=0)
    row_order = place
    if output_weight.shape[0] != width:
        wanted = jnp.arange(peers) ^ place
        wanted = wanted // PAIR + wanted % PAIR * (peers // PAIR)
        shards = columns.reshape((PAIR, peers) + output_weight.shape)
        columns = shards[:, wanted].reshape(columns.shape)
        row_order = jnp.full_like(place, -1)
    mixed = attend_finish(meta, ranges, queries, *bounds, pairs, before, after, edges, rows)
    last_weights = [columns, flipped(columns, "grp", 1)]
    parts = [mixed[0]] + [
        lax.ppermute(
            mixed[distance],
            ("tok", "grp"),
            [(source, source ^ distance) for source in range(flat)],
        )
        for distance in range(1, blocks)
    ]
    output_meta = jnp.stack([member, row_order]).astype(jnp.int32)
    attended = output_projection(output_meta, parts, last_weights)
    cache_pages = unpack(own_row, other_row).reshape(
        peers * capacity, 2 * PAGE * model_width
    )
    return attended, cache_pages


def solution(mesh):
    placed = (
        P(("tok", "grp"), None),
        P(),
        P("tok", "grp"),
        P("tok", "grp"),
        P(),
        P(("tok", "grp"), None),
    )
    return jax.shard_map(
        per_device,
        mesh=mesh,
        in_specs=placed,
        out_specs=(P(("tok", "grp"), None), P(("tok", "grp"), None)),
        check_vma=False,
    )
```

```python
import functools

import jax
import jax.numpy as jnp
from jax import lax
from jax.experimental import pallas as pl
from jax.experimental.pallas import tpu as pltpu
from jax.sharding import PartitionSpec as P

H = 16
SPAN = 1024
PAGE = 4
HEAD_DIM = 64

NEG_FILL = -1e30
ROPE_BASE = 160000.0
EPSILON = 1e-05
TILE = 256
PARTS = 3
PAIR = 2
ONES_ROWS = 16
HEAD_ROWS = HEAD_DIM + ONES_ROWS
EXTRA_ROWS = 16
KEYS = 512
SCALE = HEAD_DIM ** (-0.5)
VMEM_LIMIT = 60 * 1024 * 1024
PARAMS = pltpu.CompilerParams(vmem_limit_bytes=VMEM_LIMIT)


def flipped(value, axis, bit):
    count = lax.axis_size(axis)
    return lax.ppermute(value, axis, [(source, source ^ bit) for source in range(count)])


def shifted(value, axis, steps):
    count = lax.axis_size(axis)
    initial, last = (max(0, -steps), min(count, count - steps))
    return lax.ppermute(value, axis, [(source, source + steps) for source in range(initial, last)])


def norm_kernel(capacity, tokens, gain, owner_row, normed, owners):
    rows = tokens.shape[0]
    values = tokens[...].astype(jnp.float32)
    centred = values - jnp.mean(values, axis=-1, keepdims=True)
    spread = jnp.mean(jnp.square(centred), axis=-1, keepdims=True)
    normed[:rows, :] = (centred * lax.rsqrt(spread + EPSILON) * gain[...]).astype(jnp.bfloat16)
    pages = owner_row.shape[1]
    owners[...] = jnp.full(owners.shape, -1.0, jnp.float32)
    owners[:1, :pages] = owner_row[...].astype(jnp.float32)
    lanes = owners.shape[1]
    across = jnp.broadcast_to(owners[:1, :], (lanes, lanes))
    earlier = lax.broadcasted_iota(jnp.int32, (lanes, lanes), 0) < lax.broadcasted_iota(
        jnp.int32, (lanes, lanes), 1
    )
    same = (across.T == across) & earlier
    ranks = jnp.sum(jnp.where(same, 1.0, 0.0), axis=0, keepdims=True)
    slots = owners[:1, :] * capacity + ranks
    normed[rows:, :] = jnp.zeros((EXTRA_ROWS, normed.shape[1]), jnp.bfloat16)
    normed[rows:, :lanes] = jnp.broadcast_to(slots, (EXTRA_ROWS, lanes)).astype(jnp.bfloat16)


def layer_norm(tokens, gain, owners, capacity):
    rows, width = tokens.shape
    lanes = -(-owners.shape[0] // 128) * 128
    return pl.pallas_call(
        functools.partial(norm_kernel, capacity),
        out_shape=jax.ShapeDtypeStruct((rows + EXTRA_ROWS, width), jnp.bfloat16),
        scratch_shapes=[pltpu.VMEM((8, lanes), jnp.float32)],
        compiler_params=PARAMS,
        name="layer_norm",
    )(tokens, gain, owners[None, :])


def project_kernel(first, layout, weight_count, peers, capacity, meta, *refs):
    operands = 1 + max(entry[0] for pieces in layout for entry in pieces)
    tokens = refs[:operands]
    weights = refs[operands : operands + weight_count]
    cosine, sine = refs[operands + weight_count : operands + weight_count + 2]
    query_out, pair_out, send_out, blocks, weight, page_source, sems = refs[-7:]
    step = pl.program_id(0)
    steps = len(layout)
    rows = query_out.shape[0]
    width = query_out.shape[1]
    shard = weights[0].shape[0] // 2

    def arrivals(number):
        return [
            pltpu.make_async_copy(
                tokens[operand],
                blocks.at[number, pl.ds(offset, count), :],
                sems.at[number, place],
            )
            for place, (operand, offset, count) in enumerate(layout[number])
        ]

    @pl.when(step == 0)
    def _():
        for number in range(steps):
            for copy in arrivals(number):
                copy.start()
        for plane in range(weight_count):
            for low in range(2):
                row = pl.multiple_of((meta[1] ^ (2 * plane + low)) * shard, shard)
                for number in range(PARTS):
                    column = pl.multiple_of(meta[2 + number] * width, width)
                    weight[pl.ds(row, shard), number * width : (number + 1) * width] = weights[
                        plane
                    ][low * shard : (low + 1) * shard, pl.ds(column, width)]

    for number in range(steps):

        @pl.when(step == number)
        def _():
            for copy in arrivals(number):
                copy.wait()

    joined = jnp.dot(blocks[step, :rows, :], weight[...], preferred_element_type=jnp.float32)
    cosines = jnp.concatenate([cosine[...]] * 4, axis=0).T
    sines = jnp.concatenate([-sine[...], sine[...]] * 2, axis=0).T
    first_half = lax.rem(lax.broadcasted_iota(jnp.int32, (rows, width), 1), HEAD_DIM) < (
        HEAD_DIM // 2
    )

    def rotate(values):
        partner = jnp.where(
            first_half,
            pltpu.roll(values, width - HEAD_DIM // 2, 1),
            pltpu.roll(values, HEAD_DIM // 2, 1),
        )
        return (values * cosines + partner * sines).astype(jnp.bfloat16)

    query_out[...] = rotate(joined[:, :width]) * jnp.asarray(SCALE, jnp.bfloat16)
    keys = rotate(joined[:, width : 2 * width])
    values = joined[:, 2 * width :].astype(jnp.bfloat16)
    pair_out[:, :width] = keys
    pair_out[:, width:] = values
    page_source[0] = keys.astype(jnp.float32)
    page_source[1] = values.astype(jnp.float32)

    pages = rows // PAGE
    slot_count = peers * capacity
    slots = blocks[step, rows : rows + EXTRA_ROWS, :128].astype(jnp.float32)[:1, :pages]
    chosen = (
        lax.broadcasted_iota(jnp.int32, (slot_count, pages), 0).astype(jnp.float32) == slots
    ).astype(jnp.bfloat16)
    for turn in range(PAGE):
        page_part = jnp.concatenate(
            [
                page_source[half, pl.ds(turn, pages, stride=PAGE), :].astype(jnp.bfloat16)
                for half in range(2)
            ],
            axis=1,
        )
        placed = jnp.dot(chosen, page_part, preferred_element_type=jnp.float32)
        columns = slice(turn * 2 * width, (turn + 1) * 2 * width)
        for peer in range(peers):
            send_out[peer, 0, :, columns] = placed[
                peer * capacity : (peer + 1) * capacity
            ].astype(jnp.bfloat16)


def project(meta, first, layout, operands, weights, cosine, sine, rows, blocks, peers, capacity, into):
    steps = len(layout)
    model_width = operands[0].shape[1]
    group_rows = rows * blocks
    width = model_width // blocks
    members = blocks // PAIR
    whole = lambda shape: pl.BlockSpec(shape, lambda i, m: (0,) * len(shape))
    place = lambda i, m: m[0] ^ (first + i)
    table = pl.BlockSpec((HEAD_DIM // 2, rows), lambda i, m: (0, place(i, m)))
    send_shape = (peers, members, capacity, 2 * PAGE * width)
    return pl.pallas_call(
        functools.partial(project_kernel, first, layout, len(weights), peers, capacity),
        grid_spec=pltpu.PrefetchScalarGridSpec(
            num_scalar_prefetch=1,
            grid=(steps,),
            in_specs=[pl.BlockSpec(memory_space=pl.ANY)] * len(operands)
            + [whole(weights[0].shape)] * len(weights)
            + [table, table]
            + [pl.BlockSpec(memory_space=pl.ANY)] * len(into),
            out_specs=[
                pl.BlockSpec((rows, width), lambda i, m: (place(i, m), 0)),
                pl.BlockSpec((rows, 2 * width), lambda i, m: (place(i, m), 0)),
                pl.BlockSpec(
                    (peers, 1) + send_shape[2:], lambda i, m: (0, place(i, m) % members, 0, 0)
                ),
            ],
            scratch_shapes=[
                pltpu.VMEM((steps, rows + EXTRA_ROWS, model_width), jnp.bfloat16),
                pltpu.VMEM((model_width, PARTS * width), jnp.bfloat16),
                pltpu.VMEM((2, rows, width), jnp.float32),
                pltpu.SemaphoreType.DMA((steps, 2)),
            ],
        ),
        out_shape=[
            jax.ShapeDtypeStruct((group_rows, width), jnp.bfloat16),
            jax.ShapeDtypeStruct((group_rows, 2 * width), jnp.bfloat16),
            jax.ShapeDtypeStruct(send_shape, jnp.bfloat16),
        ],
        input_output_aliases={
            1 + len(operands) + len(weights) + 2 + number: number for number in range(len(into))
        },
        compiler_params=PARAMS,
        cost_estimate=pl.CostEstimate(
            flops=16 * steps * rows * model_width * PARTS * width,
            bytes_accessed=(3 * steps) << 19,
            transcendentals=0,
        ),
        name="project",
    )(meta, *operands, *weights, cosine, sine, *into)


def mask_heads(queries, masked):
    turned = queries[...].T
    head_of_row = lax.broadcasted_iota(jnp.int32, turned.shape, 0) // HEAD_DIM
    for head in range(masked.shape[0]):
        masked[head] = jnp.where(head_of_row == head, turned, jnp.zeros((), jnp.bfloat16))


def with_ones(values):
    turned = values.T
    ones = jnp.ones((ONES_ROWS, values.shape[0]), values.dtype)
    rows = []
    for head in range(values.shape[1] // HEAD_DIM):
        rows += [turned[head * HEAD_DIM : (head + 1) * HEAD_DIM], ones]
    return jnp.concatenate(rows, axis=0)


def sweep(jobs, peaks):
    plans = []
    steps = 0
    for begin, end, base, pairs, values_of, masked, starts, ends, total in jobs:
        held = pairs.shape[0] // TILE
        begin, end = jnp.maximum(begin, base), jnp.minimum(end, base + held)
        last = jnp.minimum(ends, end * TILE)
        steps = jnp.maximum(steps, (end - begin + KEYS // TILE - 1) // (KEYS // TILE))
        plans.append((begin, base, held, pairs, values_of, masked, starts, last, total))

    key_rows = lax.broadcasted_iota(jnp.int32, (KEYS, TILE), 0)

    def one(number, peaks):
        units = []
        for place, plan in enumerate(plans):
            begin, base, held, pairs, values_of, masked, starts, last, total = plan
            wanted = begin + number * (KEYS // TILE)
            block = jnp.minimum(wanted, base + held - KEYS // TILE)
            row = pl.multiple_of((block - base) * TILE, TILE)
            keys = pairs[pl.ds(row, KEYS), : pairs.shape[1] // 2]
            values = values_of(row)
            first_key = block * TILE
            allowed = (key_rows >= jnp.maximum(starts, wanted * TILE) - first_key) & (
                key_rows < last - first_key
            )
            units += [
                (place, head, keys, values, masked, allowed, total)
                for head in range(len(peaks[place]))
            ]

        def products(unit):
            place, head, keys, values, masked, allowed, total = unit
            return jnp.dot(keys, masked[head], preferred_element_type=jnp.float32)

        new_peaks = [[] for _ in plans]
        ahead = products(units[0])
        for number, unit in enumerate(units):
            place, head, keys, values, masked, allowed, total = unit
            scores = ahead
            if number + 1 < len(units):
                ahead = products(units[number + 1])
            scores = jnp.where(allowed, scores, NEG_FILL)
            old_peak = peaks[place][head]
            peak = jnp.maximum(old_peak, jnp.max(scores, axis=0, keepdims=True))
            fade = jnp.exp(old_peak - peak)
            weights = jnp.exp(scores - peak).astype(jnp.bfloat16)
            own = slice(head * HEAD_ROWS, (head + 1) * HEAD_ROWS)
            total[own, :] = total[own, :] * fade + jnp.dot(
                values[own, :], weights, preferred_element_type=jnp.float32
            )
            new_peaks[place].append(peak)
        return tuple(tuple(job_peaks) for job_peaks in new_peaks)

    return lax.fori_loop(0, steps, one, peaks)


def fresh_peaks(heads):
    return tuple(jnp.full((1, TILE), NEG_FILL, jnp.float32) for _ in range(heads))


def edge_kernel(edge, meta, ranges, *refs):
    rows, pairs, outs, (masked, values) = refs[:6], refs[6], refs[7:11], refs[11:]
    step = pl.program_id(0)
    width = rows[0].shape[1]
    heads = width // HEAD_DIM
    tiles = pairs.shape[0] // TILE

    @pl.when(step == 0)
    def _():
        for number in range(tiles):
            own = slice(number * TILE, (number + 1) * TILE)
            values[:, own] = with_ones(pairs[own, width:])

    jobs = []
    places = tile_places(step, edge, tiles)
    for side in range(2):
        tile = places[side]
        queries, starts, ends = rows[3 * side : 3 * side + 3]
        mask_heads(queries, masked.at[side])
        total = outs[side]
        total[...] = jnp.zeros_like(total)
        jobs.append(
            (
                ranges[0, 2 * tile],
                ranges[0, 2 * tile + 1],
                edge,
                pairs,
                lambda row: values[:, pl.ds(row, KEYS)],
                masked.at[side],
                starts[...],
                ends[...],
                total.at[0],
            )
        )
    peaks = sweep(jobs, (fresh_peaks(heads), fresh_peaks(heads)))
    for side in range(2):
        for head in range(heads):
            outs[2 + side][0, head : head + 1, :] = peaks[side][head]


def finish_kernel(edge, meta, ranges, *refs):
    rows, pairs, halos, held, held_peaks = refs[:6], refs[6], refs[7:9], refs[9:11], refs[11:13]
    outs, (masked, sums, peaks_held, mixed) = refs[13:-4], refs[-4:]
    held_steps = edge + 1
    step = pl.program_id(0)
    width = rows[0].shape[1]
    heads = width // HEAD_DIM
    tiles = pairs.shape[0] // TILE
    places = tile_places(step, edge, tiles)

    def jobs_on(keys, bases):
        jobs = []
        for side in range(2):
            queries, starts, ends = rows[3 * side : 3 * side + 3]
            mask_heads(queries, masked.at[side])
            jobs.append(
                (
                    ranges[0, 2 * places[side]],
                    ranges[0, 2 * places[side] + 1],
                    bases[side],
                    keys[side],
                    lambda row, held=keys[side]: with_ones(held[pl.ds(row, KEYS), width:]),
                    masked.at[side],
                    starts[...],
                    ends[...],
                    sums.at[side],
                )
            )
        return jobs

    @pl.when(step < held_steps)
    def _():
        for side in range(2):
            sums[side] = held[side][0]
            peaks_held[side] = held_peaks[side][0]

    @pl.when(step >= held_steps)
    def _():
        sums[...] = jnp.zeros_like(sums)
        peaks = sweep(jobs_on((pairs, pairs), (edge, edge)), (fresh_peaks(heads),) * 2)
        for side in range(2):
            for head in range(heads):
                peaks_held[side, head : head + 1, :] = peaks[side][head]

    reaches_back = ranges[0, 2 * places[0]] < edge
    reaches_ahead = ranges[0, 2 * places[1] + 1] > edge + tiles

    @pl.when((step < edge) & (reaches_back | reaches_ahead))
    def _():
        peaks = tuple(
            tuple(peaks_held[side, head : head + 1, :] for head in range(heads))
            for side in range(2)
        )
        sweep(jobs_on(halos, (0, edge + tiles)), peaks)

    for side in range(2):
        parts = []
        for head in range(heads):
            row = head * HEAD_ROWS
            parts.append(
                sums[side, row : row + HEAD_DIM, :]
                / sums[side, row + HEAD_DIM : row + HEAD_DIM + 1, :]
            )
        tile_rows = pl.ds(pl.multiple_of(places[side] * TILE, TILE), TILE)
        mixed[tile_rows, :] = jnp.concatenate(parts, axis=0).T.astype(jnp.bfloat16)

    @pl.when(step == pl.num_programs(0) - 1)
    def _():
        count = outs[0].shape[0]
        for distance, out in enumerate(outs):
            out[...] = mixed[pl.ds(pl.multiple_of((meta[0] ^ distance) * count, 128), count), :]


def tile_places(step, edge, tiles):
    middle = edge + 2 * (step - edge)
    return (
        jnp.where(step < edge, step, middle),
        jnp.where(step < edge, tiles - edge + step, middle + 1),
    )


def attend_specs(width, edge, tiles):
    specs = []
    for side in range(2):
        place = lambda i, side=side: tile_places(i, edge, tiles)[side]
        specs.append(pl.BlockSpec((TILE, width), lambda i, m, r, place=place: (place(i), 0)))
        specs += [pl.BlockSpec((1, TILE), lambda i, m, r, place=place: (0, place(i)))] * 2
    return specs + [pl.BlockSpec((tiles * TILE, 2 * width), lambda i, m, r: (0, 0))]


def attend_edges(meta, ranges, queries, starts, ends, pairs):
    group_rows, width = queries.shape
    heads = width // HEAD_DIM
    tiles, edge = group_rows // TILE, SPAN // TILE
    steps = edge + 1
    shapes = [(steps, heads * HEAD_ROWS, TILE)] * 2 + [(steps, 8, TILE)] * 2
    return pl.pallas_call(
        functools.partial(edge_kernel, edge),
        grid_spec=pltpu.PrefetchScalarGridSpec(
            num_scalar_prefetch=2,
            grid=(steps,),
            in_specs=attend_specs(width, edge, tiles),
            out_specs=[pl.BlockSpec((1,) + shape[1:], lambda i, m, r: (i, 0, 0)) for shape in shapes],
            scratch_shapes=[
                pltpu.VMEM((2, heads, width, TILE), jnp.bfloat16),
                pltpu.VMEM((heads * HEAD_ROWS, group_rows), jnp.bfloat16),
            ],
        ),
        out_shape=[jax.ShapeDtypeStruct(shape, jnp.float32) for shape in shapes],
        compiler_params=PARAMS,
        cost_estimate=pl.CostEstimate(
            flops=16 * group_rows * 1024 * width,
            bytes_accessed=5 << 20,
            transcendentals=group_rows * 1024 * heads,
        ),
        name="attend_edges",
    )(meta, ranges, queries, starts, ends, queries, starts, ends, pairs)


def attend_finish(meta, ranges, queries, starts, ends, pairs, before, after, held, rows):
    group_rows, width = queries.shape
    heads = width // HEAD_DIM
    tiles, edge = group_rows // TILE, SPAN // TILE
    members = group_rows // rows
    return pl.pallas_call(
        functools.partial(finish_kernel, edge),
        grid_spec=pltpu.PrefetchScalarGridSpec(
            num_scalar_prefetch=2,
            grid=(edge + (tiles - 2 * edge) // 2,),
            in_specs=attend_specs(width, edge, tiles)
            + [pl.BlockSpec((SPAN, 2 * width), lambda i, m, r: (0, 0))] * 2
            + [
                pl.BlockSpec(
                    (1,) + part.shape[1:], lambda i, m, r: (jnp.minimum(i, edge), 0, 0)
                )
                for part in held
            ],
            out_specs=[pl.BlockSpec((rows, width), lambda i, m, r: (0, 0))] * members,
            scratch_shapes=[
                pltpu.VMEM((2, heads, width, TILE), jnp.bfloat16),
                pltpu.VMEM((2, heads * HEAD_ROWS, TILE), jnp.float32),
                pltpu.VMEM((2, 8, TILE), jnp.float32),
                pltpu.VMEM((group_rows, width), jnp.bfloat16),
            ],
        ),
        out_shape=[jax.ShapeDtypeStruct((rows, width), jnp.bfloat16)] * members,
        compiler_params=PARAMS,
        cost_estimate=pl.CostEstimate(
            flops=16 * group_rows * 1024 * width,
            bytes_accessed=5 << 20,
            transcendentals=group_rows * 1024 * heads,
        ),
        name="attend_finish",
    )(meta, ranges, queries, starts, ends, queries, starts, ends, pairs, before, after, *held)


def output_kernel(members, meta, *refs):
    parts, weights, result, mixed = refs[:members], refs[members:-2], refs[-2], refs[-1]
    width = parts[0].shape[1]
    tile = weights[0].shape[1]
    for distance in range(members):
        source = meta[0] ^ distance
        head_pair = PAIR * (source % (members // PAIR)) + source // (members // PAIR)
        shard = head_pair ^ meta[1]
        shard = jnp.where(meta[1] < 0, head_pair, shard // PAIR + shard % PAIR * (members // PAIR))
        columns = pl.ds(pl.multiple_of(shard * width, width), width)
        mixed[:, columns] = parts[distance][...]
    depth = mixed.shape[1]
    groups = len(weights) * (weights[0].shape[0] // depth)
    for distance in range(groups):
        columns = pl.ds(pl.multiple_of((meta[0] % groups ^ distance) * tile, tile), tile)
        start = distance // len(weights) * depth
        result[:, columns] = jnp.dot(
            mixed[...],
            weights[distance % len(weights)][start : start + depth, :],
            preferred_element_type=jnp.float32,
        ).astype(jnp.bfloat16)


def output_projection(meta, parts, weights):
    rows, width = parts[0].shape
    depth, tile = width * len(parts), weights[0].shape[1]
    columns = sum(weight.shape[0] for weight in weights) // depth * tile
    whole = lambda shape: pl.BlockSpec(shape, lambda i, m: (0, 0))
    return pl.pallas_call(
        functools.partial(output_kernel, len(parts)),
        grid_spec=pltpu.PrefetchScalarGridSpec(
            num_scalar_prefetch=1,
            grid=(1,),
            in_specs=[whole(parts[0].shape)] * len(parts)
            + [whole(weight.shape) for weight in weights],
            out_specs=whole((rows, columns)),
            scratch_shapes=[pltpu.VMEM((rows, depth), jnp.bfloat16)],
        ),
        out_shape=jax.ShapeDtypeStruct((rows, columns), jnp.bfloat16),
        compiler_params=PARAMS,
        cost_estimate=pl.CostEstimate(
            flops=2 * rows * depth * columns,
            bytes_accessed=4 << 20,
            transcendentals=0,
        ),
        name="output_projection",
    )(meta, *parts, *weights)


def stack_kernel(count, *refs):
    blocks, result, sems = refs[:count], refs[count], refs[count + 1]
    rows = blocks[0].shape[0]
    copies = [
        pltpu.make_async_copy(block, result.at[pl.ds(number * rows, rows), :], sems.at[number])
        for number, block in enumerate(blocks)
    ]
    for copy in copies:
        copy.start()
    for copy in copies:
        copy.wait()


def stacked(blocks):
    rows, width = blocks[0].shape
    return pl.pallas_call(
        functools.partial(stack_kernel, len(blocks)),
        in_specs=[pl.BlockSpec(memory_space=pl.ANY)] * len(blocks),
        out_specs=pl.BlockSpec(memory_space=pl.ANY),
        out_shape=jax.ShapeDtypeStruct((len(blocks) * rows, width), blocks[0].dtype),
        scratch_shapes=[pltpu.SemaphoreType.DMA((len(blocks),))],
        compiler_params=PARAMS,
        cost_estimate=pl.CostEstimate(flops=0, bytes_accessed=2 << 20, transcendentals=0),
        name="stacked",
    )(*blocks)


def unpack_kernel(own_row, other_row, pages):
    _, pair, members, capacity, part = own_row.shape
    width = part // (2 * PAGE)
    for source in range(pair):
        for low in range(pair):
            received = own_row if source == low else other_row
            for high in range(members):
                for turn in range(2 * PAGE):
                    start = (turn * pair * members + PAIR * high + low) * width
                    pages[source, :, start : start + width] = received[
                        0, low, high, :, turn * width : (turn + 1) * width
                    ]


def unpack(own_row, other_row):
    planes, pair, members, capacity, part = own_row.shape
    block = pl.BlockSpec((1,) + own_row.shape[1:], lambda i: (i, 0, 0, 0, 0))
    return pl.pallas_call(
        unpack_kernel,
        grid=(planes,),
        in_specs=[block, block],
        out_specs=pl.BlockSpec((pair, capacity, pair * members * part), lambda i: (i, 0, 0)),
        out_shape=jax.ShapeDtypeStruct(
            (planes * pair, capacity, pair * members * part), jnp.bfloat16
        ),
        compiler_params=pltpu.CompilerParams(vmem_limit_bytes=24 * 1024 * 1024),
        cost_estimate=pl.CostEstimate(flops=0, bytes_accessed=6 << 20, transcendentals=0),
        name="unpack",
    )(own_row, other_row)


def rope_tables(positions):
    half_dim = HEAD_DIM // 2
    inverse = 1.0 / ROPE_BASE ** (jnp.arange(half_dim, dtype=jnp.float32) * 2.0 / HEAD_DIM)
    angles = inverse[:, None] * positions.astype(jnp.float32)[None, :]
    return jnp.cos(angles), jnp.sin(angles)


def bounds_kernel(ids, starts, ends, ranges):
    shape = (8, ids.shape[1])
    width = ids.shape[1]
    own = jnp.broadcast_to(ids[...], shape)
    index = lax.broadcasted_iota(jnp.int32, shape, 1)
    first = jnp.where((own != pltpu.roll(own, 1, 1)) | (index == 0), index, 0)
    after = jnp.where((own != pltpu.roll(own, width - 1, 1)) | (index == width - 1), index + 1, width)
    shift = 1
    while shift < SPAN:
        first = jnp.maximum(first, jnp.where(index >= shift, pltpu.roll(first, shift, 1), 0))
        after = jnp.minimum(
            after, jnp.where(index < width - shift, pltpu.roll(after, width - shift, 1), width)
        )
        shift *= 2
    rows = starts.shape[1]
    starts[...] = first[:1, SPAN : SPAN + rows]
    ends[...] = after[:1, SPAN : SPAN + rows]
    lane = lax.broadcasted_iota(jnp.int32, (rows, ranges.shape[1]), 0)
    entry = lax.broadcasted_iota(jnp.int32, (rows, ranges.shape[1]), 1)
    own_lane = entry // 2 * TILE + lax.rem(entry, 2) * (TILE - 1)
    chosen = jnp.where(lane == own_lane, 1.0, 0.0)
    odd = lax.rem(entry, 2) == 1
    begin = (first[:, SPAN : SPAN + rows] // TILE).astype(jnp.bfloat16)
    end = ((after[:, SPAN : SPAN + rows] + TILE - 1) // TILE).astype(jnp.bfloat16)
    from_begin = jnp.where(odd, 0.0, chosen).astype(jnp.bfloat16)
    from_end = jnp.where(odd, chosen, 0.0).astype(jnp.bfloat16)
    found = jnp.dot(begin, from_begin, preferred_element_type=jnp.float32) + jnp.dot(
        end, from_end, preferred_element_type=jnp.float32
    )
    ranges[...] = found[:1].astype(jnp.int32)


def document_bounds(window_ids, rows):
    return pl.pallas_call(
        bounds_kernel,
        out_shape=[jax.ShapeDtypeStruct((1, rows), jnp.int32)] * 2
        + [jax.ShapeDtypeStruct((1, 128), jnp.int32)],
        compiler_params=PARAMS,
        cost_estimate=pl.CostEstimate(flops=1 << 34, bytes_accessed=0, transcendentals=0),
        name="document_bounds",
    )(window_ids[None, :])


def per_device(tokens, norm_gain, input_weight, output_weight, segment_ids, page_owner):
    rows, model_width = tokens.shape
    peers, members = lax.axis_size("tok"), lax.axis_size("grp")
    place, column = lax.axis_index("tok"), lax.axis_index("grp")
    low = place % PAIR
    blocks = PAIR * members
    member = low * members + column
    group_rows = rows * blocks
    width = model_width // blocks
    pages = rows // PAGE

    flat = peers * members
    owners = page_owner[:, 0]
    capacity = max(2, (2 * pages + peers - 1) // peers)
    halves = []
    for parity in range(PAIR):
        pieces = []
        for number in range(PARTS):
            start = number * PAIR * width
            choices = [input_weight[:, start : start + width], input_weight[:, start + width : start + 2 * width]]
            piece = jnp.where((low ^ parity) == 0, choices[0], choices[1])
            route = []
            for source in range(flat):
                row, column_from = divmod(source, members)
                target = (row ^ parity) * members + (PARTS * column_from + number) % members
                route.append((source, target))
            pieces.append(lax.ppermute(piece, ("tok", "grp"), route))
        halves.append(jnp.concatenate(pieces, axis=1))
    plane = jnp.concatenate(halves, axis=0)
    own = layer_norm(tokens, norm_gain[None, :], owners, capacity)
    own, plane = lax.optimization_barrier((own, plane))

    across, along = flipped(own, "grp", 2), flipped(own, "tok", 1)
    sibling = flipped(own, "grp", 1)
    planes = {0: plane}
    bit = peers // 2
    while bit > 1:
        planes[bit] = flipped(plane, "tok", bit)
        bit //= 2
    for distance in range(PAIR, peers, PAIR):
        if distance not in planes:
            step_bit = distance & -distance
            planes[distance] = flipped(planes[distance ^ step_bit], "tok", step_bit)
    weights = [planes[distance] for distance in range(0, peers, PAIR)]

    first_row = place // PAIR * group_rows
    segment_ids, plane = lax.optimization_barrier((segment_ids, plane))
    padded_ids = jnp.concatenate(
        [
            jnp.full((SPAN,), -1, jnp.int32),
            segment_ids,
            jnp.full((SPAN,), 1 << 30, jnp.int32),
        ]
    )
    window_ids = lax.dynamic_slice_in_dim(padded_ids, first_row, group_rows + 2 * SPAN, 0)
    *bounds, ranges = document_bounds(window_ids, group_rows)
    positions = SPAN + jnp.arange(group_rows, dtype=jnp.int32) - bounds[0][0]
    order = [(number * members + column) % PARTS for number in range(PARTS)]
    meta = jnp.stack([member, place] + order).astype(jnp.int32)
    cosine, sine = rope_tables(positions)
    last_rows = output_weight
    bit = PAIR
    while 4 * bit < peers:
        last_rows = jnp.concatenate([last_rows, flipped(last_rows, "tok", bit)], axis=0)
        bit *= 2
    other_rows = flipped(last_rows, "tok", bit)
    across, along, sibling, weights, last_rows, other_rows, cosine, sine, meta = (
        lax.optimization_barrier(
            (across, along, sibling, weights, last_rows, other_rows, cosine, sine, meta)
        )
    )
    last_rows = jnp.concatenate([last_rows, other_rows], axis=0)

    half, held = rows // 2, rows + EXTRA_ROWS
    corner = [flipped(across[:half], "tok", 1), flipped(along[half:], "grp", 2)]
    across_sibling = flipped(across, "grp", 1)
    along_sibling = flipped(along, "grp", 1)
    other_rows = flipped(last_rows, "tok", peers // 2)
    near_blocks = [own, sibling, across, across_sibling]
    near_layout = [[(number, 0, held)] for number in range(4)]
    far_layout = [[(0, 0, held)], [(1, 0, held)]]
    far_layout += [[(number, 0, half), (number + 1, half, held - half)] for number in (2, 4)]

    sizes = (weights, cosine, sine, rows, blocks, peers, capacity)

    def to_owners(send):
        received = lax.all_to_all(
            send.reshape((flat,) + send.shape[2:]),
            ("tok", "grp"),
            split_axis=0,
            concat_axis=0,
            tiled=True,
        )
        return received.reshape((peers // PAIR, PAIR, members) + send.shape[2:])

    queries, pairs, send = project(meta, 0, near_layout, near_blocks, *sizes, ())
    send, corner, along_sibling, last_rows, other_rows = lax.optimization_barrier(
        (send, corner, along_sibling, last_rows, other_rows)
    )
    own_row = to_owners(send)
    corner_sibling = [flipped(block, "grp", 1) for block in corner]
    far_blocks = [along, along_sibling] + corner + corner_sibling
    last_rows = jnp.concatenate([last_rows, other_rows], axis=0)
    queries, pairs, send = project(meta, 4, far_layout, far_blocks, *sizes, (queries, pairs))
    before = shifted(pairs[group_rows - SPAN :], "tok", PAIR)
    after = shifted(pairs[:SPAN], "tok", -PAIR)
    other_rows = flipped(last_rows, "tok", 1)
    across_rows = flipped(last_rows, "grp", 2)
    corner_rows = lax.ppermute(
        last_rows,
        ("tok", "grp"),
        [(source, source ^ (members + 2)) for source in range(flat)],
    )

    edges = attend_edges(meta, ranges, queries, *bounds, pairs)
    before, after, edges, last_rows, other_rows, across_rows, corner_rows, send = (
        lax.optimization_barrier(
            (before, after, edges, last_rows, other_rows, across_rows, corner_rows, send)
        )
    )
    other_row = to_owners(send)
    columns = stacked([last_rows, other_rows, across_rows, corner_rows])
    row_order = place
    if output_weight.shape[0] != width:
        wanted = jnp.arange(peers) ^ place
        wanted = wanted // PAIR + wanted % PAIR * (peers // PAIR)
        shards = columns.reshape((PAIR, peers) + output_weight.shape)
        columns = shards[:, wanted].reshape(columns.shape)
        row_order = jnp.full_like(place, -1)
    mixed = attend_finish(meta, ranges, queries, *bounds, pairs, before, after, edges, rows)
    last_weights = [columns, flipped(columns, "grp", 1)]
    parts = [mixed[0]] + [
        lax.ppermute(
            mixed[distance],
            ("tok", "grp"),
            [(source, source ^ distance) for source in range(flat)],
        )
        for distance in range(1, blocks)
    ]
    output_meta = jnp.stack([member, row_order]).astype(jnp.int32)
    attended = output_projection(output_meta, parts, last_weights)
    cache_pages = unpack(own_row, other_row).reshape(
        peers * capacity, 2 * PAGE * model_width
    )
    return attended, cache_pages


def solution(mesh):
    placed = (
        P(("tok", "grp"), None),
        P(),
        P("tok", "grp"),
        P("tok", "grp"),
        P(),
        P(("tok", "grp"), None),
    )
    return jax.shard_map(
        per_device,
        mesh=mesh,
        in_specs=placed,
        out_specs=(P(("tok", "grp"), None), P(("tok", "grp"), None)),
        check_vma=False,
    )
```

```python
import functools

import jax
import jax.numpy as jnp
from jax import lax
from jax.experimental import pallas as pl
from jax.experimental.pallas import tpu as pltpu
from jax.sharding import PartitionSpec as P

H = 16
SPAN = 1024
PAGE = 4
HEAD_DIM = 64

NEG_FILL = -1e30
ROPE_BASE = 160000.0
EPSILON = 1e-05
TILE = 256
PARTS = 3
PAIR = 2
ONES_ROWS = 16
HEAD_ROWS = HEAD_DIM + ONES_ROWS
EXTRA_ROWS = 16
KEYS = 512
SCALE = HEAD_DIM ** (-0.5)
VMEM_LIMIT = 60 * 1024 * 1024
PARAMS = pltpu.CompilerParams(vmem_limit_bytes=VMEM_LIMIT)


def flipped(value, axis, bit):
    count = lax.axis_size(axis)
    return lax.ppermute(value, axis, [(source, source ^ bit) for source in range(count)])


def shifted(value, axis, steps):
    count = lax.axis_size(axis)
    initial, last = (max(0, -steps), min(count, count - steps))
    return lax.ppermute(value, axis, [(source, source + steps) for source in range(initial, last)])


def norm_kernel(capacity, tokens, gain, owner_row, normed, owners):
    rows = tokens.shape[0]
    values = tokens[...].astype(jnp.float32)
    centred = values - jnp.mean(values, axis=-1, keepdims=True)
    spread = jnp.mean(jnp.square(centred), axis=-1, keepdims=True)
    normed[:rows, :] = (centred * lax.rsqrt(spread + EPSILON) * gain[...]).astype(jnp.bfloat16)
    pages = owner_row.shape[1]
    owners[...] = jnp.full(owners.shape, -1.0, jnp.float32)
    owners[:1, :pages] = owner_row[...].astype(jnp.float32)
    lanes = owners.shape[1]
    across = jnp.broadcast_to(owners[:1, :], (lanes, lanes))
    earlier = lax.broadcasted_iota(jnp.int32, (lanes, lanes), 0) < lax.broadcasted_iota(
        jnp.int32, (lanes, lanes), 1
    )
    same = (across.T == across) & earlier
    ranks = jnp.sum(jnp.where(same, 1.0, 0.0), axis=0, keepdims=True)
    slots = owners[:1, :] * capacity + ranks
    normed[rows:, :] = jnp.zeros((EXTRA_ROWS, normed.shape[1]), jnp.bfloat16)
    normed[rows:, :lanes] = jnp.broadcast_to(slots, (EXTRA_ROWS, lanes)).astype(jnp.bfloat16)


def layer_norm(tokens, gain, owners, capacity):
    rows, width = tokens.shape
    lanes = -(-owners.shape[0] // 128) * 128
    return pl.pallas_call(
        functools.partial(norm_kernel, capacity),
        out_shape=jax.ShapeDtypeStruct((rows + EXTRA_ROWS, width), jnp.bfloat16),
        scratch_shapes=[pltpu.VMEM((8, lanes), jnp.float32)],
        compiler_params=PARAMS,
        name="layer_norm",
    )(tokens, gain, owners[None, :])


def project_kernel(first, layout, weight_count, peers, capacity, meta, *refs):
    operands = 1 + max(entry[0] for pieces in layout for entry in pieces)
    tokens = refs[:operands]
    weights = refs[operands : operands + weight_count]
    cosine, sine = refs[operands + weight_count : operands + weight_count + 2]
    query_out, pair_out, send_out, blocks, weight, page_source, sems = refs[-7:]
    step = pl.program_id(0)
    steps = len(layout)
    rows = query_out.shape[0]
    width = query_out.shape[1]
    shard = weights[0].shape[0] // 2

    def arrivals(number):
        return [
            pltpu.make_async_copy(
                tokens[operand],
                blocks.at[number, pl.ds(offset, count), :],
                sems.at[number, place],
            )
            for place, (operand, offset, count) in enumerate(layout[number])
        ]

    @pl.when(step == 0)
    def _():
        for number in range(steps):
            for copy in arrivals(number):
                copy.start()
        for plane in range(weight_count):
            for low in range(2):
                row = pl.multiple_of((meta[1] ^ (2 * plane + low)) * shard, shard)
                for number in range(PARTS):
                    column = pl.multiple_of(meta[2 + number] * width, width)
                    weight[pl.ds(row, shard), number * width : (number + 1) * width] = weights[
                        plane
                    ][low * shard : (low + 1) * shard, pl.ds(column, width)]

    for number in range(steps):

        @pl.when(step == number)
        def _():
            for copy in arrivals(number):
                copy.wait()

    joined = jnp.dot(blocks[step, :rows, :], weight[...], preferred_element_type=jnp.float32)
    cosines = jnp.concatenate([cosine[...]] * 4, axis=0).T
    sines = jnp.concatenate([-sine[...], sine[...]] * 2, axis=0).T
    first_half = lax.rem(lax.broadcasted_iota(jnp.int32, (rows, width), 1), HEAD_DIM) < (
        HEAD_DIM // 2
    )

    def rotate(values):
        partner = jnp.where(
            first_half,
            pltpu.roll(values, width - HEAD_DIM // 2, 1),
            pltpu.roll(values, HEAD_DIM // 2, 1),
        )
        return (values * cosines + partner * sines).astype(jnp.bfloat16)

    query_out[...] = rotate(joined[:, :width]) * jnp.asarray(SCALE, jnp.bfloat16)
    keys = rotate(joined[:, width : 2 * width])
    values = joined[:, 2 * width :].astype(jnp.bfloat16)
    pair_out[:, :width] = keys
    pair_out[:, width:] = values
    page_source[0] = keys.astype(jnp.float32)
    page_source[1] = values.astype(jnp.float32)

    pages = rows // PAGE
    slot_count = peers * capacity
    slots = blocks[step, rows : rows + EXTRA_ROWS, :128].astype(jnp.float32)[:1, :pages]
    chosen = (
        lax.broadcasted_iota(jnp.int32, (slot_count, pages), 0).astype(jnp.float32) == slots
    ).astype(jnp.bfloat16)
    for turn in range(PAGE):
        page_part = jnp.concatenate(
            [
                page_source[half, pl.ds(turn, pages, stride=PAGE), :].astype(jnp.bfloat16)
                for half in range(2)
            ],
            axis=1,
        )
        placed = jnp.dot(chosen, page_part, preferred_element_type=jnp.float32)
        columns = slice(turn * 2 * width, (turn + 1) * 2 * width)
        for peer in range(peers):
            send_out[peer, 0, :, columns] = placed[
                peer * capacity : (peer + 1) * capacity
            ].astype(jnp.bfloat16)


def project(meta, first, layout, operands, weights, cosine, sine, rows, blocks, peers, capacity, into):
    steps = len(layout)
    model_width = operands[0].shape[1]
    group_rows = rows * blocks
    width = model_width // blocks
    members = blocks // PAIR
    whole = lambda shape: pl.BlockSpec(shape, lambda i, m: (0,) * len(shape))
    place = lambda i, m: m[0] ^ (first + i)
    table = pl.BlockSpec((HEAD_DIM // 2, rows), lambda i, m: (0, place(i, m)))
    send_shape = (peers, members, capacity, 2 * PAGE * width)
    return pl.pallas_call(
        functools.partial(project_kernel, first, layout, len(weights), peers, capacity),
        grid_spec=pltpu.PrefetchScalarGridSpec(
            num_scalar_prefetch=1,
            grid=(steps,),
            in_specs=[pl.BlockSpec(memory_space=pl.ANY)] * len(operands)
            + [whole(weights[0].shape)] * len(weights)
            + [table, table]
            + [pl.BlockSpec(memory_space=pl.ANY)] * len(into),
            out_specs=[
                pl.BlockSpec((rows, width), lambda i, m: (place(i, m), 0)),
                pl.BlockSpec((rows, 2 * width), lambda i, m: (place(i, m), 0)),
                pl.BlockSpec(
                    (peers, 1) + send_shape[2:], lambda i, m: (0, place(i, m) % members, 0, 0)
                ),
            ],
            scratch_shapes=[
                pltpu.VMEM((steps, rows + EXTRA_ROWS, model_width), jnp.bfloat16),
                pltpu.VMEM((model_width, PARTS * width), jnp.bfloat16),
                pltpu.VMEM((2, rows, width), jnp.float32),
                pltpu.SemaphoreType.DMA((steps, 2)),
            ],
        ),
        out_shape=[
            jax.ShapeDtypeStruct((group_rows, width), jnp.bfloat16),
            jax.ShapeDtypeStruct((group_rows, 2 * width), jnp.bfloat16),
            jax.ShapeDtypeStruct(send_shape, jnp.bfloat16),
        ],
        input_output_aliases={
            1 + len(operands) + len(weights) + 2 + number: number for number in range(len(into))
        },
        compiler_params=PARAMS,
        cost_estimate=pl.CostEstimate(
            flops=16 * steps * rows * model_width * PARTS * width,
            bytes_accessed=(3 * steps) << 19,
            transcendentals=0,
        ),
        name="project",
    )(meta, *operands, *weights, cosine, sine, *into)


def mask_heads(queries, masked):
    turned = queries[...].T
    head_of_row = lax.broadcasted_iota(jnp.int32, turned.shape, 0) // HEAD_DIM
    for head in range(masked.shape[0]):
        masked[head] = jnp.where(head_of_row == head, turned, jnp.zeros((), jnp.bfloat16))


def with_ones(values):
    turned = values.T
    ones = jnp.ones((ONES_ROWS, values.shape[0]), values.dtype)
    rows = []
    for head in range(values.shape[1] // HEAD_DIM):
        rows += [turned[head * HEAD_DIM : (head + 1) * HEAD_DIM], ones]
    return jnp.concatenate(rows, axis=0)


def sweep(jobs, peaks):
    plans = []
    steps = 0
    for begin, end, base, pairs, values_of, masked, starts, ends, total in jobs:
        held = pairs.shape[0] // TILE
        begin, end = jnp.maximum(begin, base), jnp.minimum(end, base + held)
        last = jnp.minimum(ends, end * TILE)
        steps = jnp.maximum(steps, (end - begin + KEYS // TILE - 1) // (KEYS // TILE))
        plans.append((begin, base, held, pairs, values_of, masked, starts, last, total))

    key_rows = lax.broadcasted_iota(jnp.int32, (KEYS, TILE), 0)

    def one(number, peaks):
        units = []
        for place, plan in enumerate(plans):
            begin, base, held, pairs, values_of, masked, starts, last, total = plan
            wanted = begin + number * (KEYS // TILE)
            block = jnp.minimum(wanted, base + held - KEYS // TILE)
            row = pl.multiple_of((block - base) * TILE, TILE)
            keys = pairs[pl.ds(row, KEYS), : pairs.shape[1] // 2]
            values = values_of(row)
            first_key = block * TILE
            allowed = (key_rows >= jnp.maximum(starts, wanted * TILE) - first_key) & (
                key_rows < last - first_key
            )
            units += [
                (place, head, keys, values, masked, allowed, total)
                for head in range(len(peaks[place]))
            ]

        def products(unit):
            place, head, keys, values, masked, allowed, total = unit
            return jnp.dot(keys, masked[head], preferred_element_type=jnp.float32)

        new_peaks = [[] for _ in plans]
        ahead = products(units[0])
        for number, unit in enumerate(units):
            place, head, keys, values, masked, allowed, total = unit
            scores = ahead
            if number + 1 < len(units):
                ahead = products(units[number + 1])
            scores = jnp.where(allowed, scores, NEG_FILL)
            old_peak = peaks[place][head]
            peak = jnp.maximum(old_peak, jnp.max(scores, axis=0, keepdims=True))
            fade = jnp.exp(old_peak - peak)
            weights = jnp.exp(scores - peak).astype(jnp.bfloat16)
            own = slice(head * HEAD_ROWS, (head + 1) * HEAD_ROWS)
            total[own, :] = total[own, :] * fade + jnp.dot(
                values[own, :], weights, preferred_element_type=jnp.float32
            )
            new_peaks[place].append(peak)
        return tuple(tuple(job_peaks) for job_peaks in new_peaks)

    return lax.fori_loop(0, steps, one, peaks)


def fresh_peaks(heads):
    return tuple(jnp.full((1, TILE), NEG_FILL, jnp.float32) for _ in range(heads))


def edge_kernel(edge, meta, ranges, *refs):
    rows, pairs, outs, (masked, values) = refs[:6], refs[6], refs[7:11], refs[11:]
    step = pl.program_id(0)
    width = rows[0].shape[1]
    heads = width // HEAD_DIM
    tiles = pairs.shape[0] // TILE

    @pl.when(step == 0)
    def _():
        for number in range(tiles):
            own = slice(number * TILE, (number + 1) * TILE)
            values[:, own] = with_ones(pairs[own, width:])

    jobs = []
    places = tile_places(step, edge, tiles)
    for side in range(2):
        tile = places[side]
        queries, starts, ends = rows[3 * side : 3 * side + 3]
        mask_heads(queries, masked.at[side])
        total = outs[side]
        total[...] = jnp.zeros_like(total)
        jobs.append(
            (
                ranges[0, 2 * tile],
                ranges[0, 2 * tile + 1],
                edge,
                pairs,
                lambda row: values[:, pl.ds(row, KEYS)],
                masked.at[side],
                starts[...],
                ends[...],
                total.at[0],
            )
        )
    peaks = sweep(jobs, (fresh_peaks(heads), fresh_peaks(heads)))
    for side in range(2):
        for head in range(heads):
            outs[2 + side][0, head : head + 1, :] = peaks[side][head]


def finish_kernel(edge, meta, ranges, *refs):
    rows, pairs, halos, held, held_peaks = refs[:6], refs[6], refs[7:9], refs[9:11], refs[11:13]
    outs, (masked, sums, peaks_held, mixed) = refs[13:-4], refs[-4:]
    held_steps = edge + 1
    step = pl.program_id(0)
    width = rows[0].shape[1]
    heads = width // HEAD_DIM
    tiles = pairs.shape[0] // TILE
    places = tile_places(step, edge, tiles)

    def jobs_on(keys, bases):
        jobs = []
        for side in range(2):
            queries, starts, ends = rows[3 * side : 3 * side + 3]
            mask_heads(queries, masked.at[side])
            jobs.append(
                (
                    ranges[0, 2 * places[side]],
                    ranges[0, 2 * places[side] + 1],
                    bases[side],
                    keys[side],
                    lambda row, held=keys[side]: with_ones(held[pl.ds(row, KEYS), width:]),
                    masked.at[side],
                    starts[...],
                    ends[...],
                    sums.at[side],
                )
            )
        return jobs

    @pl.when(step < held_steps)
    def _():
        for side in range(2):
            sums[side] = held[side][0]
            peaks_held[side] = held_peaks[side][0]

    @pl.when(step >= held_steps)
    def _():
        sums[...] = jnp.zeros_like(sums)
        peaks = sweep(jobs_on((pairs, pairs), (edge, edge)), (fresh_peaks(heads),) * 2)
        for side in range(2):
            for head in range(heads):
                peaks_held[side, head : head + 1, :] = peaks[side][head]

    reaches_back = ranges[0, 2 * places[0]] < edge
    reaches_ahead = ranges[0, 2 * places[1] + 1] > edge + tiles

    @pl.when((step < edge) & (reaches_back | reaches_ahead))
    def _():
        peaks = tuple(
            tuple(peaks_held[side, head : head + 1, :] for head in range(heads))
            for side in range(2)
        )
        sweep(jobs_on(halos, (0, edge + tiles)), peaks)

    for side in range(2):
        parts = []
        for head in range(heads):
            row = head * HEAD_ROWS
            parts.append(
                sums[side, row : row + HEAD_DIM, :]
                / sums[side, row + HEAD_DIM : row + HEAD_DIM + 1, :]
            )
        tile_rows = pl.ds(pl.multiple_of(places[side] * TILE, TILE), TILE)
        mixed[tile_rows, :] = jnp.concatenate(parts, axis=0).T.astype(jnp.bfloat16)

    @pl.when(step == pl.num_programs(0) - 1)
    def _():
        count = outs[0].shape[0]
        for distance, out in enumerate(outs):
            out[...] = mixed[pl.ds(pl.multiple_of((meta[0] ^ distance) * count, 128), count), :]


def tile_places(step, edge, tiles):
    middle = edge + 2 * (step - edge)
    return (
        jnp.where(step < edge, step, middle),
        jnp.where(step < edge, tiles - edge + step, middle + 1),
    )


def attend_specs(width, edge, tiles):
    specs = []
    for side in range(2):
        place = lambda i, side=side: tile_places(i, edge, tiles)[side]
        specs.append(pl.BlockSpec((TILE, width), lambda i, m, r, place=place: (place(i), 0)))
        specs += [pl.BlockSpec((1, TILE), lambda i, m, r, place=place: (0, place(i)))] * 2
    return specs + [pl.BlockSpec((tiles * TILE, 2 * width), lambda i, m, r: (0, 0))]


def attend_edges(meta, ranges, queries, starts, ends, pairs):
    group_rows, width = queries.shape
    heads = width // HEAD_DIM
    tiles, edge = group_rows // TILE, SPAN // TILE
    steps = edge + 1
    shapes = [(steps, heads * HEAD_ROWS, TILE)] * 2 + [(steps, 8, TILE)] * 2
    return pl.pallas_call(
        functools.partial(edge_kernel, edge),
        grid_spec=pltpu.PrefetchScalarGridSpec(
            num_scalar_prefetch=2,
            grid=(steps,),
            in_specs=attend_specs(width, edge, tiles),
            out_specs=[pl.BlockSpec((1,) + shape[1:], lambda i, m, r: (i, 0, 0)) for shape in shapes],
            scratch_shapes=[
                pltpu.VMEM((2, heads, width, TILE), jnp.bfloat16),
                pltpu.VMEM((heads * HEAD_ROWS, group_rows), jnp.bfloat16),
            ],
        ),
        out_shape=[jax.ShapeDtypeStruct(shape, jnp.float32) for shape in shapes],
        compiler_params=PARAMS,
        cost_estimate=pl.CostEstimate(
            flops=16 * group_rows * 1024 * width,
            bytes_accessed=5 << 20,
            transcendentals=group_rows * 1024 * heads,
        ),
        name="attend_edges",
    )(meta, ranges, queries, starts, ends, queries, starts, ends, pairs)


def attend_finish(meta, ranges, queries, starts, ends, pairs, before, after, held, rows):
    group_rows, width = queries.shape
    heads = width // HEAD_DIM
    tiles, edge = group_rows // TILE, SPAN // TILE
    members = group_rows // rows
    return pl.pallas_call(
        functools.partial(finish_kernel, edge),
        grid_spec=pltpu.PrefetchScalarGridSpec(
            num_scalar_prefetch=2,
            grid=(edge + (tiles - 2 * edge) // 2,),
            in_specs=attend_specs(width, edge, tiles)
            + [pl.BlockSpec((SPAN, 2 * width), lambda i, m, r: (0, 0))] * 2
            + [
                pl.BlockSpec(
                    (1,) + part.shape[1:], lambda i, m, r: (jnp.minimum(i, edge), 0, 0)
                )
                for part in held
            ],
            out_specs=[pl.BlockSpec((rows, width), lambda i, m, r: (0, 0))] * members,
            scratch_shapes=[
                pltpu.VMEM((2, heads, width, TILE), jnp.bfloat16),
                pltpu.VMEM((2, heads * HEAD_ROWS, TILE), jnp.float32),
                pltpu.VMEM((2, 8, TILE), jnp.float32),
                pltpu.VMEM((group_rows, width), jnp.bfloat16),
            ],
        ),
        out_shape=[jax.ShapeDtypeStruct((rows, width), jnp.bfloat16)] * members,
        compiler_params=PARAMS,
        cost_estimate=pl.CostEstimate(
            flops=16 * group_rows * 1024 * width,
            bytes_accessed=5 << 20,
            transcendentals=group_rows * 1024 * heads,
        ),
        name="attend_finish",
    )(meta, ranges, queries, starts, ends, queries, starts, ends, pairs, before, after, *held)


def output_kernel(members, meta, *refs):
    parts, weights, result, mixed = refs[:members], refs[members:-2], refs[-2], refs[-1]
    width = parts[0].shape[1]
    tile = weights[0].shape[1]
    for distance in range(members):
        source = meta[0] ^ distance
        head_pair = PAIR * (source % (members // PAIR)) + source // (members // PAIR)
        shard = head_pair ^ meta[1]
        shard = jnp.where(meta[1] < 0, head_pair, shard // PAIR + shard % PAIR * (members // PAIR))
        columns = pl.ds(pl.multiple_of(shard * width, width), width)
        mixed[:, columns] = parts[distance][...]
    depth = mixed.shape[1]
    groups = len(weights) * (weights[0].shape[0] // depth)
    for distance in range(groups):
        columns = pl.ds(pl.multiple_of((meta[0] % groups ^ distance) * tile, tile), tile)
        start = distance // len(weights) * depth
        result[:, columns] = jnp.dot(
            mixed[...],
            weights[distance % len(weights)][start : start + depth, :],
            preferred_element_type=jnp.float32,
        ).astype(jnp.bfloat16)


def output_projection(meta, parts, weights):
    rows, width = parts[0].shape
    depth, tile = width * len(parts), weights[0].shape[1]
    columns = sum(weight.shape[0] for weight in weights) // depth * tile
    whole = lambda shape: pl.BlockSpec(shape, lambda i, m: (0, 0))
    return pl.pallas_call(
        functools.partial(output_kernel, len(parts)),
        grid_spec=pltpu.PrefetchScalarGridSpec(
            num_scalar_prefetch=1,
            grid=(1,),
            in_specs=[whole(parts[0].shape)] * len(parts)
            + [whole(weight.shape) for weight in weights],
            out_specs=whole((rows, columns)),
            scratch_shapes=[pltpu.VMEM((rows, depth), jnp.bfloat16)],
        ),
        out_shape=jax.ShapeDtypeStruct((rows, columns), jnp.bfloat16),
        compiler_params=PARAMS,
        cost_estimate=pl.CostEstimate(
            flops=2 * rows * depth * columns,
            bytes_accessed=4 << 20,
            transcendentals=0,
        ),
        name="output_projection",
    )(meta, *parts, *weights)


def stack_kernel(*refs):
    result = refs[-1]
    for number, block in enumerate(refs[:-1]):

        @pl.when(pl.program_id(0) == number)
        def _():
            result[...] = block[...]


def stacked(blocks):
    rows, width = blocks[0].shape
    return pl.pallas_call(
        stack_kernel,
        grid=(len(blocks),),
        in_specs=[pl.BlockSpec((rows, width), lambda i: (0, 0))] * len(blocks),
        out_specs=pl.BlockSpec((rows, width), lambda i: (i, 0)),
        out_shape=jax.ShapeDtypeStruct((len(blocks) * rows, width), blocks[0].dtype),
        compiler_params=PARAMS,
        cost_estimate=pl.CostEstimate(flops=0, bytes_accessed=2 << 20, transcendentals=0),
        name="stacked",
    )(*blocks)


def unpack_kernel(own_row, other_row, pages):
    _, pair, members, capacity, part = own_row.shape
    width = part // (2 * PAGE)
    for source in range(pair):
        for low in range(pair):
            received = own_row if source == low else other_row
            for high in range(members):
                for turn in range(2 * PAGE):
                    start = (turn * pair * members + PAIR * high + low) * width
                    pages[source, :, start : start + width] = received[
                        0, low, high, :, turn * width : (turn + 1) * width
                    ]


def unpack(own_row, other_row):
    planes, pair, members, capacity, part = own_row.shape
    block = pl.BlockSpec((1,) + own_row.shape[1:], lambda i: (i, 0, 0, 0, 0))
    return pl.pallas_call(
        unpack_kernel,
        grid=(planes,),
        in_specs=[block, block],
        out_specs=pl.BlockSpec((pair, capacity, pair * members * part), lambda i: (i, 0, 0)),
        out_shape=jax.ShapeDtypeStruct(
            (planes * pair, capacity, pair * members * part), jnp.bfloat16
        ),
        compiler_params=pltpu.CompilerParams(vmem_limit_bytes=24 * 1024 * 1024),
        cost_estimate=pl.CostEstimate(flops=0, bytes_accessed=6 << 20, transcendentals=0),
        name="unpack",
    )(own_row, other_row)


def rope_tables(positions):
    half_dim = HEAD_DIM // 2
    inverse = 1.0 / ROPE_BASE ** (jnp.arange(half_dim, dtype=jnp.float32) * 2.0 / HEAD_DIM)
    angles = inverse[:, None] * positions.astype(jnp.float32)[None, :]
    return jnp.cos(angles), jnp.sin(angles)


def bounds_kernel(ids, starts, ends, ranges):
    shape = (8, ids.shape[1])
    width = ids.shape[1]
    own = jnp.broadcast_to(ids[...], shape)
    index = lax.broadcasted_iota(jnp.int32, shape, 1)
    first = jnp.where((own != pltpu.roll(own, 1, 1)) | (index == 0), index, 0)
    after = jnp.where((own != pltpu.roll(own, width - 1, 1)) | (index == width - 1), index + 1, width)
    shift = 1
    while shift < SPAN:
        first = jnp.maximum(first, jnp.where(index >= shift, pltpu.roll(first, shift, 1), 0))
        after = jnp.minimum(
            after, jnp.where(index < width - shift, pltpu.roll(after, width - shift, 1), width)
        )
        shift *= 2
    rows = starts.shape[1]
    starts[...] = first[:1, SPAN : SPAN + rows]
    ends[...] = after[:1, SPAN : SPAN + rows]
    lane = lax.broadcasted_iota(jnp.int32, (rows, ranges.shape[1]), 0)
    entry = lax.broadcasted_iota(jnp.int32, (rows, ranges.shape[1]), 1)
    own_lane = entry // 2 * TILE + lax.rem(entry, 2) * (TILE - 1)
    chosen = jnp.where(lane == own_lane, 1.0, 0.0)
    odd = lax.rem(entry, 2) == 1
    begin = (first[:, SPAN : SPAN + rows] // TILE).astype(jnp.bfloat16)
    end = ((after[:, SPAN : SPAN + rows] + TILE - 1) // TILE).astype(jnp.bfloat16)
    from_begin = jnp.where(odd, 0.0, chosen).astype(jnp.bfloat16)
    from_end = jnp.where(odd, chosen, 0.0).astype(jnp.bfloat16)
    found = jnp.dot(begin, from_begin, preferred_element_type=jnp.float32) + jnp.dot(
        end, from_end, preferred_element_type=jnp.float32
    )
    ranges[...] = found[:1].astype(jnp.int32)


def document_bounds(window_ids, rows):
    return pl.pallas_call(
        bounds_kernel,
        out_shape=[jax.ShapeDtypeStruct((1, rows), jnp.int32)] * 2
        + [jax.ShapeDtypeStruct((1, 128), jnp.int32)],
        compiler_params=PARAMS,
        cost_estimate=pl.CostEstimate(flops=1 << 34, bytes_accessed=0, transcendentals=0),
        name="document_bounds",
    )(window_ids[None, :])


def per_device(tokens, norm_gain, input_weight, output_weight, segment_ids, page_owner):
    rows, model_width = tokens.shape
    peers, members = lax.axis_size("tok"), lax.axis_size("grp")
    place, column = lax.axis_index("tok"), lax.axis_index("grp")
    low = place % PAIR
    blocks = PAIR * members
    member = low * members + column
    group_rows = rows * blocks
    width = model_width // blocks
    pages = rows // PAGE

    flat = peers * members
    owners = page_owner[:, 0]
    capacity = max(2, (2 * pages + peers - 1) // peers)
    halves = []
    for parity in range(PAIR):
        pieces = []
        for number in range(PARTS):
            start = number * PAIR * width
            choices = [input_weight[:, start : start + width], input_weight[:, start + width : start + 2 * width]]
            piece = jnp.where((low ^ parity) == 0, choices[0], choices[1])
            route = []
            for source in range(flat):
                row, column_from = divmod(source, members)
                target = (row ^ parity) * members + (PARTS * column_from + number) % members
                route.append((source, target))
            pieces.append(lax.ppermute(piece, ("tok", "grp"), route))
        halves.append(jnp.concatenate(pieces, axis=1))
    plane = jnp.concatenate(halves, axis=0)
    own = layer_norm(tokens, norm_gain[None, :], owners, capacity)
    own, plane = lax.optimization_barrier((own, plane))

    across, along = flipped(own, "grp", 2), flipped(own, "tok", 1)
    sibling = flipped(own, "grp", 1)
    planes = {0: plane}
    bit = peers // 2
    while bit > 1:
        planes[bit] = flipped(plane, "tok", bit)
        bit //= 2
    for distance in range(PAIR, peers, PAIR):
        if distance not in planes:
            step_bit = distance & -distance
            planes[distance] = flipped(planes[distance ^ step_bit], "tok", step_bit)
    weights = [planes[distance] for distance in range(0, peers, PAIR)]

    first_row = place // PAIR * group_rows
    segment_ids, plane = lax.optimization_barrier((segment_ids, plane))
    padded_ids = jnp.concatenate(
        [
            jnp.full((SPAN,), -1, jnp.int32),
            segment_ids,
            jnp.full((SPAN,), 1 << 30, jnp.int32),
        ]
    )
    window_ids = lax.dynamic_slice_in_dim(padded_ids, first_row, group_rows + 2 * SPAN, 0)
    *bounds, ranges = document_bounds(window_ids, group_rows)
    positions = SPAN + jnp.arange(group_rows, dtype=jnp.int32) - bounds[0][0]
    order = [(number * members + column) % PARTS for number in range(PARTS)]
    meta = jnp.stack([member, place] + order).astype(jnp.int32)
    cosine, sine = rope_tables(positions)
    last_rows = output_weight
    bit = PAIR
    while 4 * bit < peers:
        last_rows = jnp.concatenate([last_rows, flipped(last_rows, "tok", bit)], axis=0)
        bit *= 2
    other_rows = flipped(last_rows, "tok", bit)
    across, along, sibling, weights, last_rows, other_rows, cosine, sine, meta = (
        lax.optimization_barrier(
            (across, along, sibling, weights, last_rows, other_rows, cosine, sine, meta)
        )
    )
    last_rows = jnp.concatenate([last_rows, other_rows], axis=0)

    half, held = rows // 2, rows + EXTRA_ROWS
    corner = [flipped(across[:half], "tok", 1), flipped(along[half:], "grp", 2)]
    across_sibling = flipped(across, "grp", 1)
    along_sibling = flipped(along, "grp", 1)
    other_rows = flipped(last_rows, "tok", peers // 2)
    near_blocks = [own, sibling, across, across_sibling]
    near_layout = [[(number, 0, held)] for number in range(4)]
    far_layout = [[(0, 0, held)], [(1, 0, held)]]
    far_layout += [[(number, 0, half), (number + 1, half, held - half)] for number in (2, 4)]

    sizes = (weights, cosine, sine, rows, blocks, peers, capacity)

    def to_owners(send):
        received = lax.all_to_all(
            send.reshape((flat,) + send.shape[2:]),
            ("tok", "grp"),
            split_axis=0,
            concat_axis=0,
            tiled=True,
        )
        return received.reshape((peers // PAIR, PAIR, members) + send.shape[2:])

    queries, pairs, send = project(meta, 0, near_layout, near_blocks, *sizes, ())
    send, corner, along_sibling, last_rows, other_rows = lax.optimization_barrier(
        (send, corner, along_sibling, last_rows, other_rows)
    )
    own_row = to_owners(send)
    corner_sibling = [flipped(block, "grp", 1) for block in corner]
    far_blocks = [along, along_sibling] + corner + corner_sibling
    last_rows = jnp.concatenate([last_rows, other_rows], axis=0)
    queries, pairs, send = project(meta, 4, far_layout, far_blocks, *sizes, (queries, pairs))
    before = shifted(pairs[group_rows - SPAN :], "tok", PAIR)
    after = shifted(pairs[:SPAN], "tok", -PAIR)
    other_rows = flipped(last_rows, "tok", 1)
    across_rows = flipped(last_rows, "grp", 2)
    corner_rows = lax.ppermute(
        last_rows,
        ("tok", "grp"),
        [(source, source ^ (members + 2)) for source in range(flat)],
    )

    edges = attend_edges(meta, ranges, queries, *bounds, pairs)
    before, after, edges, last_rows, other_rows, across_rows, corner_rows, send = (
        lax.optimization_barrier(
            (before, after, edges, last_rows, other_rows, across_rows, corner_rows, send)
        )
    )
    other_row = to_owners(send)
    columns = stacked([last_rows, other_rows, across_rows, corner_rows])
    row_order = place
    if output_weight.shape[0] != width:
        wanted = jnp.arange(peers) ^ place
        wanted = wanted // PAIR + wanted % PAIR * (peers // PAIR)
        shards = columns.reshape((PAIR, peers) + output_weight.shape)
        columns = shards[:, wanted].reshape(columns.shape)
        row_order = jnp.full_like(place, -1)
    mixed = attend_finish(meta, ranges, queries, *bounds, pairs, before, after, edges, rows)
    last_weights = [columns, flipped(columns, "grp", 1)]
    parts = [mixed[0]] + [
        lax.ppermute(
            mixed[distance],
            ("tok", "grp"),
            [(source, source ^ distance) for source in range(flat)],
        )
        for distance in range(1, blocks)
    ]
    output_meta = jnp.stack([member, row_order]).astype(jnp.int32)
    attended = output_projection(output_meta, parts, last_weights)
    cache_pages = unpack(own_row, other_row).reshape(
        peers * capacity, 2 * PAGE * model_width
    )
    return attended, cache_pages


def solution(mesh):
    placed = (
        P(("tok", "grp"), None),
        P(),
        P("tok", "grp"),
        P("tok", "grp"),
        P(),
        P(("tok", "grp"), None),
    )
    return jax.shard_map(
        per_device,
        mesh=mesh,
        in_specs=placed,
        out_specs=(P(("tok", "grp"), None), P(("tok", "grp"), None)),
        check_vma=False,
    )
```

```python
import functools

import jax
import jax.numpy as jnp
from jax import lax
from jax.experimental import pallas as pl
from jax.experimental.pallas import tpu as pltpu
from jax.sharding import PartitionSpec as P

H = 16
SPAN = 1024
PAGE = 4
HEAD_DIM = 64

NEG_FILL = -1e30
ROPE_BASE = 160000.0
EPSILON = 1e-05
TILE = 256
PARTS = 3
PAIR = 2
ONES_ROWS = 16
HEAD_ROWS = HEAD_DIM + ONES_ROWS
EXTRA_ROWS = 16
KEYS = 512
SCALE = HEAD_DIM ** (-0.5)
VMEM_LIMIT = 60 * 1024 * 1024
PARAMS = pltpu.CompilerParams(vmem_limit_bytes=VMEM_LIMIT)


def flipped(value, axis, bit):
    count = lax.axis_size(axis)
    return lax.ppermute(value, axis, [(source, source ^ bit) for source in range(count)])


def shifted(value, axis, steps):
    count = lax.axis_size(axis)
    initial, last = (max(0, -steps), min(count, count - steps))
    return lax.ppermute(value, axis, [(source, source + steps) for source in range(initial, last)])


def norm_kernel(capacity, tokens, gain, owner_row, normed, owners):
    rows = tokens.shape[0]
    values = tokens[...].astype(jnp.float32)
    centred = values - jnp.mean(values, axis=-1, keepdims=True)
    spread = jnp.mean(jnp.square(centred), axis=-1, keepdims=True)
    normed[:rows, :] = (centred * lax.rsqrt(spread + EPSILON) * gain[...]).astype(jnp.bfloat16)
    pages = owner_row.shape[1]
    owners[...] = jnp.full(owners.shape, -1.0, jnp.float32)
    owners[:1, :pages] = owner_row[...].astype(jnp.float32)
    lanes = owners.shape[1]
    across = jnp.broadcast_to(owners[:1, :], (lanes, lanes))
    earlier = lax.broadcasted_iota(jnp.int32, (lanes, lanes), 0) < lax.broadcasted_iota(
        jnp.int32, (lanes, lanes), 1
    )
    same = (across.T == across) & earlier
    ranks = jnp.sum(jnp.where(same, 1.0, 0.0), axis=0, keepdims=True)
    slots = owners[:1, :] * capacity + ranks
    normed[rows:, :] = jnp.zeros((EXTRA_ROWS, normed.shape[1]), jnp.bfloat16)
    normed[rows:, :lanes] = jnp.broadcast_to(slots, (EXTRA_ROWS, lanes)).astype(jnp.bfloat16)


def layer_norm(tokens, gain, owners, capacity):
    rows, width = tokens.shape
    lanes = -(-owners.shape[0] // 128) * 128
    return pl.pallas_call(
        functools.partial(norm_kernel, capacity),
        out_shape=jax.ShapeDtypeStruct((rows + EXTRA_ROWS, width), jnp.bfloat16),
        scratch_shapes=[pltpu.VMEM((8, lanes), jnp.float32)],
        compiler_params=PARAMS,
        name="layer_norm",
    )(tokens, gain, owners[None, :])


def project_kernel(first, layout, weight_count, peers, capacity, meta, *refs):
    operands = 1 + max(entry[0] for pieces in layout for entry in pieces)
    tokens = refs[:operands]
    weights = refs[operands : operands + weight_count]
    cosine, sine = refs[operands + weight_count : operands + weight_count + 2]
    query_out, pair_out, send_out, blocks, weight, page_source, sems = refs[-7:]
    step = pl.program_id(0)
    steps = len(layout)
    rows = query_out.shape[0]
    width = query_out.shape[1]
    shard = weights[0].shape[0] // 2

    def arrivals(number):
        return [
            pltpu.make_async_copy(
                tokens[operand],
                blocks.at[number, pl.ds(offset, count), :],
                sems.at[number, place],
            )
            for place, (operand, offset, count) in enumerate(layout[number])
        ]

    @pl.when(step == 0)
    def _():
        for number in range(steps):
            for copy in arrivals(number):
                copy.start()
        for plane in range(weight_count):
            for low in range(2):
                row = pl.multiple_of((meta[1] ^ (2 * plane + low)) * shard, shard)
                for number in range(PARTS):
                    column = pl.multiple_of(meta[2 + number] * width, width)
                    weight[pl.ds(row, shard), number * width : (number + 1) * width] = weights[
                        plane
                    ][low * shard : (low + 1) * shard, pl.ds(column, width)]

    for number in range(steps):

        @pl.when(step == number)
        def _():
            for copy in arrivals(number):
                copy.wait()

    joined = jnp.dot(blocks[step, :rows, :], weight[...], preferred_element_type=jnp.float32)
    cosines = jnp.concatenate([cosine[...]] * 4, axis=0).T
    sines = jnp.concatenate([-sine[...], sine[...]] * 2, axis=0).T
    first_half = lax.rem(lax.broadcasted_iota(jnp.int32, (rows, width), 1), HEAD_DIM) < (
        HEAD_DIM // 2
    )

    def rotate(values):
        partner = jnp.where(
            first_half,
            pltpu.roll(values, width - HEAD_DIM // 2, 1),
            pltpu.roll(values, HEAD_DIM // 2, 1),
        )
        return (values * cosines + partner * sines).astype(jnp.bfloat16)

    query_out[...] = rotate(joined[:, :width]) * jnp.asarray(SCALE, jnp.bfloat16)
    keys = rotate(joined[:, width : 2 * width])
    values = joined[:, 2 * width :].astype(jnp.bfloat16)
    pair_out[:, :width] = keys
    pair_out[:, width:] = values
    page_source[0] = keys.astype(jnp.float32)
    page_source[1] = values.astype(jnp.float32)

    pages = rows // PAGE
    slot_count = peers * capacity
    slots = blocks[step, rows : rows + EXTRA_ROWS, :128].astype(jnp.float32)[:1, :pages]
    chosen = (
        lax.broadcasted_iota(jnp.int32, (slot_count, pages), 0).astype(jnp.float32) == slots
    ).astype(jnp.bfloat16)
    for turn in range(PAGE):
        page_part = jnp.concatenate(
            [
                page_source[half, pl.ds(turn, pages, stride=PAGE), :].astype(jnp.bfloat16)
                for half in range(2)
            ],
            axis=1,
        )
        placed = jnp.dot(chosen, page_part, preferred_element_type=jnp.float32)
        columns = slice(turn * 2 * width, (turn + 1) * 2 * width)
        for peer in range(peers):
            send_out[peer, 0, :, columns] = placed[
                peer * capacity : (peer + 1) * capacity
            ].astype(jnp.bfloat16)


def project(meta, first, layout, operands, weights, cosine, sine, rows, blocks, peers, capacity, into):
    steps = len(layout)
    model_width = operands[0].shape[1]
    group_rows = rows * blocks
    width = model_width // blocks
    members = blocks // PAIR
    whole = lambda shape: pl.BlockSpec(shape, lambda i, m: (0,) * len(shape))
    place = lambda i, m: m[0] ^ (first + i)
    table = pl.BlockSpec((HEAD_DIM // 2, rows), lambda i, m: (0, place(i, m)))
    send_shape = (peers, members, capacity, 2 * PAGE * width)
    return pl.pallas_call(
        functools.partial(project_kernel, first, layout, len(weights), peers, capacity),
        grid_spec=pltpu.PrefetchScalarGridSpec(
            num_scalar_prefetch=1,
            grid=(steps,),
            in_specs=[pl.BlockSpec(memory_space=pl.ANY)] * len(operands)
            + [whole(weights[0].shape)] * len(weights)
            + [table, table]
            + [pl.BlockSpec(memory_space=pl.ANY)] * len(into),
            out_specs=[
                pl.BlockSpec((rows, width), lambda i, m: (place(i, m), 0)),
                pl.BlockSpec((rows, 2 * width), lambda i, m: (place(i, m), 0)),
                pl.BlockSpec(
                    (peers, 1) + send_shape[2:], lambda i, m: (0, place(i, m) % members, 0, 0)
                ),
            ],
            scratch_shapes=[
                pltpu.VMEM((steps, rows + EXTRA_ROWS, model_width), jnp.bfloat16),
                pltpu.VMEM((model_width, PARTS * width), jnp.bfloat16),
                pltpu.VMEM((2, rows, width), jnp.float32),
                pltpu.SemaphoreType.DMA((steps, 2)),
            ],
        ),
        out_shape=[
            jax.ShapeDtypeStruct((group_rows, width), jnp.bfloat16),
            jax.ShapeDtypeStruct((group_rows, 2 * width), jnp.bfloat16),
            jax.ShapeDtypeStruct(send_shape, jnp.bfloat16),
        ],
        input_output_aliases={
            1 + len(operands) + len(weights) + 2 + number: number for number in range(len(into))
        },
        compiler_params=PARAMS,
        cost_estimate=pl.CostEstimate(
            flops=16 * steps * rows * model_width * PARTS * width,
            bytes_accessed=(3 * steps) << 19,
            transcendentals=0,
        ),
        name="project",
    )(meta, *operands, *weights, cosine, sine, *into)


def mask_heads(queries, masked):
    turned = queries[...].T
    head_of_row = lax.broadcasted_iota(jnp.int32, turned.shape, 0) // HEAD_DIM
    for head in range(masked.shape[0]):
        masked[head] = jnp.where(head_of_row == head, turned, jnp.zeros((), jnp.bfloat16))


def with_ones(values):
    turned = values.T
    ones = jnp.ones((ONES_ROWS, values.shape[0]), values.dtype)
    rows = []
    for head in range(values.shape[1] // HEAD_DIM):
        rows += [turned[head * HEAD_DIM : (head + 1) * HEAD_DIM], ones]
    return jnp.concatenate(rows, axis=0)


def sweep(jobs, peaks):
    plans = []
    steps = 0
    for begin, end, base, pairs, values_of, masked, starts, ends, total in jobs:
        held = pairs.shape[0] // TILE
        begin, end = jnp.maximum(begin, base), jnp.minimum(end, base + held)
        last = jnp.minimum(ends, end * TILE)
        steps = jnp.maximum(steps, (end - begin + KEYS // TILE - 1) // (KEYS // TILE))
        plans.append((begin, base, held, pairs, values_of, masked, starts, last, total))

    key_rows = lax.broadcasted_iota(jnp.int32, (KEYS, TILE), 0)

    def one(number, peaks):
        units = []
        for place, plan in enumerate(plans):
            begin, base, held, pairs, values_of, masked, starts, last, total = plan
            wanted = begin + number * (KEYS // TILE)
            block = jnp.minimum(wanted, base + held - KEYS // TILE)
            row = pl.multiple_of((block - base) * TILE, TILE)
            keys = pairs[pl.ds(row, KEYS), : pairs.shape[1] // 2]
            values = values_of(row)
            first_key = block * TILE
            allowed = (key_rows >= jnp.maximum(starts, wanted * TILE) - first_key) & (
                key_rows < last - first_key
            )
            units += [
                (place, head, keys, values, masked, allowed, total)
                for head in range(len(peaks[place]))
            ]

        def products(unit):
            place, head, keys, values, masked, allowed, total = unit
            return jnp.dot(keys, masked[head], preferred_element_type=jnp.float32)

        new_peaks = [[] for _ in plans]
        ahead = products(units[0])
        for number, unit in enumerate(units):
            place, head, keys, values, masked, allowed, total = unit
            scores = ahead
            if number + 1 < len(units):
                ahead = products(units[number + 1])
            scores = jnp.where(allowed, scores, NEG_FILL)
            old_peak = peaks[place][head]
            peak = jnp.maximum(old_peak, jnp.max(scores, axis=0, keepdims=True))
            fade = jnp.exp(old_peak - peak)
            weights = jnp.exp(scores - peak).astype(jnp.bfloat16)
            own = slice(head * HEAD_ROWS, (head + 1) * HEAD_ROWS)
            total[own, :] = total[own, :] * fade + jnp.dot(
                values[own, :], weights, preferred_element_type=jnp.float32
            )
            new_peaks[place].append(peak)
        return tuple(tuple(job_peaks) for job_peaks in new_peaks)

    return lax.fori_loop(0, steps, one, peaks)


def fresh_peaks(heads):
    return tuple(jnp.full((1, TILE), NEG_FILL, jnp.float32) for _ in range(heads))


def edge_kernel(edge, meta, ranges, *refs):
    rows, pairs, outs, (masked, values) = refs[:6], refs[6], refs[7:11], refs[11:]
    step = pl.program_id(0)
    width = rows[0].shape[1]
    heads = width // HEAD_DIM
    tiles = pairs.shape[0] // TILE

    @pl.when(step == 0)
    def _():
        for number in range(tiles):
            own = slice(number * TILE, (number + 1) * TILE)
            values[:, own] = with_ones(pairs[own, width:])

    jobs = []
    places = tile_places(step, edge, tiles)
    for side in range(2):
        tile = places[side]
        queries, starts, ends = rows[3 * side : 3 * side + 3]
        mask_heads(queries, masked.at[side])
        total = outs[side]
        total[...] = jnp.zeros_like(total)
        jobs.append(
            (
                ranges[0, 2 * tile],
                ranges[0, 2 * tile + 1],
                edge,
                pairs,
                lambda row: values[:, pl.ds(row, KEYS)],
                masked.at[side],
                starts[...],
                ends[...],
                total.at[0],
            )
        )
    peaks = sweep(jobs, (fresh_peaks(heads), fresh_peaks(heads)))
    for side in range(2):
        for head in range(heads):
            outs[2 + side][0, head : head + 1, :] = peaks[side][head]


def finish_kernel(edge, meta, ranges, *refs):
    rows, pairs, halos, held, held_peaks = refs[:6], refs[6], refs[7:9], refs[9:11], refs[11:13]
    outs, (masked, sums, peaks_held, mixed) = refs[13:-4], refs[-4:]
    held_steps = edge + 1
    step = pl.program_id(0)
    width = rows[0].shape[1]
    heads = width // HEAD_DIM
    tiles = pairs.shape[0] // TILE
    places = tile_places(step, edge, tiles)

    def jobs_on(keys, bases):
        jobs = []
        for side in range(2):
            queries, starts, ends = rows[3 * side : 3 * side + 3]
            mask_heads(queries, masked.at[side])
            jobs.append(
                (
                    ranges[0, 2 * places[side]],
                    ranges[0, 2 * places[side] + 1],
                    bases[side],
                    keys[side],
                    lambda row, held=keys[side]: with_ones(held[pl.ds(row, KEYS), width:]),
                    masked.at[side],
                    starts[...],
                    ends[...],
                    sums.at[side],
                )
            )
        return jobs

    @pl.when(step < held_steps)
    def _():
        for side in range(2):
            sums[side] = held[side][0]
            peaks_held[side] = held_peaks[side][0]

    @pl.when(step >= held_steps)
    def _():
        sums[...] = jnp.zeros_like(sums)
        peaks = sweep(jobs_on((pairs, pairs), (edge, edge)), (fresh_peaks(heads),) * 2)
        for side in range(2):
            for head in range(heads):
                peaks_held[side, head : head + 1, :] = peaks[side][head]

    reaches_back = ranges[0, 2 * places[0]] < edge
    reaches_ahead = ranges[0, 2 * places[1] + 1] > edge + tiles

    @pl.when((step < edge) & (reaches_back | reaches_ahead))
    def _():
        peaks = tuple(
            tuple(peaks_held[side, head : head + 1, :] for head in range(heads))
            for side in range(2)
        )
        sweep(jobs_on(halos, (0, edge + tiles)), peaks)

    for side in range(2):
        parts = []
        for head in range(heads):
            row = head * HEAD_ROWS
            parts.append(
                sums[side, row : row + HEAD_DIM, :]
                / sums[side, row + HEAD_DIM : row + HEAD_DIM + 1, :]
            )
        tile_rows = pl.ds(pl.multiple_of(places[side] * TILE, TILE), TILE)
        mixed[tile_rows, :] = jnp.concatenate(parts, axis=0).T.astype(jnp.bfloat16)

    @pl.when(step == pl.num_programs(0) - 1)
    def _():
        count = outs[0].shape[0]
        for distance, out in enumerate(outs):
            out[...] = mixed[pl.ds(pl.multiple_of((meta[0] ^ distance) * count, 128), count), :]


def tile_places(step, edge, tiles):
    middle = edge + 2 * (step - edge)
    return (
        jnp.where(step < edge, step, middle),
        jnp.where(step < edge, tiles - edge + step, middle + 1),
    )


def attend_specs(width, edge, tiles):
    specs = []
    for side in range(2):
        place = lambda i, side=side: tile_places(i, edge, tiles)[side]
        specs.append(pl.BlockSpec((TILE, width), lambda i, m, r, place=place: (place(i), 0)))
        specs += [pl.BlockSpec((1, TILE), lambda i, m, r, place=place: (0, place(i)))] * 2
    return specs + [pl.BlockSpec((tiles * TILE, 2 * width), lambda i, m, r: (0, 0))]


def attend_edges(meta, ranges, queries, starts, ends, pairs):
    group_rows, width = queries.shape
    heads = width // HEAD_DIM
    tiles, edge = group_rows // TILE, SPAN // TILE
    steps = edge + 1
    shapes = [(steps, heads * HEAD_ROWS, TILE)] * 2 + [(steps, 8, TILE)] * 2
    return pl.pallas_call(
        functools.partial(edge_kernel, edge),
        grid_spec=pltpu.PrefetchScalarGridSpec(
            num_scalar_prefetch=2,
            grid=(steps,),
            in_specs=attend_specs(width, edge, tiles),
            out_specs=[pl.BlockSpec((1,) + shape[1:], lambda i, m, r: (i, 0, 0)) for shape in shapes],
            scratch_shapes=[
                pltpu.VMEM((2, heads, width, TILE), jnp.bfloat16),
                pltpu.VMEM((heads * HEAD_ROWS, group_rows), jnp.bfloat16),
            ],
        ),
        out_shape=[jax.ShapeDtypeStruct(shape, jnp.float32) for shape in shapes],
        compiler_params=PARAMS,
        cost_estimate=pl.CostEstimate(
            flops=16 * group_rows * 1024 * width,
            bytes_accessed=5 << 20,
            transcendentals=group_rows * 1024 * heads,
        ),
        name="attend_edges",
    )(meta, ranges, queries, starts, ends, queries, starts, ends, pairs)


def attend_finish(meta, ranges, queries, starts, ends, pairs, before, after, held, rows):
    group_rows, width = queries.shape
    heads = width // HEAD_DIM
    tiles, edge = group_rows // TILE, SPAN // TILE
    members = group_rows // rows
    return pl.pallas_call(
        functools.partial(finish_kernel, edge),
        grid_spec=pltpu.PrefetchScalarGridSpec(
            num_scalar_prefetch=2,
            grid=(edge + (tiles - 2 * edge) // 2,),
            in_specs=attend_specs(width, edge, tiles)
            + [pl.BlockSpec((SPAN, 2 * width), lambda i, m, r: (0, 0))] * 2
            + [
                pl.BlockSpec(
                    (1,) + part.shape[1:], lambda i, m, r: (jnp.minimum(i, edge), 0, 0)
                )
                for part in held
            ],
            out_specs=[pl.BlockSpec((rows, width), lambda i, m, r: (0, 0))] * members,
            scratch_shapes=[
                pltpu.VMEM((2, heads, width, TILE), jnp.bfloat16),
                pltpu.VMEM((2, heads * HEAD_ROWS, TILE), jnp.float32),
                pltpu.VMEM((2, 8, TILE), jnp.float32),
                pltpu.VMEM((group_rows, width), jnp.bfloat16),
            ],
        ),
        out_shape=[jax.ShapeDtypeStruct((rows, width), jnp.bfloat16)] * members,
        compiler_params=PARAMS,
        cost_estimate=pl.CostEstimate(
            flops=16 * group_rows * 1024 * width,
            bytes_accessed=5 << 20,
            transcendentals=group_rows * 1024 * heads,
        ),
        name="attend_finish",
    )(meta, ranges, queries, starts, ends, queries, starts, ends, pairs, before, after, *held)


def output_kernel(members, meta, *refs):
    parts, weights, received = refs[:members], refs[members : members + 2], refs[members + 2 : -4]
    result, pages, mixed, chosen = refs[-4:]
    step = pl.program_id(0)
    width = parts[0].shape[1]
    half = members // PAIR // 2

    @pl.when(step == 0)
    def _():
        for distance in range(members):
            source = meta[0] ^ distance
            head_pair = PAIR * (source % (members // PAIR)) + source // (members // PAIR)
            shard = head_pair ^ meta[1]
            shard = jnp.where(
                meta[1] < 0, head_pair, shard // PAIR + shard % PAIR * (members // PAIR)
            )
            columns = pl.ds(pl.multiple_of(shard * width, width), width)
            mixed[:, columns] = parts[distance][...]

    @pl.when(step < half)
    def _():
        chosen[...] = weights[0][...]

    @pl.when(step >= half)
    def _():
        chosen[...] = weights[1][...]

    result[...] = jnp.dot(
        mixed[...], chosen[...], preferred_element_type=jnp.float32
    ).astype(jnp.bfloat16)
    _, pair, count, _, part = received[0].shape
    piece = part // (2 * PAGE)
    for source in range(pair):
        for low in range(pair):
            block = received[0 if source == low else 1]
            for high in range(count):
                for turn in range(2 * PAGE):
                    start = (turn * pair * count + PAIR * high + low) * piece
                    pages[source, :, start : start + piece] = block[
                        0, low, high, :, turn * piece : (turn + 1) * piece
                    ]


def outputs(meta, parts, weights, own_row, other_row):
    rows, width = parts[0].shape
    depth, tile = width * len(parts), weights[0].shape[1]
    groups = len(parts) // PAIR
    half = groups // 2
    planes, pair, members, capacity, part = own_row.shape
    place = lambda i: jnp.minimum(i, groups - 1)
    whole = lambda shape: pl.BlockSpec(shape, lambda i, m: (0, 0))
    row_block = pl.BlockSpec((1,) + own_row.shape[1:], lambda i, m: (i, 0, 0, 0, 0))
    return pl.pallas_call(
        functools.partial(output_kernel, len(parts)),
        grid_spec=pltpu.PrefetchScalarGridSpec(
            num_scalar_prefetch=1,
            grid=(planes,),
            in_specs=[whole(parts[0].shape)] * len(parts)
            + [
                pl.BlockSpec((depth, tile), lambda i, m: (jnp.minimum(i, half - 1), 0)),
                pl.BlockSpec((depth, tile), lambda i, m: (jnp.maximum(place(i) - half, 0), 0)),
                row_block,
                row_block,
            ],
            out_specs=[
                pl.BlockSpec(
                    (rows, tile),
                    lambda i, m: (0, (m[0] % groups) ^ (2 * (place(i) % half) + place(i) // half)),
                ),
                pl.BlockSpec((pair, capacity, pair * members * part), lambda i, m: (i, 0, 0)),
            ],
            scratch_shapes=[
                pltpu.VMEM((rows, depth), jnp.bfloat16),
                pltpu.VMEM((depth, tile), jnp.bfloat16),
            ],
        ),
        out_shape=[
            jax.ShapeDtypeStruct((rows, groups * tile), jnp.bfloat16),
            jax.ShapeDtypeStruct(
                (planes * pair, capacity, pair * members * part), jnp.bfloat16
            ),
        ],
        compiler_params=pltpu.CompilerParams(vmem_limit_bytes=32 * 1024 * 1024),
        cost_estimate=pl.CostEstimate(
            flops=2 * rows * depth * groups * tile, bytes_accessed=10 << 20, transcendentals=0
        ),
        name="outputs",
    )(meta, *parts, *weights, own_row, other_row)


def stack_kernel(*refs):
    result = refs[-1]
    for number, block in enumerate(refs[:-1]):

        @pl.when(pl.program_id(0) == number)
        def _():
            result[...] = block[...]


def stacked(blocks):
    rows, width = blocks[0].shape
    return pl.pallas_call(
        stack_kernel,
        grid=(len(blocks),),
        in_specs=[pl.BlockSpec((rows, width), lambda i: (0, 0))] * len(blocks),
        out_specs=pl.BlockSpec((rows, width), lambda i: (i, 0)),
        out_shape=jax.ShapeDtypeStruct((len(blocks) * rows, width), blocks[0].dtype),
        compiler_params=PARAMS,
        cost_estimate=pl.CostEstimate(flops=0, bytes_accessed=2 << 20, transcendentals=0),
        name="stacked",
    )(*blocks)


def rope_tables(positions):
    half_dim = HEAD_DIM // 2
    inverse = 1.0 / ROPE_BASE ** (jnp.arange(half_dim, dtype=jnp.float32) * 2.0 / HEAD_DIM)
    angles = inverse[:, None] * positions.astype(jnp.float32)[None, :]
    return jnp.cos(angles), jnp.sin(angles)


def bounds_kernel(ids, starts, ends, ranges):
    shape = (8, ids.shape[1])
    width = ids.shape[1]
    own = jnp.broadcast_to(ids[...], shape)
    index = lax.broadcasted_iota(jnp.int32, shape, 1)
    first = jnp.where((own != pltpu.roll(own, 1, 1)) | (index == 0), index, 0)
    after = jnp.where((own != pltpu.roll(own, width - 1, 1)) | (index == width - 1), index + 1, width)
    shift = 1
    while shift < SPAN:
        first = jnp.maximum(first, jnp.where(index >= shift, pltpu.roll(first, shift, 1), 0))
        after = jnp.minimum(
            after, jnp.where(index < width - shift, pltpu.roll(after, width - shift, 1), width)
        )
        shift *= 2
    rows = starts.shape[1]
    starts[...] = first[:1, SPAN : SPAN + rows]
    ends[...] = after[:1, SPAN : SPAN + rows]
    lane = lax.broadcasted_iota(jnp.int32, (rows, ranges.shape[1]), 0)
    entry = lax.broadcasted_iota(jnp.int32, (rows, ranges.shape[1]), 1)
    own_lane = entry // 2 * TILE + lax.rem(entry, 2) * (TILE - 1)
    chosen = jnp.where(lane == own_lane, 1.0, 0.0)
    odd = lax.rem(entry, 2) == 1
    begin = (first[:, SPAN : SPAN + rows] // TILE).astype(jnp.bfloat16)
    end = ((after[:, SPAN : SPAN + rows] + TILE - 1) // TILE).astype(jnp.bfloat16)
    from_begin = jnp.where(odd, 0.0, chosen).astype(jnp.bfloat16)
    from_end = jnp.where(odd, chosen, 0.0).astype(jnp.bfloat16)
    found = jnp.dot(begin, from_begin, preferred_element_type=jnp.float32) + jnp.dot(
        end, from_end, preferred_element_type=jnp.float32
    )
    ranges[...] = found[:1].astype(jnp.int32)


def document_bounds(window_ids, rows):
    return pl.pallas_call(
        bounds_kernel,
        out_shape=[jax.ShapeDtypeStruct((1, rows), jnp.int32)] * 2
        + [jax.ShapeDtypeStruct((1, 128), jnp.int32)],
        compiler_params=PARAMS,
        cost_estimate=pl.CostEstimate(flops=1 << 34, bytes_accessed=0, transcendentals=0),
        name="document_bounds",
    )(window_ids[None, :])


def per_device(tokens, norm_gain, input_weight, output_weight, segment_ids, page_owner):
    rows, model_width = tokens.shape
    peers, members = lax.axis_size("tok"), lax.axis_size("grp")
    place, column = lax.axis_index("tok"), lax.axis_index("grp")
    low = place % PAIR
    blocks = PAIR * members
    member = low * members + column
    group_rows = rows * blocks
    width = model_width // blocks
    pages = rows // PAGE

    flat = peers * members
    owners = page_owner[:, 0]
    capacity = max(2, (2 * pages + peers - 1) // peers)
    halves = []
    for parity in range(PAIR):
        pieces = []
        for number in range(PARTS):
            start = number * PAIR * width
            choices = [input_weight[:, start : start + width], input_weight[:, start + width : start + 2 * width]]
            piece = jnp.where((low ^ parity) == 0, choices[0], choices[1])
            route = []
            for source in range(flat):
                row, column_from = divmod(source, members)
                target = (row ^ parity) * members + (PARTS * column_from + number) % members
                route.append((source, target))
            pieces.append(lax.ppermute(piece, ("tok", "grp"), route))
        halves.append(jnp.concatenate(pieces, axis=1))
    plane = jnp.concatenate(halves, axis=0)
    own = layer_norm(tokens, norm_gain[None, :], owners, capacity)
    own, plane = lax.optimization_barrier((own, plane))

    across, along = flipped(own, "grp", 2), flipped(own, "tok", 1)
    sibling = flipped(own, "grp", 1)
    planes = {0: plane}
    bit = peers // 2
    while bit > 1:
        planes[bit] = flipped(plane, "tok", bit)
        bit //= 2
    for distance in range(PAIR, peers, PAIR):
        if distance not in planes:
            step_bit = distance & -distance
            planes[distance] = flipped(planes[distance ^ step_bit], "tok", step_bit)
    weights = [planes[distance] for distance in range(0, peers, PAIR)]

    first_row = place // PAIR * group_rows
    segment_ids, plane = lax.optimization_barrier((segment_ids, plane))
    padded_ids = jnp.concatenate(
        [
            jnp.full((SPAN,), -1, jnp.int32),
            segment_ids,
            jnp.full((SPAN,), 1 << 30, jnp.int32),
        ]
    )
    window_ids = lax.dynamic_slice_in_dim(padded_ids, first_row, group_rows + 2 * SPAN, 0)
    *bounds, ranges = document_bounds(window_ids, group_rows)
    positions = SPAN + jnp.arange(group_rows, dtype=jnp.int32) - bounds[0][0]
    order = [(number * members + column) % PARTS for number in range(PARTS)]
    meta = jnp.stack([member, place] + order).astype(jnp.int32)
    cosine, sine = rope_tables(positions)
    last_rows = output_weight
    bit = PAIR
    while 4 * bit < peers:
        last_rows = jnp.concatenate([last_rows, flipped(last_rows, "tok", bit)], axis=0)
        bit *= 2
    other_rows = flipped(last_rows, "tok", bit)
    across, along, sibling, weights, last_rows, other_rows, cosine, sine, meta = (
        lax.optimization_barrier(
            (across, along, sibling, weights, last_rows, other_rows, cosine, sine, meta)
        )
    )
    last_rows = jnp.concatenate([last_rows, other_rows], axis=0)

    half, held = rows // 2, rows + EXTRA_ROWS
    corner = [flipped(across[:half], "tok", 1), flipped(along[half:], "grp", 2)]
    across_sibling = flipped(across, "grp", 1)
    along_sibling = flipped(along, "grp", 1)
    other_rows = flipped(last_rows, "tok", peers // 2)
    near_blocks = [own, sibling, across, across_sibling]
    near_layout = [[(number, 0, held)] for number in range(4)]
    far_layout = [[(0, 0, held)], [(1, 0, held)]]
    far_layout += [[(number, 0, half), (number + 1, half, held - half)] for number in (2, 4)]

    sizes = (weights, cosine, sine, rows, blocks, peers, capacity)

    def to_owners(send):
        received = lax.all_to_all(
            send.reshape((flat,) + send.shape[2:]),
            ("tok", "grp"),
            split_axis=0,
            concat_axis=0,
            tiled=True,
        )
        return received.reshape((peers // PAIR, PAIR, members) + send.shape[2:])

    queries, pairs, send = project(meta, 0, near_layout, near_blocks, *sizes, ())
    send, corner, along_sibling, last_rows, other_rows = lax.optimization_barrier(
        (send, corner, along_sibling, last_rows, other_rows)
    )
    own_row = to_owners(send)
    corner_sibling = [flipped(block, "grp", 1) for block in corner]
    far_blocks = [along, along_sibling] + corner + corner_sibling
    last_rows = jnp.concatenate([last_rows, other_rows], axis=0)
    queries, pairs, send = project(meta, 4, far_layout, far_blocks, *sizes, (queries, pairs))
    before = shifted(pairs[group_rows - SPAN :], "tok", PAIR)
    after = shifted(pairs[:SPAN], "tok", -PAIR)
    other_rows = flipped(last_rows, "tok", 1)
    across_rows = flipped(last_rows, "grp", 2)
    corner_rows = lax.ppermute(
        last_rows,
        ("tok", "grp"),
        [(source, source ^ (members + 2)) for source in range(flat)],
    )

    edges = attend_edges(meta, ranges, queries, *bounds, pairs)
    before, after, edges, last_rows, other_rows, across_rows, corner_rows, send = (
        lax.optimization_barrier(
            (before, after, edges, last_rows, other_rows, across_rows, corner_rows, send)
        )
    )
    other_row = to_owners(send)
    columns = stacked([last_rows, other_rows, across_rows, corner_rows])
    row_order = place
    if output_weight.shape[0] != width:
        wanted = jnp.arange(peers) ^ place
        wanted = wanted // PAIR + wanted % PAIR * (peers // PAIR)
        shards = columns.reshape((PAIR, peers) + output_weight.shape)
        columns = shards[:, wanted].reshape(columns.shape)
        row_order = jnp.full_like(place, -1)
    mixed = attend_finish(meta, ranges, queries, *bounds, pairs, before, after, edges, rows)
    last_weights = [columns, flipped(columns, "grp", 1)]
    parts = [mixed[0]] + [
        lax.ppermute(
            mixed[distance],
            ("tok", "grp"),
            [(source, source ^ distance) for source in range(flat)],
        )
        for distance in range(1, blocks)
    ]
    output_meta = jnp.stack([member, row_order]).astype(jnp.int32)
    attended, cache_pages = outputs(output_meta, parts, last_weights, own_row, other_row)
    cache_pages = cache_pages.reshape(peers * capacity, 2 * PAGE * model_width)
    return attended, cache_pages


def solution(mesh):
    placed = (
        P(("tok", "grp"), None),
        P(),
        P("tok", "grp"),
        P("tok", "grp"),
        P(),
        P(("tok", "grp"), None),
    )
    return jax.shard_map(
        per_device,
        mesh=mesh,
        in_specs=placed,
        out_specs=(P(("tok", "grp"), None), P(("tok", "grp"), None)),
        check_vma=False,
    )
```

```python
import functools

import jax
import jax.numpy as jnp
from jax import lax
from jax.experimental import pallas as pl
from jax.experimental.pallas import tpu as pltpu
from jax.sharding import PartitionSpec as P

H = 16
SPAN = 1024
PAGE = 4
HEAD_DIM = 64

NEG_FILL = -1e30
ROPE_BASE = 160000.0
EPSILON = 1e-05
TILE = 256
PARTS = 3
PAIR = 2
ONES_ROWS = 16
HEAD_ROWS = HEAD_DIM + ONES_ROWS
EXTRA_ROWS = 16
KEYS = 512
SCALE = HEAD_DIM ** (-0.5)
VMEM_LIMIT = 60 * 1024 * 1024
PARAMS = pltpu.CompilerParams(vmem_limit_bytes=VMEM_LIMIT)


def flipped(value, axis, bit):
    count = lax.axis_size(axis)
    return lax.ppermute(value, axis, [(source, source ^ bit) for source in range(count)])


def shifted(value, axis, steps):
    count = lax.axis_size(axis)
    initial, last = (max(0, -steps), min(count, count - steps))
    return lax.ppermute(value, axis, [(source, source + steps) for source in range(initial, last)])


def norm_kernel(capacity, tokens, gain, owner_row, normed, owners):
    rows = tokens.shape[0]
    values = tokens[...].astype(jnp.float32)
    centred = values - jnp.mean(values, axis=-1, keepdims=True)
    spread = jnp.mean(jnp.square(centred), axis=-1, keepdims=True)
    normed[:rows, :] = (centred * lax.rsqrt(spread + EPSILON) * gain[...]).astype(jnp.bfloat16)
    pages = owner_row.shape[1]
    owners[...] = jnp.full(owners.shape, -1.0, jnp.float32)
    owners[:1, :pages] = owner_row[...].astype(jnp.float32)
    lanes = owners.shape[1]
    across = jnp.broadcast_to(owners[:1, :], (lanes, lanes))
    earlier = lax.broadcasted_iota(jnp.int32, (lanes, lanes), 0) < lax.broadcasted_iota(
        jnp.int32, (lanes, lanes), 1
    )
    same = (across.T == across) & earlier
    ranks = jnp.sum(jnp.where(same, 1.0, 0.0), axis=0, keepdims=True)
    slots = owners[:1, :] * capacity + ranks
    normed[rows:, :] = jnp.zeros((EXTRA_ROWS, normed.shape[1]), jnp.bfloat16)
    normed[rows:, :lanes] = jnp.broadcast_to(slots, (EXTRA_ROWS, lanes)).astype(jnp.bfloat16)


def layer_norm(tokens, gain, owners, capacity):
    rows, width = tokens.shape
    lanes = -(-owners.shape[0] // 128) * 128
    return pl.pallas_call(
        functools.partial(norm_kernel, capacity),
        out_shape=jax.ShapeDtypeStruct((rows + EXTRA_ROWS, width), jnp.bfloat16),
        scratch_shapes=[pltpu.VMEM((8, lanes), jnp.float32)],
        compiler_params=PARAMS,
        name="layer_norm",
    )(tokens, gain, owners[None, :])


def project_kernel(first, layout, weight_count, peers, capacity, meta, *refs):
    operands = 1 + max(entry[0] for pieces in layout for entry in pieces)
    tokens = refs[:operands]
    weights = refs[operands : operands + weight_count]
    cosine, sine = refs[operands + weight_count : operands + weight_count + 2]
    query_out, pair_out, send_out, blocks, weight, page_source, sems = refs[-7:]
    step = pl.program_id(0)
    steps = len(layout)
    rows = query_out.shape[0]
    width = query_out.shape[1]
    shard = weights[0].shape[0] // 2

    def arrivals(number):
        return [
            pltpu.make_async_copy(
                tokens[operand],
                blocks.at[number, pl.ds(offset, count), :],
                sems.at[number, place],
            )
            for place, (operand, offset, count) in enumerate(layout[number])
        ]

    @pl.when(step == 0)
    def _():
        for number in range(steps):
            for copy in arrivals(number):
                copy.start()
        for plane in range(weight_count):
            for low in range(2):
                row = pl.multiple_of((meta[1] ^ (2 * plane + low)) * shard, shard)
                for number in range(PARTS):
                    column = pl.multiple_of(meta[2 + number] * width, width)
                    weight[pl.ds(row, shard), number * width : (number + 1) * width] = weights[
                        plane
                    ][low * shard : (low + 1) * shard, pl.ds(column, width)]

    for number in range(steps):

        @pl.when(step == number)
        def _():
            for copy in arrivals(number):
                copy.wait()

    joined = jnp.dot(blocks[step, :rows, :], weight[...], preferred_element_type=jnp.float32)
    cosines = jnp.concatenate([cosine[...]] * 4, axis=0).T
    sines = jnp.concatenate([-sine[...], sine[...]] * 2, axis=0).T
    first_half = lax.rem(lax.broadcasted_iota(jnp.int32, (rows, width), 1), HEAD_DIM) < (
        HEAD_DIM // 2
    )

    def rotate(values):
        partner = jnp.where(
            first_half,
            pltpu.roll(values, width - HEAD_DIM // 2, 1),
            pltpu.roll(values, HEAD_DIM // 2, 1),
        )
        return (values * cosines + partner * sines).astype(jnp.bfloat16)

    query_out[...] = rotate(joined[:, :width]) * jnp.asarray(SCALE, jnp.bfloat16)
    keys = rotate(joined[:, width : 2 * width])
    values = joined[:, 2 * width :].astype(jnp.bfloat16)
    pair_out[:, :width] = keys
    pair_out[:, width:] = values
    page_source[0] = keys.astype(jnp.float32)
    page_source[1] = values.astype(jnp.float32)

    pages = rows // PAGE
    slot_count = peers * capacity
    slots = blocks[step, rows : rows + EXTRA_ROWS, :128].astype(jnp.float32)[:1, :pages]
    chosen = (
        lax.broadcasted_iota(jnp.int32, (slot_count, pages), 0).astype(jnp.float32) == slots
    ).astype(jnp.bfloat16)
    for turn in range(PAGE):
        page_part = jnp.concatenate(
            [
                page_source[half, pl.ds(turn, pages, stride=PAGE), :].astype(jnp.bfloat16)
                for half in range(2)
            ],
            axis=1,
        )
        placed = jnp.dot(chosen, page_part, preferred_element_type=jnp.float32)
        columns = slice(turn * 2 * width, (turn + 1) * 2 * width)
        for peer in range(peers):
            send_out[peer, 0, :, columns] = placed[
                peer * capacity : (peer + 1) * capacity
            ].astype(jnp.bfloat16)


def project(meta, first, layout, operands, weights, cosine, sine, rows, blocks, peers, capacity, into):
    steps = len(layout)
    model_width = operands[0].shape[1]
    group_rows = rows * blocks
    width = model_width // blocks
    members = blocks // PAIR
    whole = lambda shape: pl.BlockSpec(shape, lambda i, m: (0,) * len(shape))
    place = lambda i, m: m[0] ^ (first + i)
    table = pl.BlockSpec((HEAD_DIM // 2, rows), lambda i, m: (0, place(i, m)))
    send_shape = (peers, members, capacity, 2 * PAGE * width)
    return pl.pallas_call(
        functools.partial(project_kernel, first, layout, len(weights), peers, capacity),
        grid_spec=pltpu.PrefetchScalarGridSpec(
            num_scalar_prefetch=1,
            grid=(steps,),
            in_specs=[pl.BlockSpec(memory_space=pl.ANY)] * len(operands)
            + [whole(weights[0].shape)] * len(weights)
            + [table, table]
            + [pl.BlockSpec(memory_space=pl.ANY)] * len(into),
            out_specs=[
                pl.BlockSpec((rows, width), lambda i, m: (place(i, m), 0)),
                pl.BlockSpec((rows, 2 * width), lambda i, m: (place(i, m), 0)),
                pl.BlockSpec(
                    (peers, 1) + send_shape[2:], lambda i, m: (0, place(i, m) % members, 0, 0)
                ),
            ],
            scratch_shapes=[
                pltpu.VMEM((steps, rows + EXTRA_ROWS, model_width), jnp.bfloat16),
                pltpu.VMEM((model_width, PARTS * width), jnp.bfloat16),
                pltpu.VMEM((2, rows, width), jnp.float32),
                pltpu.SemaphoreType.DMA((steps, 2)),
            ],
        ),
        out_shape=[
            jax.ShapeDtypeStruct((group_rows, width), jnp.bfloat16),
            jax.ShapeDtypeStruct((group_rows, 2 * width), jnp.bfloat16),
            jax.ShapeDtypeStruct(send_shape, jnp.bfloat16),
        ],
        input_output_aliases={
            1 + len(operands) + len(weights) + 2 + number: number for number in range(len(into))
        },
        compiler_params=PARAMS,
        cost_estimate=pl.CostEstimate(
            flops=16 * steps * rows * model_width * PARTS * width,
            bytes_accessed=(3 * steps) << 19,
            transcendentals=0,
        ),
        name="project",
    )(meta, *operands, *weights, cosine, sine, *into)


def mask_heads(queries, masked):
    turned = queries[...].T
    head_of_row = lax.broadcasted_iota(jnp.int32, turned.shape, 0) // HEAD_DIM
    for head in range(masked.shape[0]):
        masked[head] = jnp.where(head_of_row == head, turned, jnp.zeros((), jnp.bfloat16))


def with_ones(values):
    turned = values.T
    ones = jnp.ones((ONES_ROWS, values.shape[0]), values.dtype)
    rows = []
    for head in range(values.shape[1] // HEAD_DIM):
        rows += [turned[head * HEAD_DIM : (head + 1) * HEAD_DIM], ones]
    return jnp.concatenate(rows, axis=0)


def sweep(jobs, peaks):
    plans = []
    steps = 0
    for begin, end, base, pairs, values_of, masked, starts, ends, total in jobs:
        held = pairs.shape[0] // TILE
        begin, end = jnp.maximum(begin, base), jnp.minimum(end, base + held)
        last = jnp.minimum(ends, end * TILE)
        steps = jnp.maximum(steps, (end - begin + KEYS // TILE - 1) // (KEYS // TILE))
        plans.append((begin, base, held, pairs, values_of, masked, starts, last, total))

    key_rows = lax.broadcasted_iota(jnp.int32, (KEYS, TILE), 0)

    def one(number, peaks):
        units = []
        for place, plan in enumerate(plans):
            begin, base, held, pairs, values_of, masked, starts, last, total = plan
            wanted = begin + number * (KEYS // TILE)
            block = jnp.minimum(wanted, base + held - KEYS // TILE)
            row = pl.multiple_of((block - base) * TILE, TILE)
            keys = pairs[pl.ds(row, KEYS), : pairs.shape[1] // 2]
            values = values_of(row)
            first_key = block * TILE
            allowed = (key_rows >= jnp.maximum(starts, wanted * TILE) - first_key) & (
                key_rows < last - first_key
            )
            units += [
                (place, head, keys, values, masked, allowed, total)
                for head in range(len(peaks[place]))
            ]

        def products(unit):
            place, head, keys, values, masked, allowed, total = unit
            return jnp.dot(keys, masked[head], preferred_element_type=jnp.float32)

        new_peaks = [[] for _ in plans]
        ahead = products(units[0])
        for number, unit in enumerate(units):
            place, head, keys, values, masked, allowed, total = unit
            scores = ahead
            if number + 1 < len(units):
                ahead = products(units[number + 1])
            scores = jnp.where(allowed, scores, NEG_FILL)
            old_peak = peaks[place][head]
            peak = jnp.maximum(old_peak, jnp.max(scores, axis=0, keepdims=True))
            fade = jnp.exp(old_peak - peak)
            weights = jnp.exp(scores - peak).astype(jnp.bfloat16)
            own = slice(head * HEAD_ROWS, (head + 1) * HEAD_ROWS)
            total[own, :] = total[own, :] * fade + jnp.dot(
                values[own, :], weights, preferred_element_type=jnp.float32
            )
            new_peaks[place].append(peak)
        return tuple(tuple(job_peaks) for job_peaks in new_peaks)

    return lax.fori_loop(0, steps, one, peaks)


def fresh_peaks(heads):
    return tuple(jnp.full((1, TILE), NEG_FILL, jnp.float32) for _ in range(heads))


def edge_kernel(edge, meta, ranges, *refs):
    rows, pairs, outs, (masked, values) = refs[:6], refs[6], refs[7:11], refs[11:]
    step = pl.program_id(0)
    width = rows[0].shape[1]
    heads = width // HEAD_DIM
    tiles = pairs.shape[0] // TILE

    @pl.when(step == 0)
    def _():
        for number in range(tiles):
            own = slice(number * TILE, (number + 1) * TILE)
            values[:, own] = with_ones(pairs[own, width:])

    jobs = []
    places = tile_places(step, edge, tiles)
    for side in range(2):
        tile = places[side]
        queries, starts, ends = rows[3 * side : 3 * side + 3]
        mask_heads(queries, masked.at[side])
        total = outs[side]
        total[...] = jnp.zeros_like(total)
        jobs.append(
            (
                ranges[0, 2 * tile],
                ranges[0, 2 * tile + 1],
                edge,
                pairs,
                lambda row: values[:, pl.ds(row, KEYS)],
                masked.at[side],
                starts[...],
                ends[...],
                total.at[0],
            )
        )
    peaks = sweep(jobs, (fresh_peaks(heads), fresh_peaks(heads)))
    for side in range(2):
        for head in range(heads):
            outs[2 + side][0, head : head + 1, :] = peaks[side][head]


def finish_kernel(edge, meta, ranges, *refs):
    rows, pairs, halos, held, held_peaks = refs[:6], refs[6], refs[7:9], refs[9:11], refs[11:13]
    outs, (masked, sums, peaks_held, mixed) = refs[13:-4], refs[-4:]
    held_steps = edge + 1
    step = pl.program_id(0)
    width = rows[0].shape[1]
    heads = width // HEAD_DIM
    tiles = pairs.shape[0] // TILE
    places = tile_places(step, edge, tiles)

    def jobs_on(keys, bases):
        jobs = []
        for side in range(2):
            queries, starts, ends = rows[3 * side : 3 * side + 3]
            mask_heads(queries, masked.at[side])
            jobs.append(
                (
                    ranges[0, 2 * places[side]],
                    ranges[0, 2 * places[side] + 1],
                    bases[side],
                    keys[side],
                    lambda row, held=keys[side]: with_ones(held[pl.ds(row, KEYS), width:]),
                    masked.at[side],
                    starts[...],
                    ends[...],
                    sums.at[side],
                )
            )
        return jobs

    @pl.when(step < held_steps)
    def _():
        for side in range(2):
            sums[side] = held[side][0]
            peaks_held[side] = held_peaks[side][0]

    @pl.when(step >= held_steps)
    def _():
        sums[...] = jnp.zeros_like(sums)
        peaks = sweep(jobs_on((pairs, pairs), (edge, edge)), (fresh_peaks(heads),) * 2)
        for side in range(2):
            for head in range(heads):
                peaks_held[side, head : head + 1, :] = peaks[side][head]

    reaches_back = ranges[0, 2 * places[0]] < edge
    reaches_ahead = ranges[0, 2 * places[1] + 1] > edge + tiles

    @pl.when((step < edge) & (reaches_back | reaches_ahead))
    def _():
        peaks = tuple(
            tuple(peaks_held[side, head : head + 1, :] for head in range(heads))
            for side in range(2)
        )
        sweep(jobs_on(halos, (0, edge + tiles)), peaks)

    for side in range(2):
        parts = []
        for head in range(heads):
            row = head * HEAD_ROWS
            parts.append(
                sums[side, row : row + HEAD_DIM, :]
                / sums[side, row + HEAD_DIM : row + HEAD_DIM + 1, :]
            )
        tile_rows = pl.ds(pl.multiple_of(places[side] * TILE, TILE), TILE)
        mixed[tile_rows, :] = jnp.concatenate(parts, axis=0).T.astype(jnp.bfloat16)

    @pl.when(step == pl.num_programs(0) - 1)
    def _():
        count = outs[0].shape[0]
        for distance, out in enumerate(outs):
            out[...] = mixed[pl.ds(pl.multiple_of((meta[0] ^ distance) * count, 128), count), :]


def tile_places(step, edge, tiles):
    middle = edge + 2 * (step - edge)
    return (
        jnp.where(step < edge, step, middle),
        jnp.where(step < edge, tiles - edge + step, middle + 1),
    )


def attend_specs(width, edge, tiles):
    specs = []
    for side in range(2):
        place = lambda i, side=side: tile_places(i, edge, tiles)[side]
        specs.append(pl.BlockSpec((TILE, width), lambda i, m, r, place=place: (place(i), 0)))
        specs += [pl.BlockSpec((1, TILE), lambda i, m, r, place=place: (0, place(i)))] * 2
    return specs + [pl.BlockSpec((tiles * TILE, 2 * width), lambda i, m, r: (0, 0))]


def attend_edges(meta, ranges, queries, starts, ends, pairs):
    group_rows, width = queries.shape
    heads = width // HEAD_DIM
    tiles, edge = group_rows // TILE, SPAN // TILE
    steps = edge + 1
    shapes = [(steps, heads * HEAD_ROWS, TILE)] * 2 + [(steps, 8, TILE)] * 2
    return pl.pallas_call(
        functools.partial(edge_kernel, edge),
        grid_spec=pltpu.PrefetchScalarGridSpec(
            num_scalar_prefetch=2,
            grid=(steps,),
            in_specs=attend_specs(width, edge, tiles),
            out_specs=[pl.BlockSpec((1,) + shape[1:], lambda i, m, r: (i, 0, 0)) for shape in shapes],
            scratch_shapes=[
                pltpu.VMEM((2, heads, width, TILE), jnp.bfloat16),
                pltpu.VMEM((heads * HEAD_ROWS, group_rows), jnp.bfloat16),
            ],
        ),
        out_shape=[jax.ShapeDtypeStruct(shape, jnp.float32) for shape in shapes],
        compiler_params=PARAMS,
        cost_estimate=pl.CostEstimate(
            flops=16 * group_rows * 1024 * width,
            bytes_accessed=5 << 20,
            transcendentals=group_rows * 1024 * heads,
        ),
        name="attend_edges",
    )(meta, ranges, queries, starts, ends, queries, starts, ends, pairs)


def attend_finish(meta, ranges, queries, starts, ends, pairs, before, after, held, rows):
    group_rows, width = queries.shape
    heads = width // HEAD_DIM
    tiles, edge = group_rows // TILE, SPAN // TILE
    members = group_rows // rows
    return pl.pallas_call(
        functools.partial(finish_kernel, edge),
        grid_spec=pltpu.PrefetchScalarGridSpec(
            num_scalar_prefetch=2,
            grid=(edge + (tiles - 2 * edge) // 2,),
            in_specs=attend_specs(width, edge, tiles)
            + [pl.BlockSpec((SPAN, 2 * width), lambda i, m, r: (0, 0))] * 2
            + [
                pl.BlockSpec(
                    (1,) + part.shape[1:], lambda i, m, r: (jnp.minimum(i, edge), 0, 0)
                )
                for part in held
            ],
            out_specs=[pl.BlockSpec((rows, width), lambda i, m, r: (0, 0))] * members,
            scratch_shapes=[
                pltpu.VMEM((2, heads, width, TILE), jnp.bfloat16),
                pltpu.VMEM((2, heads * HEAD_ROWS, TILE), jnp.float32),
                pltpu.VMEM((2, 8, TILE), jnp.float32),
                pltpu.VMEM((group_rows, width), jnp.bfloat16),
            ],
        ),
        out_shape=[jax.ShapeDtypeStruct((rows, width), jnp.bfloat16)] * members,
        compiler_params=PARAMS,
        cost_estimate=pl.CostEstimate(
            flops=16 * group_rows * 1024 * width,
            bytes_accessed=5 << 20,
            transcendentals=group_rows * 1024 * heads,
        ),
        name="attend_finish",
    )(meta, ranges, queries, starts, ends, queries, starts, ends, pairs, before, after, *held)


def output_kernel(members, meta, *refs):
    parts, weights, received = refs[:members], refs[members : members + 2], refs[members + 2 : -4]
    result, pages, mixed, chosen = refs[-4:]
    step = pl.program_id(0)
    width = parts[0].shape[1]
    half = members // PAIR // 2

    @pl.when(step == 0)
    def _():
        for distance in range(members):
            source = meta[0] ^ distance
            head_pair = PAIR * (source % (members // PAIR)) + source // (members // PAIR)
            shard = head_pair ^ meta[1]
            shard = jnp.where(
                meta[1] < 0, head_pair, shard // PAIR + shard % PAIR * (members // PAIR)
            )
            columns = pl.ds(pl.multiple_of(shard * width, width), width)
            mixed[:, columns] = parts[distance][...]

    @pl.when(step < half)
    def _():
        chosen[...] = weights[0][...]

    @pl.when(step >= half)
    def _():
        chosen[...] = weights[1][...]

    result[...] = jnp.dot(
        mixed[...], chosen[...], preferred_element_type=jnp.float32
    ).astype(jnp.bfloat16)
    _, pair, count, _, part = received[0].shape
    piece = part // (2 * PAGE)
    for source in range(pair):
        for low in range(pair):
            block = received[0 if source == low else 1]
            for high in range(count):
                for turn in range(2 * PAGE):
                    start = (turn * pair * count + PAIR * high + low) * piece
                    pages[source, :, start : start + piece] = block[
                        0, low, high, :, turn * piece : (turn + 1) * piece
                    ]


def outputs(meta, parts, weights, own_row, other_row):
    rows, width = parts[0].shape
    depth, tile = width * len(parts), weights[0].shape[1]
    groups = len(parts) // PAIR
    half = groups // 2
    planes, pair, members, capacity, part = own_row.shape
    place = lambda i: jnp.minimum(i, groups - 1)
    whole = lambda shape: pl.BlockSpec(shape, lambda i, m: (0, 0))
    row_block = pl.BlockSpec((1,) + own_row.shape[1:], lambda i, m: (i, 0, 0, 0, 0))
    return pl.pallas_call(
        functools.partial(output_kernel, len(parts)),
        grid_spec=pltpu.PrefetchScalarGridSpec(
            num_scalar_prefetch=1,
            grid=(planes,),
            in_specs=[whole(parts[0].shape)] * len(parts)
            + [
                pl.BlockSpec((depth, tile), lambda i, m: (jnp.minimum(i, half - 1), 0)),
                pl.BlockSpec((depth, tile), lambda i, m: (jnp.maximum(place(i) - half, 0), 0)),
                row_block,
                row_block,
            ],
            out_specs=[
                pl.BlockSpec(
                    (rows, tile),
                    lambda i, m: (0, (m[0] % groups) ^ (2 * (place(i) % half) + place(i) // half)),
                ),
                pl.BlockSpec((pair, capacity, pair * members * part), lambda i, m: (i, 0, 0)),
            ],
            scratch_shapes=[
                pltpu.VMEM((rows, depth), jnp.bfloat16),
                pltpu.VMEM((depth, tile), jnp.bfloat16),
            ],
        ),
        out_shape=[
            jax.ShapeDtypeStruct((rows, groups * tile), jnp.bfloat16),
            jax.ShapeDtypeStruct(
                (planes * pair, capacity, pair * members * part), jnp.bfloat16
            ),
        ],
        compiler_params=PARAMS,
        cost_estimate=pl.CostEstimate(
            flops=2 * rows * depth * groups * tile, bytes_accessed=10 << 20, transcendentals=0
        ),
        name="outputs",
    )(meta, *parts, *weights, own_row, other_row)


def stack_kernel(*refs):
    result = refs[-1]
    for number, block in enumerate(refs[:-1]):

        @pl.when(pl.program_id(0) == number)
        def _():
            result[...] = block[...]


def stacked(blocks):
    rows, width = blocks[0].shape
    return pl.pallas_call(
        stack_kernel,
        grid=(len(blocks),),
        in_specs=[pl.BlockSpec((rows, width), lambda i: (0, 0))] * len(blocks),
        out_specs=pl.BlockSpec((rows, width), lambda i: (i, 0)),
        out_shape=jax.ShapeDtypeStruct((len(blocks) * rows, width), blocks[0].dtype),
        compiler_params=PARAMS,
        cost_estimate=pl.CostEstimate(flops=0, bytes_accessed=2 << 20, transcendentals=0),
        name="stacked",
    )(*blocks)


def rope_tables(positions):
    half_dim = HEAD_DIM // 2
    inverse = 1.0 / ROPE_BASE ** (jnp.arange(half_dim, dtype=jnp.float32) * 2.0 / HEAD_DIM)
    angles = inverse[:, None] * positions.astype(jnp.float32)[None, :]
    return jnp.cos(angles), jnp.sin(angles)


def bounds_kernel(ids, starts, ends, ranges):
    shape = (8, ids.shape[1])
    width = ids.shape[1]
    own = jnp.broadcast_to(ids[...], shape)
    index = lax.broadcasted_iota(jnp.int32, shape, 1)
    first = jnp.where((own != pltpu.roll(own, 1, 1)) | (index == 0), index, 0)
    after = jnp.where((own != pltpu.roll(own, width - 1, 1)) | (index == width - 1), index + 1, width)
    shift = 1
    while shift < SPAN:
        first = jnp.maximum(first, jnp.where(index >= shift, pltpu.roll(first, shift, 1), 0))
        after = jnp.minimum(
            after, jnp.where(index < width - shift, pltpu.roll(after, width - shift, 1), width)
        )
        shift *= 2
    rows = starts.shape[1]
    starts[...] = first[:1, SPAN : SPAN + rows]
    ends[...] = after[:1, SPAN : SPAN + rows]
    lane = lax.broadcasted_iota(jnp.int32, (rows, ranges.shape[1]), 0)
    entry = lax.broadcasted_iota(jnp.int32, (rows, ranges.shape[1]), 1)
    own_lane = entry // 2 * TILE + lax.rem(entry, 2) * (TILE - 1)
    chosen = jnp.where(lane == own_lane, 1.0, 0.0)
    odd = lax.rem(entry, 2) == 1
    begin = (first[:, SPAN : SPAN + rows] // TILE).astype(jnp.bfloat16)
    end = ((after[:, SPAN : SPAN + rows] + TILE - 1) // TILE).astype(jnp.bfloat16)
    from_begin = jnp.where(odd, 0.0, chosen).astype(jnp.bfloat16)
    from_end = jnp.where(odd, chosen, 0.0).astype(jnp.bfloat16)
    found = jnp.dot(begin, from_begin, preferred_element_type=jnp.float32) + jnp.dot(
        end, from_end, preferred_element_type=jnp.float32
    )
    ranges[...] = found[:1].astype(jnp.int32)


def document_bounds(window_ids, rows):
    return pl.pallas_call(
        bounds_kernel,
        out_shape=[jax.ShapeDtypeStruct((1, rows), jnp.int32)] * 2
        + [jax.ShapeDtypeStruct((1, 128), jnp.int32)],
        compiler_params=PARAMS,
        cost_estimate=pl.CostEstimate(flops=1 << 34, bytes_accessed=0, transcendentals=0),
        name="document_bounds",
    )(window_ids[None, :])


def per_device(tokens, norm_gain, input_weight, output_weight, segment_ids, page_owner):
    rows, model_width = tokens.shape
    peers, members = lax.axis_size("tok"), lax.axis_size("grp")
    place, column = lax.axis_index("tok"), lax.axis_index("grp")
    low = place % PAIR
    blocks = PAIR * members
    member = low * members + column
    group_rows = rows * blocks
    width = model_width // blocks
    pages = rows // PAGE

    flat = peers * members
    owners = page_owner[:, 0]
    capacity = max(2, (2 * pages + peers - 1) // peers)
    halves = []
    for parity in range(PAIR):
        pieces = []
        for number in range(PARTS):
            start = number * PAIR * width
            choices = [input_weight[:, start : start + width], input_weight[:, start + width : start + 2 * width]]
            piece = jnp.where((low ^ parity) == 0, choices[0], choices[1])
            route = []
            for source in range(flat):
                row, column_from = divmod(source, members)
                target = (row ^ parity) * members + (PARTS * column_from + number) % members
                route.append((source, target))
            pieces.append(lax.ppermute(piece, ("tok", "grp"), route))
        halves.append(jnp.concatenate(pieces, axis=1))
    plane = jnp.concatenate(halves, axis=0)
    own = layer_norm(tokens, norm_gain[None, :], owners, capacity)
    own, plane = lax.optimization_barrier((own, plane))

    across, along = flipped(own, "grp", 2), flipped(own, "tok", 1)
    sibling = flipped(own, "grp", 1)
    planes = {0: plane}
    bit = peers // 2
    while bit > 1:
        planes[bit] = flipped(plane, "tok", bit)
        bit //= 2
    for distance in range(PAIR, peers, PAIR):
        if distance not in planes:
            step_bit = distance & -distance
            planes[distance] = flipped(planes[distance ^ step_bit], "tok", step_bit)
    weights = [planes[distance] for distance in range(0, peers, PAIR)]

    first_row = place // PAIR * group_rows
    segment_ids, plane = lax.optimization_barrier((segment_ids, plane))
    padded_ids = jnp.concatenate(
        [
            jnp.full((SPAN,), -1, jnp.int32),
            segment_ids,
            jnp.full((SPAN,), 1 << 30, jnp.int32),
        ]
    )
    window_ids = lax.dynamic_slice_in_dim(padded_ids, first_row, group_rows + 2 * SPAN, 0)
    *bounds, ranges = document_bounds(window_ids, group_rows)
    positions = SPAN + jnp.arange(group_rows, dtype=jnp.int32) - bounds[0][0]
    order = [(number * members + column) % PARTS for number in range(PARTS)]
    meta = jnp.stack([member, place] + order).astype(jnp.int32)
    cosine, sine = rope_tables(positions)
    last_rows = output_weight
    bit = PAIR
    while 4 * bit < peers:
        last_rows = jnp.concatenate([last_rows, flipped(last_rows, "tok", bit)], axis=0)
        bit *= 2
    other_rows = flipped(last_rows, "tok", bit)
    across, along, sibling, weights, last_rows, other_rows, cosine, sine, meta = (
        lax.optimization_barrier(
            (across, along, sibling, weights, last_rows, other_rows, cosine, sine, meta)
        )
    )
    last_rows = jnp.concatenate([last_rows, other_rows], axis=0)

    half, held = rows // 2, rows + EXTRA_ROWS
    corner = [flipped(across[:half], "tok", 1), flipped(along[half:], "grp", 2)]
    across_sibling = flipped(across, "grp", 1)
    along_sibling = flipped(along, "grp", 1)
    other_rows = flipped(last_rows, "tok", peers // 2)
    near_blocks = [own, sibling, across, across_sibling]
    near_layout = [[(number, 0, held)] for number in range(4)]
    far_layout = [[(0, 0, held)], [(1, 0, held)]]
    far_layout += [[(number, 0, half), (number + 1, half, held - half)] for number in (2, 4)]

    sizes = (weights, cosine, sine, rows, blocks, peers, capacity)

    def to_owners(send):
        received = lax.all_to_all(
            send.reshape((flat,) + send.shape[2:]),
            ("tok", "grp"),
            split_axis=0,
            concat_axis=0,
            tiled=True,
        )
        return received.reshape((peers // PAIR, PAIR, members) + send.shape[2:])

    queries, pairs, send = project(meta, 0, near_layout, near_blocks, *sizes, ())
    send, corner, along_sibling, last_rows, other_rows = lax.optimization_barrier(
        (send, corner, along_sibling, last_rows, other_rows)
    )
    own_row = to_owners(send)
    corner_sibling = [flipped(block, "grp", 1) for block in corner]
    far_blocks = [along, along_sibling] + corner + corner_sibling
    last_rows = jnp.concatenate([last_rows, other_rows], axis=0)
    queries, pairs, send = project(meta, 4, far_layout, far_blocks, *sizes, (queries, pairs))
    before = shifted(pairs[group_rows - SPAN :], "tok", PAIR)
    after = shifted(pairs[:SPAN], "tok", -PAIR)
    other_rows = flipped(last_rows, "tok", 1)
    across_rows = flipped(last_rows, "grp", 2)
    corner_rows = lax.ppermute(
        last_rows,
        ("tok", "grp"),
        [(source, source ^ (members + 2)) for source in range(flat)],
    )

    edges = attend_edges(meta, ranges, queries, *bounds, pairs)
    before, after, edges, last_rows, other_rows, across_rows, corner_rows, send = (
        lax.optimization_barrier(
            (before, after, edges, last_rows, other_rows, across_rows, corner_rows, send)
        )
    )
    other_row = to_owners(send)
    columns = stacked([last_rows, other_rows, across_rows, corner_rows])
    row_order = place
    if output_weight.shape[0] != width:
        wanted = jnp.arange(peers) ^ place
        wanted = wanted // PAIR + wanted % PAIR * (peers // PAIR)
        shards = columns.reshape((PAIR, peers) + output_weight.shape)
        columns = shards[:, wanted].reshape(columns.shape)
        row_order = jnp.full_like(place, -1)
    mixed = attend_finish(meta, ranges, queries, *bounds, pairs, before, after, edges, rows)
    last_weights = [columns, flipped(columns, "grp", 1)]
    parts = [mixed[0]] + [
        lax.ppermute(
            mixed[distance],
            ("tok", "grp"),
            [(source, source ^ distance) for source in range(flat)],
        )
        for distance in range(1, blocks)
    ]
    output_meta = jnp.stack([member, row_order]).astype(jnp.int32)
    attended, cache_pages = outputs(output_meta, parts, last_weights, own_row, other_row)
    cache_pages = cache_pages.reshape(peers * capacity, 2 * PAGE * model_width)
    return attended, cache_pages


def solution(mesh):
    placed = (
        P(("tok", "grp"), None),
        P(),
        P("tok", "grp"),
        P("tok", "grp"),
        P(),
        P(("tok", "grp"), None),
    )
    return jax.shard_map(
        per_device,
        mesh=mesh,
        in_specs=placed,
        out_specs=(P(("tok", "grp"), None), P(("tok", "grp"), None)),
        check_vma=False,
    )
```
